32 devices in a mesh: mol: 2 (over x), orb: 8 (over z, y), aux: 2 (over core).
Axes of the slice: x: 2, y: 2, z: 4, core: 2. Of those that a mesh axis runs over, the one named last changes fastest.
Arguments:
- blocks: bfloat16 [256, 512, 256], P(('mol', 'orb'), 'aux'), parts along dimension 0, may hold values from -1.5 to 1.5
- vir_energy: float32 [256, 256], P(('mol', 'orb')), parts along dimension 0, may hold values from 0.5 to 3
- occ_energy: float32 [256], P(('mol', 'orb')), parts along dimension 0, may hold values from -1.5 to -0.3
- domain_size: int32 [256], P(('mol', 'orb')), parts along dimension 0, may hold values from 128 to 256, as said below
- partner_owner: int32 [1024, 1], P(('mol', 'orb')), parts along dimension 0, may hold values from 0 to 7; in each aligned block of 64 rows (0 to 63, 64 to 127, ...) at most 8 rows name the same one
- partner_slot: int32 [1024], P(('mol', 'orb')), parts along dimension 0, may hold values from 0 to 15
Outputs:
- pair_energy: float32 [1024], P(('mol', 'orb')), parts along dimension 0
- density: float32 [256, 256, 256], P(('mol', 'orb'), 'aux'), parts along dimension 0
The draws below stay inside these ranges and needn't reach their ends.
There are 2 independent parts, one for each index of `mol`. The reference program is written for one: setup_inputs(seed, part) draws one part's arguments, and reference() takes and returns one part's arrays. A program takes and returns all parts, laid end to end along the dimension named above; each array names one. Nothing has to cross between parts.
Inputs may be any that keep to these rules, and one draw needn't show every extreme that they name: `partner_owner`: among the 64 pairs of one device no owner is named more than 8 times, a bound that some block reaches. `domain_size`: some orbital's domain is full.
All inputs are finite; a program needn't handle non-finite values.
Results may differ from the reference program's by a relative error of at most 0.0019.
Values may be sent and summed in bfloat16 or wider, within the bound.
No kernel may reach another device: no remote copies, remote signals or barrier semaphores. Data moves between devices by JAX's collectives and lax.ppermute only.
A program may use at most 128 MiB of HBM per device.

```python
import math
import jax
import jax.numpy as jnp
import numpy as np
from jax import lax

NVD = 256
NAUXD = 512
OCC_DEV = 16
PER_ORB = 4
PAIR_DEV = 64
CAP = 8
NOCC = 128
NPAIR = 512
N_ORB = 8


def draw_domain_size(key, part):
    key = jax.random.fold_in(key, 11)
    key_vals, key_pos = jax.random.split(key)
    values = jax.random.randint(key_vals, (NOCC,), NVD // 2, NVD + 1, dtype=jnp.int32)
    where_full = jax.random.randint(key_pos, (), 0, NOCC, dtype=jnp.int32)
    values = values.at[where_full].set(NVD)
    values = values.at[(where_full + 1) % NOCC].set(NVD // 2)
    return values


def touch_ends(array, stream_key, low, largest):
    dims = array.shape
    index_at = [jax.random.randint(jax.random.fold_in(stream_key, axis), (), 0, dims[axis]) for axis in range(len(dims))]
    array = array.at[tuple(index_at)].set(low)
    longest = dims.index(max(dims))
    index_at[longest] = (index_at[longest] + 1) % dims[longest]
    return array.at[tuple(index_at)].set(largest)


def shard_levels(rng, shape, cuts, low, top_value):
    def one(position, shards_of):
        heights = jax.random.uniform(jax.random.fold_in(jax.random.fold_in(rng, 6), position), (shards_of,), jnp.float32, low / len(cuts), top_value / len(cuts))
        return jnp.repeat(jnp.exp(heights), shape[position] // shards_of).reshape((-1,) + (1,) * (len(shape) - position - 1))

    level = one(*cuts[0])
    for cut in cuts[1:]:
        level = level * one(*cut)
    return level


def shared_out(key, own, number, rows, amount, top, most, skew):
    ranking = jax.random.permutation(key, amount)
    crowded, common = portions_of(amount, rows * top, most, skew, True), portions_of(amount, rows * top, most, skew, False)
    places = jnp.arange(amount)

    def named(tallies, offset_by):
        used = int((tallies > 0).sum())
        fixed = max(1, used // 4)
        moved = fixed + (places - fixed + offset_by * (used - fixed)) % max(1, amount - fixed)
        return jnp.zeros((amount,), jnp.int32).at[ranking[jnp.where(places < fixed, places, moved)]].set(jnp.asarray(tallies, jnp.int32))

    tallies = jnp.where(number % 4 == 0, named(crowded, number // 4), named(common, number - number // 4 - 1))
    mixed = jax.random.permutation(jax.random.fold_in(own, 3), amount)
    source_of, receiver = mixed[0:amount // 2 * 2:2], mixed[1:amount // 2 * 2:2]
    slack = jnp.minimum(tallies[source_of] - 1, most - tallies[receiver]) // 2
    slack = jnp.where((source_of == ranking[0]) | (receiver == ranking[0]) | (tallies[receiver] == 0), 0, jnp.maximum(slack, 0))
    moved = jax.random.randint(jax.random.fold_in(own, 4), (amount // 2,), 0, 1 << 20) % (slack + 1)
    tallies = tallies.at[source_of].add(-moved).at[receiver].add(moved)
    members = jnp.searchsorted(jnp.cumsum(tallies), jnp.arange(rows * top), side="right").astype(jnp.int32)
    listing = members.reshape(top, rows).T
    listing = listing[jax.random.permutation(jax.random.fold_in(own, 1), rows)]
    offset_by = jax.random.randint(jax.random.fold_in(own, 2), (rows, 1), 0, top)
    return jnp.take_along_axis(listing, (jnp.arange(top)[None, :] + offset_by) % top, axis=1)


def portions_of(amount, total, most, skew, full):
    loads = [(1 << 20) // math.isqrt(grade ** skew) + 1 for grade in range(1, amount + 1)]
    largest = most if full else min(most, max(-(-total // amount), total * loads[0] // sum(loads)))
    least = 1 if total - largest >= amount - 1 else 0
    holding, surplus = [largest] + [least] * (amount - 1), total - largest - least * (amount - 1)
    while surplus > 0:
        free = [i for i in range(1, amount) if holding[i] < largest] or [i for i in range(1, amount) if holding[i] < most]
        pool, budget = sum([loads[i] for i in free]), surplus
        for i in free:
            extra = min(most - holding[i], max(1, budget * loads[i] // pool), surplus)
            holding[i] = holding[i] + extra
            surplus = surplus - extra
    return np.array(holding)


def centred(own_key, shape, scale, most, shards=(), kind=jnp.bfloat16):
    array = jax.random.normal(own_key, shape, jnp.float32) * scale
    if len(shards) > 0:
        array = shard_levels(own_key, shape, shards, -0.22, 0.18) * array
    return jnp.clip(array, min=-most, max=most).astype(kind)


def setup_inputs(seed: int = 0, part: int = 0) -> dict:
    key_of = jax.random.split(jax.random.key(seed), 7)
    own_keys = jax.random.split(jax.random.fold_in(key_of[6], part), 7)
    blocks = centred(own_keys[0], (NOCC, NAUXD, NVD), (0.5 * NAUXD ** -0.25), 1.5, ((0, 8), (1, 2)))
    vir_energy = jnp.clip(0.5 + 2.5 * jax.random.uniform(own_keys[1], (NOCC, NVD), jnp.float32) ** shard_levels(own_keys[1], (NOCC, NVD), ((0, 8),), -0.2, 0.2), 0.5, 3.0)
    occ_energy = jnp.clip(-1.5 + 1.2 * jax.random.uniform(own_keys[2], (NOCC,), jnp.float32) ** shard_levels(own_keys[2], (NOCC,), ((0, 8),), -0.2, 0.2), -1.5, -0.3)
    domain_size = draw_domain_size(jax.random.fold_in(jax.random.fold_in(key_of[6], part), 71), part)
    partner_owner_keys = jax.random.split(jax.random.fold_in(own_keys[4], 1), NPAIR // PAIR_DEV)
    partner_owner_turns = jax.random.permutation(jax.random.fold_in(own_keys[4], 3), NPAIR // PAIR_DEV)
    partner_owner = jax.vmap(lambda own, number: shared_out(jax.random.fold_in(own_keys[4], 2), own, number, PAIR_DEV, N_ORB, 1, CAP, 2))(partner_owner_keys, partner_owner_turns).reshape((NPAIR, 1))
    partner_slot = touch_ends(jax.random.randint(own_keys[5], (NPAIR,), 0, OCC_DEV), jax.random.fold_in(own_keys[5], 1), 0, OCC_DEV - 1).astype(jnp.int32)
    return {"blocks": blocks, "vir_energy": vir_energy, "occ_energy": occ_energy, "domain_size": domain_size, "partner_owner": partner_owner, "partner_slot": partner_slot}


def reference(blocks, vir_energy, occ_energy, domain_size, partner_owner, partner_slot):
    npair = partner_slot.shape[0]
    order = jnp.arange(npair, dtype=jnp.int32)
    first = (order // PAIR_DEV) * OCC_DEV + (order % PAIR_DEV) // PER_ORB
    second = partner_owner[:, 0] * OCC_DEV + partner_slot
    cols = jnp.arange(NVD, dtype=jnp.int32)

    def group(items):
        first_ids, second_ids = items
        left = blocks[first_ids].astype(jnp.float32)
        right = blocks[second_ids].astype(jnp.float32)
        kmat = jnp.einsum('pqa,pqb->pab', left, right)
        mask = (cols[None, :, None] < domain_size[first_ids][:, None, None]) & (cols[None, None, :] < domain_size[second_ids][:, None, None])
        kmat = jnp.where(mask, kmat, jnp.zeros_like(kmat))
        gap = vir_energy[first_ids][:, :, None] + vir_energy[second_ids][:, None, :] - occ_energy[first_ids][:, None, None] - occ_energy[second_ids][:, None, None]
        amp = (-kmat / gap).astype(jnp.bfloat16)
        ampf = amp.astype(jnp.float32)
        energy = jnp.sum(kmat * ampf, axis=(1, 2)) / NVD
        dens_pair = jnp.einsum('pab,pcb->pac', ampf, ampf)
        dens = dens_pair.reshape(OCC_DEV, PER_ORB, NVD, NVD).sum(axis=1)
        return energy, dens

    energy, dens = lax.map(group, (first.reshape(N_ORB, PAIR_DEV), second.reshape(N_ORB, PAIR_DEV)))
    return energy.reshape(npair), dens.reshape(NOCC, NVD, NVD)
```

```python
import jax
import jax.numpy as jnp
from jax import lax
from jax.experimental import pallas as pl
from jax.experimental.pallas import tpu as pltpu
from jax.sharding import PartitionSpec as P

f32, bf16, i32 = jnp.float32, jnp.bfloat16, jnp.int32
ANY = pl.BlockSpec(memory_space=pl.ANY)
SMEM = pl.BlockSpec(memory_space=pltpu.SMEM)
VMEM = pl.BlockSpec(memory_space=pltpu.VMEM)
LIMIT = 48 * 1024 * 1024


def slot_ranks(owner):
    count = owner.shape[0]
    order = jnp.arange(count, dtype=jnp.int32)
    same = (owner[:, None] == owner[None, :]) & (order[None, :] < order[:, None])
    return jnp.sum(same.astype(jnp.int32), axis=1)


def by_requests(blocks, vir_energy, occ_energy, domain_size, partner_owner, partner_slot):
    occ_dev, half_aux, nvd = blocks.shape
    pair_dev = partner_slot.shape[0]
    per_orb = pair_dev // occ_dev
    peers = lax.axis_size("orb")
    cap = max(2, (pair_dev + peers - 1) // peers)
    owner = partner_owner[:, 0]
    ranks = slot_ranks(owner)
    target = owner * cap + ranks
    wanted = (target[:, None] == jnp.arange(peers * cap, dtype=jnp.int32)[None, :]).astype(
        jnp.int32
    )
    requests = jnp.sum(wanted * partner_slot[:, None], axis=0).reshape(peers, cap)
    incoming = lax.all_to_all(requests, "orb", split_axis=0, concat_axis=0, tiled=True)
    flat_in = incoming.reshape(-1)
    send_blocks = jnp.take(blocks, flat_in, axis=0).reshape(peers, cap, half_aux, nvd)
    send_vir = jnp.take(vir_energy, flat_in, axis=0).reshape(peers, cap, nvd)
    send_occ = jnp.take(occ_energy, flat_in).reshape(peers, cap)
    send_size = jnp.take(domain_size, flat_in).astype(jnp.float32).reshape(peers, cap)
    got_blocks = lax.all_to_all(send_blocks, "orb", split_axis=0, concat_axis=0, tiled=True)
    got_vir, got_occ, got_size = (
        lax.all_to_all(send_vir, "orb", split_axis=0, concat_axis=0, tiled=True),
        lax.all_to_all(send_occ, "orb", split_axis=0, concat_axis=0, tiled=True),
        lax.all_to_all(send_size, "orb", split_axis=0, concat_axis=0, tiled=True),
    )
    partner = jnp.take(got_blocks.reshape(peers * cap, half_aux, nvd), target, axis=0).reshape(
        occ_dev, per_orb, half_aux, nvd
    )
    partner_vir = jnp.take(got_vir.reshape(peers * cap, nvd), target, axis=0).reshape(
        occ_dev, per_orb, nvd
    )
    partner_occ = jnp.take(got_occ.reshape(-1), target).reshape(occ_dev, per_orb)
    partner_size = jnp.take(got_size.reshape(-1), target).reshape(occ_dev, per_orb)
    half = nvd // lax.axis_size("aux")
    integrals = lax.psum_scatter(
        jnp.einsum("oqa,opqb->aopb", blocks, partner, preferred_element_type=jnp.float32),
        "aux",
        scatter_dimension=0,
        tiled=True,
    )
    row_start = lax.axis_index("aux") * half
    rows = row_start + jnp.arange(half, dtype=jnp.int32)
    cols = jnp.arange(nvd, dtype=jnp.int32).astype(jnp.float32)
    mask = (rows[:, None, None, None] < domain_size[None, :, None, None]) & (
        cols[None, None, None, :] < partner_size[None, :, :, None]
    )
    integrals = jnp.where(mask, integrals, jnp.zeros_like(integrals))
    vir_rows = lax.dynamic_slice_in_dim(vir_energy, row_start, half, 1)
    gap = (
        vir_rows.T[:, :, None, None]
        + partner_vir[None, :, :, :]
        - occ_energy[None, :, None, None]
        - partner_occ[None, :, :, None]
    )
    amp_rows = (-integrals / gap).astype(jnp.bfloat16)
    partial_energy = jnp.sum(integrals * amp_rows.astype(jnp.float32), axis=(0, 3))
    energy = lax.psum(partial_energy, "aux").reshape(pair_dev) / nvd
    density = jnp.einsum(
        "aopb,copb->oac",
        amp_rows,
        lax.all_gather(amp_rows, "aux", axis=0, tiled=True),
        preferred_element_type=jnp.float32,
    )
    return (energy, density)


def fits_line(mesh):
    return mesh.shape["orb"] == 8 and mesh.shape["aux"] == 2


def table_of(bases, fields):
    return jnp.concatenate([bases] + fields).astype(i32)


def pack_kernel(call, cap, count, tbl, x, out, sems):
    base = tbl[call]
    copies = []
    for r in range(cap):
        slot = tbl[8 + base + r]
        copies.append(pltpu.make_async_copy(x.at[slot], out.at[r], sems.at[r]))
        copies[-1].start()
    for copy in copies:
        copy.wait()


def pack(tbl, call, x, cap):
    return pl.pallas_call(
        lambda *refs: pack_kernel(call, cap, 64, *refs),
        out_shape=jax.ShapeDtypeStruct((cap,) + x.shape[1:], x.dtype),
        in_specs=[SMEM, ANY],
        out_specs=ANY,
        scratch_shapes=[pltpu.SemaphoreType.DMA((cap,))],
        compiler_params=pltpu.CompilerParams(vmem_limit_bytes=LIMIT),
        cost_estimate=pl.CostEstimate(
            flops=0, bytes_accessed=2 * cap * x.shape[1] * x.shape[2] * 2, transcendentals=0
        ),
        name="pack",
    )(tbl, x)


def amplitudes_kernel(
    call, by_slot, per_orb, tbl, rows, vcol, a0, a1, j0, j1, tin, tout, energy,
    sv, s0, s1, b0, b1, st, sem, sem_out,
):
    cap = sv.shape[0]
    n = rows.shape[0]
    base = tbl[call]
    loads = []
    for r in range(cap):
        p = tbl[8 + base + r]
        i = lax.div(p, per_orb)
        slot = tbl[8 + n + base + r] if by_slot else r
        pairs = (
            (vcol.at[i], sv.at[r]),
            (a0.at[i], s0.at[r]),
            (a1.at[i], s1.at[r]),
            (j0.at[slot], b0.at[r]),
            (j1.at[slot], b1.at[r]),
        )
        group = []
        for k, (source, target) in enumerate(pairs):
            copy = pltpu.make_async_copy(source, target, sem.at[r, k])
            copy.start()
            group.append(copy)
        loads.append(group)
    nvd, half = sv.shape[1], sv.shape[2]
    live_a = lax.broadcasted_iota(i32, (nvd, half), 0)
    live_b = lax.broadcasted_iota(i32, (nvd, half), 1)
    row8 = rows[pl.ds(pl.multiple_of(base, cap), cap), :]
    stores = []
    for r in range(cap):
        p = tbl[8 + base + r]
        size_i = tbl[8 + 2 * n + base + r]
        size_j = tbl[8 + 3 * n + base + r]
        for copy in loads[r]:
            copy.wait()
        k = jnp.dot(s0[r], b0[r], preferred_element_type=f32)
        k += jnp.dot(s1[r], b1[r], preferred_element_type=f32)
        k = jnp.where((live_a < size_i) & (live_b < size_j), k, 0.0)
        gap = sv[r] + row8[r : r + 1, :]
        t = (-k / gap).astype(bf16)
        st[r] = t
        copy = pltpu.make_async_copy(st.at[r], tout.at[p], sem_out.at[r])
        copy.start()
        stores.append(copy)
        energy[r] = jnp.sum((k * t.astype(f32)).reshape(nvd // 8, 8, half), axis=0)
    for copy in stores:
        copy.wait()


def amplitudes(call, by_slot, per_orb, tbl, rows, vcol, a0, a1, j0, j1, t_all, cap):
    nvd, half = vcol.shape[1:]
    qa = j0.shape[1]
    return pl.pallas_call(
        lambda *refs: amplitudes_kernel(call, by_slot, per_orb, *refs),
        out_shape=(
            jax.ShapeDtypeStruct(t_all.shape, t_all.dtype),
            jax.ShapeDtypeStruct((cap, 8, half), f32),
        ),
        in_specs=[SMEM, VMEM, ANY, ANY, ANY, ANY, ANY, ANY],
        out_specs=(ANY, VMEM),
        scratch_shapes=[
            pltpu.VMEM((cap, nvd, half), f32),
            pltpu.VMEM((cap, nvd, qa), bf16),
            pltpu.VMEM((cap, nvd, qa), bf16),
            pltpu.VMEM((cap, qa, half), bf16),
            pltpu.VMEM((cap, qa, half), bf16),
            pltpu.VMEM((cap, nvd, half), bf16),
            pltpu.SemaphoreType.DMA((cap, 5)),
            pltpu.SemaphoreType.DMA((cap,)),
        ],
        input_output_aliases={7: 0},
        compiler_params=pltpu.CompilerParams(vmem_limit_bytes=LIMIT),
        cost_estimate=pl.CostEstimate(
            flops=cap * 4 * nvd * qa * half,
            bytes_accessed=cap * (nvd * half * 6 + 4 * nvd * qa + 4 * qa * half),
            transcendentals=0,
        ),
        name="amplitudes",
    )(tbl, rows, vcol, a0, a1, j0, j1, t_all)


def density_kernel(start, t, d):
    half = d.shape[1]
    first = pl.multiple_of(start[0], half)
    left = jnp.concatenate([t[k, pl.ds(first, half), :] for k in range(t.shape[0])], axis=1)
    right = jnp.concatenate([t[k] for k in range(t.shape[0])], axis=1)
    d[0] = lax.dot_general(left, right, (((1,), (1,)), ((), ())), preferred_element_type=f32)


def density_rows(t_all, start, per_orb, half):
    npair, nvd, width = t_all.shape
    occ = npair // per_orb
    return pl.pallas_call(
        density_kernel,
        out_shape=jax.ShapeDtypeStruct((occ, half, nvd), f32),
        grid_spec=pltpu.PrefetchScalarGridSpec(
            num_scalar_prefetch=1,
            grid=(occ,),
            in_specs=[pl.BlockSpec((per_orb, nvd, width), lambda i, s: (i, 0, 0))],
            out_specs=pl.BlockSpec((1, half, nvd), lambda i, s: (i, 0, 0)),
        ),
        compiler_params=pltpu.CompilerParams(vmem_limit_bytes=LIMIT),
        cost_estimate=pl.CostEstimate(
            flops=2 * npair * half * nvd * width,
            bytes_accessed=npair * nvd * width * 2 + occ * half * nvd * 4,
            transcendentals=0,
        ),
        name="density_rows",
    )(start.reshape(1), t_all)


def line_plan(blocks, vir_energy, occ_energy, domain_size, partner_owner, partner_slot):
    occ, qa, nvd = blocks.shape
    pair_dev = partner_slot.shape[0]
    per_orb = pair_dev // occ
    peers = 8
    cap = pair_dev // peers
    half = nvd // 2
    me, core = lax.axis_index("orb"), lax.axis_index("aux")
    z, y = me // 2, me % 2
    middle = (z == 1) | (z == 2)
    swap_core = [(0, 1), (1, 0)]
    swap_y = [(o, o ^ 1) for o in range(peers)]
    swap_half = [(o, o ^ 2) for o in range(peers)]
    cross = [(2, 4), (3, 5), (4, 2), (5, 3)]
    outward = [(2, 0), (3, 1), (4, 6), (5, 7)]

    other = lax.ppermute(blocks, "aux", swap_core)
    col0 = core * half
    own = [lax.dynamic_slice_in_dim(x, col0, half, 2) for x in (blocks, other)]

    owner = partner_owner[:, 0]
    target = owner * cap + slot_ranks(owner)
    hit = target[None, :] == jnp.arange(pair_dev, dtype=i32)[:, None]
    pairs = jnp.arange(pair_dev, dtype=i32)
    order = jnp.sum(jnp.where(hit, pairs[None, :], 0), axis=1)
    slots = jnp.sum(jnp.where(hit, partner_slot[None, :], 0), axis=1)
    small = jnp.concatenate(
        [
            vir_energy,
            occ_energy[:, None],
            domain_size.astype(f32)[:, None],
            jnp.zeros((occ, 126), f32),
        ],
        axis=1,
    )
    every = lax.all_gather(small, "orb", axis=0, tiled=True)
    theirs = jnp.take(every, (pairs // cap) * occ + slots, axis=0)
    mine = jnp.take(small, order // per_orb, axis=0)
    rows = lax.dynamic_slice_in_dim(theirs, col0, half, 1) - (
        theirs[:, nvd : nvd + 1] + mine[:, nvd : nvd + 1]
    )
    size_i = mine[:, nvd + 1].astype(i32)
    size_j = theirs[:, nvd + 1].astype(i32) - col0
    lower = z < 2
    column = jnp.stack([z, z ^ 1, jnp.where(lower, 2, 1), jnp.where(lower, 3, 0)])
    bases = jnp.concatenate([column * 2 + y, column * 2 + (1 - y)]) * cap
    tbl = table_of(bases, [order, slots, size_i, size_j])
    wanted = table_of(bases, [lax.ppermute(slots, "orb", swap_y)])
    vcol = jnp.broadcast_to(vir_energy[:, :, None], (occ, nvd, half))
    left = [jnp.swapaxes(x, 1, 2) for x in (blocks, other)]

    near = [lax.ppermute(x, "orb", swap_half) for x in own]
    mid = [lax.ppermute(x, "orb", cross) for x in own]
    mid_out = [lax.ppermute(x, "orb", outward) for x in mid]
    far = [lax.ppermute(x, "orb", cross) for x in near]
    far_out = [lax.ppermute(x, "orb", outward) for x in far]
    third = [jnp.where(middle, a, b) for a, b in zip(mid, mid_out)]
    fourth = [jnp.where(middle, a, b) for a, b in zip(far, far_out)]
    sources = [own, near, third, fourth]
    beside = [
        [lax.ppermute(pack(wanted, k, x, cap), "orb", swap_y) for x in source]
        for k, source in enumerate(sources)
    ]

    t_all = jnp.zeros((pair_dev, nvd, half), bf16)
    energies = [None] * 8
    for k in (0, 1, 4, 2, 5, 3, 6, 7):
        j0, j1 = sources[k] if k < 4 else beside[k - 4]
        t_all, energies[k] = amplitudes(
            k, k < 4, per_orb, tbl, rows, vcol, left[0], left[1], j0, j1, t_all, cap
        )
    away = lax.ppermute(density_rows(t_all, (1 - core) * half, per_orb, half), "aux", swap_core)
    density = density_rows(t_all, core * half, per_orb, half) + away

    sums = jnp.sum(jnp.stack(energies), axis=(2, 3)).reshape(pair_dev)
    place = (bases[:, None] + jnp.arange(cap, dtype=i32)[None, :]).reshape(pair_dev)
    spot = target[:, None] == place[None, :]
    energy = lax.psum(jnp.sum(jnp.where(spot, sums[None, :], 0.0), axis=1), "aux") / nvd
    return (energy, density)


def solution(mesh):
    in_specs = (
        P(("mol", "orb"), "aux", None),
        P(("mol", "orb"), None),
        P(("mol", "orb")),
        P(("mol", "orb")),
        P(("mol", "orb"), None),
        P(("mol", "orb")),
    )
    out_specs = (P(("mol", "orb")), P(("mol", "orb"), "aux", None))
    return jax.shard_map(
        line_plan if fits_line(mesh) else by_requests, mesh=mesh, in_specs=in_specs, out_specs=out_specs, check_vma=False
    )
```

```python
import jax
import jax.numpy as jnp
from jax import lax
from jax.experimental import pallas as pl
from jax.experimental.pallas import tpu as pltpu
from jax.sharding import PartitionSpec as P

f32, bf16, i32 = jnp.float32, jnp.bfloat16, jnp.int32
HBM = pl.BlockSpec(memory_space=pltpu.HBM)
SMEM = pl.BlockSpec(memory_space=pltpu.SMEM)
VMEM = pl.BlockSpec(memory_space=pltpu.VMEM)
LIMIT = 48 * 1024 * 1024


def slot_ranks(owner):
    count = owner.shape[0]
    order = jnp.arange(count, dtype=jnp.int32)
    same = (owner[:, None] == owner[None, :]) & (order[None, :] < order[:, None])
    return jnp.sum(same.astype(jnp.int32), axis=1)


def by_requests(blocks, vir_energy, occ_energy, domain_size, partner_owner, partner_slot):
    occ_dev, half_aux, nvd = blocks.shape
    pair_dev = partner_slot.shape[0]
    per_orb = pair_dev // occ_dev
    peers = lax.axis_size("orb")
    cap = max(2, (pair_dev + peers - 1) // peers)
    owner = partner_owner[:, 0]
    ranks = slot_ranks(owner)
    target = owner * cap + ranks
    wanted = (target[:, None] == jnp.arange(peers * cap, dtype=jnp.int32)[None, :]).astype(
        jnp.int32
    )
    requests = jnp.sum(wanted * partner_slot[:, None], axis=0).reshape(peers, cap)
    incoming = lax.all_to_all(requests, "orb", split_axis=0, concat_axis=0, tiled=True)
    flat_in = incoming.reshape(-1)
    send_blocks = jnp.take(blocks, flat_in, axis=0).reshape(peers, cap, half_aux, nvd)
    send_vir = jnp.take(vir_energy, flat_in, axis=0).reshape(peers, cap, nvd)
    send_occ = jnp.take(occ_energy, flat_in).reshape(peers, cap)
    send_size = jnp.take(domain_size, flat_in).astype(jnp.float32).reshape(peers, cap)
    got_blocks = lax.all_to_all(send_blocks, "orb", split_axis=0, concat_axis=0, tiled=True)
    got_vir, got_occ, got_size = (
        lax.all_to_all(send_vir, "orb", split_axis=0, concat_axis=0, tiled=True),
        lax.all_to_all(send_occ, "orb", split_axis=0, concat_axis=0, tiled=True),
        lax.all_to_all(send_size, "orb", split_axis=0, concat_axis=0, tiled=True),
    )
    partner = jnp.take(got_blocks.reshape(peers * cap, half_aux, nvd), target, axis=0).reshape(
        occ_dev, per_orb, half_aux, nvd
    )
    partner_vir = jnp.take(got_vir.reshape(peers * cap, nvd), target, axis=0).reshape(
        occ_dev, per_orb, nvd
    )
    partner_occ = jnp.take(got_occ.reshape(-1), target).reshape(occ_dev, per_orb)
    partner_size = jnp.take(got_size.reshape(-1), target).reshape(occ_dev, per_orb)
    half = nvd // lax.axis_size("aux")
    integrals = lax.psum_scatter(
        jnp.einsum("oqa,opqb->aopb", blocks, partner, preferred_element_type=jnp.float32),
        "aux",
        scatter_dimension=0,
        tiled=True,
    )
    row_start = lax.axis_index("aux") * half
    rows = row_start + jnp.arange(half, dtype=jnp.int32)
    cols = jnp.arange(nvd, dtype=jnp.int32).astype(jnp.float32)
    mask = (rows[:, None, None, None] < domain_size[None, :, None, None]) & (
        cols[None, None, None, :] < partner_size[None, :, :, None]
    )
    integrals = jnp.where(mask, integrals, jnp.zeros_like(integrals))
    vir_rows = lax.dynamic_slice_in_dim(vir_energy, row_start, half, 1)
    gap = (
        vir_rows.T[:, :, None, None]
        + partner_vir[None, :, :, :]
        - occ_energy[None, :, None, None]
        - partner_occ[None, :, :, None]
    )
    amp_rows = (-integrals / gap).astype(jnp.bfloat16)
    partial_energy = jnp.sum(integrals * amp_rows.astype(jnp.float32), axis=(0, 3))
    energy = lax.psum(partial_energy, "aux").reshape(pair_dev) / nvd
    density = jnp.einsum(
        "aopb,copb->oac",
        amp_rows,
        lax.all_gather(amp_rows, "aux", axis=0, tiled=True),
        preferred_element_type=jnp.float32,
    )
    return (energy, density)


def fits_line(mesh):
    return mesh.shape["orb"] == 8 and mesh.shape["aux"] == 2


def table_of(bases, fields):
    return jnp.concatenate([bases] + [x.astype(i32) for x in fields])


def pack_kernel(call, cap, tbl, *refs):
    sources, out, sems = refs[:-2], refs[-2], refs[-1]
    base = tbl[call]

    def move(x):
        copies = []
        for r in range(cap):
            slot = tbl[9 + base + r]
            copies.append(pltpu.make_async_copy(x.at[slot], out.at[r], sems.at[r]))
            copies[-1].start()
        for copy in copies:
            copy.wait()

    by_place(tbl, sources, move)


def by_place(tbl, sources, act):
    if len(sources) == 1:
        act(*sources)
    else:
        pl.when(tbl[8] == 1)(lambda: act(sources[0]))
        pl.when(tbl[8] == 0)(lambda: act(sources[1]))


def pack(tbl, call, sources, cap):
    x = sources[0]
    return pl.pallas_call(
        lambda *refs: pack_kernel(call, cap, *refs),
        out_shape=jax.ShapeDtypeStruct((cap,) + x.shape[1:], x.dtype),
        in_specs=[SMEM] + [HBM] * len(sources),
        out_specs=HBM,
        scratch_shapes=[pltpu.SemaphoreType.DMA((cap,))],
        compiler_params=pltpu.CompilerParams(vmem_limit_bytes=LIMIT),
        cost_estimate=pl.CostEstimate(
            flops=0, bytes_accessed=2 * cap * x.shape[1] * x.shape[2] * 2, transcendentals=0
        ),
        name="pack",
    )(tbl, *sources)


def turn_kernel(x, out):
    for r in range(x.shape[0]):
        out[r] = x[r].T


def turn(x):
    count, rows, cols = x.shape
    step = 4 if count % 4 == 0 else 1
    return pl.pallas_call(
        turn_kernel,
        out_shape=jax.ShapeDtypeStruct((count, cols, rows), x.dtype),
        grid=(count // step,),
        in_specs=[pl.BlockSpec((step, rows, cols), lambda i: (i, 0, 0))],
        out_specs=pl.BlockSpec((step, cols, rows), lambda i: (i, 0, 0)),
        compiler_params=pltpu.CompilerParams(vmem_limit_bytes=LIMIT),
        cost_estimate=pl.CostEstimate(
            flops=0, bytes_accessed=2 * count * rows * cols * 2, transcendentals=0
        ),
        name="turn",
    )(x)


def amplitudes_kernel(call, by_slot, per_orb, places, tbl, rows, vcol, a0, a1, *refs):
    js, (tin, tout, energy, sv, s0, s1, b0, b1, st, sem, sem_out) = refs[:-11], refs[-11:]
    cap = sv.shape[0]
    n = rows.shape[0]
    base = tbl[call]

    def loads_of(r, j0, j1):
        i = lax.div(tbl[9 + base + r], per_orb)
        slot = tbl[9 + n + base + r] if by_slot else r
        pairs = (
            (vcol.at[i], sv.at[r]),
            (a0.at[i], s0.at[r]),
            (a1.at[i], s1.at[r]),
            (j0.at[slot], b0.at[r]),
            (j1.at[slot], b1.at[r]),
        )
        return [pltpu.make_async_copy(x, to, sem.at[r, k]) for k, (x, to) in enumerate(pairs)]

    def load(j):
        copies = [copy for r in range(cap) for copy in loads_of(r, *j)]
        for copy in copies:
            copy.start()
        for copy in copies:
            copy.wait()

    by_place(tbl, [js[2 * k : 2 * k + 2] for k in range(places)], load)
    nvd, half = sv.shape[1], sv.shape[2]
    live_a = lax.broadcasted_iota(i32, (nvd, half), 0)
    live_b = lax.broadcasted_iota(i32, (nvd, half), 1)
    row8 = rows[pl.ds(pl.multiple_of(base, cap), cap), :]
    for r in range(cap):
        size_i = tbl[9 + 2 * n + base + r]
        size_j = tbl[9 + 3 * n + base + r]
        k = jnp.dot(s0[r], b0[r], preferred_element_type=f32)
        k += jnp.dot(s1[r], b1[r], preferred_element_type=f32)
        k = jnp.where((live_a < size_i) & (live_b < size_j), k, 0.0)
        gap = sv[r] + row8[r : r + 1, :]
        t = (-k / gap).astype(bf16)
        st[r] = t
        energy[r] = jnp.sum((k * t.astype(f32)).reshape(nvd // 8, 8, half), axis=0)
    stores = [
        pltpu.make_async_copy(st.at[r], tout.at[tbl[9 + base + r]], sem_out.at[r])
        for r in range(cap)
    ]
    for copy in stores:
        copy.start()
    for copy in stores:
        copy.wait()


def amplitudes(call, by_slot, per_orb, tbl, rows, vcol, left, sources, t_all, cap):
    nvd, half = vcol.shape[1:]
    qa = left[0].shape[2]
    blocks = [x for pair in sources for x in pair]
    return pl.pallas_call(
        lambda *refs: amplitudes_kernel(call, by_slot, per_orb, len(sources), *refs),
        out_shape=(
            jax.ShapeDtypeStruct(t_all.shape, t_all.dtype),
            jax.ShapeDtypeStruct((cap, 8, half), f32),
        ),
        in_specs=[SMEM, VMEM, HBM, HBM, HBM] + [HBM] * len(blocks) + [HBM],
        out_specs=(HBM, VMEM),
        scratch_shapes=[
            pltpu.VMEM((cap, nvd, half), f32),
            pltpu.VMEM((cap, nvd, qa), bf16),
            pltpu.VMEM((cap, nvd, qa), bf16),
            pltpu.VMEM((cap, qa, half), bf16),
            pltpu.VMEM((cap, qa, half), bf16),
            pltpu.VMEM((cap, nvd, half), bf16),
            pltpu.SemaphoreType.DMA((cap, 5)),
            pltpu.SemaphoreType.DMA((cap,)),
        ],
        input_output_aliases={5 + len(blocks): 0},
        compiler_params=pltpu.CompilerParams(vmem_limit_bytes=LIMIT),
        cost_estimate=pl.CostEstimate(
            flops=cap * 4 * nvd * qa * half,
            bytes_accessed=cap * (nvd * half * 6 + 4 * nvd * qa + 4 * qa * half),
            transcendentals=0,
        ),
        name="amplitudes",
    )(tbl, rows, vcol, *left, *blocks, t_all)


def density_kernel(start, t, d):
    count, half = d.shape[:2]
    per_orb = t.shape[0] // count
    first = pl.multiple_of(start[0], half)
    for o in range(count):
        own = range(o * per_orb, (o + 1) * per_orb)
        left = jnp.concatenate([t[k, pl.ds(first, half), :] for k in own], axis=1)
        right = jnp.concatenate([t[k] for k in own], axis=1)
        d[o] = lax.dot_general(left, right, (((1,), (1,)), ((), ())), preferred_element_type=f32)


def density_rows(t_all, start, per_orb, half):
    npair, nvd, width = t_all.shape
    occ = npair // per_orb
    step = 4 if occ % 4 == 0 else 1
    return pl.pallas_call(
        density_kernel,
        out_shape=jax.ShapeDtypeStruct((occ, half, nvd), f32),
        grid_spec=pltpu.PrefetchScalarGridSpec(
            num_scalar_prefetch=1,
            grid=(occ // step,),
            in_specs=[pl.BlockSpec((step * per_orb, nvd, width), lambda i, s: (i, 0, 0))],
            out_specs=pl.BlockSpec((step, half, nvd), lambda i, s: (i, 0, 0)),
        ),
        compiler_params=pltpu.CompilerParams(vmem_limit_bytes=LIMIT),
        cost_estimate=pl.CostEstimate(
            flops=2 * npair * half * nvd * width,
            bytes_accessed=npair * nvd * width * 2 + occ * half * nvd * 4,
            transcendentals=0,
        ),
        name="density_rows",
    )(start.reshape(1), t_all)


def line_plan(blocks, vir_energy, occ_energy, domain_size, partner_owner, partner_slot):
    occ, qa, nvd = blocks.shape
    pair_dev = partner_slot.shape[0]
    per_orb = pair_dev // occ
    peers = 8
    cap = pair_dev // peers
    half = nvd // 2
    me, core = lax.axis_index("orb"), lax.axis_index("aux")
    z, y = me // 2, me % 2
    middle = (z == 1) | (z == 2)
    swap_core = [(0, 1), (1, 0)]
    swap_y = [(o, o ^ 1) for o in range(peers)]
    swap_half = [(o, o ^ 2) for o in range(peers)]
    cross = [(2, 4), (3, 5), (4, 2), (5, 3)]
    outward = [(2, 0), (3, 1), (4, 6), (5, 7)]

    other = lax.ppermute(blocks, "aux", swap_core)
    col0 = core * half
    own = [lax.dynamic_slice_in_dim(x, col0, half, 2) for x in (blocks, other)]

    owner = partner_owner[:, 0]
    target = owner * cap + slot_ranks(owner)
    hit = target[None, :] == jnp.arange(pair_dev, dtype=i32)[:, None]
    pairs = jnp.arange(pair_dev, dtype=i32)
    order = jnp.sum(jnp.where(hit, pairs[None, :], 0), axis=1)
    slots = jnp.sum(jnp.where(hit, partner_slot[None, :], 0), axis=1)
    small = jnp.concatenate(
        [
            vir_energy,
            occ_energy[:, None],
            domain_size.astype(f32)[:, None],
            jnp.zeros((occ, 126), f32),
        ],
        axis=1,
    )
    every = small[None]
    for bit in (1, 2, 4):
        got = lax.ppermute(every, "orb", [(o, o ^ bit) for o in range(peers)])
        every = jnp.concatenate([every, got])
    theirs = jnp.take(every.reshape(peers * occ, -1), ((pairs // cap) ^ me) * occ + slots, axis=0)
    mine = jnp.take(small, order // per_orb, axis=0)
    rows = lax.dynamic_slice_in_dim(theirs, col0, half, 1) - (
        theirs[:, nvd : nvd + 1] + mine[:, nvd : nvd + 1]
    )
    size_i = mine[:, nvd + 1].astype(i32)
    size_j = theirs[:, nvd + 1].astype(i32) - col0
    lower = z < 2
    column = jnp.stack([z, z ^ 1, jnp.where(lower, 2, 1), jnp.where(lower, 3, 0)])
    bases = jnp.concatenate([column * 2 + y, column * 2 + (1 - y)]) * cap
    tbl = table_of(bases, [middle[None], order, slots, size_i, size_j])
    wanted = table_of(bases, [middle[None], lax.ppermute(slots, "orb", swap_y)])
    vcol = jnp.broadcast_to(vir_energy[:, :, None], (occ, nvd, half))
    left = [turn(x) for x in (blocks, other)]

    near = [lax.ppermute(x, "orb", swap_half) for x in own]
    mid = [lax.ppermute(x, "orb", cross) for x in own]
    mid_out = [lax.ppermute(x, "orb", outward) for x in mid]
    far = [lax.ppermute(x, "orb", cross) for x in near]
    far_out = [lax.ppermute(x, "orb", outward) for x in far]
    sources = [[own], [near], [mid, mid_out], [far, far_out]]
    beside = [
        [lax.ppermute(pack(wanted, k, x, cap), "orb", swap_y) for x in zip(*source)]
        for k, source in enumerate(sources)
    ]

    t_all = jnp.zeros((pair_dev, nvd, half), bf16)
    energies = [None] * 8
    for k in (0, 1, 4, 2, 5, 3, 6, 7):
        source = sources[k] if k < 4 else [beside[k - 4]]
        t_all, energies[k] = amplitudes(
            k, k < 4, per_orb, tbl, rows, vcol, left, source, t_all, cap
        )
    away = lax.ppermute(density_rows(t_all, (1 - core) * half, per_orb, half), "aux", swap_core)
    density = density_rows(t_all, core * half, per_orb, half) + away

    sums = jnp.sum(jnp.stack(energies), axis=(2, 3)).reshape(pair_dev)
    place = (bases[:, None] + jnp.arange(cap, dtype=i32)[None, :]).reshape(pair_dev)
    spot = target[:, None] == place[None, :]
    energy = jnp.sum(jnp.where(spot, sums[None, :], 0.0), axis=1)
    energy = (energy + lax.ppermute(energy, "aux", swap_core)) / nvd
    return (energy, density)


def solution(mesh):
    in_specs = (
        P(("mol", "orb"), "aux", None),
        P(("mol", "orb"), None),
        P(("mol", "orb")),
        P(("mol", "orb")),
        P(("mol", "orb"), None),
        P(("mol", "orb")),
    )
    out_specs = (P(("mol", "orb")), P(("mol", "orb"), "aux", None))
    return jax.shard_map(
        line_plan if fits_line(mesh) else by_requests, mesh=mesh, in_specs=in_specs, out_specs=out_specs, check_vma=False
    )
```

```python
import jax
import jax.numpy as jnp
from jax import lax
from jax.experimental import pallas as pl
from jax.experimental.pallas import tpu as pltpu
from jax.sharding import PartitionSpec as P

f32, bf16, i32 = jnp.float32, jnp.bfloat16, jnp.int32
HBM = pl.BlockSpec(memory_space=pltpu.HBM)
SMEM = pl.BlockSpec(memory_space=pltpu.SMEM)
VMEM = pl.BlockSpec(memory_space=pltpu.VMEM)
LIMIT = 48 * 1024 * 1024


def slot_ranks(owner):
    count = owner.shape[0]
    order = jnp.arange(count, dtype=jnp.int32)
    same = (owner[:, None] == owner[None, :]) & (order[None, :] < order[:, None])
    return jnp.sum(same.astype(jnp.int32), axis=1)


def by_requests(blocks, vir_energy, occ_energy, domain_size, partner_owner, partner_slot):
    occ_dev, half_aux, nvd = blocks.shape
    pair_dev = partner_slot.shape[0]
    per_orb = pair_dev // occ_dev
    peers = lax.axis_size("orb")
    cap = max(2, (pair_dev + peers - 1) // peers)
    owner = partner_owner[:, 0]
    ranks = slot_ranks(owner)
    target = owner * cap + ranks
    wanted = (target[:, None] == jnp.arange(peers * cap, dtype=jnp.int32)[None, :]).astype(
        jnp.int32
    )
    requests = jnp.sum(wanted * partner_slot[:, None], axis=0).reshape(peers, cap)
    incoming = lax.all_to_all(requests, "orb", split_axis=0, concat_axis=0, tiled=True)
    flat_in = incoming.reshape(-1)
    send_blocks = jnp.take(blocks, flat_in, axis=0).reshape(peers, cap, half_aux, nvd)
    send_vir = jnp.take(vir_energy, flat_in, axis=0).reshape(peers, cap, nvd)
    send_occ = jnp.take(occ_energy, flat_in).reshape(peers, cap)
    send_size = jnp.take(domain_size, flat_in).astype(jnp.float32).reshape(peers, cap)
    got_blocks = lax.all_to_all(send_blocks, "orb", split_axis=0, concat_axis=0, tiled=True)
    got_vir, got_occ, got_size = (
        lax.all_to_all(send_vir, "orb", split_axis=0, concat_axis=0, tiled=True),
        lax.all_to_all(send_occ, "orb", split_axis=0, concat_axis=0, tiled=True),
        lax.all_to_all(send_size, "orb", split_axis=0, concat_axis=0, tiled=True),
    )
    partner = jnp.take(got_blocks.reshape(peers * cap, half_aux, nvd), target, axis=0).reshape(
        occ_dev, per_orb, half_aux, nvd
    )
    partner_vir = jnp.take(got_vir.reshape(peers * cap, nvd), target, axis=0).reshape(
        occ_dev, per_orb, nvd
    )
    partner_occ = jnp.take(got_occ.reshape(-1), target).reshape(occ_dev, per_orb)
    partner_size = jnp.take(got_size.reshape(-1), target).reshape(occ_dev, per_orb)
    half = nvd // lax.axis_size("aux")
    integrals = lax.psum_scatter(
        jnp.einsum("oqa,opqb->aopb", blocks, partner, preferred_element_type=jnp.float32),
        "aux",
        scatter_dimension=0,
        tiled=True,
    )
    row_start = lax.axis_index("aux") * half
    rows = row_start + jnp.arange(half, dtype=jnp.int32)
    cols = jnp.arange(nvd, dtype=jnp.int32).astype(jnp.float32)
    mask = (rows[:, None, None, None] < domain_size[None, :, None, None]) & (
        cols[None, None, None, :] < partner_size[None, :, :, None]
    )
    integrals = jnp.where(mask, integrals, jnp.zeros_like(integrals))
    vir_rows = lax.dynamic_slice_in_dim(vir_energy, row_start, half, 1)
    gap = (
        vir_rows.T[:, :, None, None]
        + partner_vir[None, :, :, :]
        - occ_energy[None, :, None, None]
        - partner_occ[None, :, :, None]
    )
    amp_rows = (-integrals / gap).astype(jnp.bfloat16)
    partial_energy = jnp.sum(integrals * amp_rows.astype(jnp.float32), axis=(0, 3))
    energy = lax.psum(partial_energy, "aux").reshape(pair_dev) / nvd
    density = jnp.einsum(
        "aopb,copb->oac",
        amp_rows,
        lax.all_gather(amp_rows, "aux", axis=0, tiled=True),
        preferred_element_type=jnp.float32,
    )
    return (energy, density)


def fits_line(mesh):
    return mesh.shape["orb"] == 8 and mesh.shape["aux"] == 2


HEAD = 10


def table_of(fields):
    return jnp.concatenate([x.astype(i32) for x in fields])


def pack_kernel(call, after, tbl, x, *refs):
    out, sems = refs[after:]
    cap = out.shape[0]
    base = tbl[call]
    copies = []
    for r in range(cap):
        slot = tbl[HEAD + base + r]
        copies.append(pltpu.make_async_copy(x.at[slot], out.at[r], sems.at[r]))
        copies[-1].start()
    for copy in copies:
        copy.wait()


def pack(tbl, call, x, cap, after=()):
    return pl.pallas_call(
        lambda *refs: pack_kernel(call, len(after), *refs),
        out_shape=jax.ShapeDtypeStruct((cap,) + x.shape[1:], x.dtype),
        in_specs=[SMEM, HBM] + [HBM] * len(after),
        out_specs=VMEM,
        scratch_shapes=[pltpu.SemaphoreType.DMA((cap,))],
        compiler_params=pltpu.CompilerParams(vmem_limit_bytes=LIMIT),
        cost_estimate=pl.CostEstimate(
            flops=0, bytes_accessed=2 * cap * x.shape[1] * x.shape[2] * 2, transcendentals=0
        ),
        name="pack",
    )(tbl, x, *after)


def turn_kernel(x, out):
    for r in range(x.shape[0]):
        out[r] = x[r].T


def turn(x):
    count, rows, cols = x.shape
    step = 4 if count % 4 == 0 else 1
    return pl.pallas_call(
        turn_kernel,
        out_shape=jax.ShapeDtypeStruct((count, cols, rows), x.dtype),
        grid=(count // step,),
        in_specs=[pl.BlockSpec((step, rows, cols), lambda i: (i, 0, 0))],
        out_specs=pl.BlockSpec((step, cols, rows), lambda i: (i, 0, 0)),
        compiler_params=pltpu.CompilerParams(vmem_limit_bytes=LIMIT),
        cost_estimate=pl.CostEstimate(
            flops=0, bytes_accessed=2 * count * rows * cols * 2, transcendentals=0
        ),
        name="turn",
    )(x)


def amplitudes_kernel(mode, call, per_orb, after, tbl, rows, vcol, *refs):
    outs, (energy, sv, s0, s1, b0, b1, st, sem, sem_out) = refs[:-9], refs[-9:]
    if mode == "client":
        left, js, tout = outs[:4], outs[4:6], outs[-1]
    else:
        left, js, ready, tout = outs[:2], outs[2:], outs[-3 - after], outs[-1]
    cap = sv.shape[0]
    n = rows.shape[0]
    nvd, half = sv.shape[1], sv.shape[2]
    base = tbl[call]
    middle = tbl[8] == 1

    def place(r):
        return tbl[HEAD + base + r]

    def load(j0, j1):
        copies = []
        for r in range(cap):
            i = lax.div(place(r), per_orb)
            slot = r if mode == "asked" else tbl[HEAD + n + base + r]
            todo = [(vcol.at[i], sv.at[r]), (j0.at[slot], b0.at[r]), (j1.at[slot], b1.at[r])]
            if mode == "client":
                here = pl.ds(pl.multiple_of(tbl[9], half), half)
                there = pl.ds(pl.multiple_of(half - tbl[9], half), half)
                todo += [
                    (left[0].at[i], s0.at[r, here, :]),
                    (left[1].at[i], s1.at[r, here, :]),
                    (left[2].at[i], s1.at[r, there, :]),
                    (left[3].at[i], s0.at[r, there, :]),
                ]
            else:
                todo += [(left[0].at[i], s0.at[r]), (left[1].at[i], s1.at[r])]
            copies += [
                pltpu.make_async_copy(x, to, sem.at[r, k]) for k, (x, to) in enumerate(todo)
            ]
        for copy in copies:
            copy.start()
        for copy in copies:
            copy.wait()

    def make():
        live_a = lax.broadcasted_iota(i32, (nvd, half), 0)
        live_b = lax.broadcasted_iota(i32, (nvd, half), 1)
        row8 = rows[pl.ds(pl.multiple_of(base, cap), cap), :]
        for r in range(cap):
            size_i = tbl[HEAD + 2 * n + base + r]
            size_j = tbl[HEAD + 3 * n + base + r]
            k = jnp.dot(s0[r], b0[r], preferred_element_type=f32)
            k += jnp.dot(s1[r], b1[r], preferred_element_type=f32)
            k = jnp.where((live_a < size_i) & (live_b < size_j), k, 0.0)
            gap = sv[r] + row8[r : r + 1, :]
            t = (-k / gap).astype(bf16)
            st[r] = t
            energy[r] = jnp.sum((k * t.astype(f32)).reshape(nvd // 8, 8, half), axis=0)

    def store():
        stores = [
            pltpu.make_async_copy(st.at[r], tout.at[place(r)], sem_out.at[r]) for r in range(cap)
        ]
        for copy in stores:
            copy.start()
        for copy in stores:
            copy.wait()

    if mode == "slots":
        load(js[0], js[1])
        make()
        store()
    elif mode == "asked":
        if len(js) - 2 - after >= 4:
            pl.when(middle)(lambda: load(js[0], js[1]))
            pl.when(jnp.logical_not(middle))(lambda: load(js[2], js[3]))
        else:
            load(js[0], js[1])
        make()
        store()
    elif mode == "served":

        @pl.when(middle)
        def _():
            load(js[0], js[1])
            make()

        @pl.when(jnp.logical_not(middle))
        def _():
            energy[...] = jnp.zeros_like(energy)
            copies = [
                pltpu.make_async_copy(ready.at[r], st.at[r], sem.at[r, 0]) for r in range(cap)
            ]
            for copy in copies:
                copy.start()
            for copy in copies:
                copy.wait()

        store()
    else:

        @pl.when(middle)
        def _():
            load(js[0], js[1])
            make()
            tout[...] = st[...]

        @pl.when(jnp.logical_not(middle))
        def _():
            energy[...] = jnp.zeros_like(energy)
            tout[...] = jnp.zeros_like(tout)


def amplitudes(mode, call, per_orb, tables, left, sources, t_all, cap, after=()):
    tbl, rows, vcol = tables
    nvd, half = vcol.shape[1:]
    qa = left[0].shape[2]
    operands = (tbl, rows, vcol, *left, *sources, *after)
    client = mode == "client"
    aliases = {} if client else {len(operands): 0}
    if not client:
        operands += (t_all,)
    t_shape = (cap, nvd, half) if client else t_all.shape
    return pl.pallas_call(
        lambda *refs: amplitudes_kernel(mode, call, per_orb, len(after), *refs),
        out_shape=(
            jax.ShapeDtypeStruct(t_shape, bf16),
            jax.ShapeDtypeStruct((cap, 8, half), f32),
        ),
        in_specs=[SMEM, VMEM] + [HBM] * (len(operands) - 2),
        out_specs=(VMEM if client else HBM, VMEM),
        scratch_shapes=[
            pltpu.VMEM((cap, nvd, half), f32),
            pltpu.VMEM((cap, nvd, qa), bf16),
            pltpu.VMEM((cap, nvd, qa), bf16),
            pltpu.VMEM((cap, qa, half), bf16),
            pltpu.VMEM((cap, qa, half), bf16),
            pltpu.VMEM((cap, nvd, half), bf16),
            pltpu.SemaphoreType.DMA((cap, 7)),
            pltpu.SemaphoreType.DMA((cap,)),
        ],
        input_output_aliases=aliases,
        compiler_params=pltpu.CompilerParams(vmem_limit_bytes=LIMIT),
        cost_estimate=pl.CostEstimate(
            flops=cap * 4 * nvd * qa * half,
            bytes_accessed=cap * (nvd * half * 6 + 4 * nvd * qa + 4 * qa * half),
            transcendentals=0,
        ),
        name="amplitudes",
    )(*operands)


def density_kernel(start, t, d):
    count, half = d.shape[:2]
    per_orb = t.shape[0] // count
    first = pl.multiple_of(start[0], half)
    for o in range(count):
        own = range(o * per_orb, (o + 1) * per_orb)
        left = jnp.concatenate([t[k, pl.ds(first, half), :] for k in own], axis=1)
        right = jnp.concatenate([t[k] for k in own], axis=1)
        d[o] = lax.dot_general(left, right, (((1,), (1,)), ((), ())), preferred_element_type=f32)


def density_rows(t_all, start, per_orb, half):
    npair, nvd, width = t_all.shape
    occ = npair // per_orb
    step = 4 if occ % 4 == 0 else 1
    return pl.pallas_call(
        density_kernel,
        out_shape=jax.ShapeDtypeStruct((occ, half, nvd), f32),
        grid_spec=pltpu.PrefetchScalarGridSpec(
            num_scalar_prefetch=1,
            grid=(occ // step,),
            in_specs=[pl.BlockSpec((step * per_orb, nvd, width), lambda i, s: (i, 0, 0))],
            out_specs=pl.BlockSpec((step, half, nvd), lambda i, s: (i, 0, 0)),
        ),
        compiler_params=pltpu.CompilerParams(vmem_limit_bytes=LIMIT),
        cost_estimate=pl.CostEstimate(
            flops=2 * npair * half * nvd * width,
            bytes_accessed=npair * nvd * width * 2 + occ * half * nvd * 4,
            transcendentals=0,
        ),
        name="density_rows",
    )(start.reshape(1), t_all)


def line_plan(blocks, vir_energy, occ_energy, domain_size, partner_owner, partner_slot):
    occ, qa, nvd = blocks.shape
    pair_dev = partner_slot.shape[0]
    per_orb = pair_dev // occ
    peers = 8
    cap = pair_dev // peers
    half = nvd // 2
    wide = nvd + 128
    me, core = lax.axis_index("orb"), lax.axis_index("aux")
    z, y = me // 2, me % 2
    lower = z < 2
    middle = (z == 1) | (z == 2)
    col0 = core * half

    def pp(x, perm):
        return lax.ppermute(x, "orb", perm)

    def swap_core(x):
        return lax.ppermute(x, "aux", [(0, 1), (1, 0)])

    def flip(bit):
        return [(o, o ^ bit) for o in range(peers)]

    cross = [(2, 4), (3, 5), (4, 2), (5, 3)]
    outward = [(2, 0), (3, 1), (4, 6), (5, 7)]
    y_middle = [(2, 3), (3, 2), (4, 5), (5, 4)]
    y_end = [(0, 1), (1, 0), (6, 7), (7, 6)]

    other = swap_core(blocks)
    own = [lax.dynamic_slice_in_dim(x, col0, half, 2) for x in (blocks, other)]

    owner = partner_owner[:, 0]
    target = owner * cap + slot_ranks(owner)
    pairs = jnp.arange(pair_dev, dtype=i32)
    hit = target[None, :] == pairs[:, None]
    order = jnp.sum(jnp.where(hit, pairs[None, :], 0), axis=1)
    slots = jnp.sum(jnp.where(hit, partner_slot[None, :], 0), axis=1)
    lists = jnp.concatenate([order, slots]).astype(f32)
    small = jnp.concatenate(
        [
            jnp.concatenate(
                [
                    vir_energy,
                    occ_energy[:, None],
                    domain_size.astype(f32)[:, None],
                    jnp.zeros((occ, wide - nvd - 2), f32),
                ],
                axis=1,
            ),
            jnp.pad(lists[None], ((0, 7), (0, wide - lists.shape[0]))),
        ]
    )
    both = jnp.stack([small, pp(small, flip(1))])
    every = jnp.concatenate([both] + [pp(both, flip(bit)) for bit in (2, 4, 6)])
    orbitals = every[:, :occ].reshape(peers * occ, wide)

    column = jnp.stack([z, z ^ 1, jnp.where(lower, 2, 1), jnp.where(lower, 3, 0)])
    bases = jnp.concatenate([column * 2 + y, column * 2 + (1 - y)]) * cap
    head = [bases, middle[None], col0[None]]

    def lists_of(x):
        found = every[x, occ, : 2 * pair_dev].astype(i32)
        return found[:pair_dev], found[pair_dev:]

    def tables_of(x):
        order, slots = lists_of(x)
        theirs = jnp.take(orbitals, ((pairs // cap) ^ me) * occ + slots, axis=0)
        mine = jnp.take(every[x, :occ], order // per_orb, axis=0)
        rows = lax.dynamic_slice_in_dim(theirs, col0, half, 1) - (
            theirs[:, nvd : nvd + 1] + mine[:, nvd : nvd + 1]
        )
        size_i, size_j = mine[:, nvd + 1], theirs[:, nvd + 1].astype(i32) - col0
        vcol = jnp.broadcast_to(every[x, :occ, :nvd, None], (occ, nvd, half))
        return table_of(head + [order, slots, size_i, size_j]), rows, vcol

    tables = tables_of(0)
    beside_list = table_of(head + [lists_of(1)[1]])
    relay_list = table_of(head + [lists_of(3)[1]])
    own, tables, beside_list, relay_list = lax.optimization_barrier(
        (own, tables, beside_list, relay_list)
    )
    near = [pp(x, flip(2)) for x in own]
    mid = [pp(x, cross) for x in own]
    beside = [[pp(pack(beside_list, 0, x, cap), flip(1)) for x in own]]
    left = [turn(x) for x in (blocks, other)]
    energies = [None] * 8
    t_all = jnp.zeros((pair_dev, nvd, half), bf16)

    def own_pairs(k, mode, sources, t_all, after=()):
        t_all, energies[k] = amplitudes(
            mode, k, per_orb, tables, left, sources, t_all, cap, after
        )
        return t_all

    t_all = own_pairs(0, "slots", own, t_all)
    far = [pp(x, cross) for x in near]
    token = energies[0]
    beside_near, third_y, third_relay, across = [], [], [], []
    for q in range(2):
        x = pack(beside_list, 1, near[q], cap, (token,))
        beside_near.append(pp(x, flip(1)))
        across.append(swap_core(near[q]))
        x = pack(relay_list, 2, mid[q], cap, (x,))
        third_relay.append(pp(x, outward))
        token = pack(beside_list, 2, mid[q], cap, (x,))
        third_y.append(pp(token, y_middle))
    t_all = own_pairs(4, "asked", beside[0], t_all, (token,))
    t_all = own_pairs(1, "slots", near, t_all)
    client_left = [turn(x) for x in near + across]
    client = tables_of(2)
    gone_2, client_energy_2 = amplitudes(
        "client", 2, per_orb, client, client_left, mid, None, cap, (energies[1],)
    )
    ready_2 = pp(gone_2, outward)
    third_end = [pp(x, y_end) for x in third_relay]
    t_all = own_pairs(5, "asked", beside_near, t_all, (client_energy_2, *third_relay))
    fourth_y, fourth_relay = [], []
    token = energies[5]
    for q in range(2):
        x = pack(relay_list, 3, far[q], cap, (token,))
        fourth_relay.append(pp(x, outward))
        token = pack(beside_list, 3, far[q], cap, (x,))
        fourth_y.append(pp(token, y_middle))
    gone_3, client_energy_3 = amplitudes(
        "client", 3, per_orb, client, client_left, far, None, cap, (token,)
    )
    ready_3 = pp(gone_3, outward)
    fourth_end = [pp(x, y_end) for x in fourth_relay]
    t_all = own_pairs(
        2, "served", mid + [ready_2], t_all, (client_energy_3, fourth_relay[0])
    )
    t_all = own_pairs(6, "asked", third_y + third_end, t_all)
    t_all = own_pairs(3, "served", far + [ready_3], t_all, (fourth_relay[1],))
    t_all = own_pairs(7, "asked", fourth_y + fourth_end, t_all)

    away = swap_core(density_rows(t_all, (1 - core) * half, per_orb, half))
    density = density_rows(t_all, core * half, per_orb, half) + away

    sums = jnp.sum(jnp.stack(energies), axis=(2, 3))
    served = pp(jnp.sum(jnp.stack([client_energy_2, client_energy_3]), axis=(2, 3)), outward)
    sums = jnp.concatenate([sums[:2], sums[2:4] + served, sums[4:]]).reshape(pair_dev)
    place = (bases[:, None] + jnp.arange(cap, dtype=i32)[None, :]).reshape(pair_dev)
    spot = target[:, None] == place[None, :]
    energy = jnp.sum(jnp.where(spot, sums[None, :], 0.0), axis=1)
    energy = (energy + swap_core(energy)) / nvd
    return (energy, density)


def solution(mesh):
    in_specs = (
        P(("mol", "orb"), "aux", None),
        P(("mol", "orb"), None),
        P(("mol", "orb")),
        P(("mol", "orb")),
        P(("mol", "orb"), None),
        P(("mol", "orb")),
    )
    out_specs = (P(("mol", "orb")), P(("mol", "orb"), "aux", None))
    return jax.shard_map(
        line_plan if fits_line(mesh) else by_requests, mesh=mesh, in_specs=in_specs, out_specs=out_specs, check_vma=False
    )
```

```python
import jax
import jax.numpy as jnp
from jax import lax
from jax.experimental import pallas as pl
from jax.experimental.pallas import tpu as pltpu
from jax.sharding import PartitionSpec as P

f32, bf16, i32 = jnp.float32, jnp.bfloat16, jnp.int32
HBM = pl.BlockSpec(memory_space=pltpu.HBM)
SMEM = pl.BlockSpec(memory_space=pltpu.SMEM)
VMEM = pl.BlockSpec(memory_space=pltpu.VMEM)
LIMIT = 48 * 1024 * 1024


def slot_ranks(owner):
    count = owner.shape[0]
    order = jnp.arange(count, dtype=jnp.int32)
    same = (owner[:, None] == owner[None, :]) & (order[None, :] < order[:, None])
    return jnp.sum(same.astype(jnp.int32), axis=1)


def by_requests(blocks, vir_energy, occ_energy, domain_size, partner_owner, partner_slot):
    occ_dev, half_aux, nvd = blocks.shape
    pair_dev = partner_slot.shape[0]
    per_orb = pair_dev // occ_dev
    peers = lax.axis_size("orb")
    cap = max(2, (pair_dev + peers - 1) // peers)
    owner = partner_owner[:, 0]
    ranks = slot_ranks(owner)
    target = owner * cap + ranks
    wanted = (target[:, None] == jnp.arange(peers * cap, dtype=jnp.int32)[None, :]).astype(
        jnp.int32
    )
    requests = jnp.sum(wanted * partner_slot[:, None], axis=0).reshape(peers, cap)
    incoming = lax.all_to_all(requests, "orb", split_axis=0, concat_axis=0, tiled=True)
    flat_in = incoming.reshape(-1)
    send_blocks = jnp.take(blocks, flat_in, axis=0).reshape(peers, cap, half_aux, nvd)
    send_vir = jnp.take(vir_energy, flat_in, axis=0).reshape(peers, cap, nvd)
    send_occ = jnp.take(occ_energy, flat_in).reshape(peers, cap)
    send_size = jnp.take(domain_size, flat_in).astype(jnp.float32).reshape(peers, cap)
    got_blocks = lax.all_to_all(send_blocks, "orb", split_axis=0, concat_axis=0, tiled=True)
    got_vir, got_occ, got_size = (
        lax.all_to_all(send_vir, "orb", split_axis=0, concat_axis=0, tiled=True),
        lax.all_to_all(send_occ, "orb", split_axis=0, concat_axis=0, tiled=True),
        lax.all_to_all(send_size, "orb", split_axis=0, concat_axis=0, tiled=True),
    )
    partner = jnp.take(got_blocks.reshape(peers * cap, half_aux, nvd), target, axis=0).reshape(
        occ_dev, per_orb, half_aux, nvd
    )
    partner_vir = jnp.take(got_vir.reshape(peers * cap, nvd), target, axis=0).reshape(
        occ_dev, per_orb, nvd
    )
    partner_occ = jnp.take(got_occ.reshape(-1), target).reshape(occ_dev, per_orb)
    partner_size = jnp.take(got_size.reshape(-1), target).reshape(occ_dev, per_orb)
    half = nvd // lax.axis_size("aux")
    integrals = lax.psum_scatter(
        jnp.einsum("oqa,opqb->aopb", blocks, partner, preferred_element_type=jnp.float32),
        "aux",
        scatter_dimension=0,
        tiled=True,
    )
    row_start = lax.axis_index("aux") * half
    rows = row_start + jnp.arange(half, dtype=jnp.int32)
    cols = jnp.arange(nvd, dtype=jnp.int32).astype(jnp.float32)
    mask = (rows[:, None, None, None] < domain_size[None, :, None, None]) & (
        cols[None, None, None, :] < partner_size[None, :, :, None]
    )
    integrals = jnp.where(mask, integrals, jnp.zeros_like(integrals))
    vir_rows = lax.dynamic_slice_in_dim(vir_energy, row_start, half, 1)
    gap = (
        vir_rows.T[:, :, None, None]
        + partner_vir[None, :, :, :]
        - occ_energy[None, :, None, None]
        - partner_occ[None, :, :, None]
    )
    amp_rows = (-integrals / gap).astype(jnp.bfloat16)
    partial_energy = jnp.sum(integrals * amp_rows.astype(jnp.float32), axis=(0, 3))
    energy = lax.psum(partial_energy, "aux").reshape(pair_dev) / nvd
    density = jnp.einsum(
        "aopb,copb->oac",
        amp_rows,
        lax.all_gather(amp_rows, "aux", axis=0, tiled=True),
        preferred_element_type=jnp.float32,
    )
    return (energy, density)


def fits_line(mesh):
    return mesh.shape["orb"] == 8 and mesh.shape["aux"] == 2


HEAD = 10


def table_of(fields):
    return jnp.concatenate([x.astype(i32) for x in fields])


TINY = pl.CostEstimate(flops=1, bytes_accessed=1, transcendentals=0)
PARAMS = pltpu.CompilerParams(vmem_limit_bytes=LIMIT)


def pack_kernel(call, only_middle, relayed, after, tbl, *refs):
    out, sems = refs[-2:]
    halves, cap = out.shape[:2]
    base = tbl[call]
    middle = tbl[8] == 1

    def run(copies):
        for copy in copies:
            copy.start()
        for copy in copies:
            copy.wait()

    def gather():
        run(
            [
                pltpu.make_async_copy(
                    refs[q].at[tbl[HEAD + base + r]], out.at[q, r], sems.at[q, r]
                )
                for q in range(halves)
                for r in range(cap)
            ]
        )

    if not only_middle and not relayed:
        gather()
    else:
        pl.when(middle)(gather)
    if relayed:
        came = refs[halves]

        @pl.when(jnp.logical_not(middle))
        def _():
            run(
                [pltpu.make_async_copy(came.at[q], out.at[q], sems.at[q, 0]) for q in range(halves)]
            )


def pack(tbl, call, sources, cap, only_middle=False, relayed=None, after=()):
    halves = len(sources)
    shape = (halves, cap) + sources[0].shape[1:]
    operands = (*sources, *(() if relayed is None else (relayed,)), *after)
    return pl.pallas_call(
        lambda *refs: pack_kernel(call, only_middle, relayed is not None, len(after), *refs),
        out_shape=jax.ShapeDtypeStruct(shape, bf16),
        in_specs=[SMEM] + [HBM] * len(operands),
        out_specs=VMEM,
        scratch_shapes=[pltpu.SemaphoreType.DMA((halves, cap))],
        compiler_params=PARAMS,
        cost_estimate=TINY,
        name="pack",
    )(tbl, *operands)


def turn_kernel(*refs):
    half = len(refs) // 2
    for x, out in zip(refs[:half], refs[half:]):
        for r in range(x.shape[0]):
            out[r] = x[r].T


def turn(arrays):
    count, rows, cols = arrays[0].shape
    step = 4 if count % 4 == 0 else 1
    n = len(arrays)
    return pl.pallas_call(
        turn_kernel,
        out_shape=[jax.ShapeDtypeStruct((count, cols, rows), bf16)] * n,
        grid=(count // step,),
        in_specs=[pl.BlockSpec((step, rows, cols), lambda i: (i, 0, 0))] * n,
        out_specs=[pl.BlockSpec((step, cols, rows), lambda i: (i, 0, 0))] * n,
        compiler_params=PARAMS,
        cost_estimate=TINY,
        name="turn",
    )(*arrays)


def amplitudes_kernel(mode, call, per_orb, first, tbl, rows, vcol, *refs):
    sv, s0, s1, b0, b1, st, se, sem, sem_out = refs[-9:]
    client = mode == "client"
    if client:
        tout = refs[-10]
        left, js = refs[:4], refs[4:6]
    else:
        tout, eout = refs[-11:-9]
        left, js = refs[:2], refs[2:5]
    if mode == "asked":
        js = (js[0].at[0], js[0].at[1])
    if mode == "asked_two":
        js = (js[0].at[0], js[1].at[0])
    cap = sv.shape[0]
    n = rows.shape[0]
    nvd, half = sv.shape[1], sv.shape[2]
    base = tbl[call]
    middle = tbl[8] == 1

    def place(r):
        return tbl[HEAD + base + r]

    def run(copies):
        for copy in copies:
            copy.start()
        for copy in copies:
            copy.wait()

    def load():
        copies = []
        for r in range(cap):
            i = lax.div(place(r), per_orb)
            slot = r if mode.startswith("asked") else tbl[HEAD + n + base + r]
            todo = [
                (vcol.at[i], sv.at[r]),
                (js[0].at[slot], b0.at[r]),
                (js[1].at[slot], b1.at[r]),
            ]
            if client:
                here = pl.ds(pl.multiple_of(tbl[9], half), half)
                there = pl.ds(pl.multiple_of(half - tbl[9], half), half)
                todo += [
                    (left[0].at[i], s0.at[r, here, :]),
                    (left[1].at[i], s1.at[r, here, :]),
                    (left[2].at[i], s1.at[r, there, :]),
                    (left[3].at[i], s0.at[r, there, :]),
                ]
            else:
                todo += [(left[0].at[i], s0.at[r]), (left[1].at[i], s1.at[r])]
            copies += [
                pltpu.make_async_copy(x, to, sem.at[r, k]) for k, (x, to) in enumerate(todo)
            ]
        run(copies)

    def gaps():
        row8 = rows[pl.ds(pl.multiple_of(base, cap), cap), :]
        return [sv[r] + row8[r : r + 1, :] for r in range(cap)]

    def make():
        live_a = lax.broadcasted_iota(i32, (nvd, half), 0)
        live_b = lax.broadcasted_iota(i32, (nvd, half), 1)
        for r, gap in enumerate(gaps()):
            size_i = tbl[HEAD + 2 * n + base + r]
            size_j = tbl[HEAD + 3 * n + base + r]
            k = jnp.dot(s0[r], b0[r], preferred_element_type=f32)
            k += jnp.dot(s1[r], b1[r], preferred_element_type=f32)
            k = jnp.where((live_a < size_i) & (live_b < size_j), k, 0.0)
            t = (-k / gap).astype(bf16)
            st[r] = t
            if not client:
                se[r : r + 1, :] = jnp.sum(k * t.astype(f32), axis=0, keepdims=True)

    def take():
        ready = js[2]
        copies = [pltpu.make_async_copy(ready.at[r], st.at[r], sem.at[r, 0]) for r in range(cap)]
        copies += [
            pltpu.make_async_copy(vcol.at[lax.div(place(r), per_orb)], sv.at[r], sem.at[r, 1])
            for r in range(cap)
        ]
        run(copies)
        for r, gap in enumerate(gaps()):
            t = st[r].astype(f32)
            se[r : r + 1, :] = -jnp.sum(t * t * gap, axis=0, keepdims=True)

    if client:

        @pl.when(middle)
        def _():
            load()
            make()
            tout[...] = st[...]

        return
    if mode == "served":

        @pl.when(middle)
        def _():
            load()
            make()

        pl.when(jnp.logical_not(middle))(take)
    else:
        load()
        make()
    run(
        [pltpu.make_async_copy(st.at[r], tout.at[place(r)], sem_out.at[r]) for r in range(cap)]
        + [
            pltpu.make_async_copy(
                se, eout.at[pl.ds(pl.multiple_of(base, cap), cap), :], sem_out.at[cap]
            )
        ]
    )


def amplitudes(mode, call, per_orb, tables, left, sources, cap, held=(), after=()):
    tbl, rows, vcol = tables
    occ, nvd, half = vcol.shape
    qa = left[0].shape[2]
    client = mode == "client"
    operands = (tbl, rows, vcol, *left, *sources, *after)
    aliases = {len(operands) + k: k for k in range(len(held))}
    operands += tuple(held)
    if client:
        out_shape = jax.ShapeDtypeStruct((cap, nvd, half), bf16)
        out_specs = VMEM
    else:
        out_shape = (
            jax.ShapeDtypeStruct((occ * per_orb, nvd, half), bf16),
            jax.ShapeDtypeStruct((occ * per_orb, half), f32),
        )
        out_specs = (HBM, HBM)
    return pl.pallas_call(
        lambda *refs: amplitudes_kernel(mode, call, per_orb, not held, *refs),
        out_shape=out_shape,
        in_specs=[SMEM, VMEM] + [HBM] * (len(operands) - 2),
        out_specs=out_specs,
        scratch_shapes=[
            pltpu.VMEM((cap, nvd, half), f32),
            pltpu.VMEM((cap, nvd, qa), bf16),
            pltpu.VMEM((cap, nvd, qa), bf16),
            pltpu.VMEM((cap, qa, half), bf16),
            pltpu.VMEM((cap, qa, half), bf16),
            pltpu.VMEM((cap, nvd, half), bf16),
            pltpu.VMEM((cap, half), f32),
            pltpu.SemaphoreType.DMA((cap, 7)),
            pltpu.SemaphoreType.DMA((cap + 1,)),
        ],
        input_output_aliases=aliases,
        compiler_params=PARAMS,
        cost_estimate=TINY,
        name="amplitudes",
    )(*operands)


def density_kernel(start, t, d):
    count, half = d.shape[:2]
    per_orb = t.shape[0] // count
    first = pl.multiple_of(start[0], half)
    for o in range(count):
        own = range(o * per_orb, (o + 1) * per_orb)
        left = jnp.concatenate([t[k, pl.ds(first, half), :] for k in own], axis=1)
        right = jnp.concatenate([t[k] for k in own], axis=1)
        d[o] = lax.dot_general(left, right, (((1,), (1,)), ((), ())), preferred_element_type=f32)


def density_rows(t_all, start, per_orb, half):
    npair, nvd, width = t_all.shape
    occ = npair // per_orb
    step = 4 if occ % 4 == 0 else 1
    return pl.pallas_call(
        density_kernel,
        out_shape=jax.ShapeDtypeStruct((occ, half, nvd), f32),
        grid_spec=pltpu.PrefetchScalarGridSpec(
            num_scalar_prefetch=1,
            grid=(occ // step,),
            in_specs=[pl.BlockSpec((step * per_orb, nvd, width), lambda i, s: (i, 0, 0))],
            out_specs=pl.BlockSpec((step, half, nvd), lambda i, s: (i, 0, 0)),
        ),
        compiler_params=pltpu.CompilerParams(vmem_limit_bytes=LIMIT),
        cost_estimate=TINY,
        name="density_rows",
    )(start.reshape(1), t_all)


def line_plan(blocks, vir_energy, occ_energy, domain_size, partner_owner, partner_slot):
    occ, qa, nvd = blocks.shape
    pair_dev = partner_slot.shape[0]
    per_orb = pair_dev // occ
    peers = 8
    cap = pair_dev // peers
    half = nvd // 2
    wide = nvd + 128
    me, core = lax.axis_index("orb"), lax.axis_index("aux")
    z, y = me // 2, me % 2
    lower = z < 2
    middle = (z == 1) | (z == 2)
    col0 = core * half

    def pp(x, perm):
        return lax.ppermute(x, "orb", perm)

    def swap_core(x):
        return lax.ppermute(x, "aux", [(0, 1), (1, 0)])

    def flip(bit):
        return [(o, o ^ bit) for o in range(peers)]

    cross = [(2, 4), (3, 5), (4, 2), (5, 3)]
    outward = [(2, 0), (3, 1), (4, 6), (5, 7)]
    y_middle = [(2, 3), (3, 2), (4, 5), (5, 4)]
    y_end = [(0, 1), (1, 0), (6, 7), (7, 6)]

    other = swap_core(blocks)
    first = lax.dynamic_slice_in_dim(blocks, col0, half, 2)
    near_first, mid_first = pp(first, flip(2)), pp(first, cross)

    owner = partner_owner[:, 0]
    target = owner * cap + slot_ranks(owner)
    pairs = jnp.arange(pair_dev, dtype=i32)
    hit = target[None, :] == pairs[:, None]
    order = jnp.sum(jnp.where(hit, pairs[None, :], 0), axis=1)
    slots = jnp.sum(jnp.where(hit, partner_slot[None, :], 0), axis=1)
    lists = jnp.concatenate([order, slots]).astype(f32)
    small = jnp.concatenate(
        [
            jnp.concatenate(
                [
                    vir_energy,
                    occ_energy[:, None],
                    domain_size.astype(f32)[:, None],
                    jnp.zeros((occ, wide - nvd - 2), f32),
                ],
                axis=1,
            ),
            jnp.pad(lists[None], ((0, 7), (0, wide - lists.shape[0]))),
        ]
    )
    both = jnp.stack([small, pp(small, flip(1))])
    every = jnp.concatenate([both] + [pp(both, flip(bit)) for bit in (2, 4, 6)])

    column = jnp.stack([z, z ^ 1, jnp.where(lower, 2, 1), jnp.where(lower, 3, 0)])
    bases = jnp.concatenate([column * 2 + y, column * 2 + (1 - y)]) * cap
    head = [bases, middle[None], col0[None]]

    def lists_of(x):
        found = every[x, occ, : 2 * pair_dev].astype(i32)
        return found[:pair_dev], found[pair_dev:]

    def tables_of(x):
        order, slots = lists_of(x)
        theirs = jnp.take(orbitals, ((pairs // cap) ^ me) * occ + slots, axis=0)
        mine = jnp.take(every[x, :occ], order // per_orb, axis=0)
        rows = lax.dynamic_slice_in_dim(theirs, col0, half, 1) - (
            theirs[:, nvd : nvd + 1] + mine[:, nvd : nvd + 1]
        )
        size_i, size_j = mine[:, nvd + 1], theirs[:, nvd + 1].astype(i32) - col0
        vcol = jnp.broadcast_to(every[x, :occ, :nvd, None], (occ, nvd, half))
        return table_of(head + [order, slots, size_i, size_j]), rows, vcol

    second = lax.dynamic_slice_in_dim(other, col0, half, 2)
    every, second = lax.optimization_barrier((every, second))
    orbitals = every[:, :occ].reshape(peers * occ, wide)
    tables = tables_of(0)
    beside_list = table_of(head + [lists_of(1)[1]])
    relay_list = table_of(head + [lists_of(3)[1]])
    own = [first, second]
    near = [near_first, pp(second, flip(2))]
    mid = [mid_first, pp(second, cross)]
    far = [pp(x, cross) for x in near]
    left = turn([blocks, other])

    def own_pairs(k, mode, sources, held=(), after=()):
        return amplitudes(mode, k, per_orb, tables, left, sources, cap, held, after)

    beside = pp(pack(beside_list, 0, own, cap), flip(1))
    held = own_pairs(0, "slots", own)
    packed = pack(beside_list, 1, near, cap, after=(held[1],))
    beside_near = pp(packed, flip(1))
    relay = pp(pack(relay_list, 2, mid, cap, only_middle=True, after=(packed,)), outward)
    across = [swap_core(x) for x in near]
    held = own_pairs(4, "asked", [beside], held, (packed,))
    held = own_pairs(1, "slots", near, held)
    client_left = turn(near + across)
    client = tables_of(2)
    gone = amplitudes("client", 2, per_orb, client, client_left, mid, cap, after=(held[1],))
    ready_2 = pp(gone, outward)
    held = own_pairs(5, "asked", [beside_near], held, (gone,))
    packed = pack(beside_list, 2, mid, cap, relayed=relay, after=(held[1],))
    third = pp(packed, flip(1))
    relays = []
    for x in far:
        packed = pack(relay_list, 3, [x], cap, only_middle=True, after=(packed,))
        relays.append(pp(packed, outward))
    gone = amplitudes("client", 3, per_orb, client, client_left, far, cap, after=(packed,))
    ready_3 = pp(gone, outward)
    fourth = []
    packed = gone
    for x, came in zip(far, relays):
        packed = pack(beside_list, 3, [x], cap, relayed=came, after=(packed,))
        fourth.append(pp(packed, flip(1)))
        if len(fourth) == 1:
            held = own_pairs(2, "served", mid + [ready_2], held, (packed,))
            held = own_pairs(6, "asked", [third], held)
            packed = held[1]
    held = own_pairs(3, "served", far + [ready_3], held, (packed,))
    t_all, e_all = own_pairs(7, "asked_two", fourth, held)

    away = swap_core(density_rows(t_all, (1 - core) * half, per_orb, half))
    density = density_rows(t_all, core * half, per_orb, half) + away

    sums = jnp.sum(e_all, axis=1)
    energy = jnp.sum(jnp.where(hit, sums[:, None], 0.0), axis=0)
    energy = (energy + swap_core(energy)) / nvd
    return (energy, density)


def solution(mesh):
    in_specs = (
        P(("mol", "orb"), "aux", None),
        P(("mol", "orb"), None),
        P(("mol", "orb")),
        P(("mol", "orb")),
        P(("mol", "orb"), None),
        P(("mol", "orb")),
    )
    out_specs = (P(("mol", "orb")), P(("mol", "orb"), "aux", None))
    return jax.shard_map(
        line_plan if fits_line(mesh) else by_requests, mesh=mesh, in_specs=in_specs, out_specs=out_specs, check_vma=False
    )
```

```python
import jax
import jax.numpy as jnp
from jax import lax
from jax.experimental import pallas as pl
from jax.experimental.pallas import tpu as pltpu
from jax.sharding import PartitionSpec as P

f32, bf16, i32 = jnp.float32, jnp.bfloat16, jnp.int32
HBM = pl.BlockSpec(memory_space=pltpu.HBM)
SMEM = pl.BlockSpec(memory_space=pltpu.SMEM)
VMEM = pl.BlockSpec(memory_space=pltpu.VMEM)
LIMIT = 48 * 1024 * 1024


def slot_ranks(owner):
    count = owner.shape[0]
    order = jnp.arange(count, dtype=jnp.int32)
    same = (owner[:, None] == owner[None, :]) & (order[None, :] < order[:, None])
    return jnp.sum(same.astype(jnp.int32), axis=1)


def by_requests(blocks, vir_energy, occ_energy, domain_size, partner_owner, partner_slot):
    occ_dev, half_aux, nvd = blocks.shape
    pair_dev = partner_slot.shape[0]
    per_orb = pair_dev // occ_dev
    peers = lax.axis_size("orb")
    cap = max(2, (pair_dev + peers - 1) // peers)
    owner = partner_owner[:, 0]
    ranks = slot_ranks(owner)
    target = owner * cap + ranks
    wanted = (target[:, None] == jnp.arange(peers * cap, dtype=jnp.int32)[None, :]).astype(
        jnp.int32
    )
    requests = jnp.sum(wanted * partner_slot[:, None], axis=0).reshape(peers, cap)
    incoming = lax.all_to_all(requests, "orb", split_axis=0, concat_axis=0, tiled=True)
    flat_in = incoming.reshape(-1)
    send_blocks = jnp.take(blocks, flat_in, axis=0).reshape(peers, cap, half_aux, nvd)
    send_vir = jnp.take(vir_energy, flat_in, axis=0).reshape(peers, cap, nvd)
    send_occ = jnp.take(occ_energy, flat_in).reshape(peers, cap)
    send_size = jnp.take(domain_size, flat_in).astype(jnp.float32).reshape(peers, cap)
    got_blocks = lax.all_to_all(send_blocks, "orb", split_axis=0, concat_axis=0, tiled=True)
    got_vir, got_occ, got_size = (
        lax.all_to_all(send_vir, "orb", split_axis=0, concat_axis=0, tiled=True),
        lax.all_to_all(send_occ, "orb", split_axis=0, concat_axis=0, tiled=True),
        lax.all_to_all(send_size, "orb", split_axis=0, concat_axis=0, tiled=True),
    )
    partner = jnp.take(got_blocks.reshape(peers * cap, half_aux, nvd), target, axis=0).reshape(
        occ_dev, per_orb, half_aux, nvd
    )
    partner_vir = jnp.take(got_vir.reshape(peers * cap, nvd), target, axis=0).reshape(
        occ_dev, per_orb, nvd
    )
    partner_occ = jnp.take(got_occ.reshape(-1), target).reshape(occ_dev, per_orb)
    partner_size = jnp.take(got_size.reshape(-1), target).reshape(occ_dev, per_orb)
    half = nvd // lax.axis_size("aux")
    integrals = lax.psum_scatter(
        jnp.einsum("oqa,opqb->aopb", blocks, partner, preferred_element_type=jnp.float32),
        "aux",
        scatter_dimension=0,
        tiled=True,
    )
    row_start = lax.axis_index("aux") * half
    rows = row_start + jnp.arange(half, dtype=jnp.int32)
    cols = jnp.arange(nvd, dtype=jnp.int32).astype(jnp.float32)
    mask = (rows[:, None, None, None] < domain_size[None, :, None, None]) & (
        cols[None, None, None, :] < partner_size[None, :, :, None]
    )
    integrals = jnp.where(mask, integrals, jnp.zeros_like(integrals))
    vir_rows = lax.dynamic_slice_in_dim(vir_energy, row_start, half, 1)
    gap = (
        vir_rows.T[:, :, None, None]
        + partner_vir[None, :, :, :]
        - occ_energy[None, :, None, None]
        - partner_occ[None, :, :, None]
    )
    amp_rows = (-integrals / gap).astype(jnp.bfloat16)
    partial_energy = jnp.sum(integrals * amp_rows.astype(jnp.float32), axis=(0, 3))
    energy = lax.psum(partial_energy, "aux").reshape(pair_dev) / nvd
    density = jnp.einsum(
        "aopb,copb->oac",
        amp_rows,
        lax.all_gather(amp_rows, "aux", axis=0, tiled=True),
        preferred_element_type=jnp.float32,
    )
    return (energy, density)


def fits_line(mesh):
    return mesh.shape["orb"] == 8 and mesh.shape["aux"] == 2


TINY = pl.CostEstimate(flops=1, bytes_accessed=1, transcendentals=0)
PARAMS = pltpu.CompilerParams(vmem_limit_bytes=LIMIT)


def lists_kernel(cap, vir, occ, size, owner, slot, small, hit):
    n, (count, nvd) = hit.shape[0], vir.shape

    def column(row, m):
        eye = lax.broadcasted_iota(i32, (m, m), 0) == lax.broadcasted_iota(i32, (m, m), 1)
        return jnp.sum(jnp.where(eye, row, 0.0), axis=1, keepdims=True)

    down = lax.broadcasted_iota(i32, (n, n), 0).astype(f32)
    along = lax.broadcasted_iota(i32, (n, n), 1).astype(f32)
    owner_row = owner[...].astype(f32)
    owner_col = column(owner_row, n)
    before = (owner_col == owner_row) & (along < down)
    target = owner_col * cap + jnp.sum(jnp.where(before, 1.0, 0.0), axis=1, keepdims=True)
    found = target == along
    hit[...] = jnp.where(found, 1.0, 0.0)
    small[...] = jnp.zeros_like(small)
    small[:count, :nvd] = vir[...]
    lane = lax.broadcasted_iota(i32, (count, 128), 1)
    occ_col, size_col = column(occ[...], count), column(size[...].astype(f32), count)
    small[:count, nvd:] = jnp.where(lane == 0, occ_col, jnp.where(lane == 1, size_col, 0.0))
    small[count : count + 1, :n] = jnp.sum(jnp.where(found, down, 0.0), axis=0, keepdims=True)
    slot_col = column(slot[...].astype(f32), n)
    small[count : count + 1, 128 : 128 + n] = jnp.sum(
        jnp.where(found, slot_col, 0.0), axis=0, keepdims=True
    )


def lists(vir, occ, size, owner, slot, cap):
    count, nvd = vir.shape
    n = slot.shape[0]
    return pl.pallas_call(
        lambda *refs: lists_kernel(cap, *refs),
        out_shape=(
            jax.ShapeDtypeStruct((count + 8, nvd + 128), f32),
            jax.ShapeDtypeStruct((n, n), f32),
        ),
        in_specs=[VMEM] * 5,
        out_specs=(VMEM, VMEM),
        compiler_params=PARAMS,
        cost_estimate=TINY,
        name="lists",
    )(vir, occ.reshape(1, -1), size.reshape(1, -1), owner.reshape(1, -1), slot.reshape(1, -1))


ORDER, SLOT, SIZE_I, SIZE_J, HEAD = range(5)
MIDDLE, COLUMN = 8, 9


def pick(one, values):
    return lax.dot_general(
        one, values, (((0,), (0,)), ((), ())),
        precision=lax.Precision.HIGHEST, preferred_element_type=f32,
    )


def tables_kernel(cap, per_orb, meta, *refs):
    smalls, outs = refs[:8], refs[8:]
    count, nvd = smalls[0].shape[0] - 8, smalls[0].shape[1] - 128
    n = 8 * cap
    me, col0 = meta[0], meta[1]
    z, y = me // 2, me % 2
    lower = z < 2
    middle = jnp.where((z == 1) | (z == 2), 1, 0)
    places = [z, z ^ 1, jnp.where(lower, 2, 1), jnp.where(lower, 3, 0)]
    head = [(2 * p + y) * cap for p in places] + [(2 * p + 1 - y) * cap for p in places]
    lane = lax.broadcasted_iota(i32, (1, 128), 1)
    head_row = jnp.zeros((1, 128), i32)
    for k, value in enumerate(head + [middle, col0]):
        head_row = jnp.where(lane == k, value, head_row)
    orbitals = jnp.concatenate([x[:count, :] for x in smalls], axis=0)
    columns = jnp.where(col0 == 0, orbitals[:, : nvd // 2], orbitals[:, nvd // 2 : nvd])
    extra = orbitals[:, nvd:]

    def build(x, tbl, rows=None):
        order = smalls[x][count : count + 1, :n].astype(i32)
        slots = smalls[x][count : count + 1, 128 : 128 + n].astype(i32)
        tbl[...] = jnp.zeros_like(tbl)
        tbl[HEAD : HEAD + 1, :] = head_row
        tbl[SLOT : SLOT + 1, :n] = slots
        if rows is None:
            return
        tbl[ORDER : ORDER + 1, :n] = order
        pair = lax.broadcasted_iota(i32, (1, n), 1)
        owner = sum(jnp.where(pair >= k * cap, 1, 0) for k in range(1, 8))
        index = (owner ^ me) * count + slots
        theirs = jnp.where(lax.broadcasted_iota(i32, (8 * count, n), 0) == index, 1.0, 0.0)
        first = sum(jnp.where(order >= k * per_orb, 1, 0) for k in range(1, count))
        mine = jnp.where(lax.broadcasted_iota(i32, (count, n), 0) == first, 1.0, 0.0)
        own = smalls[x][:count, nvd:]
        rows[...] = pick(theirs, columns) - (pick(theirs, extra)[:, :1] + pick(mine, own)[:, :1])
        tbl[SIZE_I : SIZE_I + 1, :n] = pick(own, mine)[1:2, :].astype(i32)
        tbl[SIZE_J : SIZE_J + 1, :n] = pick(extra, theirs)[1:2, :].astype(i32) - col0

    build(0, outs[0], outs[1])
    build(2, outs[2], outs[3])
    build(1, outs[4])
    build(3, outs[5])


def tables_of(meta, smalls, cap, per_orb, half):
    table = jax.ShapeDtypeStruct((8, 128), i32)
    rows = jax.ShapeDtypeStruct((8 * cap, half), f32)
    return pl.pallas_call(
        lambda *refs: tables_kernel(cap, per_orb, *refs),
        out_shape=(table, rows, table, rows, table, table),
        in_specs=[SMEM] + [VMEM] * 8,
        out_specs=[VMEM] * 6,
        compiler_params=PARAMS,
        cost_estimate=TINY,
        name="tables",
    )(meta, *smalls)


def pack_kernel(call, only_middle, relayed, after, tbl, *refs):
    out, sems = refs[-2:]
    halves, cap = out.shape[:2]
    base = tbl[HEAD, call]
    middle = tbl[HEAD, MIDDLE] == 1

    def run(copies):
        for copy in copies:
            copy.start()
        for copy in copies:
            copy.wait()

    def gather():
        run(
            [
                pltpu.make_async_copy(
                    refs[q].at[tbl[SLOT, base + r]], out.at[q, r], sems.at[q, r]
                )
                for q in range(halves)
                for r in range(cap)
            ]
        )

    if not only_middle and not relayed:
        gather()
    else:
        pl.when(middle)(gather)
    if relayed:
        came = refs[halves]

        @pl.when(jnp.logical_not(middle))
        def _():
            run(
                [pltpu.make_async_copy(came.at[q], out.at[q], sems.at[q, 0]) for q in range(halves)]
            )


def pack(tbl, call, sources, cap, only_middle=False, relayed=None, after=()):
    halves = len(sources)
    shape = (halves, cap) + sources[0].shape[1:]
    operands = (*sources, *(() if relayed is None else (relayed,)), *after)
    return pl.pallas_call(
        lambda *refs: pack_kernel(call, only_middle, relayed is not None, len(after), *refs),
        out_shape=jax.ShapeDtypeStruct(shape, bf16),
        in_specs=[SMEM] + [HBM] * len(operands),
        out_specs=VMEM,
        scratch_shapes=[pltpu.SemaphoreType.DMA((halves, cap))],
        compiler_params=PARAMS,
        cost_estimate=TINY,
        name="pack",
    )(tbl, *operands)


def turn_kernel(*refs):
    half = len(refs) // 2
    for x, out in zip(refs[:half], refs[half:]):
        for r in range(x.shape[0]):
            out[r] = x[r].T


def turn(arrays):
    count, rows, cols = arrays[0].shape
    step = 4 if count % 4 == 0 else 1
    n = len(arrays)
    return pl.pallas_call(
        turn_kernel,
        out_shape=[jax.ShapeDtypeStruct((count, cols, rows), bf16)] * n,
        grid=(count // step,),
        in_specs=[pl.BlockSpec((step, rows, cols), lambda i: (i, 0, 0))] * n,
        out_specs=[pl.BlockSpec((step, cols, rows), lambda i: (i, 0, 0))] * n,
        compiler_params=PARAMS,
        cost_estimate=TINY,
        name="turn",
    )(*arrays)


def amplitudes_kernel(mode, call, per_orb, first, tbl, rows, vcol, *refs):
    sv, s0, s1, b0, b1, st, se, sem, sem_out = refs[-9:]
    client = mode == "client"
    if client:
        tout = refs[-10]
        left, js = refs[:4], refs[4:6]
    else:
        tout, eout = refs[-11:-9]
        left, js = refs[:2], refs[2:5]
    if mode == "asked":
        js = (js[0].at[0], js[0].at[1])
    if mode == "asked_two":
        js = (js[0].at[0], js[1].at[0])
    cap = sv.shape[0]
    nvd, half = sv.shape[1], sv.shape[2]
    base = tbl[HEAD, call]
    middle = tbl[HEAD, MIDDLE] == 1

    def place(r):
        return tbl[ORDER, base + r]

    def run(copies):
        for copy in copies:
            copy.start()
        for copy in copies:
            copy.wait()

    def load():
        copies = []
        for r in range(cap):
            i = lax.div(place(r), per_orb)
            slot = r if mode.startswith("asked") else tbl[SLOT, base + r]
            todo = [
                (vcol.at[i], sv.at[r]),
                (js[0].at[slot], b0.at[r]),
                (js[1].at[slot], b1.at[r]),
            ]
            if client:
                here = pl.ds(pl.multiple_of(tbl[HEAD, COLUMN], half), half)
                there = pl.ds(pl.multiple_of(half - tbl[HEAD, COLUMN], half), half)
                todo += [
                    (left[0].at[i], s0.at[r, here, :]),
                    (left[1].at[i], s1.at[r, here, :]),
                    (left[2].at[i], s1.at[r, there, :]),
                    (left[3].at[i], s0.at[r, there, :]),
                ]
            else:
                todo += [(left[0].at[i], s0.at[r]), (left[1].at[i], s1.at[r])]
            copies += [
                pltpu.make_async_copy(x, to, sem.at[r, k]) for k, (x, to) in enumerate(todo)
            ]
        run(copies)

    def gaps():
        row8 = rows[pl.ds(pl.multiple_of(base, cap), cap), :]
        return [sv[r] + row8[r : r + 1, :] for r in range(cap)]

    def make():
        live_a = lax.broadcasted_iota(i32, (nvd, half), 0)
        live_b = lax.broadcasted_iota(i32, (nvd, half), 1)
        for r, gap in enumerate(gaps()):
            size_i = tbl[SIZE_I, base + r]
            size_j = tbl[SIZE_J, base + r]
            k = jnp.dot(s0[r], b0[r], preferred_element_type=f32)
            k += jnp.dot(s1[r], b1[r], preferred_element_type=f32)
            k = jnp.where((live_a < size_i) & (live_b < size_j), k, 0.0)
            t = (-k / gap).astype(bf16)
            st[r] = t
            if not client:
                se[r : r + 1, :] = jnp.sum(k * t.astype(f32), axis=0, keepdims=True)

    def take():
        ready = js[2]
        copies = [pltpu.make_async_copy(ready.at[r], st.at[r], sem.at[r, 0]) for r in range(cap)]
        copies += [
            pltpu.make_async_copy(vcol.at[lax.div(place(r), per_orb)], sv.at[r], sem.at[r, 1])
            for r in range(cap)
        ]
        run(copies)
        for r, gap in enumerate(gaps()):
            t = st[r].astype(f32)
            se[r : r + 1, :] = -jnp.sum(t * t * gap, axis=0, keepdims=True)

    if client:

        @pl.when(middle)
        def _():
            load()
            make()
            tout[...] = st[...]

        return
    if mode == "served":

        @pl.when(middle)
        def _():
            load()
            make()

        pl.when(jnp.logical_not(middle))(take)
    else:
        load()
        make()
    run(
        [pltpu.make_async_copy(st.at[r], tout.at[place(r)], sem_out.at[r]) for r in range(cap)]
        + [
            pltpu.make_async_copy(
                se, eout.at[pl.ds(pl.multiple_of(base, cap), cap), :], sem_out.at[cap]
            )
        ]
    )


def amplitudes(mode, call, per_orb, tables, left, sources, cap, held=(), after=()):
    tbl, rows, vcol = tables
    occ, nvd, half = vcol.shape
    qa = left[0].shape[2]
    client = mode == "client"
    operands = (tbl, rows, vcol, *left, *sources, *after)
    aliases = {len(operands) + k: k for k in range(len(held))}
    operands += tuple(held)
    if client:
        out_shape = jax.ShapeDtypeStruct((cap, nvd, half), bf16)
        out_specs = VMEM
    else:
        out_shape = (
            jax.ShapeDtypeStruct((occ * per_orb, nvd, half), bf16),
            jax.ShapeDtypeStruct((occ * per_orb, half), f32),
        )
        out_specs = (HBM, HBM)
    return pl.pallas_call(
        lambda *refs: amplitudes_kernel(mode, call, per_orb, not held, *refs),
        out_shape=out_shape,
        in_specs=[SMEM, VMEM] + [HBM] * (len(operands) - 2),
        out_specs=out_specs,
        scratch_shapes=[
            pltpu.VMEM((cap, nvd, half), f32),
            pltpu.VMEM((cap, nvd, qa), bf16),
            pltpu.VMEM((cap, nvd, qa), bf16),
            pltpu.VMEM((cap, qa, half), bf16),
            pltpu.VMEM((cap, qa, half), bf16),
            pltpu.VMEM((cap, nvd, half), bf16),
            pltpu.VMEM((cap, half), f32),
            pltpu.SemaphoreType.DMA((cap, 7)),
            pltpu.SemaphoreType.DMA((cap + 1,)),
        ],
        input_output_aliases=aliases,
        compiler_params=PARAMS,
        cost_estimate=TINY,
        name="amplitudes",
    )(*operands)


def density_kernel(start, t, d):
    count, half = d.shape[:2]
    per_orb = t.shape[0] // count
    first = pl.multiple_of(start[0], half)
    for o in range(count):
        own = range(o * per_orb, (o + 1) * per_orb)
        left = jnp.concatenate([t[k, pl.ds(first, half), :] for k in own], axis=1)
        right = jnp.concatenate([t[k] for k in own], axis=1)
        d[o] = lax.dot_general(left, right, (((1,), (1,)), ((), ())), preferred_element_type=f32)


def density_rows(t_all, start, per_orb, half):
    npair, nvd, width = t_all.shape
    occ = npair // per_orb
    step = 4 if occ % 4 == 0 else 1
    return pl.pallas_call(
        density_kernel,
        out_shape=jax.ShapeDtypeStruct((occ, half, nvd), f32),
        grid_spec=pltpu.PrefetchScalarGridSpec(
            num_scalar_prefetch=1,
            grid=(occ // step,),
            in_specs=[pl.BlockSpec((step * per_orb, nvd, width), lambda i, s: (i, 0, 0))],
            out_specs=pl.BlockSpec((step, half, nvd), lambda i, s: (i, 0, 0)),
        ),
        compiler_params=pltpu.CompilerParams(vmem_limit_bytes=LIMIT),
        cost_estimate=TINY,
        name="density_rows",
    )(start.reshape(1), t_all)


def line_plan(blocks, vir_energy, occ_energy, domain_size, partner_owner, partner_slot):
    occ, qa, nvd = blocks.shape
    pair_dev = partner_slot.shape[0]
    per_orb = pair_dev // occ
    peers = 8
    cap = pair_dev // peers
    half = nvd // 2
    me, core = lax.axis_index("orb"), lax.axis_index("aux")
    col0 = core * half

    def pp(x, perm):
        return lax.ppermute(x, "orb", perm)

    def swap_core(x):
        return lax.ppermute(x, "aux", [(0, 1), (1, 0)])

    def flip(bits):
        return [(o, o ^ bits) for o in range(peers)]

    cross = [(2, 4), (3, 5), (4, 2), (5, 3)]
    outward = [(2, 0), (3, 1), (4, 6), (5, 7)]

    small, hit = lists(vir_energy, occ_energy, domain_size, partner_owner, partner_slot, cap)
    smalls = [small] + [pp(small, flip(bits)) for bits in range(1, peers)]

    other = swap_core(blocks)
    own = [lax.dynamic_slice_in_dim(x, col0, half, 2) for x in (blocks, other)]
    sent, smalls = lax.optimization_barrier((own[0], smalls))
    near = [pp(x, flip(2)) for x in (sent, own[1])]
    mid = [pp(x, cross) for x in (sent, own[1])]
    tbl, rows, client_tbl, client_rows, beside_list, relay_list = tables_of(
        jnp.stack([me, col0]), smalls, cap, per_orb, half
    )

    def spread(vir):
        return jnp.broadcast_to(vir[:, :, None], (occ, nvd, half))

    tables = (tbl, rows, spread(vir_energy))
    client = (client_tbl, client_rows, spread(smalls[2][:occ, :nvd]))

    def own_pairs(k, mode, sources, held=(), after=()):
        return amplitudes(mode, k, per_orb, tables, left, sources, cap, held, after)

    packed = pack(beside_list, 0, own, cap)
    beside = pp(packed, flip(1))
    left = turn([blocks, other])
    held = own_pairs(0, "slots", own, after=(packed,))
    first, held = lax.optimization_barrier((near[0], held))
    far = [pp(first, cross)]
    across = [swap_core(first)]
    held = own_pairs(4, "asked", [beside], held)
    second, held = lax.optimization_barrier((near[1], held))
    far.append(pp(second, cross))
    across.append(swap_core(second))
    near = [first, second]
    packed = pack(relay_list, 2, mid, cap, only_middle=True, after=(held[1],))
    relay = pp(packed, outward)
    packed = pack(beside_list, 1, near, cap, after=(packed,))
    beside_near = pp(packed, flip(1))
    client_left = turn(near + across)
    gone = amplitudes("client", 2, per_orb, client, client_left, mid, cap, after=(packed,))
    ready_2 = pp(gone, outward)
    held = own_pairs(1, "slots", near, held, (gone,))
    relays = []
    packed = pack(relay_list, 3, far[:1], cap, only_middle=True, after=(held[1],))
    relays.append(pp(packed, outward))
    packed = pack(beside_list, 2, mid, cap, relayed=relay, after=(packed,))
    third = pp(packed, flip(1))
    held = own_pairs(5, "asked", [beside_near], held, (packed,))
    packed = pack(relay_list, 3, far[1:], cap, only_middle=True, after=(held[1],))
    relays.append(pp(packed, outward))
    gone = amplitudes("client", 3, per_orb, client, client_left, far, cap, after=(packed,))
    ready_3 = pp(gone, outward)
    packed = pack(beside_list, 3, far[:1], cap, relayed=relays[0], after=(gone,))
    fourth = [pp(packed, flip(1))]
    held = own_pairs(2, "served", mid + [ready_2], held, (packed,))
    held = own_pairs(6, "asked", [third], held)
    packed = pack(beside_list, 3, far[1:], cap, relayed=relays[1], after=(held[1],))
    fourth.append(pp(packed, flip(1)))
    held = own_pairs(3, "served", far + [ready_3], held, (packed,))
    t_all, e_all = own_pairs(7, "asked_two", fourth, held)

    away = swap_core(density_rows(t_all, (1 - core) * half, per_orb, half))
    density = density_rows(t_all, core * half, per_orb, half) + away

    energy = jnp.sum(hit * jnp.sum(e_all, axis=1)[None, :], axis=1)
    energy = (energy + swap_core(energy)) / nvd
    return (energy, density)


def solution(mesh):
    in_specs = (
        P(("mol", "orb"), "aux", None),
        P(("mol", "orb"), None),
        P(("mol", "orb")),
        P(("mol", "orb")),
        P(("mol", "orb"), None),
        P(("mol", "orb")),
    )
    out_specs = (P(("mol", "orb")), P(("mol", "orb"), "aux", None))
    return jax.shard_map(
        line_plan if fits_line(mesh) else by_requests, mesh=mesh, in_specs=in_specs, out_specs=out_specs, check_vma=False
    )
```

```python
import jax
import jax.numpy as jnp
from jax import lax
from jax.experimental import pallas as pl
from jax.experimental.pallas import tpu as pltpu
from jax.sharding import PartitionSpec as P

f32, bf16, i32 = jnp.float32, jnp.bfloat16, jnp.int32
HBM = pl.BlockSpec(memory_space=pltpu.HBM)
SMEM = pl.BlockSpec(memory_space=pltpu.SMEM)
VMEM = pl.BlockSpec(memory_space=pltpu.VMEM)
LIMIT = 48 * 1024 * 1024


def slot_ranks(owner):
    count = owner.shape[0]
    order = jnp.arange(count, dtype=jnp.int32)
    same = (owner[:, None] == owner[None, :]) & (order[None, :] < order[:, None])
    return jnp.sum(same.astype(jnp.int32), axis=1)


def by_requests(blocks, vir_energy, occ_energy, domain_size, partner_owner, partner_slot):
    occ_dev, half_aux, nvd = blocks.shape
    pair_dev = partner_slot.shape[0]
    per_orb = pair_dev // occ_dev
    peers = lax.axis_size("orb")
    cap = max(2, (pair_dev + peers - 1) // peers)
    owner = partner_owner[:, 0]
    ranks = slot_ranks(owner)
    target = owner * cap + ranks
    wanted = (target[:, None] == jnp.arange(peers * cap, dtype=jnp.int32)[None, :]).astype(
        jnp.int32
    )
    requests = jnp.sum(wanted * partner_slot[:, None], axis=0).reshape(peers, cap)
    incoming = lax.all_to_all(requests, "orb", split_axis=0, concat_axis=0, tiled=True)
    flat_in = incoming.reshape(-1)
    send_blocks = jnp.take(blocks, flat_in, axis=0).reshape(peers, cap, half_aux, nvd)
    send_vir = jnp.take(vir_energy, flat_in, axis=0).reshape(peers, cap, nvd)
    send_occ = jnp.take(occ_energy, flat_in).reshape(peers, cap)
    send_size = jnp.take(domain_size, flat_in).astype(jnp.float32).reshape(peers, cap)
    got_blocks = lax.all_to_all(send_blocks, "orb", split_axis=0, concat_axis=0, tiled=True)
    got_vir, got_occ, got_size = (
        lax.all_to_all(send_vir, "orb", split_axis=0, concat_axis=0, tiled=True),
        lax.all_to_all(send_occ, "orb", split_axis=0, concat_axis=0, tiled=True),
        lax.all_to_all(send_size, "orb", split_axis=0, concat_axis=0, tiled=True),
    )
    partner = jnp.take(got_blocks.reshape(peers * cap, half_aux, nvd), target, axis=0).reshape(
        occ_dev, per_orb, half_aux, nvd
    )
    partner_vir = jnp.take(got_vir.reshape(peers * cap, nvd), target, axis=0).reshape(
        occ_dev, per_orb, nvd
    )
    partner_occ = jnp.take(got_occ.reshape(-1), target).reshape(occ_dev, per_orb)
    partner_size = jnp.take(got_size.reshape(-1), target).reshape(occ_dev, per_orb)
    half = nvd // lax.axis_size("aux")
    integrals = lax.psum_scatter(
        jnp.einsum("oqa,opqb->aopb", blocks, partner, preferred_element_type=jnp.float32),
        "aux",
        scatter_dimension=0,
        tiled=True,
    )
    row_start = lax.axis_index("aux") * half
    rows = row_start + jnp.arange(half, dtype=jnp.int32)
    cols = jnp.arange(nvd, dtype=jnp.int32).astype(jnp.float32)
    mask = (rows[:, None, None, None] < domain_size[None, :, None, None]) & (
        cols[None, None, None, :] < partner_size[None, :, :, None]
    )
    integrals = jnp.where(mask, integrals, jnp.zeros_like(integrals))
    vir_rows = lax.dynamic_slice_in_dim(vir_energy, row_start, half, 1)
    gap = (
        vir_rows.T[:, :, None, None]
        + partner_vir[None, :, :, :]
        - occ_energy[None, :, None, None]
        - partner_occ[None, :, :, None]
    )
    amp_rows = (-integrals / gap).astype(jnp.bfloat16)
    partial_energy = jnp.sum(integrals * amp_rows.astype(jnp.float32), axis=(0, 3))
    energy = lax.psum(partial_energy, "aux").reshape(pair_dev) / nvd
    density = jnp.einsum(
        "aopb,copb->oac",
        amp_rows,
        lax.all_gather(amp_rows, "aux", axis=0, tiled=True),
        preferred_element_type=jnp.float32,
    )
    return (energy, density)


def fits_line(mesh):
    return mesh.shape["orb"] == 8 and mesh.shape["aux"] == 2


TINY = pl.CostEstimate(flops=1, bytes_accessed=1, transcendentals=0)
PARAMS = pltpu.CompilerParams(vmem_limit_bytes=LIMIT)


def lists_kernel(cap, vir, occ, size, owner, slot, small, hit):
    n, (count, nvd) = hit.shape[0], vir.shape

    def column(row, m):
        eye = lax.broadcasted_iota(i32, (m, m), 0) == lax.broadcasted_iota(i32, (m, m), 1)
        return jnp.sum(jnp.where(eye, row, 0.0), axis=1, keepdims=True)

    down = lax.broadcasted_iota(i32, (n, n), 0).astype(f32)
    along = lax.broadcasted_iota(i32, (n, n), 1).astype(f32)
    owner_row = owner[...].astype(f32)
    owner_col = column(owner_row, n)
    before = (owner_col == owner_row) & (along < down)
    target = owner_col * cap + jnp.sum(jnp.where(before, 1.0, 0.0), axis=1, keepdims=True)
    found = target == along
    hit[...] = jnp.where(found, 1.0, 0.0)
    small[...] = jnp.zeros_like(small)
    small[:count, :nvd] = vir[...]
    lane = lax.broadcasted_iota(i32, (count, 128), 1)
    occ_col, size_col = column(occ[...], count), column(size[...].astype(f32), count)
    small[:count, nvd:] = jnp.where(lane == 0, occ_col, jnp.where(lane == 1, size_col, 0.0))
    small[count : count + 1, :n] = jnp.sum(jnp.where(found, down, 0.0), axis=0, keepdims=True)
    slot_col = column(slot[...].astype(f32), n)
    small[count : count + 1, 128 : 128 + n] = jnp.sum(
        jnp.where(found, slot_col, 0.0), axis=0, keepdims=True
    )


def lists(vir, occ, size, owner, slot, cap):
    count, nvd = vir.shape
    n = slot.shape[0]
    return pl.pallas_call(
        lambda *refs: lists_kernel(cap, *refs),
        out_shape=(
            jax.ShapeDtypeStruct((count + 8, nvd + 128), f32),
            jax.ShapeDtypeStruct((n, n), f32),
        ),
        in_specs=[VMEM] * 5,
        out_specs=(VMEM, VMEM),
        compiler_params=PARAMS,
        cost_estimate=TINY,
        name="lists",
    )(vir, occ.reshape(1, -1), size.reshape(1, -1), owner.reshape(1, -1), slot.reshape(1, -1))


ORDER, SLOT, SIZE_I, SIZE_J, HEAD = range(5)
MIDDLE, COLUMN = 8, 9


def pick(one, values):
    return lax.dot_general(
        one, values, (((0,), (0,)), ((), ())),
        precision=lax.Precision.HIGHEST, preferred_element_type=f32,
    )


def tables_kernel(cap, per_orb, meta, *refs):
    smalls, outs = refs[:8], refs[8:]
    count, nvd = smalls[0].shape[0] - 8, smalls[0].shape[1] - 128
    n = 8 * cap
    me, col0 = meta[0], meta[1]
    z, y = me // 2, me % 2
    lower = z < 2
    middle = jnp.where((z == 1) | (z == 2), 1, 0)
    places = [z, z ^ 1, jnp.where(lower, 2, 1), jnp.where(lower, 3, 0)]
    head = [(2 * p + y) * cap for p in places] + [(2 * p + 1 - y) * cap for p in places]
    lane = lax.broadcasted_iota(i32, (1, 128), 1)
    head_row = jnp.zeros((1, 128), i32)
    for k, value in enumerate(head + [middle, col0]):
        head_row = jnp.where(lane == k, value, head_row)
    orbitals = jnp.concatenate([x[:count, :] for x in smalls], axis=0)
    columns = jnp.where(col0 == 0, orbitals[:, : nvd // 2], orbitals[:, nvd // 2 : nvd])
    extra = orbitals[:, nvd:]

    def build(x, tbl, rows=None):
        order = smalls[x][count : count + 1, :n].astype(i32)
        slots = smalls[x][count : count + 1, 128 : 128 + n].astype(i32)
        tbl[...] = jnp.zeros_like(tbl)
        tbl[HEAD : HEAD + 1, :] = head_row
        tbl[SLOT : SLOT + 1, :n] = slots
        if rows is None:
            return
        tbl[ORDER : ORDER + 1, :n] = order
        pair = lax.broadcasted_iota(i32, (1, n), 1)
        owner = sum(jnp.where(pair >= k * cap, 1, 0) for k in range(1, 8))
        index = (owner ^ me) * count + slots
        theirs = jnp.where(lax.broadcasted_iota(i32, (8 * count, n), 0) == index, 1.0, 0.0)
        first = sum(jnp.where(order >= k * per_orb, 1, 0) for k in range(1, count))
        mine = jnp.where(lax.broadcasted_iota(i32, (count, n), 0) == first, 1.0, 0.0)
        own = smalls[x][:count, nvd:]
        rows[...] = pick(theirs, columns) - (pick(theirs, extra)[:, :1] + pick(mine, own)[:, :1])
        tbl[SIZE_I : SIZE_I + 1, :n] = pick(own, mine)[1:2, :].astype(i32)
        tbl[SIZE_J : SIZE_J + 1, :n] = pick(extra, theirs)[1:2, :].astype(i32) - col0

    build(0, outs[0], outs[1])
    build(2, outs[2], outs[3])
    build(1, outs[4])
    build(3, outs[5])


def tables_of(meta, smalls, cap, per_orb, half):
    table = jax.ShapeDtypeStruct((8, 128), i32)
    rows = jax.ShapeDtypeStruct((8 * cap, half), f32)
    return pl.pallas_call(
        lambda *refs: tables_kernel(cap, per_orb, *refs),
        out_shape=(table, rows, table, rows, table, table),
        in_specs=[SMEM] + [VMEM] * 8,
        out_specs=[VMEM] * 6,
        compiler_params=PARAMS,
        cost_estimate=TINY,
        name="tables",
    )(meta, *smalls)


def pack_kernel(call, only_middle, relayed, after, tbl, *refs):
    out, sems = refs[-2:]
    halves, cap = out.shape[:2]
    base = tbl[HEAD, call]
    middle = tbl[HEAD, MIDDLE] == 1

    def run(copies):
        for copy in copies:
            copy.start()
        for copy in copies:
            copy.wait()

    def gather():
        run(
            [
                pltpu.make_async_copy(
                    refs[q].at[tbl[SLOT, base + r]], out.at[q, r], sems.at[q, r]
                )
                for q in range(halves)
                for r in range(cap)
            ]
        )

    if not only_middle and not relayed:
        gather()
    else:
        pl.when(middle)(gather)
    if relayed:

        @pl.when(jnp.logical_not(middle))
        def _():
            run(
                [
                    pltpu.make_async_copy(refs[halves + q].at[0], out.at[q], sems.at[q, 0])
                    for q in range(halves)
                ]
            )


def pack(tbl, call, sources, cap, only_middle=False, relayed=None, after=()):
    halves = len(sources)
    shape = (halves, cap) + sources[0].shape[1:]
    operands = (*sources, *(relayed or ()), *after)
    return pl.pallas_call(
        lambda *refs: pack_kernel(call, only_middle, relayed is not None, len(after), *refs),
        out_shape=jax.ShapeDtypeStruct(shape, bf16),
        in_specs=[SMEM] + [HBM] * len(operands),
        out_specs=VMEM,
        scratch_shapes=[pltpu.SemaphoreType.DMA((halves, cap))],
        compiler_params=PARAMS,
        cost_estimate=TINY,
        name="pack",
    )(tbl, *operands)


def turn_kernel(*refs):
    half = len(refs) // 2
    for x, out in zip(refs[:half], refs[half:]):
        for r in range(x.shape[0]):
            out[r] = x[r].T


def turn(arrays):
    count, rows, cols = arrays[0].shape
    step = 4 if count % 4 == 0 else 1
    n = len(arrays)
    return pl.pallas_call(
        turn_kernel,
        out_shape=[jax.ShapeDtypeStruct((count, cols, rows), bf16)] * n,
        grid=(count // step,),
        in_specs=[pl.BlockSpec((step, rows, cols), lambda i: (i, 0, 0))] * n,
        out_specs=[pl.BlockSpec((step, cols, rows), lambda i: (i, 0, 0))] * n,
        compiler_params=PARAMS,
        cost_estimate=TINY,
        name="turn",
    )(*arrays)


def amplitudes_kernel(mode, call, per_orb, first, tbl, rows, vcol, *refs):
    sv, s0, s1, b0, b1, st, se, sem, sem_out = refs[-9:]
    client = mode == "client"
    elsewhere = None
    if client:
        tout = refs[-10]
        left, js = refs[:4], refs[4:6]
    else:
        tout, eout = refs[-11:-9]
        left, js = refs[:2], refs[2:5]
    if mode == "asked":
        js = (js[0].at[0], js[0].at[1])
    if mode == "asked_two":
        js, elsewhere = [[x.at[0] for x in refs[k : k + 2]] for k in (2, 4)]
    cap = sv.shape[0]
    nvd, half = sv.shape[1], sv.shape[2]
    base = tbl[HEAD, call]
    middle = tbl[HEAD, MIDDLE] == 1

    def place(r):
        return tbl[ORDER, base + r]

    def run(copies):
        for copy in copies:
            copy.start()
        for copy in copies:
            copy.wait()

    def load(js=js):
        copies = []
        for r in range(cap):
            i = lax.div(place(r), per_orb)
            slot = r if mode.startswith("asked") else tbl[SLOT, base + r]
            todo = [
                (vcol.at[i], sv.at[r]),
                (js[0].at[slot], b0.at[r]),
                (js[1].at[slot], b1.at[r]),
            ]
            if client:
                here = pl.ds(pl.multiple_of(tbl[HEAD, COLUMN], half), half)
                there = pl.ds(pl.multiple_of(half - tbl[HEAD, COLUMN], half), half)
                todo += [
                    (left[0].at[i], s0.at[r, here, :]),
                    (left[1].at[i], s1.at[r, here, :]),
                    (left[2].at[i], s1.at[r, there, :]),
                    (left[3].at[i], s0.at[r, there, :]),
                ]
            else:
                todo += [(left[0].at[i], s0.at[r]), (left[1].at[i], s1.at[r])]
            copies += [
                pltpu.make_async_copy(x, to, sem.at[r, k]) for k, (x, to) in enumerate(todo)
            ]
        run(copies)

    def gaps():
        row8 = rows[pl.ds(pl.multiple_of(base, cap), cap), :]
        return [sv[r] + row8[r : r + 1, :] for r in range(cap)]

    def make():
        live_a = lax.broadcasted_iota(i32, (nvd, half), 0)
        live_b = lax.broadcasted_iota(i32, (nvd, half), 1)
        for r, gap in enumerate(gaps()):
            size_i = tbl[SIZE_I, base + r]
            size_j = tbl[SIZE_J, base + r]
            k = jnp.dot(s0[r], b0[r], preferred_element_type=f32)
            k += jnp.dot(s1[r], b1[r], preferred_element_type=f32)
            k = jnp.where((live_a < size_i) & (live_b < size_j), k, 0.0)
            t = (-k / gap).astype(bf16)
            st[r] = t
            if not client:
                se[r : r + 1, :] = jnp.sum(k * t.astype(f32), axis=0, keepdims=True)

    def take():
        ready = js[2]
        copies = [pltpu.make_async_copy(ready.at[r], st.at[r], sem.at[r, 0]) for r in range(cap)]
        copies += [
            pltpu.make_async_copy(vcol.at[lax.div(place(r), per_orb)], sv.at[r], sem.at[r, 1])
            for r in range(cap)
        ]
        run(copies)
        for r, gap in enumerate(gaps()):
            t = st[r].astype(f32)
            se[r : r + 1, :] = -jnp.sum(t * t * gap, axis=0, keepdims=True)

    if client:

        @pl.when(middle)
        def _():
            load()
            make()
            tout[...] = st[...]

        return
    if mode == "served":

        @pl.when(middle)
        def _():
            load()
            make()

        pl.when(jnp.logical_not(middle))(take)
    elif elsewhere is not None:
        pl.when(middle)(load)
        pl.when(jnp.logical_not(middle))(lambda: load(elsewhere))
        make()
    else:
        load()
        make()
    run(
        [pltpu.make_async_copy(st.at[r], tout.at[place(r)], sem_out.at[r]) for r in range(cap)]
        + [
            pltpu.make_async_copy(
                se, eout.at[pl.ds(pl.multiple_of(base, cap), cap), :], sem_out.at[cap]
            )
        ]
    )


def amplitudes(mode, call, per_orb, tables, left, sources, cap, held=(), after=()):
    tbl, rows, vcol = tables
    occ, nvd, half = vcol.shape
    qa = left[0].shape[2]
    client = mode == "client"
    operands = (tbl, rows, vcol, *left, *sources, *after)
    aliases = {len(operands) + k: k for k in range(len(held))}
    operands += tuple(held)
    if client:
        out_shape = jax.ShapeDtypeStruct((cap, nvd, half), bf16)
        out_specs = VMEM
    else:
        out_shape = (
            jax.ShapeDtypeStruct((occ * per_orb, nvd, half), bf16),
            jax.ShapeDtypeStruct((occ * per_orb, half), f32),
        )
        out_specs = (HBM, HBM)
    return pl.pallas_call(
        lambda *refs: amplitudes_kernel(mode, call, per_orb, not held, *refs),
        out_shape=out_shape,
        in_specs=[SMEM, VMEM] + [HBM] * (len(operands) - 2),
        out_specs=out_specs,
        scratch_shapes=[
            pltpu.VMEM((cap, nvd, half), f32),
            pltpu.VMEM((cap, nvd, qa), bf16),
            pltpu.VMEM((cap, nvd, qa), bf16),
            pltpu.VMEM((cap, qa, half), bf16),
            pltpu.VMEM((cap, qa, half), bf16),
            pltpu.VMEM((cap, nvd, half), bf16),
            pltpu.VMEM((cap, half), f32),
            pltpu.SemaphoreType.DMA((cap, 7)),
            pltpu.SemaphoreType.DMA((cap + 1,)),
        ],
        input_output_aliases=aliases,
        compiler_params=PARAMS,
        cost_estimate=TINY,
        name="amplitudes",
    )(*operands)


def density_kernel(start, t, d):
    count, half = d.shape[:2]
    per_orb = t.shape[0] // count
    first = pl.multiple_of(start[0], half)
    for o in range(count):
        own = range(o * per_orb, (o + 1) * per_orb)
        left = jnp.concatenate([t[k, pl.ds(first, half), :] for k in own], axis=1)
        right = jnp.concatenate([t[k] for k in own], axis=1)
        d[o] = lax.dot_general(left, right, (((1,), (1,)), ((), ())), preferred_element_type=f32)


def density_rows(t_all, start, per_orb, half):
    npair, nvd, width = t_all.shape
    occ = npair // per_orb
    step = 4 if occ % 4 == 0 else 1
    return pl.pallas_call(
        density_kernel,
        out_shape=jax.ShapeDtypeStruct((occ, half, nvd), f32),
        grid_spec=pltpu.PrefetchScalarGridSpec(
            num_scalar_prefetch=1,
            grid=(occ // step,),
            in_specs=[pl.BlockSpec((step * per_orb, nvd, width), lambda i, s: (i, 0, 0))],
            out_specs=pl.BlockSpec((step, half, nvd), lambda i, s: (i, 0, 0)),
        ),
        compiler_params=pltpu.CompilerParams(vmem_limit_bytes=LIMIT),
        cost_estimate=TINY,
        name="density_rows",
    )(start.reshape(1), t_all)


def line_plan(blocks, vir_energy, occ_energy, domain_size, partner_owner, partner_slot):
    occ, qa, nvd = blocks.shape
    pair_dev = partner_slot.shape[0]
    per_orb = pair_dev // occ
    peers = 8
    cap = pair_dev // peers
    half = nvd // 2
    me, core = lax.axis_index("orb"), lax.axis_index("aux")
    col0 = core * half

    def pp(x, perm):
        return lax.ppermute(x, "orb", perm)

    def swap_core(x):
        return lax.ppermute(x, "aux", [(0, 1), (1, 0)])

    def flip(bits):
        return [(o, o ^ bits) for o in range(peers)]

    cross = [(2, 4), (3, 5), (4, 2), (5, 3)]
    outward = [(2, 0), (3, 1), (4, 6), (5, 7)]
    outward_diagonal = [(2, 1), (3, 0), (4, 7), (5, 6)]
    y_middle = [(2, 3), (3, 2), (4, 5), (5, 4)]

    small, hit = lists(vir_energy, occ_energy, domain_size, partner_owner, partner_slot, cap)
    smalls = [small] + [pp(small, flip(bits)) for bits in range(1, peers)]

    other = swap_core(blocks)
    own = [lax.dynamic_slice_in_dim(x, col0, half, 2) for x in (blocks, other)]
    sent, smalls = lax.optimization_barrier((own[0], smalls))
    near = [pp(x, flip(2)) for x in (sent, own[1])]
    mid = [pp(x, cross) for x in (sent, own[1])]
    tbl, rows, client_tbl, client_rows, beside_list, relay_list = tables_of(
        jnp.stack([me, col0]), smalls, cap, per_orb, half
    )

    def spread(vir):
        return jnp.broadcast_to(vir[:, :, None], (occ, nvd, half))

    tables = (tbl, rows, spread(vir_energy))
    client = (client_tbl, client_rows, spread(smalls[2][:occ, :nvd]))

    def own_pairs(k, mode, sources, held=(), after=()):
        return amplitudes(mode, k, per_orb, tables, left, sources, cap, held, after)

    packed = pack(beside_list, 0, own, cap)
    beside = pp(packed, flip(1))
    left = turn([blocks, other])
    held = own_pairs(0, "slots", own, after=(packed,))
    first, held = lax.optimization_barrier((near[0], held))
    far = [pp(first, cross)]
    across = [swap_core(first)]
    packed = pack(relay_list, 2, mid[:1], cap, only_middle=True, after=(held[1],))
    relays = [pp(packed, outward)]
    held = own_pairs(4, "asked", [beside], held, (packed,))
    second, held = lax.optimization_barrier((near[1], held))
    far.append(pp(second, cross))
    across.append(swap_core(second))
    near = [first, second]
    packed = pack(relay_list, 2, mid[1:], cap, only_middle=True, after=(held[1],))
    relays.append(pp(packed, outward))
    packed = pack(beside_list, 1, near, cap, after=(packed,))
    beside_near = pp(packed, flip(1))
    client_left = turn(near + across)
    gone = amplitudes("client", 2, per_orb, client, client_left, mid, cap, after=(packed, relays[0]))
    ready_2 = pp(gone, outward)
    held = own_pairs(1, "slots", near, held, (gone, relays[1]))
    diagonal, fourth = [], []

    def send_far(q, token):
        packed = pack(relay_list, 3, far[q : q + 1], cap, only_middle=True, after=(token,))
        diagonal.append(pp(packed, outward_diagonal))
        packed = pack(beside_list, 3, far[q : q + 1], cap, only_middle=True, after=(packed,))
        fourth.append(pp(packed, y_middle))
        return packed

    packed = send_far(0, held[1])
    held = own_pairs(2, "served", mid + [ready_2], held, (packed, beside_near))
    packed = pack(beside_list, 2, mid, cap, relayed=relays, after=(held[1],))
    third = pp(packed, flip(1))
    held = own_pairs(5, "asked", [beside_near], held, (packed, diagonal[0]))
    packed = send_far(1, held[1])
    gone = amplitudes("client", 3, per_orb, client, client_left, far, cap, after=(packed, diagonal[0], fourth[0]))
    ready_3 = pp(gone, outward)
    held = own_pairs(6, "asked", [third], held, (gone,))
    held = own_pairs(7, "asked_two", fourth + diagonal, held)
    t_all, e_all = own_pairs(3, "served", far + [ready_3], held)

    away = swap_core(density_rows(t_all, (1 - core) * half, per_orb, half))
    density = density_rows(t_all, core * half, per_orb, half) + away

    energy = jnp.sum(hit * jnp.sum(e_all, axis=1)[None, :], axis=1)
    energy = (energy + swap_core(energy)) / nvd
    return (energy, density)


def solution(mesh):
    in_specs = (
        P(("mol", "orb"), "aux", None),
        P(("mol", "orb"), None),
        P(("mol", "orb")),
        P(("mol", "orb")),
        P(("mol", "orb"), None),
        P(("mol", "orb")),
    )
    out_specs = (P(("mol", "orb")), P(("mol", "orb"), "aux", None))
    return jax.shard_map(
        line_plan if fits_line(mesh) else by_requests, mesh=mesh, in_specs=in_specs, out_specs=out_specs, check_vma=False
    )
```

```python
import jax
import jax.numpy as jnp
from jax import lax
from jax.experimental import pallas as pl
from jax.experimental.pallas import tpu as pltpu
from jax.sharding import PartitionSpec as P

f32, bf16, i32 = jnp.float32, jnp.bfloat16, jnp.int32
HBM = pl.BlockSpec(memory_space=pltpu.HBM)
SMEM = pl.BlockSpec(memory_space=pltpu.SMEM)
VMEM = pl.BlockSpec(memory_space=pltpu.VMEM)
LIMIT = 48 * 1024 * 1024


def slot_ranks(owner):
    count = owner.shape[0]
    order = jnp.arange(count, dtype=jnp.int32)
    same = (owner[:, None] == owner[None, :]) & (order[None, :] < order[:, None])
    return jnp.sum(same.astype(jnp.int32), axis=1)


def by_requests(blocks, vir_energy, occ_energy, domain_size, partner_owner, partner_slot):
    occ_dev, half_aux, nvd = blocks.shape
    pair_dev = partner_slot.shape[0]
    per_orb = pair_dev // occ_dev
    peers = lax.axis_size("orb")
    cap = max(2, (pair_dev + peers - 1) // peers)
    owner = partner_owner[:, 0]
    ranks = slot_ranks(owner)
    target = owner * cap + ranks
    wanted = (target[:, None] == jnp.arange(peers * cap, dtype=jnp.int32)[None, :]).astype(
        jnp.int32
    )
    requests = jnp.sum(wanted * partner_slot[:, None], axis=0).reshape(peers, cap)
    incoming = lax.all_to_all(requests, "orb", split_axis=0, concat_axis=0, tiled=True)
    flat_in = incoming.reshape(-1)
    send_blocks = jnp.take(blocks, flat_in, axis=0).reshape(peers, cap, half_aux, nvd)
    send_vir = jnp.take(vir_energy, flat_in, axis=0).reshape(peers, cap, nvd)
    send_occ = jnp.take(occ_energy, flat_in).reshape(peers, cap)
    send_size = jnp.take(domain_size, flat_in).astype(jnp.float32).reshape(peers, cap)
    got_blocks = lax.all_to_all(send_blocks, "orb", split_axis=0, concat_axis=0, tiled=True)
    got_vir, got_occ, got_size = (
        lax.all_to_all(send_vir, "orb", split_axis=0, concat_axis=0, tiled=True),
        lax.all_to_all(send_occ, "orb", split_axis=0, concat_axis=0, tiled=True),
        lax.all_to_all(send_size, "orb", split_axis=0, concat_axis=0, tiled=True),
    )
    partner = jnp.take(got_blocks.reshape(peers * cap, half_aux, nvd), target, axis=0).reshape(
        occ_dev, per_orb, half_aux, nvd
    )
    partner_vir = jnp.take(got_vir.reshape(peers * cap, nvd), target, axis=0).reshape(
        occ_dev, per_orb, nvd
    )
    partner_occ = jnp.take(got_occ.reshape(-1), target).reshape(occ_dev, per_orb)
    partner_size = jnp.take(got_size.reshape(-1), target).reshape(occ_dev, per_orb)
    half = nvd // lax.axis_size("aux")
    integrals = lax.psum_scatter(
        jnp.einsum("oqa,opqb->aopb", blocks, partner, preferred_element_type=jnp.float32),
        "aux",
        scatter_dimension=0,
        tiled=True,
    )
    row_start = lax.axis_index("aux") * half
    rows = row_start + jnp.arange(half, dtype=jnp.int32)
    cols = jnp.arange(nvd, dtype=jnp.int32).astype(jnp.float32)
    mask = (rows[:, None, None, None] < domain_size[None, :, None, None]) & (
        cols[None, None, None, :] < partner_size[None, :, :, None]
    )
    integrals = jnp.where(mask, integrals, jnp.zeros_like(integrals))
    vir_rows = lax.dynamic_slice_in_dim(vir_energy, row_start, half, 1)
    gap = (
        vir_rows.T[:, :, None, None]
        + partner_vir[None, :, :, :]
        - occ_energy[None, :, None, None]
        - partner_occ[None, :, :, None]
    )
    amp_rows = (-integrals / gap).astype(jnp.bfloat16)
    partial_energy = jnp.sum(integrals * amp_rows.astype(jnp.float32), axis=(0, 3))
    energy = lax.psum(partial_energy, "aux").reshape(pair_dev) / nvd
    density = jnp.einsum(
        "aopb,copb->oac",
        amp_rows,
        lax.all_gather(amp_rows, "aux", axis=0, tiled=True),
        preferred_element_type=jnp.float32,
    )
    return (energy, density)


def fits_line(mesh):
    return mesh.shape["orb"] == 8 and mesh.shape["aux"] == 2


TINY = pl.CostEstimate(flops=1, bytes_accessed=1, transcendentals=0)
PARAMS = pltpu.CompilerParams(vmem_limit_bytes=LIMIT)


def lists_kernel(cap, *refs):
    small, hit = refs[5:7]
    sems = refs[-1]
    copies = [
        pltpu.make_async_copy(x, to, sems.at[k])
        for k, (x, to) in enumerate(zip(refs[:5], refs[7:12]))
    ]
    for copy in copies:
        copy.start()
    for copy in copies:
        copy.wait()
    vir, occ, size, owner, slot = refs[7:12]
    n, (count, nvd) = hit.shape[0], vir.shape

    def column(row, m):
        eye = lax.broadcasted_iota(i32, (m, m), 0) == lax.broadcasted_iota(i32, (m, m), 1)
        return jnp.sum(jnp.where(eye, row, 0.0), axis=1, keepdims=True)

    down = lax.broadcasted_iota(i32, (n, n), 0).astype(f32)
    along = lax.broadcasted_iota(i32, (n, n), 1).astype(f32)
    owner_row = owner[...].astype(f32)
    owner_col = column(owner_row, n)
    before = (owner_col == owner_row) & (along < down)
    target = owner_col * cap + jnp.sum(jnp.where(before, 1.0, 0.0), axis=1, keepdims=True)
    found = target == along
    hit[...] = jnp.where(found, 1.0, 0.0)
    small[...] = jnp.zeros_like(small)
    small[:count, :nvd] = vir[...]
    lane = lax.broadcasted_iota(i32, (count, 128), 1)
    occ_col, size_col = column(occ[...], count), column(size[...].astype(f32), count)
    small[:count, nvd:] = jnp.where(lane == 0, occ_col, jnp.where(lane == 1, size_col, 0.0))
    small[count : count + 1, :n] = jnp.sum(jnp.where(found, down, 0.0), axis=0, keepdims=True)
    slot_col = column(slot[...].astype(f32), n)
    small[count : count + 1, 128 : 128 + n] = jnp.sum(
        jnp.where(found, slot_col, 0.0), axis=0, keepdims=True
    )


def lists(vir, occ, size, owner, slot, cap):
    count, nvd = vir.shape
    n = slot.shape[0]
    return pl.pallas_call(
        lambda *refs: lists_kernel(cap, *refs),
        out_shape=(
            jax.ShapeDtypeStruct((count + 8, nvd + 128), f32),
            jax.ShapeDtypeStruct((n, n), f32),
        ),
        in_specs=[HBM] * 5,
        out_specs=(VMEM, VMEM),
        scratch_shapes=[
            pltpu.VMEM((count, nvd), f32),
            pltpu.VMEM((1, count), f32),
            pltpu.VMEM((1, count), i32),
            pltpu.VMEM((1, n), i32),
            pltpu.VMEM((1, n), i32),
            pltpu.SemaphoreType.DMA((5,)),
        ],
        compiler_params=PARAMS,
        cost_estimate=TINY,
        name="lists",
    )(vir, occ.reshape(1, -1), size.reshape(1, -1), owner.reshape(1, -1), slot.reshape(1, -1))


ORDER, SLOT, SIZE_I, SIZE_J, HEAD = range(5)
MIDDLE, COLUMN = 8, 9


def pick(one, values):
    return lax.dot_general(
        one, values, (((0,), (0,)), ((), ())),
        precision=lax.Precision.HIGHEST, preferred_element_type=f32,
    )


def tables_kernel(cap, per_orb, meta, every, *outs):
    count, nvd = every.shape[1] - 8, every.shape[2] - 128
    n = 8 * cap
    me, col0 = meta[0], meta[1]
    z, y = me // 2, me % 2
    lower = z < 2
    middle = jnp.where((z == 1) | (z == 2), 1, 0)
    places = [z, z ^ 1, jnp.where(lower, 2, 1), jnp.where(lower, 3, 0)]
    head = [(2 * p + y) * cap for p in places] + [(2 * p + 1 - y) * cap for p in places]
    lane = lax.broadcasted_iota(i32, (1, 128), 1)
    head_row = jnp.zeros((1, 128), i32)
    for k, value in enumerate(head + [middle, col0]):
        head_row = jnp.where(lane == k, value, head_row)
    orbitals = jnp.concatenate([every[d, :count, :] for d in range(8)], axis=0)
    columns = jnp.where(col0 == 0, orbitals[:, : nvd // 2], orbitals[:, nvd // 2 : nvd])
    extra = orbitals[:, nvd:]

    def build(x, tbl, rows=None):
        packet = every[me ^ x]
        order = packet[count : count + 1, :n].astype(i32)
        slots = packet[count : count + 1, 128 : 128 + n].astype(i32)
        tbl[...] = jnp.zeros_like(tbl)
        tbl[HEAD : HEAD + 1, :] = head_row
        tbl[SLOT : SLOT + 1, :n] = slots
        if rows is None:
            return
        tbl[ORDER : ORDER + 1, :n] = order
        pair = lax.broadcasted_iota(i32, (1, n), 1)
        owner = sum(jnp.where(pair >= k * cap, 1, 0) for k in range(1, 8))
        index = owner * count + slots
        theirs = jnp.where(lax.broadcasted_iota(i32, (8 * count, n), 0) == index, 1.0, 0.0)
        first = sum(jnp.where(order >= k * per_orb, 1, 0) for k in range(1, count))
        mine = jnp.where(lax.broadcasted_iota(i32, (count, n), 0) == first, 1.0, 0.0)
        own = packet[:count, nvd:]
        rows[...] = pick(theirs, columns) - (pick(theirs, extra)[:, :1] + pick(mine, own)[:, :1])
        tbl[SIZE_I : SIZE_I + 1, :n] = pick(own, mine)[1:2, :].astype(i32)
        tbl[SIZE_J : SIZE_J + 1, :n] = pick(extra, theirs)[1:2, :].astype(i32) - col0

    build(0, outs[0], outs[1])
    build(2, outs[2], outs[3])
    build(1, outs[4])
    build(3, outs[5])


def tables_of(meta, every, cap, per_orb, half):
    table = jax.ShapeDtypeStruct((8, 128), i32)
    rows = jax.ShapeDtypeStruct((8 * cap, half), f32)
    return pl.pallas_call(
        lambda *refs: tables_kernel(cap, per_orb, *refs),
        out_shape=(table, rows, table, rows, table, table),
        in_specs=[SMEM, VMEM],
        out_specs=[VMEM] * 6,
        compiler_params=PARAMS,
        cost_estimate=TINY,
        name="tables",
    )(meta, every)


def pack_kernel(jobs, tables, after, *refs):
    tbls, sources = refs[:tables], refs[tables : tables + len(jobs)]
    outs, sems = refs[tables + len(jobs) + after : -1], refs[-1]

    def copies(only_middle):
        made = []
        for k, (table, call, middle) in enumerate(jobs):
            if middle == only_middle:
                base = tbls[table][HEAD, call]
                for r in range(outs[k].shape[0]):
                    slot = tbls[table][SLOT, base + r]
                    made.append(
                        pltpu.make_async_copy(sources[k].at[slot], outs[k].at[r], sems.at[k, r])
                    )
        return made

    everywhere = copies(False)
    for copy in everywhere:
        copy.start()

    @pl.when(tbls[0][HEAD, MIDDLE] == 1)
    def _():
        some = copies(True)
        for copy in some:
            copy.start()
        for copy in some:
            copy.wait()

    for copy in everywhere:
        copy.wait()


def pack(tbls, jobs, cap, after=()):
    sources = [source for _, _, source, _ in jobs]
    shape = jax.ShapeDtypeStruct((cap,) + sources[0].shape[1:], bf16)
    kinds = [(table, call, middle) for table, call, _, middle in jobs]
    return pl.pallas_call(
        lambda *refs: pack_kernel(kinds, len(tbls), len(after), *refs),
        out_shape=[shape] * len(jobs),
        in_specs=[SMEM] * len(tbls) + [HBM] * (len(jobs) + len(after)),
        out_specs=[VMEM] * len(jobs),
        scratch_shapes=[pltpu.SemaphoreType.DMA((len(jobs), cap))],
        compiler_params=PARAMS,
        cost_estimate=TINY,
        name="pack",
    )(*tbls, *sources, *after)


def turn_kernel(*refs):
    half = len(refs) // 2
    for x, out in zip(refs[:half], refs[half:]):
        for r in range(x.shape[0]):
            out[r] = x[r].T


def turn(arrays):
    count, rows, cols = arrays[0].shape
    step = 4 if count % 4 == 0 else 1
    n = len(arrays)
    return pl.pallas_call(
        turn_kernel,
        out_shape=[jax.ShapeDtypeStruct((count, cols, rows), bf16)] * n,
        grid=(count // step,),
        in_specs=[pl.BlockSpec((step, rows, cols), lambda i: (i, 0, 0))] * n,
        out_specs=[pl.BlockSpec((step, cols, rows), lambda i: (i, 0, 0))] * n,
        compiler_params=PARAMS,
        cost_estimate=TINY,
        name="turn",
    )(*arrays)


def amplitudes_kernel(mode, call, per_orb, first, tbl, rows, vcol, *refs):
    sv, s0, s1, b0, b1, st, se, sem, sem_out = refs[-9:]
    client = mode == "client"
    elsewhere = None
    if client:
        tout = refs[-10]
        left, js = refs[:4], refs[4:6]
    else:
        tout, eout = refs[-11:-9]
        left, js = refs[:2], refs[2:5]
    if mode == "asked_two":
        js, elsewhere = refs[2:4], refs[4:6]
    cap = sv.shape[0]
    nvd, half = sv.shape[1], sv.shape[2]
    base = tbl[HEAD, call]
    middle = tbl[HEAD, MIDDLE] == 1

    def place(r):
        return tbl[ORDER, base + r]

    def run(copies):
        for copy in copies:
            copy.start()
        for copy in copies:
            copy.wait()

    def load(js=js):
        copies = []
        for r in range(cap):
            i = lax.div(place(r), per_orb)
            slot = r if mode.startswith("asked") else tbl[SLOT, base + r]
            todo = [
                (vcol.at[i], sv.at[r]),
                (js[0].at[slot], b0.at[r]),
                (js[1].at[slot], b1.at[r]),
            ]
            if client:
                here = pl.ds(pl.multiple_of(tbl[HEAD, COLUMN], half), half)
                there = pl.ds(pl.multiple_of(half - tbl[HEAD, COLUMN], half), half)
                todo += [
                    (left[0].at[i], s0.at[r, here, :]),
                    (left[1].at[i], s1.at[r, here, :]),
                    (left[2].at[i], s1.at[r, there, :]),
                    (left[3].at[i], s0.at[r, there, :]),
                ]
            else:
                todo += [(left[0].at[i], s0.at[r]), (left[1].at[i], s1.at[r])]
            copies += [
                pltpu.make_async_copy(x, to, sem.at[r, k]) for k, (x, to) in enumerate(todo)
            ]
        run(copies)

    def gaps():
        row8 = rows[pl.ds(pl.multiple_of(base, cap), cap), :]
        return [sv[r] + row8[r : r + 1, :] for r in range(cap)]

    def make():
        live_a = lax.broadcasted_iota(i32, (nvd, half), 0)
        live_b = lax.broadcasted_iota(i32, (nvd, half), 1)
        for r, gap in enumerate(gaps()):
            size_i = tbl[SIZE_I, base + r]
            size_j = tbl[SIZE_J, base + r]
            k = jnp.dot(s0[r], b0[r], preferred_element_type=f32)
            k += jnp.dot(s1[r], b1[r], preferred_element_type=f32)
            k = jnp.where((live_a < size_i) & (live_b < size_j), k, 0.0)
            t = (-k / gap).astype(bf16)
            st[r] = t
            if not client:
                se[r : r + 1, :] = jnp.sum(k * t.astype(f32), axis=0, keepdims=True)

    def take():
        ready = js[2]
        copies = [pltpu.make_async_copy(ready.at[r], st.at[r], sem.at[r, 0]) for r in range(cap)]
        copies += [
            pltpu.make_async_copy(vcol.at[lax.div(place(r), per_orb)], sv.at[r], sem.at[r, 1])
            for r in range(cap)
        ]
        run(copies)
        for r, gap in enumerate(gaps()):
            t = st[r].astype(f32)
            se[r : r + 1, :] = -jnp.sum(t * t * gap, axis=0, keepdims=True)

    if client:

        @pl.when(middle)
        def _():
            load()
            make()
            tout[...] = st[...]

        return
    if mode == "served":

        @pl.when(middle)
        def _():
            load()
            make()

        pl.when(jnp.logical_not(middle))(take)
    elif elsewhere is not None:
        pl.when(middle)(load)
        pl.when(jnp.logical_not(middle))(lambda: load(elsewhere))
        make()
    else:
        load()
        make()
    run(
        [pltpu.make_async_copy(st.at[r], tout.at[place(r)], sem_out.at[r]) for r in range(cap)]
        + [
            pltpu.make_async_copy(
                se, eout.at[pl.ds(pl.multiple_of(base, cap), cap), :], sem_out.at[cap]
            )
        ]
    )


def amplitudes(mode, call, per_orb, tables, left, sources, cap, held=(), after=()):
    tbl, rows, vcol = tables
    occ, nvd, half = vcol.shape
    qa = left[0].shape[2]
    client = mode == "client"
    operands = (tbl, rows, vcol, *left, *sources, *after)
    aliases = {len(operands) + k: k for k in range(len(held))}
    operands += tuple(held)
    if client:
        out_shape = jax.ShapeDtypeStruct((cap, nvd, half), bf16)
        out_specs = VMEM
    else:
        out_shape = (
            jax.ShapeDtypeStruct((occ * per_orb, nvd, half), bf16),
            jax.ShapeDtypeStruct((occ * per_orb, half), f32),
        )
        out_specs = (HBM, HBM)
    return pl.pallas_call(
        lambda *refs: amplitudes_kernel(mode, call, per_orb, not held, *refs),
        out_shape=out_shape,
        in_specs=[SMEM, VMEM] + [HBM] * (len(operands) - 2),
        out_specs=out_specs,
        scratch_shapes=[
            pltpu.VMEM((cap, nvd, half), f32),
            pltpu.VMEM((cap, nvd, qa), bf16),
            pltpu.VMEM((cap, nvd, qa), bf16),
            pltpu.VMEM((cap, qa, half), bf16),
            pltpu.VMEM((cap, qa, half), bf16),
            pltpu.VMEM((cap, nvd, half), bf16),
            pltpu.VMEM((cap, half), f32),
            pltpu.SemaphoreType.DMA((cap, 7)),
            pltpu.SemaphoreType.DMA((cap + 1,)),
        ],
        input_output_aliases=aliases,
        compiler_params=PARAMS,
        cost_estimate=TINY,
        name="amplitudes",
    )(*operands)


def density_kernel(start, t, d):
    count, half = d.shape[:2]
    per_orb = t.shape[0] // count
    first = pl.multiple_of(start[0], half)
    for o in range(count):
        own = range(o * per_orb, (o + 1) * per_orb)
        left = jnp.concatenate([t[k, pl.ds(first, half), :] for k in own], axis=1)
        right = jnp.concatenate([t[k] for k in own], axis=1)
        d[o] = lax.dot_general(left, right, (((1,), (1,)), ((), ())), preferred_element_type=f32)


def density_rows(t_all, start, per_orb, half):
    npair, nvd, width = t_all.shape
    occ = npair // per_orb
    step = 4 if occ % 4 == 0 else 1
    return pl.pallas_call(
        density_kernel,
        out_shape=jax.ShapeDtypeStruct((occ, half, nvd), f32),
        grid_spec=pltpu.PrefetchScalarGridSpec(
            num_scalar_prefetch=1,
            grid=(occ // step,),
            in_specs=[pl.BlockSpec((step * per_orb, nvd, width), lambda i, s: (i, 0, 0))],
            out_specs=pl.BlockSpec((step, half, nvd), lambda i, s: (i, 0, 0)),
        ),
        compiler_params=pltpu.CompilerParams(vmem_limit_bytes=LIMIT),
        cost_estimate=TINY,
        name="density_rows",
    )(start.reshape(1), t_all)


def line_plan(blocks, vir_energy, occ_energy, domain_size, partner_owner, partner_slot):
    occ, qa, nvd = blocks.shape
    pair_dev = partner_slot.shape[0]
    per_orb = pair_dev // occ
    peers = 8
    cap = pair_dev // peers
    half = nvd // 2
    me, core = lax.axis_index("orb"), lax.axis_index("aux")
    col0 = core * half

    def pp(x, perm):
        return lax.ppermute(x, "orb", perm)

    def swap_core(x):
        return lax.ppermute(x, "aux", [(0, 1), (1, 0)])

    def flip(bits):
        return [(o, o ^ bits) for o in range(peers)]

    cross = [(2, 4), (3, 5), (4, 2), (5, 3)]
    outward = [(2, 0), (3, 1), (4, 6), (5, 7)]
    diagonal = [(2, 1), (3, 0), (4, 7), (5, 6)]
    y_middle = [(2, 3), (3, 2), (4, 5), (5, 4)]

    small, hit = lists(vir_energy, occ_energy, domain_size, partner_owner, partner_slot, cap)
    every = lax.all_gather(small, "orb")

    other = swap_core(blocks)
    own = [lax.dynamic_slice_in_dim(x, col0, half, 2) for x in (blocks, other)]
    sent, every = lax.optimization_barrier((own[0], every))
    near = [pp(x, flip(2)) for x in (sent, own[1])]
    mid = [pp(x, cross) for x in (sent, own[1])]
    tbl, rows, client_tbl, client_rows, beside_list, relay_list = tables_of(
        jnp.stack([me, col0]), every, cap, per_orb, half
    )

    def spread(vir):
        return jnp.broadcast_to(vir[:, :, None], (occ, nvd, half))

    tables = (tbl, rows, spread(vir_energy))
    client_vir = lax.dynamic_index_in_dim(every, me ^ 2, 0, keepdims=False)[:occ, :nvd]
    client = (client_tbl, client_rows, spread(client_vir))
    lists_of = [beside_list, relay_list]

    def own_pairs(k, mode, sources, held=(), after=()):
        return amplitudes(mode, k, per_orb, tables, left, sources, cap, held, after)

    packed = pack(lists_of, [(0, 0, x, False) for x in own], cap)
    beside = [pp(x, flip(1)) for x in packed]
    left = turn([blocks, other])
    held = own_pairs(0, "slots", own, after=(packed[1],))

    def send_on(x, y, token):
        jobs = [(0, 1, x, False), (1, 2, y, True), (0, 2, y, True)]
        packed = pack(lists_of, jobs, cap, after=(token,))
        perms = (flip(1), diagonal, y_middle)
        return packed[0], [pp(part, perm) for part, perm in zip(packed, perms)]

    first, held = lax.optimization_barrier((near[0], held))
    far = [pp(first, cross)]
    across = [swap_core(first)]
    packed, sent_first = send_on(first, mid[0], held[1])
    held = own_pairs(4, "asked", beside, held, (packed,))
    second, held = lax.optimization_barrier((near[1], held))
    far.append(pp(second, cross))
    across.append(swap_core(second))
    near = [first, second]
    packed, sent_second = send_on(second, mid[1], held[1])
    beside_near, third_diagonal, third = zip(sent_first, sent_second)
    client_left = turn(near + across)
    gone = amplitudes(
        "client", 2, per_orb, client, client_left, mid, cap, after=(packed, third_diagonal[0], third[0])
    )
    ready_2 = pp(gone, outward)
    held = own_pairs(1, "slots", near, held, (gone, third_diagonal[1], beside_near[0]))
    fourth_diagonal, fourth = [], []

    def send_far(q, token):
        jobs = [(1, 3, far[q], True), (0, 3, far[q], True)]
        packed = pack(lists_of, jobs, cap, after=(token,))
        fourth_diagonal.append(pp(packed[0], diagonal))
        fourth.append(pp(packed[1], y_middle))
        return packed[0]

    packed = send_far(0, held[1])
    held = own_pairs(2, "served", mid + [ready_2], held, (packed, third[1]))
    held = own_pairs(5, "asked", beside_near, held, (fourth_diagonal[0],))
    held = own_pairs(6, "asked_two", third + third_diagonal, held)
    packed = send_far(1, held[1])
    gone = amplitudes("client", 3, per_orb, client, client_left, far, cap, after=(packed,))
    ready_3 = pp(gone, outward)
    held = own_pairs(7, "asked_two", fourth + fourth_diagonal, held, (gone,))
    t_all, e_all = own_pairs(3, "served", far + [ready_3], held)

    away = swap_core(density_rows(t_all, (1 - core) * half, per_orb, half))
    density = density_rows(t_all, core * half, per_orb, half) + away

    energy = jnp.sum(hit * jnp.sum(e_all, axis=1)[None, :], axis=1)
    energy = (energy + swap_core(energy)) / nvd
    return (energy, density)


def solution(mesh):
    in_specs = (
        P(("mol", "orb"), "aux", None),
        P(("mol", "orb"), None),
        P(("mol", "orb")),
        P(("mol", "orb")),
        P(("mol", "orb"), None),
        P(("mol", "orb")),
    )
    out_specs = (P(("mol", "orb")), P(("mol", "orb"), "aux", None))
    return jax.shard_map(
        line_plan if fits_line(mesh) else by_requests, mesh=mesh, in_specs=in_specs, out_specs=out_specs, check_vma=False
    )
```

```python
import jax
import jax.numpy as jnp
from jax import lax
from jax.experimental import pallas as pl
from jax.experimental.pallas import tpu as pltpu
from jax.sharding import PartitionSpec as P

f32, bf16, i32 = jnp.float32, jnp.bfloat16, jnp.int32
HBM = pl.BlockSpec(memory_space=pltpu.HBM)
SMEM = pl.BlockSpec(memory_space=pltpu.SMEM)
VMEM = pl.BlockSpec(memory_space=pltpu.VMEM)
LIMIT = 48 * 1024 * 1024


def slot_ranks(owner):
    count = owner.shape[0]
    order = jnp.arange(count, dtype=jnp.int32)
    same = (owner[:, None] == owner[None, :]) & (order[None, :] < order[:, None])
    return jnp.sum(same.astype(jnp.int32), axis=1)


def by_requests(blocks, vir_energy, occ_energy, domain_size, partner_owner, partner_slot):
    occ_dev, half_aux, nvd = blocks.shape
    pair_dev = partner_slot.shape[0]
    per_orb = pair_dev // occ_dev
    peers = lax.axis_size("orb")
    cap = max(2, (pair_dev + peers - 1) // peers)
    owner = partner_owner[:, 0]
    ranks = slot_ranks(owner)
    target = owner * cap + ranks
    wanted = (target[:, None] == jnp.arange(peers * cap, dtype=jnp.int32)[None, :]).astype(
        jnp.int32
    )
    requests = jnp.sum(wanted * partner_slot[:, None], axis=0).reshape(peers, cap)
    incoming = lax.all_to_all(requests, "orb", split_axis=0, concat_axis=0, tiled=True)
    flat_in = incoming.reshape(-1)
    send_blocks = jnp.take(blocks, flat_in, axis=0).reshape(peers, cap, half_aux, nvd)
    send_vir = jnp.take(vir_energy, flat_in, axis=0).reshape(peers, cap, nvd)
    send_occ = jnp.take(occ_energy, flat_in).reshape(peers, cap)
    send_size = jnp.take(domain_size, flat_in).astype(jnp.float32).reshape(peers, cap)
    got_blocks = lax.all_to_all(send_blocks, "orb", split_axis=0, concat_axis=0, tiled=True)
    got_vir, got_occ, got_size = (
        lax.all_to_all(send_vir, "orb", split_axis=0, concat_axis=0, tiled=True),
        lax.all_to_all(send_occ, "orb", split_axis=0, concat_axis=0, tiled=True),
        lax.all_to_all(send_size, "orb", split_axis=0, concat_axis=0, tiled=True),
    )
    partner = jnp.take(got_blocks.reshape(peers * cap, half_aux, nvd), target, axis=0).reshape(
        occ_dev, per_orb, half_aux, nvd
    )
    partner_vir = jnp.take(got_vir.reshape(peers * cap, nvd), target, axis=0).reshape(
        occ_dev, per_orb, nvd
    )
    partner_occ = jnp.take(got_occ.reshape(-1), target).reshape(occ_dev, per_orb)
    partner_size = jnp.take(got_size.reshape(-1), target).reshape(occ_dev, per_orb)
    half = nvd // lax.axis_size("aux")
    integrals = lax.psum_scatter(
        jnp.einsum("oqa,opqb->aopb", blocks, partner, preferred_element_type=jnp.float32),
        "aux",
        scatter_dimension=0,
        tiled=True,
    )
    row_start = lax.axis_index("aux") * half
    rows = row_start + jnp.arange(half, dtype=jnp.int32)
    cols = jnp.arange(nvd, dtype=jnp.int32).astype(jnp.float32)
    mask = (rows[:, None, None, None] < domain_size[None, :, None, None]) & (
        cols[None, None, None, :] < partner_size[None, :, :, None]
    )
    integrals = jnp.where(mask, integrals, jnp.zeros_like(integrals))
    vir_rows = lax.dynamic_slice_in_dim(vir_energy, row_start, half, 1)
    gap = (
        vir_rows.T[:, :, None, None]
        + partner_vir[None, :, :, :]
        - occ_energy[None, :, None, None]
        - partner_occ[None, :, :, None]
    )
    amp_rows = (-integrals / gap).astype(jnp.bfloat16)
    partial_energy = jnp.sum(integrals * amp_rows.astype(jnp.float32), axis=(0, 3))
    energy = lax.psum(partial_energy, "aux").reshape(pair_dev) / nvd
    density = jnp.einsum(
        "aopb,copb->oac",
        amp_rows,
        lax.all_gather(amp_rows, "aux", axis=0, tiled=True),
        preferred_element_type=jnp.float32,
    )
    return (energy, density)


def fits_line(mesh):
    return mesh.shape["orb"] == 8 and mesh.shape["aux"] == 2


TINY = pl.CostEstimate(flops=1, bytes_accessed=1, transcendentals=0)
PARAMS = pltpu.CompilerParams(vmem_limit_bytes=LIMIT)


def lists_kernel(cap, *refs):
    small, hit = refs[5:7]
    sems = refs[-1]
    copies = [
        pltpu.make_async_copy(x, to, sems.at[k])
        for k, (x, to) in enumerate(zip(refs[:5], refs[7:12]))
    ]
    for copy in copies:
        copy.start()
    for copy in copies:
        copy.wait()
    vir, occ, size, owner, slot = refs[7:12]
    n, (count, nvd) = hit.shape[0], vir.shape

    def column(row, m):
        eye = lax.broadcasted_iota(i32, (m, m), 0) == lax.broadcasted_iota(i32, (m, m), 1)
        return jnp.sum(jnp.where(eye, row, 0.0), axis=1, keepdims=True)

    down = lax.broadcasted_iota(i32, (n, n), 0).astype(f32)
    along = lax.broadcasted_iota(i32, (n, n), 1).astype(f32)
    owner_row = owner[...].astype(f32)
    owner_col = column(owner_row, n)
    before = (owner_col == owner_row) & (along < down)
    target = owner_col * cap + jnp.sum(jnp.where(before, 1.0, 0.0), axis=1, keepdims=True)
    found = target == along
    hit[...] = jnp.where(found, 1.0, 0.0)
    small[...] = jnp.zeros_like(small)
    small[:count, :nvd] = vir[...]
    lane = lax.broadcasted_iota(i32, (count, 128), 1)
    occ_col, size_col = column(occ[...], count), column(size[...].astype(f32), count)
    small[:count, nvd:] = jnp.where(lane == 0, occ_col, jnp.where(lane == 1, size_col, 0.0))
    small[count : count + 1, :n] = jnp.sum(jnp.where(found, down, 0.0), axis=0, keepdims=True)
    slot_col = column(slot[...].astype(f32), n)
    small[count : count + 1, 128 : 128 + n] = jnp.sum(
        jnp.where(found, slot_col, 0.0), axis=0, keepdims=True
    )


def lists(vir, occ, size, owner, slot, cap):
    count, nvd = vir.shape
    n = slot.shape[0]
    return pl.pallas_call(
        lambda *refs: lists_kernel(cap, *refs),
        out_shape=(
            jax.ShapeDtypeStruct((count + 8, nvd + 128), f32),
            jax.ShapeDtypeStruct((n, n), f32),
        ),
        in_specs=[HBM] * 5,
        out_specs=(VMEM, VMEM),
        scratch_shapes=[
            pltpu.VMEM((count, nvd), f32),
            pltpu.VMEM((1, count), f32),
            pltpu.VMEM((1, count), i32),
            pltpu.VMEM((1, n), i32),
            pltpu.VMEM((1, n), i32),
            pltpu.SemaphoreType.DMA((5,)),
        ],
        compiler_params=PARAMS,
        cost_estimate=TINY,
        name="lists",
    )(vir, occ.reshape(1, -1), size.reshape(1, -1), owner.reshape(1, -1), slot.reshape(1, -1))


ORDER, SLOT, SIZE_I, SIZE_J, HEAD = range(5)
MIDDLE, COLUMN = 8, 9


def pick(one, values):
    return lax.dot_general(
        one, values, (((0,), (0,)), ((), ())),
        precision=lax.Precision.HIGHEST, preferred_element_type=f32,
    )


def tables_kernel(cap, per_orb, meta, *refs):
    smalls, outs = refs[:8], refs[8:]
    count, nvd = smalls[0].shape[0] - 8, smalls[0].shape[1] - 128
    n = 8 * cap
    me, col0 = meta[0], meta[1]
    z, y = me // 2, me % 2
    lower = z < 2
    middle = jnp.where((z == 1) | (z == 2), 1, 0)
    places = [z, z ^ 1, jnp.where(lower, 2, 1), jnp.where(lower, 3, 0)]
    head = [(2 * p + y) * cap for p in places] + [(2 * p + 1 - y) * cap for p in places]
    lane = lax.broadcasted_iota(i32, (1, 128), 1)
    head_row = jnp.zeros((1, 128), i32)
    for k, value in enumerate(head + [middle, col0]):
        head_row = jnp.where(lane == k, value, head_row)
    orbitals = jnp.concatenate([x[:count, :] for x in smalls], axis=0)
    columns = jnp.where(col0 == 0, orbitals[:, : nvd // 2], orbitals[:, nvd // 2 : nvd])
    extra = orbitals[:, nvd:]

    def build(x, tbl, rows=None):
        packet = smalls[x]
        order = packet[count : count + 1, :n].astype(i32)
        slots = packet[count : count + 1, 128 : 128 + n].astype(i32)
        tbl[...] = jnp.zeros_like(tbl)
        tbl[HEAD : HEAD + 1, :] = head_row
        tbl[SLOT : SLOT + 1, :n] = slots
        if rows is None:
            return
        tbl[ORDER : ORDER + 1, :n] = order
        pair = lax.broadcasted_iota(i32, (1, n), 1)
        owner = sum(jnp.where(pair >= k * cap, 1, 0) for k in range(1, 8))
        index = (owner ^ me) * count + slots
        theirs = jnp.where(lax.broadcasted_iota(i32, (8 * count, n), 0) == index, 1.0, 0.0)
        first = sum(jnp.where(order >= k * per_orb, 1, 0) for k in range(1, count))
        mine = jnp.where(lax.broadcasted_iota(i32, (count, n), 0) == first, 1.0, 0.0)
        own = packet[:count, nvd:]
        rows[...] = pick(theirs, columns) - (pick(theirs, extra)[:, :1] + pick(mine, own)[:, :1])
        tbl[SIZE_I : SIZE_I + 1, :n] = pick(own, mine)[1:2, :].astype(i32)
        tbl[SIZE_J : SIZE_J + 1, :n] = pick(extra, theirs)[1:2, :].astype(i32) - col0

    build(0, outs[0], outs[1])
    build(2, outs[2], outs[3])
    build(1, outs[4])
    build(3, outs[5])


def tables_of(meta, smalls, cap, per_orb, half):
    table = jax.ShapeDtypeStruct((8, 128), i32)
    rows = jax.ShapeDtypeStruct((8 * cap, half), f32)
    return pl.pallas_call(
        lambda *refs: tables_kernel(cap, per_orb, *refs),
        out_shape=(table, rows, table, rows, table, table),
        in_specs=[SMEM] + [VMEM] * 8,
        out_specs=[VMEM] * 6,
        compiler_params=PARAMS,
        cost_estimate=TINY,
        name="tables",
    )(meta, *smalls)


def pack_kernel(jobs, tables, after, *refs):
    tbls, sources = refs[:tables], refs[tables : tables + len(jobs)]
    outs, sems = refs[tables + len(jobs) + after : -1], refs[-1]

    def copies(only_middle):
        made = []
        for k, (table, call, middle) in enumerate(jobs):
            if middle == only_middle:
                base = tbls[table][HEAD, call]
                halves, cap = outs[k].shape[:2]
                for r in range(cap):
                    slot = tbls[table][SLOT, base + r]
                    made += [
                        pltpu.make_async_copy(
                            sources[k].at[q, slot], outs[k].at[q, r], sems.at[k, q, r]
                        )
                        for q in range(halves)
                    ]
        return made

    everywhere = copies(False)
    for copy in everywhere:
        copy.start()

    @pl.when(tbls[0][HEAD, MIDDLE] == 1)
    def _():
        some = copies(True)
        for copy in some:
            copy.start()
        for copy in some:
            copy.wait()

    for copy in everywhere:
        copy.wait()


def pack(tbls, jobs, cap, after=()):
    sources = [source for _, _, source, _ in jobs]
    halves, _, *block = sources[0].shape
    shape = jax.ShapeDtypeStruct((halves, cap, *block), bf16)
    kinds = [(table, call, middle) for table, call, _, middle in jobs]
    return pl.pallas_call(
        lambda *refs: pack_kernel(kinds, len(tbls), len(after), *refs),
        out_shape=[shape] * len(jobs),
        in_specs=[SMEM] * len(tbls) + [HBM] * (len(jobs) + len(after)),
        out_specs=[VMEM] * len(jobs),
        scratch_shapes=[pltpu.SemaphoreType.DMA((len(jobs), halves, cap))],
        compiler_params=PARAMS,
        cost_estimate=TINY,
        name="pack",
    )(*tbls, *sources, *after)


def turn_kernel(*refs):
    half = len(refs) // 2
    for x, out in zip(refs[:half], refs[half:]):
        for r in range(x.shape[0]):
            out[r] = x[r].T


def turn(arrays):
    count, rows, cols = arrays[0].shape
    step = count // 4
    n = len(arrays)
    return pl.pallas_call(
        turn_kernel,
        out_shape=[jax.ShapeDtypeStruct((count, cols, rows), bf16)] * n,
        grid=(count // step,),
        in_specs=[pl.BlockSpec((step, rows, cols), lambda i: (i, 0, 0))] * n,
        out_specs=[pl.BlockSpec((step, cols, rows), lambda i: (i, 0, 0))] * n,
        compiler_params=PARAMS,
        cost_estimate=TINY,
        name="turn",
    )(*arrays)


def amplitudes_kernel(mode, call, per_orb, groups, tbl, rows, vcol, *refs):
    sv, s0, s1, b0, b1, st, se, sem, sem_out = refs[-9:]
    client = mode == "client"
    if client:
        tout = refs[-10]
        left, rest = refs[:1], refs[1:]
    else:
        tout, eout = refs[-11:-9]
        left, rest = refs[:2], refs[2:]
    places = []
    for arrays in groups:
        places.append([rest[0].at[0], rest[arrays - 1].at[2 - arrays]])
        rest = rest[arrays:]
    cap = sv.shape[0]
    nvd, half = sv.shape[1], sv.shape[2]
    base = tbl[HEAD, call]
    middle = tbl[HEAD, MIDDLE] == 1

    def place(r):
        return tbl[ORDER, base + r]

    def run(copies):
        for copy in copies:
            copy.start()
        for copy in copies:
            copy.wait()

    def load(js):
        copies = []
        for r in range(cap):
            i = lax.div(place(r), per_orb)
            slot = r if mode == "asked" else tbl[SLOT, base + r]
            todo = [
                (vcol.at[i], sv.at[r]),
                (js[0].at[slot], b0.at[r]),
                (js[1].at[slot], b1.at[r]),
            ]
            if client:
                core = lax.div(tbl[HEAD, COLUMN], half)
                for c, swapped in ((0, core), (1, 1 - core)):
                    rows_c = pl.ds(c * half, half)
                    todo += [
                        (left[0].at[2 * c + swapped, i], s0.at[r, rows_c, :]),
                        (left[0].at[2 * c + 1 - swapped, i], s1.at[r, rows_c, :]),
                    ]
            else:
                todo += [(left[0].at[i], s0.at[r]), (left[1].at[i], s1.at[r])]
            copies += [
                pltpu.make_async_copy(x, to, sem.at[r, k]) for k, (x, to) in enumerate(todo)
            ]
        run(copies)

    def gaps():
        row8 = rows[pl.ds(pl.multiple_of(base, cap), cap), :]
        return [sv[r] + row8[r : r + 1, :] for r in range(cap)]

    def make():
        live_a = lax.broadcasted_iota(i32, (nvd, half), 0)
        live_b = lax.broadcasted_iota(i32, (nvd, half), 1)
        for r, gap in enumerate(gaps()):
            size_i = tbl[SIZE_I, base + r]
            size_j = tbl[SIZE_J, base + r]
            k = jnp.dot(s0[r], b0[r], preferred_element_type=f32)
            k += jnp.dot(s1[r], b1[r], preferred_element_type=f32)
            k = jnp.where((live_a < size_i) & (live_b < size_j), k, 0.0)
            t = (-k / gap).astype(bf16)
            st[r] = t
            if not client:
                se[r : r + 1, :] = jnp.sum(k * t.astype(f32), axis=0, keepdims=True)

    def take():
        ready = rest[0]
        copies = [pltpu.make_async_copy(ready.at[r], st.at[r], sem.at[r, 0]) for r in range(cap)]
        copies += [
            pltpu.make_async_copy(vcol.at[lax.div(place(r), per_orb)], sv.at[r], sem.at[r, 1])
            for r in range(cap)
        ]
        run(copies)
        for r, gap in enumerate(gaps()):
            t = st[r].astype(f32)
            se[r : r + 1, :] = -jnp.sum(t * t * gap, axis=0, keepdims=True)

    if client:

        @pl.when(middle)
        def _():
            load(places[0])
            make()
            tout[...] = st[...]

        return
    if mode == "served":

        @pl.when(middle)
        def _():
            load(places[0])
            make()

        pl.when(jnp.logical_not(middle))(take)
    elif len(places) == 2:
        pl.when(middle)(lambda: load(places[0]))
        pl.when(jnp.logical_not(middle))(lambda: load(places[1]))
        make()
    else:
        load(places[0])
        make()
    run(
        [pltpu.make_async_copy(st.at[r], tout.at[place(r)], sem_out.at[r]) for r in range(cap)]
        + [
            pltpu.make_async_copy(
                se, eout.at[pl.ds(pl.multiple_of(base, cap), cap), :], sem_out.at[cap]
            )
        ]
    )


def amplitudes(mode, call, per_orb, tables, left, groups, cap, held=(), after=()):
    tbl, rows, vcol = tables
    occ, nvd, half = vcol.shape
    qa = left[0].shape[-1]
    sources = [x for group in groups for x in group]
    client = mode == "client"
    operands = (tbl, rows, vcol, *left, *sources, *after)
    aliases = {len(operands) + k: k for k in range(len(held))}
    operands += tuple(held)
    if client:
        out_shape = jax.ShapeDtypeStruct((cap, nvd, half), bf16)
        out_specs = VMEM
    else:
        out_shape = (
            jax.ShapeDtypeStruct((occ * per_orb, nvd, half), bf16),
            jax.ShapeDtypeStruct((occ * per_orb, half), f32),
        )
        out_specs = (HBM, HBM)
    return pl.pallas_call(
        lambda *refs: amplitudes_kernel(mode, call, per_orb, [len(g) for g in groups], *refs),
        out_shape=out_shape,
        in_specs=[SMEM, VMEM] + [HBM] * (len(operands) - 2),
        out_specs=out_specs,
        scratch_shapes=[
            pltpu.VMEM((cap, nvd, half), f32),
            pltpu.VMEM((cap, nvd, qa), bf16),
            pltpu.VMEM((cap, nvd, qa), bf16),
            pltpu.VMEM((cap, qa, half), bf16),
            pltpu.VMEM((cap, qa, half), bf16),
            pltpu.VMEM((cap, nvd, half), bf16),
            pltpu.VMEM((cap, half), f32),
            pltpu.SemaphoreType.DMA((cap, 7)),
            pltpu.SemaphoreType.DMA((cap + 1,)),
        ],
        input_output_aliases=aliases,
        compiler_params=PARAMS,
        cost_estimate=TINY,
        name="amplitudes",
    )(*operands)


def density_kernel(start, t, d):
    count, half = d.shape[:2]
    per_orb = t.shape[0] // count
    first = pl.multiple_of(start[0], half)
    for o in range(count):
        own = range(o * per_orb, (o + 1) * per_orb)
        left = jnp.concatenate([t[k, pl.ds(first, half), :] for k in own], axis=1)
        right = jnp.concatenate([t[k] for k in own], axis=1)
        d[o] = lax.dot_general(left, right, (((1,), (1,)), ((), ())), preferred_element_type=f32)


def density_rows(t_all, start, per_orb, half):
    npair, nvd, width = t_all.shape
    occ = npair // per_orb
    step = 4 if occ % 4 == 0 else 1
    return pl.pallas_call(
        density_kernel,
        out_shape=jax.ShapeDtypeStruct((occ, half, nvd), f32),
        grid_spec=pltpu.PrefetchScalarGridSpec(
            num_scalar_prefetch=1,
            grid=(occ // step,),
            in_specs=[pl.BlockSpec((step * per_orb, nvd, width), lambda i, s: (i, 0, 0))],
            out_specs=pl.BlockSpec((step, half, nvd), lambda i, s: (i, 0, 0)),
        ),
        compiler_params=pltpu.CompilerParams(vmem_limit_bytes=LIMIT),
        cost_estimate=TINY,
        name="density_rows",
    )(start.reshape(1), t_all)


def line_plan(blocks, vir_energy, occ_energy, domain_size, partner_owner, partner_slot):
    occ, qa, nvd = blocks.shape
    pair_dev = partner_slot.shape[0]
    per_orb = pair_dev // occ
    peers = 8
    cap = pair_dev // peers
    half = nvd // 2
    me, core = lax.axis_index("orb"), lax.axis_index("aux")
    col0 = core * half

    def pp(x, perm):
        return lax.ppermute(x, "orb", perm)

    def swap_core(x):
        return lax.ppermute(x, "aux", [(0, 1), (1, 0)])

    def flip(bits):
        return [(o, o ^ bits) for o in range(peers)]

    cross = [(2, 4), (3, 5), (4, 2), (5, 3)]
    outward = [(2, 0), (3, 1), (4, 6), (5, 7)]
    diagonal = [(2, 1), (3, 0), (4, 7), (5, 6)]
    y_middle = [(2, 3), (3, 2), (4, 5), (5, 4)]

    small, hit = lists(vir_energy, occ_energy, domain_size, partner_owner, partner_slot, cap)
    smalls = [small] + [pp(small, flip(bits)) for bits in range(1, peers)]

    other = swap_core(blocks)
    own = jnp.stack([lax.dynamic_slice_in_dim(x, col0, half, 2) for x in (blocks, other)])
    sent, smalls = lax.optimization_barrier((own, smalls))
    near, mid = pp(sent, flip(2)), pp(sent, cross)

    tbl, rows, client_tbl, client_rows, beside_list, relay_list = tables_of(
        jnp.stack([me, col0]), smalls, cap, per_orb, half
    )

    def spread(vir):
        return jnp.broadcast_to(vir[:, :, None], (occ, nvd, half))

    tables = (tbl, rows, spread(vir_energy))
    client = (client_tbl, client_rows, spread(smalls[2][:occ, :nvd]))
    lists_of = [beside_list, relay_list]

    def own_pairs(k, mode, groups, held=(), after=()):
        return amplitudes(mode, k, per_orb, tables, left, groups, cap, held, after)

    (packed,) = pack(lists_of, [(0, 0, own, False)], cap)
    beside = pp(packed, flip(1))
    left = turn([blocks, other])
    held = own_pairs(0, "slots", [[own]], after=(packed,))
    held = own_pairs(4, "asked", [[beside]], held)
    near, held = lax.optimization_barrier((near, held))
    far = [pp(near[q : q + 1], cross) for q in range(2)]
    columns = lax.all_gather(near, "aux").reshape(4 * occ, qa, half)
    (packed,) = pack(lists_of, [(0, 1, near, False)], cap, after=(held[1],))
    beside_near = pp(packed, flip(1))
    packed = pack(lists_of, [(1, 2, mid, True), (0, 2, mid, True)], cap, after=(packed,))
    third_diagonal = pp(packed[0], diagonal)
    third = pp(packed[1], y_middle)
    client_left = [x.reshape(4, occ, half, qa) for x in turn([columns])]
    gone = amplitudes(
        "client", 2, per_orb, client, client_left, [[mid]], cap, after=(packed[0],)
    )
    ready_2 = pp(gone, outward)
    held = own_pairs(1, "slots", [[near]], held, (gone, third_diagonal))
    fourth_diagonal, fourth = [], []

    def send_far(q, token):
        packed = pack(lists_of, [(1, 3, far[q], True), (0, 3, far[q], True)], cap, after=(token,))
        fourth_diagonal.append(pp(packed[0], diagonal))
        fourth.append(pp(packed[1], y_middle))
        return packed[0]

    packed = send_far(0, held[1])
    held = own_pairs(2, "served", [[mid]], held, (ready_2, packed))
    held = own_pairs(5, "asked", [[beside_near]], held)
    held = own_pairs(6, "asked", [[third], [third_diagonal]], held, (fourth_diagonal[0],))
    packed = send_far(1, held[1])
    gone = amplitudes("client", 3, per_orb, client, client_left, [far], cap, after=(packed,))
    ready_3 = pp(gone, outward)
    held = own_pairs(7, "asked", [fourth, fourth_diagonal], held, (gone,))
    t_all, e_all = own_pairs(3, "served", [far], held, (ready_3,))

    away = swap_core(density_rows(t_all, (1 - core) * half, per_orb, half))
    density = density_rows(t_all, core * half, per_orb, half) + away

    energy = jnp.sum(hit * jnp.sum(e_all, axis=1)[None, :], axis=1)
    energy = (energy + swap_core(energy)) / nvd
    return (energy, density)


def solution(mesh):
    in_specs = (
        P(("mol", "orb"), "aux", None),
        P(("mol", "orb"), None),
        P(("mol", "orb")),
        P(("mol", "orb")),
        P(("mol", "orb"), None),
        P(("mol", "orb")),
    )
    out_specs = (P(("mol", "orb")), P(("mol", "orb"), "aux", None))
    return jax.shard_map(
        line_plan if fits_line(mesh) else by_requests, mesh=mesh, in_specs=in_specs, out_specs=out_specs, check_vma=False
    )
```

```python
import jax
import jax.numpy as jnp
from jax import lax
from jax.experimental import pallas as pl
from jax.experimental.pallas import tpu as pltpu
from jax.sharding import PartitionSpec as P

f32, bf16, i32 = jnp.float32, jnp.bfloat16, jnp.int32
HBM = pl.BlockSpec(memory_space=pltpu.HBM)
SMEM = pl.BlockSpec(memory_space=pltpu.SMEM)
VMEM = pl.BlockSpec(memory_space=pltpu.VMEM)
LIMIT = 24 * 1024 * 1024


def slot_ranks(owner):
    count = owner.shape[0]
    order = jnp.arange(count, dtype=jnp.int32)
    same = (owner[:, None] == owner[None, :]) & (order[None, :] < order[:, None])
    return jnp.sum(same.astype(jnp.int32), axis=1)


def by_requests(blocks, vir_energy, occ_energy, domain_size, partner_owner, partner_slot):
    occ_dev, half_aux, nvd = blocks.shape
    pair_dev = partner_slot.shape[0]
    per_orb = pair_dev // occ_dev
    peers = lax.axis_size("orb")
    cap = max(2, (pair_dev + peers - 1) // peers)
    owner = partner_owner[:, 0]
    ranks = slot_ranks(owner)
    target = owner * cap + ranks
    wanted = (target[:, None] == jnp.arange(peers * cap, dtype=jnp.int32)[None, :]).astype(
        jnp.int32
    )
    requests = jnp.sum(wanted * partner_slot[:, None], axis=0).reshape(peers, cap)
    incoming = lax.all_to_all(requests, "orb", split_axis=0, concat_axis=0, tiled=True)
    flat_in = incoming.reshape(-1)
    send_blocks = jnp.take(blocks, flat_in, axis=0).reshape(peers, cap, half_aux, nvd)
    send_vir = jnp.take(vir_energy, flat_in, axis=0).reshape(peers, cap, nvd)
    send_occ = jnp.take(occ_energy, flat_in).reshape(peers, cap)
    send_size = jnp.take(domain_size, flat_in).astype(jnp.float32).reshape(peers, cap)
    got_blocks = lax.all_to_all(send_blocks, "orb", split_axis=0, concat_axis=0, tiled=True)
    got_vir, got_occ, got_size = (
        lax.all_to_all(send_vir, "orb", split_axis=0, concat_axis=0, tiled=True),
        lax.all_to_all(send_occ, "orb", split_axis=0, concat_axis=0, tiled=True),
        lax.all_to_all(send_size, "orb", split_axis=0, concat_axis=0, tiled=True),
    )
    partner = jnp.take(got_blocks.reshape(peers * cap, half_aux, nvd), target, axis=0).reshape(
        occ_dev, per_orb, half_aux, nvd
    )
    partner_vir = jnp.take(got_vir.reshape(peers * cap, nvd), target, axis=0).reshape(
        occ_dev, per_orb, nvd
    )
    partner_occ = jnp.take(got_occ.reshape(-1), target).reshape(occ_dev, per_orb)
    partner_size = jnp.take(got_size.reshape(-1), target).reshape(occ_dev, per_orb)
    half = nvd // lax.axis_size("aux")
    integrals = lax.psum_scatter(
        jnp.einsum("oqa,opqb->aopb", blocks, partner, preferred_element_type=jnp.float32),
        "aux",
        scatter_dimension=0,
        tiled=True,
    )
    row_start = lax.axis_index("aux") * half
    rows = row_start + jnp.arange(half, dtype=jnp.int32)
    cols = jnp.arange(nvd, dtype=jnp.int32).astype(jnp.float32)
    mask = (rows[:, None, None, None] < domain_size[None, :, None, None]) & (
        cols[None, None, None, :] < partner_size[None, :, :, None]
    )
    integrals = jnp.where(mask, integrals, jnp.zeros_like(integrals))
    vir_rows = lax.dynamic_slice_in_dim(vir_energy, row_start, half, 1)
    gap = (
        vir_rows.T[:, :, None, None]
        + partner_vir[None, :, :, :]
        - occ_energy[None, :, None, None]
        - partner_occ[None, :, :, None]
    )
    amp_rows = (-integrals / gap).astype(jnp.bfloat16)
    partial_energy = jnp.sum(integrals * amp_rows.astype(jnp.float32), axis=(0, 3))
    energy = lax.psum(partial_energy, "aux").reshape(pair_dev) / nvd
    density = jnp.einsum(
        "aopb,copb->oac",
        amp_rows,
        lax.all_gather(amp_rows, "aux", axis=0, tiled=True),
        preferred_element_type=jnp.float32,
    )
    return (energy, density)


def fits_line(mesh):
    return mesh.shape["orb"] == 8 and mesh.shape["aux"] == 2


TINY = pl.CostEstimate(flops=1, bytes_accessed=1, transcendentals=0)
PARAMS = pltpu.CompilerParams(vmem_limit_bytes=LIMIT)


def lists_kernel(cap, vir, occ, size, owner, slot, small, hit):
    n, (count, nvd) = hit.shape[0], vir.shape

    def column(row, m):
        eye = lax.broadcasted_iota(i32, (m, m), 0) == lax.broadcasted_iota(i32, (m, m), 1)
        return jnp.sum(jnp.where(eye, row, 0.0), axis=1, keepdims=True)

    down = lax.broadcasted_iota(i32, (n, n), 0).astype(f32)
    along = lax.broadcasted_iota(i32, (n, n), 1).astype(f32)
    owner_row = owner[...].astype(f32)
    owner_col = column(owner_row, n)
    before = (owner_col == owner_row) & (along < down)
    target = owner_col * cap + jnp.sum(jnp.where(before, 1.0, 0.0), axis=1, keepdims=True)
    found = target == along
    hit[...] = jnp.where(found, 1.0, 0.0)
    small[...] = jnp.zeros_like(small)
    small[:count, :nvd] = vir[...]
    lane = lax.broadcasted_iota(i32, (count, 128), 1)
    occ_col, size_col = column(occ[...], count), column(size[...].astype(f32), count)
    small[:count, nvd:] = jnp.where(lane == 0, occ_col, jnp.where(lane == 1, size_col, 0.0))
    small[count : count + 1, :n] = jnp.sum(jnp.where(found, down, 0.0), axis=0, keepdims=True)
    slot_col = column(slot[...].astype(f32), n)
    small[count : count + 1, 128 : 128 + n] = jnp.sum(
        jnp.where(found, slot_col, 0.0), axis=0, keepdims=True
    )


def lists(vir, occ, size, owner, slot, cap):
    count, nvd = vir.shape
    n = slot.shape[0]
    return pl.pallas_call(
        lambda *refs: lists_kernel(cap, *refs),
        out_shape=(
            jax.ShapeDtypeStruct((count + 8, nvd + 128), f32),
            jax.ShapeDtypeStruct((n, n), f32),
        ),
        in_specs=[VMEM] * 5,
        out_specs=(VMEM, VMEM),
        compiler_params=PARAMS,
        cost_estimate=TINY,
        name="lists",
    )(vir, occ.reshape(1, -1), size.reshape(1, -1), owner.reshape(1, -1), slot.reshape(1, -1))


ORDER, SLOT, SIZE_I, SIZE_J, HEAD = range(5)
MIDDLE, COLUMN = 8, 9


def pick(one, values):
    return lax.dot_general(
        one, values, (((0,), (0,)), ((), ())),
        precision=lax.Precision.HIGHEST, preferred_element_type=f32,
    )


def tables_kernel(cap, per_orb, meta, *refs):
    smalls, outs = refs[:8], refs[8:]
    count, nvd = smalls[0].shape[0] - 8, smalls[0].shape[1] - 128
    n = 8 * cap
    me, col0 = meta[0], meta[1]
    z, y = me // 2, me % 2
    lower = z < 2
    middle = jnp.where((z == 1) | (z == 2), 1, 0)
    places = [z, z ^ 1, jnp.where(lower, 2, 1), jnp.where(lower, 3, 0)]
    head = [(2 * p + y) * cap for p in places] + [(2 * p + 1 - y) * cap for p in places]
    lane = lax.broadcasted_iota(i32, (1, 128), 1)
    head_row = jnp.zeros((1, 128), i32)
    for k, value in enumerate(head + [middle, col0]):
        head_row = jnp.where(lane == k, value, head_row)
    orbitals = jnp.concatenate([x[:count, :] for x in smalls], axis=0)
    columns = jnp.where(col0 == 0, orbitals[:, : nvd // 2], orbitals[:, nvd // 2 : nvd])
    extra = orbitals[:, nvd:]

    def build(x, tbl, rows=None):
        order = smalls[x][count : count + 1, :n].astype(i32)
        slots = smalls[x][count : count + 1, 128 : 128 + n].astype(i32)
        tbl[...] = jnp.zeros_like(tbl)
        tbl[HEAD : HEAD + 1, :] = head_row
        tbl[SLOT : SLOT + 1, :n] = slots
        if rows is None:
            return
        tbl[ORDER : ORDER + 1, :n] = order
        pair = lax.broadcasted_iota(i32, (1, n), 1)
        owner = sum(jnp.where(pair >= k * cap, 1, 0) for k in range(1, 8))
        index = (owner ^ me) * count + slots
        theirs = jnp.where(lax.broadcasted_iota(i32, (8 * count, n), 0) == index, 1.0, 0.0)
        first = sum(jnp.where(order >= k * per_orb, 1, 0) for k in range(1, count))
        mine = jnp.where(lax.broadcasted_iota(i32, (count, n), 0) == first, 1.0, 0.0)
        own = smalls[x][:count, nvd:]
        rows[...] = pick(theirs, columns) - (pick(theirs, extra)[:, :1] + pick(mine, own)[:, :1])
        tbl[SIZE_I : SIZE_I + 1, :n] = pick(own, mine)[1:2, :].astype(i32)
        tbl[SIZE_J : SIZE_J + 1, :n] = pick(extra, theirs)[1:2, :].astype(i32) - col0

    build(0, outs[0], outs[1])
    build(2, outs[2], outs[3])
    build(1, outs[4])
    build(3, outs[5])


def tables_of(meta, smalls, cap, per_orb, half):
    table = jax.ShapeDtypeStruct((8, 128), i32)
    rows = jax.ShapeDtypeStruct((8 * cap, half), f32)
    return pl.pallas_call(
        lambda *refs: tables_kernel(cap, per_orb, *refs),
        out_shape=(table, rows, table, rows, table, table),
        in_specs=[SMEM] + [VMEM] * 8,
        out_specs=[VMEM] * 6,
        compiler_params=PARAMS,
        cost_estimate=TINY,
        name="tables",
    )(meta, *smalls)


def pack_kernel(call, only_middle, relayed, tbl, *refs):
    out = refs[-1]
    halves, cap = out.shape[:2]
    base = tbl[HEAD, call]
    middle = tbl[HEAD, MIDDLE] == 1

    def gather():
        for q in range(halves):
            for r in range(cap):
                out[q, r] = refs[q][tbl[SLOT, base + r]]

    if not only_middle and not relayed:
        gather()
    else:
        pl.when(middle)(gather)
    if relayed:

        @pl.when(jnp.logical_not(middle))
        def _():
            for q in range(halves):
                out[q] = refs[halves + q][0]


def pack(tbl, call, sources, cap, only_middle=False, relayed=None, after=()):
    halves = len(sources)
    shape = (halves, cap) + sources[0].shape[1:]
    operands = (*sources, *(relayed or ()))
    return pl.pallas_call(
        lambda *refs: pack_kernel(call, only_middle, relayed is not None, *refs),
        out_shape=jax.ShapeDtypeStruct(shape, bf16),
        in_specs=[SMEM] + [VMEM] * len(operands) + [HBM] * len(after),
        out_specs=VMEM,
        compiler_params=PARAMS,
        cost_estimate=TINY,
        name="pack",
    )(tbl, *operands, *after)


def turn_kernel(*refs):
    half = len(refs) // 2
    for x, out in zip(refs[:half], refs[half:]):
        for r in range(x.shape[0]):
            out[r] = x[r].T


def turn(arrays):
    count, rows, cols = arrays[0].shape
    step = 4 if count % 4 == 0 else 1
    n = len(arrays)
    return pl.pallas_call(
        turn_kernel,
        out_shape=[jax.ShapeDtypeStruct((count, cols, rows), bf16)] * n,
        grid=(count // step,),
        in_specs=[pl.BlockSpec((step, rows, cols), lambda i: (i, 0, 0))] * n,
        out_specs=[pl.BlockSpec((step, cols, rows), lambda i: (i, 0, 0))] * n,
        compiler_params=PARAMS,
        cost_estimate=TINY,
        name="turn",
    )(*arrays)


def amplitudes_kernel(mode, call, per_orb, groups, tbl, rows, vcol, *refs):
    client = mode == "client"
    if client:
        tout = refs[-1]
        left, rest = refs[:4], refs[4:]
    else:
        tout, eout = refs[-2:]
        left, rest = refs[:2], refs[2:]
    places = []
    for arrays in groups:
        if arrays == 1:
            places.append([rest[0].at[0], rest[0].at[1]])
        elif len(rest[0].shape) == 4:
            places.append([rest[0].at[0], rest[1].at[0]])
        else:
            places.append(rest[:2])
        rest = rest[arrays:]
    cap = rows.shape[0] // 8
    nvd, half = vcol.shape[1:]
    base = pl.multiple_of(tbl[HEAD, call], cap)
    middle = tbl[HEAD, MIDDLE] == 1
    row8 = rows[pl.ds(base, cap), :]

    def gap(r, i):
        return vcol[i] + row8[r : r + 1, :]

    def make(r):
        p = tbl[ORDER, base + r]
        i = lax.div(p, per_orb)
        slot = r if mode == "asked" else tbl[SLOT, base + r]
        b0, b1 = [x[slot] for x in places[0]]
        if len(places) == 2:
            b0, b1 = [jnp.where(middle, b, x[slot]) for b, x in zip((b0, b1), places[1])]

        def product(x0, x1):
            return jnp.dot(x0[i], b0, preferred_element_type=f32) + jnp.dot(
                x1[i], b1, preferred_element_type=f32
            )

        if client:
            here, there = product(left[0], left[1]), product(left[3], left[2])
            first = tbl[HEAD, COLUMN] == 0
            k = jnp.concatenate(
                [jnp.where(first, here, there), jnp.where(first, there, here)], axis=0
            )
        else:
            k = product(left[0], left[1])
        live_a = lax.broadcasted_iota(i32, (nvd, half), 0)
        live_b = lax.broadcasted_iota(i32, (nvd, half), 1)
        live = (live_a < tbl[SIZE_I, base + r]) & (live_b < tbl[SIZE_J, base + r])
        k = jnp.where(live, k, 0.0)
        t = (-k / gap(r, i)).astype(bf16)
        if client:
            tout[r] = t
            return None
        tout[p] = t
        return jnp.sum(k * t.astype(f32), axis=0, keepdims=True)

    def take(r):
        p = tbl[ORDER, base + r]
        ready = rest[0][r]
        tout[p] = ready
        t = ready.astype(f32)
        return -jnp.sum(t * t * gap(r, lax.div(p, per_orb)), axis=0, keepdims=True)

    def each(step):
        parts = [step(r) for r in range(cap)]
        if not client:
            eout[pl.ds(base, cap), :] = jnp.concatenate(parts, axis=0)

    if mode == "served":
        pl.when(middle)(lambda: each(make))
        pl.when(jnp.logical_not(middle))(lambda: each(take))
    elif client:
        pl.when(middle)(lambda: each(make))
    else:
        each(make)


def amplitudes(mode, call, per_orb, tables, left, groups, cap, held=(), after=(), ready=()):
    tbl, rows, vcol = tables
    occ, nvd, half = vcol.shape
    client = mode == "client"
    sources = [x for group in groups for x in group]
    blocks = (rows, vcol, *left, *sources, *ready)
    operands = (tbl, *blocks, *after)
    aliases = {len(operands) + k: k for k in range(len(held))}
    if client:
        out_shape = jax.ShapeDtypeStruct((cap, nvd, half), bf16)
        out_specs = VMEM
    else:
        out_shape = (
            jax.ShapeDtypeStruct((occ * per_orb, nvd, half), bf16),
            jax.ShapeDtypeStruct((occ * per_orb, half), f32),
        )
        out_specs = (VMEM, VMEM)
    return pl.pallas_call(
        lambda *refs: amplitudes_kernel(mode, call, per_orb, [len(g) for g in groups], *refs),
        out_shape=out_shape,
        in_specs=[SMEM] + [VMEM] * len(blocks) + [HBM] * len(after) + [VMEM] * len(held),
        out_specs=out_specs,
        input_output_aliases=aliases,
        compiler_params=PARAMS,
        cost_estimate=TINY,
        name="amplitudes",
    )(*operands, *held)


def density_kernel(start, t, d):
    count, half = d.shape[:2]
    per_orb = t.shape[0] // count
    first = pl.multiple_of(start[0], half)
    for o in range(count):
        own = range(o * per_orb, (o + 1) * per_orb)
        left = jnp.concatenate([t[k, pl.ds(first, half), :] for k in own], axis=1)
        right = jnp.concatenate([t[k] for k in own], axis=1)
        d[o] = lax.dot_general(left, right, (((1,), (1,)), ((), ())), preferred_element_type=f32)


def density_rows(t_all, start, per_orb, half):
    npair, nvd, width = t_all.shape
    occ = npair // per_orb
    step = 4 if occ % 4 == 0 else 1
    return pl.pallas_call(
        density_kernel,
        out_shape=jax.ShapeDtypeStruct((occ, half, nvd), f32),
        grid_spec=pltpu.PrefetchScalarGridSpec(
            num_scalar_prefetch=1,
            grid=(occ // step,),
            in_specs=[pl.BlockSpec((step * per_orb, nvd, width), lambda i, s: (i, 0, 0))],
            out_specs=pl.BlockSpec((step, half, nvd), lambda i, s: (i, 0, 0)),
        ),
        compiler_params=pltpu.CompilerParams(vmem_limit_bytes=LIMIT),
        cost_estimate=TINY,
        name="density_rows",
    )(start.reshape(1), t_all)


def line_plan(blocks, vir_energy, occ_energy, domain_size, partner_owner, partner_slot):
    occ, qa, nvd = blocks.shape
    pair_dev = partner_slot.shape[0]
    per_orb = pair_dev // occ
    peers = 8
    cap = pair_dev // peers
    half = nvd // 2
    me, core = lax.axis_index("orb"), lax.axis_index("aux")
    col0 = core * half

    def pp(x, perm):
        return lax.ppermute(x, "orb", perm)

    def swap_core(x):
        return lax.ppermute(x, "aux", [(0, 1), (1, 0)])

    def flip(bits):
        return [(o, o ^ bits) for o in range(peers)]

    cross = [(2, 4), (3, 5), (4, 2), (5, 3)]
    outward = [(2, 0), (3, 1), (4, 6), (5, 7)]
    diagonal = [(2, 1), (3, 0), (4, 7), (5, 6)]
    y_middle = [(2, 3), (3, 2), (4, 5), (5, 4)]

    small, hit = lists(vir_energy, occ_energy, domain_size, partner_owner, partner_slot, cap)
    smalls = [small] + [pp(small, flip(bits)) for bits in range(1, peers)]

    other = swap_core(blocks)
    own = [lax.dynamic_slice_in_dim(x, col0, half, 2) for x in (blocks, other)]
    sent, smalls = lax.optimization_barrier((own[0], smalls))
    near = [pp(x, flip(2)) for x in (sent, own[1])]
    mid = [pp(x, cross) for x in (sent, own[1])]
    tbl, rows, client_tbl, client_rows, beside_list, relay_list = tables_of(
        jnp.stack([me, col0]), smalls, cap, per_orb, half
    )

    def spread(vir):
        return jnp.broadcast_to(vir[:, :, None], (occ, nvd, half))

    tables = (tbl, rows, spread(vir_energy))
    client = (client_tbl, client_rows, spread(smalls[2][:occ, :nvd]))

    def own_pairs(k, mode, groups, held=(), after=(), ready=()):
        return amplitudes(mode, k, per_orb, tables, left, groups, cap, held, after, ready)

    packed = pack(beside_list, 0, own, cap)
    beside = pp(packed, flip(1))
    left = turn([blocks, other])
    held = own_pairs(0, "slots", [own], after=(packed,))
    first, held = lax.optimization_barrier((near[0], held))
    far = [pp(first, cross)]
    across = [swap_core(first)]
    packed = pack(relay_list, 2, mid[:1], cap, only_middle=True, after=(held[1],))
    relays = [pp(packed, outward)]
    held = own_pairs(4, "asked", [[beside]], held, (packed,))
    second, held = lax.optimization_barrier((near[1], held))
    far.append(pp(second, cross))
    across.append(swap_core(second))
    near = [first, second]
    packed = pack(relay_list, 2, mid[1:], cap, only_middle=True, after=(held[1],))
    relays.append(pp(packed, outward))
    packed = pack(beside_list, 1, near, cap, after=(packed,))
    beside_near = pp(packed, flip(1))
    client_left = turn(near + across)
    gone = amplitudes(
        "client", 2, per_orb, client, client_left, [mid], cap, after=(packed, relays[0])
    )
    ready_2 = pp(gone, outward)
    held = own_pairs(1, "slots", [near], held, (gone,))
    packed = pack(beside_list, 2, mid, cap, relayed=relays, after=(held[1],))
    third = pp(packed, flip(1))
    fourth_diagonal, fourth = [], []

    def send_far(q, token):
        packed = pack(relay_list, 3, far[q : q + 1], cap, only_middle=True, after=(token,))
        fourth_diagonal.append(pp(packed, diagonal))
        packed = pack(beside_list, 3, far[q : q + 1], cap, only_middle=True, after=(packed,))
        fourth.append(pp(packed, y_middle))
        return packed

    packed = send_far(0, packed)
    held = own_pairs(2, "served", [mid], held, (packed, beside_near), (ready_2,))
    held = own_pairs(5, "asked", [[beside_near]], held, (fourth_diagonal[0],))
    packed = send_far(1, held[1])
    gone = amplitudes("client", 3, per_orb, client, client_left, [far], cap, after=(packed,))
    ready_3 = pp(gone, outward)
    held = own_pairs(6, "asked", [[third]], held, (gone,))
    held = own_pairs(7, "asked", [fourth, fourth_diagonal], held)
    t_all, e_all = own_pairs(3, "served", [far], held, ready=(ready_3,))

    away = swap_core(density_rows(t_all, (1 - core) * half, per_orb, half))
    density = density_rows(t_all, core * half, per_orb, half) + away

    energy = jnp.sum(hit * jnp.sum(e_all, axis=1)[None, :], axis=1)
    energy = (energy + swap_core(energy)) / nvd
    return (energy, density)


def solution(mesh):
    in_specs = (
        P(("mol", "orb"), "aux", None),
        P(("mol", "orb"), None),
        P(("mol", "orb")),
        P(("mol", "orb")),
        P(("mol", "orb"), None),
        P(("mol", "orb")),
    )
    out_specs = (P(("mol", "orb")), P(("mol", "orb"), "aux", None))
    return jax.shard_map(
        line_plan if fits_line(mesh) else by_requests, mesh=mesh, in_specs=in_specs, out_specs=out_specs, check_vma=False
    )
```

```python
import functools

import jax
import jax.numpy as jnp
from jax import lax
from jax.experimental import pallas as pl
from jax.experimental.pallas import tpu as pltpu
from jax.sharding import PartitionSpec as P

f32, bf16, i32 = jnp.float32, jnp.bfloat16, jnp.int32
HBM = pl.BlockSpec(memory_space=pltpu.HBM)
SMEM = pl.BlockSpec(memory_space=pltpu.SMEM)
VMEM = pl.BlockSpec(memory_space=pltpu.VMEM)
LIMIT = 12 * 1024 * 1024


def slot_ranks(owner):
    count = owner.shape[0]
    order = jnp.arange(count, dtype=jnp.int32)
    same = (owner[:, None] == owner[None, :]) & (order[None, :] < order[:, None])
    return jnp.sum(same.astype(jnp.int32), axis=1)


def by_requests(blocks, vir_energy, occ_energy, domain_size, partner_owner, partner_slot):
    occ_dev, half_aux, nvd = blocks.shape
    pair_dev = partner_slot.shape[0]
    per_orb = pair_dev // occ_dev
    peers = lax.axis_size("orb")
    cap = max(2, (pair_dev + peers - 1) // peers)
    owner = partner_owner[:, 0]
    ranks = slot_ranks(owner)
    target = owner * cap + ranks
    wanted = (target[:, None] == jnp.arange(peers * cap, dtype=jnp.int32)[None, :]).astype(
        jnp.int32
    )
    requests = jnp.sum(wanted * partner_slot[:, None], axis=0).reshape(peers, cap)
    incoming = lax.all_to_all(requests, "orb", split_axis=0, concat_axis=0, tiled=True)
    flat_in = incoming.reshape(-1)
    send_blocks = jnp.take(blocks, flat_in, axis=0).reshape(peers, cap, half_aux, nvd)
    send_vir = jnp.take(vir_energy, flat_in, axis=0).reshape(peers, cap, nvd)
    send_occ = jnp.take(occ_energy, flat_in).reshape(peers, cap)
    send_size = jnp.take(domain_size, flat_in).astype(jnp.float32).reshape(peers, cap)
    got_blocks = lax.all_to_all(send_blocks, "orb", split_axis=0, concat_axis=0, tiled=True)
    got_vir, got_occ, got_size = (
        lax.all_to_all(send_vir, "orb", split_axis=0, concat_axis=0, tiled=True),
        lax.all_to_all(send_occ, "orb", split_axis=0, concat_axis=0, tiled=True),
        lax.all_to_all(send_size, "orb", split_axis=0, concat_axis=0, tiled=True),
    )
    partner = jnp.take(got_blocks.reshape(peers * cap, half_aux, nvd), target, axis=0).reshape(
        occ_dev, per_orb, half_aux, nvd
    )
    partner_vir = jnp.take(got_vir.reshape(peers * cap, nvd), target, axis=0).reshape(
        occ_dev, per_orb, nvd
    )
    partner_occ = jnp.take(got_occ.reshape(-1), target).reshape(occ_dev, per_orb)
    partner_size = jnp.take(got_size.reshape(-1), target).reshape(occ_dev, per_orb)
    half = nvd // lax.axis_size("aux")
    integrals = lax.psum_scatter(
        jnp.einsum("oqa,opqb->aopb", blocks, partner, preferred_element_type=jnp.float32),
        "aux",
        scatter_dimension=0,
        tiled=True,
    )
    row_start = lax.axis_index("aux") * half
    rows = row_start + jnp.arange(half, dtype=jnp.int32)
    cols = jnp.arange(nvd, dtype=jnp.int32).astype(jnp.float32)
    mask = (rows[:, None, None, None] < domain_size[None, :, None, None]) & (
        cols[None, None, None, :] < partner_size[None, :, :, None]
    )
    integrals = jnp.where(mask, integrals, jnp.zeros_like(integrals))
    vir_rows = lax.dynamic_slice_in_dim(vir_energy, row_start, half, 1)
    gap = (
        vir_rows.T[:, :, None, None]
        + partner_vir[None, :, :, :]
        - occ_energy[None, :, None, None]
        - partner_occ[None, :, :, None]
    )
    amp_rows = (-integrals / gap).astype(jnp.bfloat16)
    partial_energy = jnp.sum(integrals * amp_rows.astype(jnp.float32), axis=(0, 3))
    energy = lax.psum(partial_energy, "aux").reshape(pair_dev) / nvd
    density = jnp.einsum(
        "aopb,copb->oac",
        amp_rows,
        lax.all_gather(amp_rows, "aux", axis=0, tiled=True),
        preferred_element_type=jnp.float32,
    )
    return (energy, density)


def fits_line(mesh):
    return mesh.shape["orb"] == 8 and mesh.shape["aux"] == 2


TINY = pl.CostEstimate(flops=1, bytes_accessed=1, transcendentals=0)
PARAMS = pltpu.CompilerParams(vmem_limit_bytes=LIMIT)


def lists_kernel(cap, vir, occ, size, owner, slot, small, hit):
    n, (count, nvd) = hit.shape[0], vir.shape

    def column(row, m):
        eye = lax.broadcasted_iota(i32, (m, m), 0) == lax.broadcasted_iota(i32, (m, m), 1)
        return jnp.sum(jnp.where(eye, row, 0.0), axis=1, keepdims=True)

    down = lax.broadcasted_iota(i32, (n, n), 0).astype(f32)
    along = lax.broadcasted_iota(i32, (n, n), 1).astype(f32)
    owner_row = owner[...].astype(f32)
    owner_col = column(owner_row, n)
    before = (owner_col == owner_row) & (along < down)
    target = owner_col * cap + jnp.sum(jnp.where(before, 1.0, 0.0), axis=1, keepdims=True)
    found = target == along
    hit[...] = jnp.where(found, 1.0, 0.0)
    small[...] = jnp.zeros_like(small)
    small[:count, :nvd] = vir[...]
    lane = lax.broadcasted_iota(i32, (count, 128), 1)
    occ_col, size_col = column(occ[...], count), column(size[...].astype(f32), count)
    small[:count, nvd:] = jnp.where(lane == 0, occ_col, jnp.where(lane == 1, size_col, 0.0))
    small[count : count + 1, :n] = jnp.sum(jnp.where(found, down, 0.0), axis=0, keepdims=True)
    slot_col = column(slot[...].astype(f32), n)
    small[count : count + 1, 128 : 128 + n] = jnp.sum(
        jnp.where(found, slot_col, 0.0), axis=0, keepdims=True
    )


def lists(vir, occ, size, owner, slot, cap):
    count, nvd = vir.shape
    n = slot.shape[0]
    return pl.pallas_call(
        lambda *refs: lists_kernel(cap, *refs),
        out_shape=(
            jax.ShapeDtypeStruct((count + 8, nvd + 128), f32),
            jax.ShapeDtypeStruct((n, n), f32),
        ),
        in_specs=[VMEM] * 5,
        out_specs=(VMEM, VMEM),
        compiler_params=PARAMS,
        cost_estimate=TINY,
        name="lists",
    )(vir, occ.reshape(1, -1), size.reshape(1, -1), owner.reshape(1, -1), slot.reshape(1, -1))


ORDER, SLOT, SIZE_I, SIZE_J, HEAD = range(5)
MIDDLE, COLUMN = 8, 9


def pick(one, values):
    return lax.dot_general(
        one, values, (((0,), (0,)), ((), ())),
        precision=lax.Precision.HIGHEST, preferred_element_type=f32,
    )


def tables_kernel(cap, per_orb, meta, *refs):
    smalls, outs = refs[:8], refs[8:]
    count, nvd = smalls[0].shape[0] - 8, smalls[0].shape[1] - 128
    n = 8 * cap
    me, col0 = meta[0], meta[1]
    z, y = me // 2, me % 2
    lower = z < 2
    middle = jnp.where((z == 1) | (z == 2), 1, 0)
    places = [z, z ^ 1, jnp.where(lower, 2, 1), jnp.where(lower, 3, 0)]
    head = [(2 * p + y) * cap for p in places] + [(2 * p + 1 - y) * cap for p in places]
    lane = lax.broadcasted_iota(i32, (1, 128), 1)
    head_row = jnp.zeros((1, 128), i32)
    for k, value in enumerate(head + [middle, col0]):
        head_row = jnp.where(lane == k, value, head_row)
    orbitals = jnp.concatenate([x[:count, :] for x in smalls], axis=0)
    columns = jnp.where(col0 == 0, orbitals[:, : nvd // 2], orbitals[:, nvd // 2 : nvd])
    extra = orbitals[:, nvd:]

    def build(x, tbl, rows=None):
        order = smalls[x][count : count + 1, :n].astype(i32)
        slots = smalls[x][count : count + 1, 128 : 128 + n].astype(i32)
        tbl[...] = jnp.zeros_like(tbl)
        tbl[HEAD : HEAD + 1, :] = head_row
        tbl[SLOT : SLOT + 1, :n] = slots
        if rows is None:
            return
        tbl[ORDER : ORDER + 1, :n] = order
        pair = lax.broadcasted_iota(i32, (1, n), 1)
        owner = sum(jnp.where(pair >= k * cap, 1, 0) for k in range(1, 8))
        index = (owner ^ me) * count + slots
        theirs = jnp.where(lax.broadcasted_iota(i32, (8 * count, n), 0) == index, 1.0, 0.0)
        first = sum(jnp.where(order >= k * per_orb, 1, 0) for k in range(1, count))
        mine = jnp.where(lax.broadcasted_iota(i32, (count, n), 0) == first, 1.0, 0.0)
        own = smalls[x][:count, nvd:]
        rows[...] = pick(theirs, columns) - (pick(theirs, extra)[:, :1] + pick(mine, own)[:, :1])
        tbl[SIZE_I : SIZE_I + 1, :n] = pick(own, mine)[1:2, :].astype(i32)
        tbl[SIZE_J : SIZE_J + 1, :n] = pick(extra, theirs)[1:2, :].astype(i32) - col0

    build(0, outs[0], outs[1])
    build(2, outs[2], outs[3])
    build(1, outs[4])
    build(3, outs[5])


def tables_of(meta, smalls, cap, per_orb, half):
    table = jax.ShapeDtypeStruct((8, 128), i32)
    rows = jax.ShapeDtypeStruct((8 * cap, half), f32)
    return pl.pallas_call(
        lambda *refs: tables_kernel(cap, per_orb, *refs),
        out_shape=(table, rows, table, rows, table, table),
        in_specs=[SMEM] + [VMEM] * 8,
        out_specs=[VMEM] * 6,
        compiler_params=PARAMS,
        cost_estimate=TINY,
        name="tables",
    )(meta, *smalls)


def pack_kernel(jobs, tables, *refs):
    tbls, rest = refs[:tables], refs[tables:]
    outs = refs[-len(jobs) :]
    middle = tbls[0][HEAD, MIDDLE] == 1

    def gather(out, sources, tbl, call):
        base = tbl[HEAD, call]
        for q in range(out.shape[0]):
            for r in range(out.shape[1]):
                out[q, r] = sources[q][tbl[SLOT, base + r]]

    for out, (table, call, halves, only_middle) in zip(outs, jobs):
        sources, rest = rest[:halves], rest[halves:]
        if only_middle:
            pl.when(middle)(functools.partial(gather, out, sources, tbls[table], call))
        else:
            gather(out, sources, tbls[table], call)


def pack(tbls, jobs, cap, after=()):
    operands = [x for _, _, sources, _ in jobs for x in sources]
    kinds = [(table, call, len(sources), middle) for table, call, sources, middle in jobs]
    block = operands[0].shape[1:]
    return pl.pallas_call(
        lambda *refs: pack_kernel(kinds, len(tbls), *refs),
        out_shape=[jax.ShapeDtypeStruct((k[2], cap) + block, bf16) for k in kinds],
        in_specs=[SMEM] * len(tbls) + [VMEM] * len(operands) + [HBM] * len(after),
        out_specs=[VMEM] * len(jobs),
        compiler_params=PARAMS,
        cost_estimate=TINY,
        name="pack",
    )(*tbls, *operands, *after)


def turn_kernel(*refs):
    half = len(refs) // 2
    for x, out in zip(refs[:half], refs[half:]):
        for r in range(x.shape[0]):
            out[r] = x[r].T


def turn(arrays):
    count, rows, cols = arrays[0].shape
    step = 4 if count % 4 == 0 else 1
    n = len(arrays)
    return pl.pallas_call(
        turn_kernel,
        out_shape=[jax.ShapeDtypeStruct((count, cols, rows), bf16)] * n,
        grid=(count // step,),
        in_specs=[pl.BlockSpec((step, rows, cols), lambda i: (i, 0, 0))] * n,
        out_specs=[pl.BlockSpec((step, cols, rows), lambda i: (i, 0, 0))] * n,
        compiler_params=PARAMS,
        cost_estimate=TINY,
        name="turn",
    )(*arrays)


def amplitudes_kernel(mode, call, per_orb, groups, tbl, rows, vcol, *refs):
    client = mode == "client"
    if client:
        tout = refs[-1]
        left, rest = refs[:4], refs[4:]
    else:
        tout, eout = refs[-2:]
        left, rest = refs[:2], refs[2:]
    places = []
    for arrays in groups:
        if arrays == 1:
            places.append([rest[0].at[0], rest[0].at[1]])
        elif len(rest[0].shape) == 4:
            places.append([rest[0].at[0], rest[1].at[0]])
        else:
            places.append(rest[:2])
        rest = rest[arrays:]
    cap = rows.shape[0] // 8
    nvd, half = vcol.shape[1:]
    base = pl.multiple_of(tbl[HEAD, call], cap)
    middle = tbl[HEAD, MIDDLE] == 1
    row8 = rows[pl.ds(base, cap), :]

    def gap(r, i):
        return vcol[i] + row8[r : r + 1, :]

    def make(r):
        p = tbl[ORDER, base + r]
        i = lax.div(p, per_orb)
        slot = r if mode == "asked" else tbl[SLOT, base + r]
        b0, b1 = [x[slot] for x in places[0]]
        if len(places) == 2:
            b0, b1 = [jnp.where(middle, b, x[slot]) for b, x in zip((b0, b1), places[1])]

        def product(x0, x1):
            return jnp.dot(x0[i], b0, preferred_element_type=f32) + jnp.dot(
                x1[i], b1, preferred_element_type=f32
            )

        if client:
            here, there = product(left[0], left[1]), product(left[3], left[2])
            first = tbl[HEAD, COLUMN] == 0
            k = jnp.concatenate(
                [jnp.where(first, here, there), jnp.where(first, there, here)], axis=0
            )
        else:
            k = product(left[0], left[1])
        live_a = lax.broadcasted_iota(i32, (nvd, half), 0)
        live_b = lax.broadcasted_iota(i32, (nvd, half), 1)
        live = (live_a < tbl[SIZE_I, base + r]) & (live_b < tbl[SIZE_J, base + r])
        k = jnp.where(live, k, 0.0)
        t = (-k / gap(r, i)).astype(bf16)
        if client:
            tout[r] = t
            return None
        tout[p] = t
        return jnp.sum(k * t.astype(f32), axis=0, keepdims=True)

    def take(r):
        p = tbl[ORDER, base + r]
        ready = rest[0][r]
        tout[p] = ready
        t = ready.astype(f32)
        return -jnp.sum(t * t * gap(r, lax.div(p, per_orb)), axis=0, keepdims=True)

    def each(step):
        parts = [step(r) for r in range(cap)]
        if not client:
            eout[pl.ds(base, cap), :] = jnp.concatenate(parts, axis=0)

    if mode == "served":
        pl.when(middle)(lambda: each(make))
        pl.when(jnp.logical_not(middle))(lambda: each(take))
    elif client:
        pl.when(middle)(lambda: each(make))
    else:
        each(make)


def amplitudes(mode, call, per_orb, tables, left, groups, cap, held=(), after=(), ready=()):
    tbl, rows, vcol = tables
    occ, nvd, half = vcol.shape
    client = mode == "client"
    sources = [x for group in groups for x in group]
    blocks = (rows, vcol, *left, *sources, *ready)
    operands = (tbl, *blocks, *after)
    aliases = {len(operands) + k: k for k in range(len(held))}
    if client:
        out_shape = jax.ShapeDtypeStruct((cap, nvd, half), bf16)
        out_specs = VMEM
    else:
        out_shape = (
            jax.ShapeDtypeStruct((occ * per_orb, nvd, half), bf16),
            jax.ShapeDtypeStruct((occ * per_orb, half), f32),
        )
        out_specs = (VMEM, VMEM)
    return pl.pallas_call(
        lambda *refs: amplitudes_kernel(mode, call, per_orb, [len(g) for g in groups], *refs),
        out_shape=out_shape,
        in_specs=[SMEM] + [VMEM] * len(blocks) + [HBM] * len(after) + [VMEM] * len(held),
        out_specs=out_specs,
        input_output_aliases=aliases,
        compiler_params=PARAMS,
        cost_estimate=TINY,
        name="amplitudes",
    )(*operands, *held)


def density_kernel(start, t, d):
    count, half = d.shape[:2]
    per_orb = t.shape[0] // count
    first = pl.multiple_of(start[0], half)
    for o in range(count):
        own = range(o * per_orb, (o + 1) * per_orb)
        left = jnp.concatenate([t[k, pl.ds(first, half), :] for k in own], axis=1)
        right = jnp.concatenate([t[k] for k in own], axis=1)
        d[o] = lax.dot_general(left, right, (((1,), (1,)), ((), ())), preferred_element_type=f32)


def density_rows(t_all, start, per_orb, half):
    npair, nvd, width = t_all.shape
    occ = npair // per_orb
    step = 4 if occ % 4 == 0 else 1
    return pl.pallas_call(
        density_kernel,
        out_shape=jax.ShapeDtypeStruct((occ, half, nvd), f32),
        grid_spec=pltpu.PrefetchScalarGridSpec(
            num_scalar_prefetch=1,
            grid=(occ // step,),
            in_specs=[pl.BlockSpec((step * per_orb, nvd, width), lambda i, s: (i, 0, 0))],
            out_specs=pl.BlockSpec((step, half, nvd), lambda i, s: (i, 0, 0)),
        ),
        compiler_params=pltpu.CompilerParams(vmem_limit_bytes=LIMIT),
        cost_estimate=TINY,
        name="density_rows",
    )(start.reshape(1), t_all)


def line_plan(blocks, vir_energy, occ_energy, domain_size, partner_owner, partner_slot):
    occ, qa, nvd = blocks.shape
    pair_dev = partner_slot.shape[0]
    per_orb = pair_dev // occ
    peers = 8
    cap = pair_dev // peers
    half = nvd // 2
    me, core = lax.axis_index("orb"), lax.axis_index("aux")
    col0 = core * half

    def pp(x, perm):
        return lax.ppermute(x, "orb", perm)

    def swap_core(x):
        return lax.ppermute(x, "aux", [(0, 1), (1, 0)])

    def flip(bits):
        return [(o, o ^ bits) for o in range(peers)]

    cross = [(2, 4), (3, 5), (4, 2), (5, 3)]
    outward = [(2, 0), (3, 1), (4, 6), (5, 7)]
    diagonal = [(2, 1), (3, 0), (4, 7), (5, 6)]
    y_middle = [(2, 3), (3, 2), (4, 5), (5, 4)]

    small, hit = lists(vir_energy, occ_energy, domain_size, partner_owner, partner_slot, cap)
    smalls = [small] + [pp(small, flip(bits)) for bits in range(1, peers)]

    other = swap_core(blocks)
    own = [lax.dynamic_slice_in_dim(x, col0, half, 2) for x in (blocks, other)]
    sent, smalls = lax.optimization_barrier((own[0], smalls))
    mid = [pp(x, cross) for x in (sent, own[1])]
    near = [pp(x, flip(2)) for x in (sent, own[1])]
    tbl, rows, client_tbl, client_rows, beside_list, relay_list = tables_of(
        jnp.stack([me, col0]), smalls, cap, per_orb, half
    )
    lists_of = [beside_list, relay_list]

    def spread(vir):
        return jnp.broadcast_to(vir[:, :, None], (occ, nvd, half))

    tables = (tbl, rows, spread(vir_energy))
    client = (client_tbl, client_rows, spread(smalls[2][:occ, :nvd]))

    def own_pairs(k, mode, groups, held=(), after=(), ready=()):
        return amplitudes(mode, k, per_orb, tables, left, groups, cap, held, after, ready)

    (packed,) = pack(lists_of, [(0, 0, own, False)], cap)
    beside = pp(packed, flip(1))
    left = turn([blocks, other])
    held = own_pairs(0, "slots", [own], after=(packed,))
    first, held = lax.optimization_barrier((near[0], held))
    far = [pp(first, cross)]
    across = [swap_core(first)]
    (packed,) = pack(lists_of, [(0, 1, [first], False)], cap, after=(held[1], mid[0]))
    beside_near = [pp(packed, flip(1))]
    held = own_pairs(4, "asked", [[beside]], held, (packed, beside_near[0]))
    second, held = lax.optimization_barrier((near[1], held))
    far.append(pp(second, cross))
    across.append(swap_core(second))
    near = [first, second]
    packed = pack(lists_of, [(1, 2, mid, True), (0, 2, mid, True)], cap, after=(held[1],))
    third_diagonal, third = pp(packed[0], diagonal), pp(packed[1], y_middle)
    (packed,) = pack(lists_of, [(0, 1, [second], False)], cap, after=(packed[0],))
    beside_near.append(pp(packed, flip(1)))
    client_left = turn(near + across)
    gone = amplitudes("client", 2, per_orb, client, client_left, [mid], cap, after=(packed,))
    ready_2 = pp(gone, outward)
    held = own_pairs(1, "slots", [near], held, (gone, third_diagonal))
    held = own_pairs(5, "asked", [beside_near], held)
    fourth_diagonal, fourth = [], []

    def send_far(q, token):
        jobs = [(1, 3, far[q : q + 1], True), (0, 3, far[q : q + 1], True)]
        packed = pack(lists_of, jobs, cap, after=(token,))
        fourth_diagonal.append(pp(packed[0], diagonal))
        fourth.append(pp(packed[1], y_middle))
        return packed[0]

    packed = send_far(0, held[1])
    held = own_pairs(2, "served", [mid], held, (packed,), (ready_2,))
    held = own_pairs(
        6, "asked", [[third], [third_diagonal]], held, (fourth[0], fourth_diagonal[0])
    )
    packed = send_far(1, held[1])
    gone = amplitudes("client", 3, per_orb, client, client_left, [far], cap, after=(packed,))
    ready_3 = pp(gone, outward)
    held = own_pairs(7, "asked", [fourth, fourth_diagonal], held, (gone,))
    t_all, e_all = own_pairs(3, "served", [far], held, ready=(ready_3,))

    away = swap_core(density_rows(t_all, (1 - core) * half, per_orb, half))
    density = density_rows(t_all, core * half, per_orb, half) + away

    energy = jnp.sum(hit * jnp.sum(e_all, axis=1)[None, :], axis=1)
    energy = (energy + swap_core(energy)) / nvd
    return (energy, density)


def solution(mesh):
    in_specs = (
        P(("mol", "orb"), "aux", None),
        P(("mol", "orb"), None),
        P(("mol", "orb")),
        P(("mol", "orb")),
        P(("mol", "orb"), None),
        P(("mol", "orb")),
    )
    out_specs = (P(("mol", "orb")), P(("mol", "orb"), "aux", None))
    return jax.shard_map(
        line_plan if fits_line(mesh) else by_requests, mesh=mesh, in_specs=in_specs, out_specs=out_specs, check_vma=False
    )
```

```python
import functools

import jax
import jax.numpy as jnp
from jax import lax
from jax.experimental import pallas as pl
from jax.experimental.pallas import tpu as pltpu
from jax.sharding import PartitionSpec as P

f32, bf16, i32 = jnp.float32, jnp.bfloat16, jnp.int32
HBM = pl.BlockSpec(memory_space=pltpu.HBM)
SMEM = pl.BlockSpec(memory_space=pltpu.SMEM)
VMEM = pl.BlockSpec(memory_space=pltpu.VMEM)
LIMIT = 12 * 1024 * 1024


def slot_ranks(owner):
    count = owner.shape[0]
    order = jnp.arange(count, dtype=jnp.int32)
    same = (owner[:, None] == owner[None, :]) & (order[None, :] < order[:, None])
    return jnp.sum(same.astype(jnp.int32), axis=1)


def by_requests(blocks, vir_energy, occ_energy, domain_size, partner_owner, partner_slot):
    occ_dev, half_aux, nvd = blocks.shape
    pair_dev = partner_slot.shape[0]
    per_orb = pair_dev // occ_dev
    peers = lax.axis_size("orb")
    cap = max(2, (pair_dev + peers - 1) // peers)
    owner = partner_owner[:, 0]
    ranks = slot_ranks(owner)
    target = owner * cap + ranks
    wanted = (target[:, None] == jnp.arange(peers * cap, dtype=jnp.int32)[None, :]).astype(
        jnp.int32
    )
    requests = jnp.sum(wanted * partner_slot[:, None], axis=0).reshape(peers, cap)
    incoming = lax.all_to_all(requests, "orb", split_axis=0, concat_axis=0, tiled=True)
    flat_in = incoming.reshape(-1)
    send_blocks = jnp.take(blocks, flat_in, axis=0).reshape(peers, cap, half_aux, nvd)
    send_vir = jnp.take(vir_energy, flat_in, axis=0).reshape(peers, cap, nvd)
    send_occ = jnp.take(occ_energy, flat_in).reshape(peers, cap)
    send_size = jnp.take(domain_size, flat_in).astype(jnp.float32).reshape(peers, cap)
    got_blocks = lax.all_to_all(send_blocks, "orb", split_axis=0, concat_axis=0, tiled=True)
    got_vir, got_occ, got_size = (
        lax.all_to_all(send_vir, "orb", split_axis=0, concat_axis=0, tiled=True),
        lax.all_to_all(send_occ, "orb", split_axis=0, concat_axis=0, tiled=True),
        lax.all_to_all(send_size, "orb", split_axis=0, concat_axis=0, tiled=True),
    )
    partner = jnp.take(got_blocks.reshape(peers * cap, half_aux, nvd), target, axis=0).reshape(
        occ_dev, per_orb, half_aux, nvd
    )
    partner_vir = jnp.take(got_vir.reshape(peers * cap, nvd), target, axis=0).reshape(
        occ_dev, per_orb, nvd
    )
    partner_occ = jnp.take(got_occ.reshape(-1), target).reshape(occ_dev, per_orb)
    partner_size = jnp.take(got_size.reshape(-1), target).reshape(occ_dev, per_orb)
    half = nvd // lax.axis_size("aux")
    integrals = lax.psum_scatter(
        jnp.einsum("oqa,opqb->aopb", blocks, partner, preferred_element_type=jnp.float32),
        "aux",
        scatter_dimension=0,
        tiled=True,
    )
    row_start = lax.axis_index("aux") * half
    rows = row_start + jnp.arange(half, dtype=jnp.int32)
    cols = jnp.arange(nvd, dtype=jnp.int32).astype(jnp.float32)
    mask = (rows[:, None, None, None] < domain_size[None, :, None, None]) & (
        cols[None, None, None, :] < partner_size[None, :, :, None]
    )
    integrals = jnp.where(mask, integrals, jnp.zeros_like(integrals))
    vir_rows = lax.dynamic_slice_in_dim(vir_energy, row_start, half, 1)
    gap = (
        vir_rows.T[:, :, None, None]
        + partner_vir[None, :, :, :]
        - occ_energy[None, :, None, None]
        - partner_occ[None, :, :, None]
    )
    amp_rows = (-integrals / gap).astype(jnp.bfloat16)
    partial_energy = jnp.sum(integrals * amp_rows.astype(jnp.float32), axis=(0, 3))
    energy = lax.psum(partial_energy, "aux").reshape(pair_dev) / nvd
    density = jnp.einsum(
        "aopb,copb->oac",
        amp_rows,
        lax.all_gather(amp_rows, "aux", axis=0, tiled=True),
        preferred_element_type=jnp.float32,
    )
    return (energy, density)


def fits_line(mesh):
    return mesh.shape["orb"] == 8 and mesh.shape["aux"] == 2


TINY = pl.CostEstimate(flops=1, bytes_accessed=1, transcendentals=0)
PARAMS = pltpu.CompilerParams(vmem_limit_bytes=LIMIT)


def lists_kernel(cap, vir, occ, size, owner, slot, small, hit):
    n, (count, nvd) = hit.shape[0], vir.shape

    def column(row, m):
        eye = lax.broadcasted_iota(i32, (m, m), 0) == lax.broadcasted_iota(i32, (m, m), 1)
        return jnp.sum(jnp.where(eye, row, 0.0), axis=1, keepdims=True)

    down = lax.broadcasted_iota(i32, (n, n), 0).astype(f32)
    along = lax.broadcasted_iota(i32, (n, n), 1).astype(f32)
    owner_row = owner[...].astype(f32)
    owner_col = column(owner_row, n)
    before = (owner_col == owner_row) & (along < down)
    target = owner_col * cap + jnp.sum(jnp.where(before, 1.0, 0.0), axis=1, keepdims=True)
    found = target == along
    hit[...] = jnp.where(found, 1.0, 0.0)
    small[...] = jnp.zeros_like(small)
    small[:count, :nvd] = vir[...]
    lane = lax.broadcasted_iota(i32, (count, 128), 1)
    occ_col, size_col = column(occ[...], count), column(size[...].astype(f32), count)
    small[:count, nvd:] = jnp.where(lane == 0, occ_col, jnp.where(lane == 1, size_col, 0.0))
    small[count : count + 1, :n] = jnp.sum(jnp.where(found, down, 0.0), axis=0, keepdims=True)
    slot_col = column(slot[...].astype(f32), n)
    small[count : count + 1, 128 : 128 + n] = jnp.sum(
        jnp.where(found, slot_col, 0.0), axis=0, keepdims=True
    )


def lists(vir, occ, size, owner, slot, cap):
    count, nvd = vir.shape
    n = slot.shape[0]
    return pl.pallas_call(
        lambda *refs: lists_kernel(cap, *refs),
        out_shape=(
            jax.ShapeDtypeStruct((count + 8, nvd + 128), f32),
            jax.ShapeDtypeStruct((n, n), f32),
        ),
        in_specs=[VMEM] * 5,
        out_specs=(VMEM, VMEM),
        compiler_params=PARAMS,
        cost_estimate=TINY,
        name="lists",
    )(vir, occ.reshape(1, -1), size.reshape(1, -1), owner.reshape(1, -1), slot.reshape(1, -1))


ORDER, SLOT, SIZE_I, SIZE_J, HEAD = range(5)
MIDDLE, COLUMN = 8, 9


def pick(one, values):
    return lax.dot_general(
        one, values, (((0,), (0,)), ((), ())),
        precision=lax.Precision.HIGHEST, preferred_element_type=f32,
    )


def tables_kernel(cap, per_orb, meta, *refs):
    smalls, outs = refs[:8], refs[8:]
    count, nvd = smalls[0].shape[0] - 8, smalls[0].shape[1] - 128
    n = 8 * cap
    me, col0 = meta[0], meta[1]
    z, y = me // 2, me % 2
    lower = z < 2
    middle = jnp.where((z == 1) | (z == 2), 1, 0)
    places = [z, z ^ 1, jnp.where(lower, 2, 1), jnp.where(lower, 3, 0)]
    head = [(2 * p + y) * cap for p in places] + [(2 * p + 1 - y) * cap for p in places]
    lane = lax.broadcasted_iota(i32, (1, 128), 1)
    head_row = jnp.zeros((1, 128), i32)
    for k, value in enumerate(head + [middle, col0]):
        head_row = jnp.where(lane == k, value, head_row)
    orbitals = jnp.concatenate([x[:count, :] for x in smalls], axis=0)
    columns = jnp.where(col0 == 0, orbitals[:, : nvd // 2], orbitals[:, nvd // 2 : nvd])
    extra = orbitals[:, nvd:]

    def build(x, tbl, rows=None):
        order = smalls[x][count : count + 1, :n].astype(i32)
        slots = smalls[x][count : count + 1, 128 : 128 + n].astype(i32)
        tbl[...] = jnp.zeros_like(tbl)
        tbl[HEAD : HEAD + 1, :] = head_row
        tbl[SLOT : SLOT + 1, :n] = slots
        if rows is None:
            return
        tbl[ORDER : ORDER + 1, :n] = order
        pair = lax.broadcasted_iota(i32, (1, n), 1)
        owner = sum(jnp.where(pair >= k * cap, 1, 0) for k in range(1, 8))
        index = (owner ^ me) * count + slots
        theirs = jnp.where(lax.broadcasted_iota(i32, (8 * count, n), 0) == index, 1.0, 0.0)
        first = sum(jnp.where(order >= k * per_orb, 1, 0) for k in range(1, count))
        mine = jnp.where(lax.broadcasted_iota(i32, (count, n), 0) == first, 1.0, 0.0)
        own = smalls[x][:count, nvd:]
        rows[...] = pick(theirs, columns) - (pick(theirs, extra)[:, :1] + pick(mine, own)[:, :1])
        tbl[SIZE_I : SIZE_I + 1, :n] = pick(own, mine)[1:2, :].astype(i32)
        tbl[SIZE_J : SIZE_J + 1, :n] = pick(extra, theirs)[1:2, :].astype(i32) - col0

    build(0, outs[0], outs[1])
    build(2, outs[2], outs[3])
    build(1, outs[4])
    build(3, outs[5])


def tables_of(meta, smalls, cap, per_orb, half):
    table = jax.ShapeDtypeStruct((8, 128), i32)
    rows = jax.ShapeDtypeStruct((8 * cap, half), f32)
    return pl.pallas_call(
        lambda *refs: tables_kernel(cap, per_orb, *refs),
        out_shape=(table, rows, table, rows, table, table),
        in_specs=[SMEM] + [VMEM] * 8,
        out_specs=[VMEM] * 6,
        compiler_params=PARAMS,
        cost_estimate=TINY,
        name="tables",
    )(meta, *smalls)


def pack_kernel(jobs, tables, *refs):
    tbls, rest = refs[:tables], refs[tables:]
    outs = refs[-len(jobs) :]
    middle = tbls[0][HEAD, MIDDLE] == 1

    def gather(out, sources, tbl, call):
        base = tbl[HEAD, call]
        for q in range(out.shape[0]):
            for r in range(out.shape[1]):
                out[q, r] = sources[q][tbl[SLOT, base + r]]

    for out, (table, call, halves, only_middle) in zip(outs, jobs):
        sources, rest = rest[:halves], rest[halves:]
        if only_middle:
            pl.when(middle)(functools.partial(gather, out, sources, tbls[table], call))
        else:
            gather(out, sources, tbls[table], call)


def pack(tbls, jobs, cap, after=()):
    operands = [x for _, _, sources, _ in jobs for x in sources]
    kinds = [(table, call, len(sources), middle) for table, call, sources, middle in jobs]
    block = operands[0].shape[1:]
    return pl.pallas_call(
        lambda *refs: pack_kernel(kinds, len(tbls), *refs),
        out_shape=[jax.ShapeDtypeStruct((k[2], cap) + block, bf16) for k in kinds],
        in_specs=[SMEM] * len(tbls) + [VMEM] * len(operands) + [HBM] * len(after),
        out_specs=[VMEM] * len(jobs),
        compiler_params=PARAMS,
        cost_estimate=TINY,
        name="pack",
    )(*tbls, *operands, *after)


def turn_kernel(*refs):
    half = len(refs) // 2
    for x, out in zip(refs[:half], refs[half:]):
        for r in range(x.shape[0]):
            out[r] = x[r].T


def turn(arrays):
    count, rows, cols = arrays[0].shape
    step = 4 if count % 4 == 0 else 1
    n = len(arrays)
    return pl.pallas_call(
        turn_kernel,
        out_shape=[jax.ShapeDtypeStruct((count, cols, rows), bf16)] * n,
        grid=(count // step,),
        in_specs=[pl.BlockSpec((step, rows, cols), lambda i: (i, 0, 0))] * n,
        out_specs=[pl.BlockSpec((step, cols, rows), lambda i: (i, 0, 0))] * n,
        compiler_params=PARAMS,
        cost_estimate=TINY,
        name="turn",
    )(*arrays)


def amplitudes_kernel(mode, call, per_orb, groups, tbl, rows, vcol, *refs):
    client = mode == "client"
    if client:
        tout = refs[-1]
        left, rest = refs[:4], refs[4:]
    else:
        tout, eout = refs[-2:]
        left, rest = refs[:2], refs[2:]
    places = []
    for arrays in groups:
        if arrays == 1:
            places.append([rest[0].at[0], rest[0].at[1]])
        elif len(rest[0].shape) == 4:
            places.append([rest[0].at[0], rest[1].at[0]])
        else:
            places.append(rest[:2])
        rest = rest[arrays:]
    cap = rows.shape[0] // 8
    nvd, half = vcol.shape[1:]
    base = pl.multiple_of(tbl[HEAD, call], cap)
    middle = tbl[HEAD, MIDDLE] == 1
    row8 = rows[pl.ds(base, cap), :]

    def gap(r, i):
        return vcol[i] + row8[r : r + 1, :]

    def make(r):
        p = tbl[ORDER, base + r]
        i = lax.div(p, per_orb)
        slot = r if mode == "asked" else tbl[SLOT, base + r]
        b0, b1 = [x[slot] for x in places[0]]
        if len(places) == 2:
            b0, b1 = [jnp.where(middle, b, x[slot]) for b, x in zip((b0, b1), places[1])]

        def product(x0, x1):
            return jnp.dot(x0[i], b0, preferred_element_type=f32) + jnp.dot(
                x1[i], b1, preferred_element_type=f32
            )

        if client:
            here, there = product(left[0], left[1]), product(left[3], left[2])
            first = tbl[HEAD, COLUMN] == 0
            k = jnp.concatenate(
                [jnp.where(first, here, there), jnp.where(first, there, here)], axis=0
            )
        else:
            k = product(left[0], left[1])
        live_a = lax.broadcasted_iota(i32, (nvd, half), 0)
        live_b = lax.broadcasted_iota(i32, (nvd, half), 1)
        live = (live_a < tbl[SIZE_I, base + r]) & (live_b < tbl[SIZE_J, base + r])
        k = jnp.where(live, k, 0.0)
        t = (-k / gap(r, i)).astype(bf16)
        if client:
            tout[r] = t
            return None
        tout[p] = t
        return jnp.sum(k * t.astype(f32), axis=0, keepdims=True)

    def take(r):
        p = tbl[ORDER, base + r]
        ready = rest[0][r]
        tout[p] = ready
        t = ready.astype(f32)
        return -jnp.sum(t * t * gap(r, lax.div(p, per_orb)), axis=0, keepdims=True)

    def each(step):
        parts = [step(r) for r in range(cap)]
        if not client:
            eout[pl.ds(base, cap), :] = jnp.concatenate(parts, axis=0)

    if mode == "served":
        pl.when(middle)(lambda: each(make))
        pl.when(jnp.logical_not(middle))(lambda: each(take))
    elif client:
        pl.when(middle)(lambda: each(make))
    else:
        each(make)


def amplitudes(mode, call, per_orb, tables, left, groups, cap, held=(), after=(), ready=()):
    tbl, rows, vcol = tables
    occ, nvd, half = vcol.shape
    client = mode == "client"
    sources = [x for group in groups for x in group]
    blocks = (rows, vcol, *left, *sources, *ready)
    operands = (tbl, *blocks, *after)
    aliases = {len(operands) + k: k for k in range(len(held))}
    if client:
        out_shape = jax.ShapeDtypeStruct((cap, nvd, half), bf16)
        out_specs = VMEM
    else:
        out_shape = (
            jax.ShapeDtypeStruct((occ * per_orb, nvd, half), bf16),
            jax.ShapeDtypeStruct((occ * per_orb, half), f32),
        )
        out_specs = (VMEM, VMEM)
    return pl.pallas_call(
        lambda *refs: amplitudes_kernel(mode, call, per_orb, [len(g) for g in groups], *refs),
        out_shape=out_shape,
        in_specs=[SMEM] + [VMEM] * len(blocks) + [HBM] * len(after) + [VMEM] * len(held),
        out_specs=out_specs,
        input_output_aliases=aliases,
        compiler_params=PARAMS,
        cost_estimate=TINY,
        name="amplitudes",
    )(*operands, *held)


def density_kernel(start, t, *refs):
    d = refs[-1]
    count, half = d.shape[:2]
    per_orb = t.shape[0] // count
    first = pl.multiple_of(start[0], half)
    for o in range(count):
        own = range(o * per_orb, (o + 1) * per_orb)
        left = jnp.concatenate([t[k, pl.ds(first, half), :] for k in own], axis=1)
        right = jnp.concatenate([t[k] for k in own], axis=1)
        rows = lax.dot_general(left, right, (((1,), (1,)), ((), ())), preferred_element_type=f32)
        d[o] = rows if len(refs) == 1 else rows + refs[0][o]


def density_rows(t_all, start, per_orb, half, *away):
    npair, nvd, width = t_all.shape
    occ = npair // per_orb
    step = 4 if occ % 4 == 0 else 1
    return pl.pallas_call(
        density_kernel,
        out_shape=jax.ShapeDtypeStruct((occ, half, nvd), f32),
        grid_spec=pltpu.PrefetchScalarGridSpec(
            num_scalar_prefetch=1,
            grid=(occ // step,),
            in_specs=[pl.BlockSpec((step * per_orb, nvd, width), lambda i, s: (i, 0, 0))]
            + [pl.BlockSpec((step, half, nvd), lambda i, s: (i, 0, 0))] * len(away),
            out_specs=pl.BlockSpec((step, half, nvd), lambda i, s: (i, 0, 0)),
        ),
        compiler_params=pltpu.CompilerParams(vmem_limit_bytes=LIMIT),
        cost_estimate=TINY,
        name="density_rows",
    )(start.reshape(1), t_all, *away)


def line_plan(blocks, vir_energy, occ_energy, domain_size, partner_owner, partner_slot):
    occ, qa, nvd = blocks.shape
    pair_dev = partner_slot.shape[0]
    per_orb = pair_dev // occ
    peers = 8
    cap = pair_dev // peers
    half = nvd // 2
    me, core = lax.axis_index("orb"), lax.axis_index("aux")
    col0 = core * half

    def pp(x, perm):
        return lax.ppermute(x, "orb", perm)

    def swap_core(x):
        return lax.ppermute(x, "aux", [(0, 1), (1, 0)])

    def flip(bits):
        return [(o, o ^ bits) for o in range(peers)]

    cross = [(2, 4), (3, 5), (4, 2), (5, 3)]
    outward = [(2, 0), (3, 1), (4, 6), (5, 7)]
    diagonal = [(2, 1), (3, 0), (4, 7), (5, 6)]
    y_middle = [(2, 3), (3, 2), (4, 5), (5, 4)]

    small, hit = lists(vir_energy, occ_energy, domain_size, partner_owner, partner_slot, cap)
    smalls = [small] + [pp(small, flip(bits)) for bits in range(1, peers)]

    other = swap_core(blocks)
    own = [lax.dynamic_slice_in_dim(x, col0, half, 2) for x in (blocks, other)]
    sent, smalls = lax.optimization_barrier((own[0], smalls))
    mid = [pp(x, cross) for x in (sent, own[1])]
    near = [pp(x, flip(2)) for x in (sent, own[1])]
    tbl, rows, client_tbl, client_rows, beside_list, relay_list = tables_of(
        jnp.stack([me, col0]), smalls, cap, per_orb, half
    )
    lists_of = [beside_list, relay_list]

    def spread(vir):
        return jnp.broadcast_to(vir[:, :, None], (occ, nvd, half))

    tables = (tbl, rows, spread(vir_energy))
    client = (client_tbl, client_rows, spread(smalls[2][:occ, :nvd]))

    def own_pairs(k, mode, groups, held=(), after=(), ready=()):
        return amplitudes(mode, k, per_orb, tables, left, groups, cap, held, after, ready)

    (packed,) = pack(lists_of, [(0, 0, own, False)], cap)
    beside = pp(packed, flip(1))
    left = turn([blocks, other])
    held = own_pairs(0, "slots", [own], after=(packed,))
    first, held = lax.optimization_barrier((near[0], held))
    far = [pp(first, cross)]
    across = [swap_core(first)]
    (packed,) = pack(lists_of, [(0, 1, [first], False)], cap, after=(held[1], mid[0]))
    beside_near = [pp(packed, flip(1))]
    held = own_pairs(4, "asked", [[beside]], held, (packed, beside_near[0]))
    second, held = lax.optimization_barrier((near[1], held))
    far.append(pp(second, cross))
    across.append(swap_core(second))
    near = [first, second]
    packed = pack(lists_of, [(1, 2, mid, True), (0, 2, mid, True)], cap, after=(held[1],))
    third_diagonal, third = pp(packed[0], diagonal), pp(packed[1], y_middle)
    (packed,) = pack(lists_of, [(0, 1, [second], False)], cap, after=(packed[0],))
    beside_near.append(pp(packed, flip(1)))
    client_left = turn(near + across)
    gone = amplitudes("client", 2, per_orb, client, client_left, [mid], cap, after=(packed,))
    ready_2 = pp(gone, outward)
    held = own_pairs(1, "slots", [near], held, (gone, third_diagonal))
    held = own_pairs(5, "asked", [beside_near], held)
    jobs = [(1, 3, far[:1], True), (0, 3, far[:1], True)]
    packed = pack(lists_of, jobs, cap, after=(held[1],))
    fourth_diagonal, fourth = [pp(packed[0], diagonal)], [pp(packed[1], y_middle)]
    held = own_pairs(2, "served", [mid], held, (packed[0],), (ready_2,))
    (packed,) = pack(lists_of, [(1, 3, far[1:], True)], cap, after=(held[1],))
    fourth_diagonal.append(pp(packed, diagonal))
    gone = amplitudes("client", 3, per_orb, client, client_left, [far], cap, after=(packed,))
    ready_3 = pp(gone, outward)
    (packed,) = pack(
        lists_of, [(0, 3, far[1:], True)], cap, after=(gone,)
    )
    fourth.append(pp(packed, y_middle))
    held = own_pairs(
        6, "asked", [[third], [third_diagonal]], held, (packed, fourth[0], *fourth_diagonal)
    )
    held = own_pairs(3, "served", [far], held, ready=(ready_3,))
    t_all, e_all = own_pairs(7, "asked", [fourth, fourth_diagonal], held)

    away = swap_core(density_rows(t_all, (1 - core) * half, per_orb, half))
    density = density_rows(t_all, core * half, per_orb, half, away)

    energy = jnp.sum(hit * jnp.sum(e_all, axis=1)[None, :], axis=1)
    energy = (energy + swap_core(energy)) / nvd
    return (energy, density)


def solution(mesh):
    in_specs = (
        P(("mol", "orb"), "aux", None),
        P(("mol", "orb"), None),
        P(("mol", "orb")),
        P(("mol", "orb")),
        P(("mol", "orb"), None),
        P(("mol", "orb")),
    )
    out_specs = (P(("mol", "orb")), P(("mol", "orb"), "aux", None))
    return jax.shard_map(
        line_plan if fits_line(mesh) else by_requests, mesh=mesh, in_specs=in_specs, out_specs=out_specs, check_vma=False
    )
```

```python
import functools

import jax
import jax.numpy as jnp
from jax import lax
from jax.experimental import pallas as pl
from jax.experimental.pallas import tpu as pltpu
from jax.sharding import PartitionSpec as P

f32, bf16, i32 = jnp.float32, jnp.bfloat16, jnp.int32
HBM = pl.BlockSpec(memory_space=pltpu.HBM)
SMEM = pl.BlockSpec(memory_space=pltpu.SMEM)
VMEM = pl.BlockSpec(memory_space=pltpu.VMEM)
LIMIT = 12 * 1024 * 1024


def slot_ranks(owner):
    count = owner.shape[0]
    order = jnp.arange(count, dtype=jnp.int32)
    same = (owner[:, None] == owner[None, :]) & (order[None, :] < order[:, None])
    return jnp.sum(same.astype(jnp.int32), axis=1)


def by_requests(blocks, vir_energy, occ_energy, domain_size, partner_owner, partner_slot):
    occ_dev, half_aux, nvd = blocks.shape
    pair_dev = partner_slot.shape[0]
    per_orb = pair_dev // occ_dev
    peers = lax.axis_size("orb")
    cap = max(2, (pair_dev + peers - 1) // peers)
    owner = partner_owner[:, 0]
    ranks = slot_ranks(owner)
    target = owner * cap + ranks
    wanted = (target[:, None] == jnp.arange(peers * cap, dtype=jnp.int32)[None, :]).astype(
        jnp.int32
    )
    requests = jnp.sum(wanted * partner_slot[:, None], axis=0).reshape(peers, cap)
    incoming = lax.all_to_all(requests, "orb", split_axis=0, concat_axis=0, tiled=True)
    flat_in = incoming.reshape(-1)
    send_blocks = jnp.take(blocks, flat_in, axis=0).reshape(peers, cap, half_aux, nvd)
    send_vir = jnp.take(vir_energy, flat_in, axis=0).reshape(peers, cap, nvd)
    send_occ = jnp.take(occ_energy, flat_in).reshape(peers, cap)
    send_size = jnp.take(domain_size, flat_in).astype(jnp.float32).reshape(peers, cap)
    got_blocks = lax.all_to_all(send_blocks, "orb", split_axis=0, concat_axis=0, tiled=True)
    got_vir, got_occ, got_size = (
        lax.all_to_all(send_vir, "orb", split_axis=0, concat_axis=0, tiled=True),
        lax.all_to_all(send_occ, "orb", split_axis=0, concat_axis=0, tiled=True),
        lax.all_to_all(send_size, "orb", split_axis=0, concat_axis=0, tiled=True),
    )
    partner = jnp.take(got_blocks.reshape(peers * cap, half_aux, nvd), target, axis=0).reshape(
        occ_dev, per_orb, half_aux, nvd
    )
    partner_vir = jnp.take(got_vir.reshape(peers * cap, nvd), target, axis=0).reshape(
        occ_dev, per_orb, nvd
    )
    partner_occ = jnp.take(got_occ.reshape(-1), target).reshape(occ_dev, per_orb)
    partner_size = jnp.take(got_size.reshape(-1), target).reshape(occ_dev, per_orb)
    half = nvd // lax.axis_size("aux")
    integrals = lax.psum_scatter(
        jnp.einsum("oqa,opqb->aopb", blocks, partner, preferred_element_type=jnp.float32),
        "aux",
        scatter_dimension=0,
        tiled=True,
    )
    row_start = lax.axis_index("aux") * half
    rows = row_start + jnp.arange(half, dtype=jnp.int32)
    cols = jnp.arange(nvd, dtype=jnp.int32).astype(jnp.float32)
    mask = (rows[:, None, None, None] < domain_size[None, :, None, None]) & (
        cols[None, None, None, :] < partner_size[None, :, :, None]
    )
    integrals = jnp.where(mask, integrals, jnp.zeros_like(integrals))
    vir_rows = lax.dynamic_slice_in_dim(vir_energy, row_start, half, 1)
    gap = (
        vir_rows.T[:, :, None, None]
        + partner_vir[None, :, :, :]
        - occ_energy[None, :, None, None]
        - partner_occ[None, :, :, None]
    )
    amp_rows = (-integrals / gap).astype(jnp.bfloat16)
    partial_energy = jnp.sum(integrals * amp_rows.astype(jnp.float32), axis=(0, 3))
    energy = lax.psum(partial_energy, "aux").reshape(pair_dev) / nvd
    density = jnp.einsum(
        "aopb,copb->oac",
        amp_rows,
        lax.all_gather(amp_rows, "aux", axis=0, tiled=True),
        preferred_element_type=jnp.float32,
    )
    return (energy, density)


def fits_line(mesh):
    return mesh.shape["orb"] == 8 and mesh.shape["aux"] == 2


TINY = pl.CostEstimate(flops=1, bytes_accessed=1, transcendentals=0)
PARAMS = pltpu.CompilerParams(vmem_limit_bytes=LIMIT)
LIGHT = pltpu.CompilerParams(vmem_limit_bytes=LIMIT // 4)


def lists_kernel(cap, vir, occ, size, owner, slot, small, hit):
    n, (count, nvd) = hit.shape[0], vir.shape

    def column(row, m):
        eye = lax.broadcasted_iota(i32, (m, m), 0) == lax.broadcasted_iota(i32, (m, m), 1)
        return jnp.sum(jnp.where(eye, row, 0.0), axis=1, keepdims=True)

    down = lax.broadcasted_iota(i32, (n, n), 0).astype(f32)
    along = lax.broadcasted_iota(i32, (n, n), 1).astype(f32)
    owner_row = owner[...].astype(f32)
    owner_col = column(owner_row, n)
    before = (owner_col == owner_row) & (along < down)
    target = owner_col * cap + jnp.sum(jnp.where(before, 1.0, 0.0), axis=1, keepdims=True)
    found = target == along
    hit[...] = jnp.where(found, 1.0, 0.0)
    small[...] = jnp.zeros_like(small)
    small[:count, :nvd] = vir[...]
    lane = lax.broadcasted_iota(i32, (count, 128), 1)
    occ_col, size_col = column(occ[...], count), column(size[...].astype(f32), count)
    small[:count, nvd:] = jnp.where(lane == 0, occ_col, jnp.where(lane == 1, size_col, 0.0))
    small[count : count + 1, :n] = jnp.sum(jnp.where(found, down, 0.0), axis=0, keepdims=True)
    slot_col = column(slot[...].astype(f32), n)
    small[count : count + 1, 128 : 128 + n] = jnp.sum(
        jnp.where(found, slot_col, 0.0), axis=0, keepdims=True
    )


def lists(vir, occ, size, owner, slot, cap):
    count, nvd = vir.shape
    n = slot.shape[0]
    return pl.pallas_call(
        lambda *refs: lists_kernel(cap, *refs),
        out_shape=(
            jax.ShapeDtypeStruct((count + 8, nvd + 128), f32),
            jax.ShapeDtypeStruct((n, n), f32),
        ),
        in_specs=[VMEM] * 5,
        out_specs=(VMEM, VMEM),
        compiler_params=PARAMS,
        cost_estimate=TINY,
        name="lists",
    )(vir, occ.reshape(1, -1), size.reshape(1, -1), owner.reshape(1, -1), slot.reshape(1, -1))


ORDER, SLOT, SIZE_I, SIZE_J, HEAD = range(5)
MIDDLE, COLUMN = 8, 9


def pick(one, values):
    return lax.dot_general(
        one, values, (((0,), (0,)), ((), ())),
        precision=lax.Precision.HIGHEST, preferred_element_type=f32,
    )


def tables_kernel(cap, per_orb, meta, *refs):
    smalls, outs = refs[:8], refs[8:]
    count, nvd = smalls[0].shape[0] - 8, smalls[0].shape[1] - 128
    n = 8 * cap
    me, col0 = meta[0], meta[1]
    z, y = me // 2, me % 2
    lower = z < 2
    middle = jnp.where((z == 1) | (z == 2), 1, 0)
    places = [z, z ^ 1, jnp.where(lower, 2, 1), jnp.where(lower, 3, 0)]
    head = [(2 * p + y) * cap for p in places] + [(2 * p + 1 - y) * cap for p in places]
    lane = lax.broadcasted_iota(i32, (1, 128), 1)
    head_row = jnp.zeros((1, 128), i32)
    for k, value in enumerate(head + [middle, col0]):
        head_row = jnp.where(lane == k, value, head_row)
    orbitals = jnp.concatenate([x[:count, :] for x in smalls], axis=0)
    columns = jnp.where(col0 == 0, orbitals[:, : nvd // 2], orbitals[:, nvd // 2 : nvd])
    extra = orbitals[:, nvd:]

    def build(x, tbl, rows=None):
        order = smalls[x][count : count + 1, :n].astype(i32)
        slots = smalls[x][count : count + 1, 128 : 128 + n].astype(i32)
        tbl[...] = jnp.zeros_like(tbl)
        tbl[HEAD : HEAD + 1, :] = head_row
        tbl[SLOT : SLOT + 1, :n] = slots
        if rows is None:
            return
        tbl[ORDER : ORDER + 1, :n] = order
        pair = lax.broadcasted_iota(i32, (1, n), 1)
        owner = sum(jnp.where(pair >= k * cap, 1, 0) for k in range(1, 8))
        index = (owner ^ me) * count + slots
        theirs = jnp.where(lax.broadcasted_iota(i32, (8 * count, n), 0) == index, 1.0, 0.0)
        first = sum(jnp.where(order >= k * per_orb, 1, 0) for k in range(1, count))
        mine = jnp.where(lax.broadcasted_iota(i32, (count, n), 0) == first, 1.0, 0.0)
        own = smalls[x][:count, nvd:]
        rows[...] = pick(theirs, columns) - (pick(theirs, extra)[:, :1] + pick(mine, own)[:, :1])
        tbl[SIZE_I : SIZE_I + 1, :n] = pick(own, mine)[1:2, :].astype(i32)
        tbl[SIZE_J : SIZE_J + 1, :n] = pick(extra, theirs)[1:2, :].astype(i32) - col0

    build(0, outs[0], outs[1])
    build(2, outs[2], outs[3])
    build(1, outs[4])
    build(3, outs[5])


def tables_of(meta, smalls, cap, per_orb, half):
    table = jax.ShapeDtypeStruct((8, 128), i32)
    rows = jax.ShapeDtypeStruct((8 * cap, half), f32)
    return pl.pallas_call(
        lambda *refs: tables_kernel(cap, per_orb, *refs),
        out_shape=(table, rows, table, rows, table, table),
        in_specs=[SMEM] + [VMEM] * 8,
        out_specs=[VMEM] * 6,
        compiler_params=LIGHT,
        cost_estimate=TINY,
        name="tables",
    )(meta, *smalls)


def pack_kernel(jobs, tables, *refs):
    tbls, rest = refs[:tables], refs[tables:]
    outs = refs[-len(jobs) :]
    middle = tbls[0][HEAD, MIDDLE] == 1

    def gather(out, sources, tbl, call):
        base = tbl[HEAD, call]
        for q in range(out.shape[0]):
            for r in range(out.shape[1]):
                out[q, r] = sources[q][tbl[SLOT, base + r]]

    for out, (table, call, halves, only_middle) in zip(outs, jobs):
        sources, rest = rest[:halves], rest[halves:]
        if only_middle:
            pl.when(middle)(functools.partial(gather, out, sources, tbls[table], call))
        else:
            gather(out, sources, tbls[table], call)


def pack(tbls, jobs, cap, after=()):
    operands = [x for _, _, sources, _ in jobs for x in sources]
    kinds = [(table, call, len(sources), middle) for table, call, sources, middle in jobs]
    block = operands[0].shape[1:]
    return pl.pallas_call(
        lambda *refs: pack_kernel(kinds, len(tbls), *refs),
        out_shape=[jax.ShapeDtypeStruct((k[2], cap) + block, bf16) for k in kinds],
        in_specs=[SMEM] * len(tbls) + [VMEM] * len(operands) + [HBM] * len(after),
        out_specs=[VMEM] * len(jobs),
        compiler_params=LIGHT,
        cost_estimate=TINY,
        name="pack",
    )(*tbls, *operands, *after)


def turn_kernel(*refs):
    half = len(refs) // 2
    for x, out in zip(refs[:half], refs[half:]):
        for r in range(x.shape[0]):
            out[r] = x[r].T


def turn(arrays):
    count, rows, cols = arrays[0].shape
    step = 4 if count % 4 == 0 else 1
    n = len(arrays)
    return pl.pallas_call(
        turn_kernel,
        out_shape=[jax.ShapeDtypeStruct((count, cols, rows), bf16)] * n,
        grid=(count // step,),
        in_specs=[pl.BlockSpec((step, rows, cols), lambda i: (i, 0, 0))] * n,
        out_specs=[pl.BlockSpec((step, cols, rows), lambda i: (i, 0, 0))] * n,
        compiler_params=PARAMS,
        cost_estimate=TINY,
        name="turn",
    )(*arrays)


def amplitudes_kernel(mode, call, per_orb, groups, tbl, rows, vcol, *refs):
    client = mode == "client"
    if client:
        tout = refs[-1]
        left, rest = refs[:4], refs[4:]
    else:
        tout, eout = refs[-2:]
        left, rest = refs[:2], refs[2:]
    places = []
    for arrays in groups:
        if arrays == 1:
            places.append([rest[0].at[0], rest[0].at[1]])
        elif len(rest[0].shape) == 4:
            places.append([rest[0].at[0], rest[1].at[0]])
        else:
            places.append(rest[:2])
        rest = rest[arrays:]
    cap = rows.shape[0] // 8
    nvd, half = vcol.shape[1:]
    base = pl.multiple_of(tbl[HEAD, call], cap)
    middle = tbl[HEAD, MIDDLE] == 1
    row8 = rows[pl.ds(base, cap), :]

    def gap(r, i):
        return vcol[i] + row8[r : r + 1, :]

    def make(r):
        p = tbl[ORDER, base + r]
        i = lax.div(p, per_orb)
        slot = r if mode == "asked" else tbl[SLOT, base + r]
        b0, b1 = [x[slot] for x in places[0]]
        if len(places) == 2:
            b0, b1 = [jnp.where(middle, b, x[slot]) for b, x in zip((b0, b1), places[1])]

        def product(x0, x1):
            return jnp.dot(x0[i], b0, preferred_element_type=f32) + jnp.dot(
                x1[i], b1, preferred_element_type=f32
            )

        if client:
            here, there = product(left[0], left[1]), product(left[3], left[2])
            first = tbl[HEAD, COLUMN] == 0
            k = jnp.concatenate(
                [jnp.where(first, here, there), jnp.where(first, there, here)], axis=0
            )
        else:
            k = product(left[0], left[1])
        live_a = lax.broadcasted_iota(i32, (nvd, half), 0)
        live_b = lax.broadcasted_iota(i32, (nvd, half), 1)
        live = (live_a < tbl[SIZE_I, base + r]) & (live_b < tbl[SIZE_J, base + r])
        k = jnp.where(live, k, 0.0)
        t = (-k / gap(r, i)).astype(bf16)
        if client:
            tout[r] = t
            return None
        tout[p] = t
        return jnp.sum(k * t.astype(f32), axis=0, keepdims=True)

    def take(r):
        p = tbl[ORDER, base + r]
        ready = rest[0][r]
        tout[p] = ready
        t = ready.astype(f32)
        return -jnp.sum(t * t * gap(r, lax.div(p, per_orb)), axis=0, keepdims=True)

    def each(step):
        parts = [step(r) for r in range(cap)]
        if not client:
            eout[pl.ds(base, cap), :] = jnp.concatenate(parts, axis=0)

    if mode == "served":
        pl.when(middle)(lambda: each(make))
        pl.when(jnp.logical_not(middle))(lambda: each(take))
    elif client:
        pl.when(middle)(lambda: each(make))
    else:
        each(make)


def amplitudes(mode, call, per_orb, tables, left, groups, cap, held=(), after=(), ready=()):
    tbl, rows, vcol = tables
    occ, nvd, half = vcol.shape
    client = mode == "client"
    sources = [x for group in groups for x in group]
    blocks = (rows, vcol, *left, *sources, *ready)
    operands = (tbl, *blocks, *after)
    aliases = {len(operands) + k: k for k in range(len(held))}
    if client:
        out_shape = jax.ShapeDtypeStruct((cap, nvd, half), bf16)
        out_specs = VMEM
    else:
        out_shape = (
            jax.ShapeDtypeStruct((occ * per_orb, nvd, half), bf16),
            jax.ShapeDtypeStruct((occ * per_orb, half), f32),
        )
        out_specs = (VMEM, VMEM)
    return pl.pallas_call(
        lambda *refs: amplitudes_kernel(mode, call, per_orb, [len(g) for g in groups], *refs),
        out_shape=out_shape,
        in_specs=[SMEM] + [VMEM] * len(blocks) + [HBM] * len(after) + [VMEM] * len(held),
        out_specs=out_specs,
        input_output_aliases=aliases,
        compiler_params=LIGHT,
        cost_estimate=TINY,
        name="amplitudes",
    )(*operands, *held)


def density_kernel(start, t, d):
    count, half = d.shape[:2]
    per_orb = t.shape[0] // count
    first = pl.multiple_of(start[0], half)
    for o in range(count):
        own = range(o * per_orb, (o + 1) * per_orb)
        left = jnp.concatenate([t[k, pl.ds(first, half), :] for k in own], axis=1)
        right = jnp.concatenate([t[k] for k in own], axis=1)
        d[o] = lax.dot_general(left, right, (((1,), (1,)), ((), ())), preferred_element_type=f32)


def density_rows(t_all, start, per_orb, half):
    npair, nvd, width = t_all.shape
    occ = npair // per_orb
    step = 4 if occ % 4 == 0 else 1
    return pl.pallas_call(
        density_kernel,
        out_shape=jax.ShapeDtypeStruct((occ, half, nvd), f32),
        grid_spec=pltpu.PrefetchScalarGridSpec(
            num_scalar_prefetch=1,
            grid=(occ // step,),
            in_specs=[pl.BlockSpec((step * per_orb, nvd, width), lambda i, s: (i, 0, 0))],
            out_specs=pl.BlockSpec((step, half, nvd), lambda i, s: (i, 0, 0)),
        ),
        compiler_params=pltpu.CompilerParams(vmem_limit_bytes=LIMIT),
        cost_estimate=TINY,
        name="density_rows",
    )(start.reshape(1), t_all)


def line_plan(blocks, vir_energy, occ_energy, domain_size, partner_owner, partner_slot):
    occ, qa, nvd = blocks.shape
    pair_dev = partner_slot.shape[0]
    per_orb = pair_dev // occ
    peers = 8
    cap = pair_dev // peers
    half = nvd // 2
    me, core = lax.axis_index("orb"), lax.axis_index("aux")
    col0 = core * half

    def pp(x, perm):
        return lax.ppermute(x, "orb", perm)

    def swap_core(x):
        return lax.ppermute(x, "aux", [(0, 1), (1, 0)])

    def flip(bits):
        return [(o, o ^ bits) for o in range(peers)]

    cross = [(2, 4), (3, 5), (4, 2), (5, 3)]
    outward = [(2, 0), (3, 1), (4, 6), (5, 7)]
    diagonal = [(2, 1), (3, 0), (4, 7), (5, 6)]
    y_middle = [(2, 3), (3, 2), (4, 5), (5, 4)]

    small, hit = lists(vir_energy, occ_energy, domain_size, partner_owner, partner_slot, cap)
    smalls = [small] + [pp(small, flip(bits)) for bits in range(1, peers)]

    other = swap_core(blocks)
    own = [lax.dynamic_slice_in_dim(x, col0, half, 2) for x in (blocks, other)]
    sent, smalls = lax.optimization_barrier((own[0], smalls))
    mid = [pp(x, cross) for x in (sent, own[1])]
    near = [pp(x, flip(2)) for x in (sent, own[1])]
    tbl, rows, client_tbl, client_rows, beside_list, relay_list = tables_of(
        jnp.stack([me, col0]), smalls, cap, per_orb, half
    )
    lists_of = [beside_list, relay_list]

    def spread(vir):
        return jnp.broadcast_to(vir[:, :, None], (occ, nvd, half))

    tables = (tbl, rows, spread(vir_energy))
    client = (client_tbl, client_rows, spread(smalls[2][:occ, :nvd]))

    def own_pairs(k, mode, groups, held=(), after=(), ready=()):
        return amplitudes(mode, k, per_orb, tables, left, groups, cap, held, after, ready)

    (packed,) = pack(lists_of, [(0, 0, own, False)], cap)
    beside = pp(packed, flip(1))
    left = turn([blocks, other])
    held = own_pairs(0, "slots", [own], after=(packed,))
    first, held = lax.optimization_barrier((near[0], held))
    far = [pp(first, cross)]
    across = [swap_core(first)]
    (packed,) = pack(lists_of, [(0, 1, [first], False)], cap, after=(held[1], mid[0]))
    beside_near = [pp(packed, flip(1))]
    held = own_pairs(4, "asked", [[beside]], held, (packed, beside_near[0]))
    second, held = lax.optimization_barrier((near[1], held))
    far.append(pp(second, cross))
    across.append(swap_core(second))
    near = [first, second]
    packed = pack(lists_of, [(1, 2, mid, True), (0, 2, mid, True)], cap, after=(held[1],))
    third_diagonal, third = pp(packed[0], diagonal), pp(packed[1], y_middle)
    (packed,) = pack(lists_of, [(0, 1, [second], False)], cap, after=(packed[0],))
    beside_near.append(pp(packed, flip(1)))
    client_left = turn(near + across)
    gone = amplitudes("client", 2, per_orb, client, client_left, [mid], cap, after=(packed,))
    ready_2 = pp(gone, outward)
    held = own_pairs(1, "slots", [near], held, (gone, third_diagonal))
    jobs = [(1, 3, far[:1], True), (0, 3, far[:1], True)]
    packed = pack(lists_of, jobs, cap, after=(held[1],))
    fourth_diagonal, fourth = [pp(packed[0], diagonal)], [pp(packed[1], y_middle)]
    held = own_pairs(2, "served", [mid], held, (packed[0],), (ready_2,))
    held = own_pairs(5, "asked", [beside_near], held)
    (packed,) = pack(lists_of, [(1, 3, far[1:], True)], cap, after=(held[1],))
    fourth_diagonal.append(pp(packed, diagonal))
    gone = amplitudes("client", 3, per_orb, client, client_left, [far], cap, after=(packed,))
    ready_3 = pp(gone, outward)
    (packed,) = pack(
        lists_of, [(0, 3, far[1:], True)], cap, after=(gone,)
    )
    fourth.append(pp(packed, y_middle))
    held = own_pairs(
        6, "asked", [[third], [third_diagonal]], held, (packed, fourth[0], *fourth_diagonal)
    )
    held = own_pairs(3, "served", [far], held, ready=(ready_3,))
    t_all, e_all = own_pairs(7, "asked", [fourth, fourth_diagonal], held)

    away = swap_core(density_rows(t_all, (1 - core) * half, per_orb, half))
    density = density_rows(t_all, core * half, per_orb, half) + away

    energy = jnp.sum(hit * jnp.sum(e_all, axis=1)[None, :], axis=1)
    energy = (energy + swap_core(energy)) / nvd
    return (energy, density)


def solution(mesh):
    in_specs = (
        P(("mol", "orb"), "aux", None),
        P(("mol", "orb"), None),
        P(("mol", "orb")),
        P(("mol", "orb")),
        P(("mol", "orb"), None),
        P(("mol", "orb")),
    )
    out_specs = (P(("mol", "orb")), P(("mol", "orb"), "aux", None))
    return jax.shard_map(
        line_plan if fits_line(mesh) else by_requests, mesh=mesh, in_specs=in_specs, out_specs=out_specs, check_vma=False
    )
```

```python
import functools

import jax
import jax.numpy as jnp
from jax import lax
from jax.experimental import pallas as pl
from jax.experimental.pallas import tpu as pltpu
from jax.sharding import PartitionSpec as P

f32, bf16, i32 = jnp.float32, jnp.bfloat16, jnp.int32
HBM = pl.BlockSpec(memory_space=pltpu.HBM)
SMEM = pl.BlockSpec(memory_space=pltpu.SMEM)
VMEM = pl.BlockSpec(memory_space=pltpu.VMEM)
LIMIT = 12 * 1024 * 1024


def slot_ranks(owner):
    count = owner.shape[0]
    order = jnp.arange(count, dtype=jnp.int32)
    same = (owner[:, None] == owner[None, :]) & (order[None, :] < order[:, None])
    return jnp.sum(same.astype(jnp.int32), axis=1)


def by_requests(blocks, vir_energy, occ_energy, domain_size, partner_owner, partner_slot):
    occ_dev, half_aux, nvd = blocks.shape
    pair_dev = partner_slot.shape[0]
    per_orb = pair_dev // occ_dev
    peers = lax.axis_size("orb")
    cap = max(2, (pair_dev + peers - 1) // peers)
    owner = partner_owner[:, 0]
    ranks = slot_ranks(owner)
    target = owner * cap + ranks
    wanted = (target[:, None] == jnp.arange(peers * cap, dtype=jnp.int32)[None, :]).astype(
        jnp.int32
    )
    requests = jnp.sum(wanted * partner_slot[:, None], axis=0).reshape(peers, cap)
    incoming = lax.all_to_all(requests, "orb", split_axis=0, concat_axis=0, tiled=True)
    flat_in = incoming.reshape(-1)
    send_blocks = jnp.take(blocks, flat_in, axis=0).reshape(peers, cap, half_aux, nvd)
    send_vir = jnp.take(vir_energy, flat_in, axis=0).reshape(peers, cap, nvd)
    send_occ = jnp.take(occ_energy, flat_in).reshape(peers, cap)
    send_size = jnp.take(domain_size, flat_in).astype(jnp.float32).reshape(peers, cap)
    got_blocks = lax.all_to_all(send_blocks, "orb", split_axis=0, concat_axis=0, tiled=True)
    got_vir, got_occ, got_size = (
        lax.all_to_all(send_vir, "orb", split_axis=0, concat_axis=0, tiled=True),
        lax.all_to_all(send_occ, "orb", split_axis=0, concat_axis=0, tiled=True),
        lax.all_to_all(send_size, "orb", split_axis=0, concat_axis=0, tiled=True),
    )
    partner = jnp.take(got_blocks.reshape(peers * cap, half_aux, nvd), target, axis=0).reshape(
        occ_dev, per_orb, half_aux, nvd
    )
    partner_vir = jnp.take(got_vir.reshape(peers * cap, nvd), target, axis=0).reshape(
        occ_dev, per_orb, nvd
    )
    partner_occ = jnp.take(got_occ.reshape(-1), target).reshape(occ_dev, per_orb)
    partner_size = jnp.take(got_size.reshape(-1), target).reshape(occ_dev, per_orb)
    half = nvd // lax.axis_size("aux")
    integrals = lax.psum_scatter(
        jnp.einsum("oqa,opqb->aopb", blocks, partner, preferred_element_type=jnp.float32),
        "aux",
        scatter_dimension=0,
        tiled=True,
    )
    row_start = lax.axis_index("aux") * half
    rows = row_start + jnp.arange(half, dtype=jnp.int32)
    cols = jnp.arange(nvd, dtype=jnp.int32).astype(jnp.float32)
    mask = (rows[:, None, None, None] < domain_size[None, :, None, None]) & (
        cols[None, None, None, :] < partner_size[None, :, :, None]
    )
    integrals = jnp.where(mask, integrals, jnp.zeros_like(integrals))
    vir_rows = lax.dynamic_slice_in_dim(vir_energy, row_start, half, 1)
    gap = (
        vir_rows.T[:, :, None, None]
        + partner_vir[None, :, :, :]
        - occ_energy[None, :, None, None]
        - partner_occ[None, :, :, None]
    )
    amp_rows = (-integrals / gap).astype(jnp.bfloat16)
    partial_energy = jnp.sum(integrals * amp_rows.astype(jnp.float32), axis=(0, 3))
    energy = lax.psum(partial_energy, "aux").reshape(pair_dev) / nvd
    density = jnp.einsum(
        "aopb,copb->oac",
        amp_rows,
        lax.all_gather(amp_rows, "aux", axis=0, tiled=True),
        preferred_element_type=jnp.float32,
    )
    return (energy, density)


def fits_line(mesh):
    return mesh.shape["orb"] == 8 and mesh.shape["aux"] == 2


TINY = pl.CostEstimate(flops=1, bytes_accessed=1, transcendentals=0)
PARAMS = pltpu.CompilerParams(vmem_limit_bytes=LIMIT)
LIGHT = pltpu.CompilerParams(vmem_limit_bytes=LIMIT // 4)


def lists_kernel(cap, vir, occ, size, owner, slot, small, hit):
    n, (count, nvd) = hit.shape[0], vir.shape

    def column(row, m):
        eye = lax.broadcasted_iota(i32, (m, m), 0) == lax.broadcasted_iota(i32, (m, m), 1)
        return jnp.sum(jnp.where(eye, row, 0.0), axis=1, keepdims=True)

    down = lax.broadcasted_iota(i32, (n, n), 0).astype(f32)
    along = lax.broadcasted_iota(i32, (n, n), 1).astype(f32)
    owner_row = owner[...].astype(f32)
    owner_col = column(owner_row, n)
    before = (owner_col == owner_row) & (along < down)
    target = owner_col * cap + jnp.sum(jnp.where(before, 1.0, 0.0), axis=1, keepdims=True)
    found = target == along
    hit[...] = jnp.where(found, 1.0, 0.0)
    small[...] = jnp.zeros_like(small)
    small[:count, :nvd] = vir[...]
    lane = lax.broadcasted_iota(i32, (count, 128), 1)
    occ_col, size_col = column(occ[...], count), column(size[...].astype(f32), count)
    small[:count, nvd:] = jnp.where(lane == 0, occ_col, jnp.where(lane == 1, size_col, 0.0))
    small[count : count + 1, :n] = jnp.sum(jnp.where(found, down, 0.0), axis=0, keepdims=True)
    slot_col = column(slot[...].astype(f32), n)
    small[count : count + 1, 128 : 128 + n] = jnp.sum(
        jnp.where(found, slot_col, 0.0), axis=0, keepdims=True
    )


def lists(vir, occ, size, owner, slot, cap):
    count, nvd = vir.shape
    n = slot.shape[0]
    return pl.pallas_call(
        lambda *refs: lists_kernel(cap, *refs),
        out_shape=(
            jax.ShapeDtypeStruct((count + 8, nvd + 128), f32),
            jax.ShapeDtypeStruct((n, n), f32),
        ),
        in_specs=[VMEM] * 5,
        out_specs=(VMEM, VMEM),
        compiler_params=PARAMS,
        cost_estimate=TINY,
        name="lists",
    )(vir, occ.reshape(1, -1), size.reshape(1, -1), owner.reshape(1, -1), slot.reshape(1, -1))


ORDER, SLOT, SIZE_I, SIZE_J, HEAD = range(5)
MIDDLE, COLUMN = 8, 9


def pick(one, values):
    return lax.dot_general(
        one, values, (((0,), (0,)), ((), ())),
        precision=lax.Precision.HIGHEST, preferred_element_type=f32,
    )


def tables_kernel(cap, per_orb, meta, *refs):
    smalls, outs = refs[:8], refs[8:]
    count, nvd = smalls[0].shape[0] - 8, smalls[0].shape[1] - 128
    n = 8 * cap
    me, col0 = meta[0], meta[1]
    z, y = me // 2, me % 2
    lower = z < 2
    middle = jnp.where((z == 1) | (z == 2), 1, 0)
    places = [z, z ^ 1, jnp.where(lower, 2, 1), jnp.where(lower, 3, 0)]
    head = [(2 * p + y) * cap for p in places] + [(2 * p + 1 - y) * cap for p in places]
    lane = lax.broadcasted_iota(i32, (1, 128), 1)
    head_row = jnp.zeros((1, 128), i32)
    for k, value in enumerate(head + [middle, col0]):
        head_row = jnp.where(lane == k, value, head_row)
    orbitals = jnp.concatenate([x[:count, :] for x in smalls], axis=0)
    columns = jnp.where(col0 == 0, orbitals[:, : nvd // 2], orbitals[:, nvd // 2 : nvd])
    extra = orbitals[:, nvd:]

    def build(x, tbl, rows=None):
        order = smalls[x][count : count + 1, :n].astype(i32)
        slots = smalls[x][count : count + 1, 128 : 128 + n].astype(i32)
        tbl[...] = jnp.zeros_like(tbl)
        tbl[HEAD : HEAD + 1, :] = head_row
        tbl[SLOT : SLOT + 1, :n] = slots
        if rows is None:
            return
        tbl[ORDER : ORDER + 1, :n] = order
        pair = lax.broadcasted_iota(i32, (1, n), 1)
        owner = sum(jnp.where(pair >= k * cap, 1, 0) for k in range(1, 8))
        index = (owner ^ me) * count + slots
        theirs = jnp.where(lax.broadcasted_iota(i32, (8 * count, n), 0) == index, 1.0, 0.0)
        first = sum(jnp.where(order >= k * per_orb, 1, 0) for k in range(1, count))
        mine = jnp.where(lax.broadcasted_iota(i32, (count, n), 0) == first, 1.0, 0.0)
        own = smalls[x][:count, nvd:]
        rows[...] = pick(theirs, columns) - (pick(theirs, extra)[:, :1] + pick(mine, own)[:, :1])
        tbl[SIZE_I : SIZE_I + 1, :n] = pick(own, mine)[1:2, :].astype(i32)
        tbl[SIZE_J : SIZE_J + 1, :n] = pick(extra, theirs)[1:2, :].astype(i32) - col0

    build(0, outs[0], outs[1])
    build(2, outs[2], outs[3])
    build(1, outs[4])
    build(3, outs[5])


def tables_of(meta, smalls, cap, per_orb, half):
    table = jax.ShapeDtypeStruct((8, 128), i32)
    rows = jax.ShapeDtypeStruct((8 * cap, half), f32)
    return pl.pallas_call(
        lambda *refs: tables_kernel(cap, per_orb, *refs),
        out_shape=(table, rows, table, rows, table, table),
        in_specs=[SMEM] + [VMEM] * 8,
        out_specs=[VMEM] * 6,
        compiler_params=LIGHT,
        cost_estimate=TINY,
        name="tables",
    )(meta, *smalls)


def pack_kernel(jobs, tables, *refs):
    tbls, rest = refs[:tables], refs[tables:]
    outs = refs[-len(jobs) :]
    middle = tbls[0][HEAD, MIDDLE] == 1

    def gather(out, sources, tbl, call):
        base = tbl[HEAD, call]
        for q in range(out.shape[0]):
            for r in range(out.shape[1]):
                out[q, r] = sources[q][tbl[SLOT, base + r]]

    for out, (table, call, halves, only_middle) in zip(outs, jobs):
        sources, rest = rest[:halves], rest[halves:]
        if only_middle:
            pl.when(middle)(functools.partial(gather, out, sources, tbls[table], call))
        else:
            gather(out, sources, tbls[table], call)


def pack(tbls, jobs, cap, after=()):
    operands = [x for _, _, sources, _ in jobs for x in sources]
    kinds = [(table, call, len(sources), middle) for table, call, sources, middle in jobs]
    block = operands[0].shape[1:]
    return pl.pallas_call(
        lambda *refs: pack_kernel(kinds, len(tbls), *refs),
        out_shape=[jax.ShapeDtypeStruct((k[2], cap) + block, bf16) for k in kinds],
        in_specs=[SMEM] * len(tbls) + [VMEM] * len(operands) + [HBM] * len(after),
        out_specs=[VMEM] * len(jobs),
        compiler_params=LIGHT,
        cost_estimate=TINY,
        name="pack",
    )(*tbls, *operands, *after)


def turn_kernel(*refs):
    half = len(refs) // 2
    for x, out in zip(refs[:half], refs[half:]):
        for r in range(x.shape[0]):
            out[r] = x[r].T


def turn(arrays):
    count, rows, cols = arrays[0].shape
    step = 4 if count % 4 == 0 else 1
    n = len(arrays)
    return pl.pallas_call(
        turn_kernel,
        out_shape=[jax.ShapeDtypeStruct((count, cols, rows), bf16)] * n,
        grid=(count // step,),
        in_specs=[pl.BlockSpec((step, rows, cols), lambda i: (i, 0, 0))] * n,
        out_specs=[pl.BlockSpec((step, cols, rows), lambda i: (i, 0, 0))] * n,
        compiler_params=PARAMS,
        cost_estimate=TINY,
        name="turn",
    )(*arrays)


def amplitudes_kernel(mode, call, per_orb, groups, tbl, rows, vcol, *refs):
    client = mode == "client"
    if client:
        tout = refs[-1]
        left, rest = refs[:4], refs[4:]
    else:
        tout, eout = refs[-2:]
        left, rest = refs[:2], refs[2:]
    places = []
    for arrays in groups:
        if arrays == 1:
            places.append([rest[0].at[0], rest[0].at[1]])
        elif len(rest[0].shape) == 4:
            places.append([rest[0].at[0], rest[1].at[0]])
        else:
            places.append(rest[:2])
        rest = rest[arrays:]
    cap = rows.shape[0] // 8
    nvd, half = vcol.shape[1:]
    base = pl.multiple_of(tbl[HEAD, call], cap)
    middle = tbl[HEAD, MIDDLE] == 1
    row8 = rows[pl.ds(base, cap), :]

    def gap(r, i):
        return vcol[i] + row8[r : r + 1, :]

    def make(r):
        p = tbl[ORDER, base + r]
        i = lax.div(p, per_orb)
        slot = r if mode == "asked" else tbl[SLOT, base + r]
        b0, b1 = [x[slot] for x in places[0]]
        if len(places) == 2:
            b0, b1 = [jnp.where(middle, b, x[slot]) for b, x in zip((b0, b1), places[1])]

        def product(x0, x1):
            return jnp.dot(x0[i], b0, preferred_element_type=f32) + jnp.dot(
                x1[i], b1, preferred_element_type=f32
            )

        if client:
            here, there = product(left[0], left[1]), product(left[3], left[2])
            first = tbl[HEAD, COLUMN] == 0
            k = jnp.concatenate(
                [jnp.where(first, here, there), jnp.where(first, there, here)], axis=0
            )
        else:
            k = product(left[0], left[1])
        live_a = lax.broadcasted_iota(i32, (nvd, half), 0)
        live_b = lax.broadcasted_iota(i32, (nvd, half), 1)
        live = (live_a < tbl[SIZE_I, base + r]) & (live_b < tbl[SIZE_J, base + r])
        k = jnp.where(live, k, 0.0)
        t = (-k / gap(r, i)).astype(bf16)
        if client:
            tout[r] = t
            return None
        tout[p] = t
        return jnp.sum(k * t.astype(f32), axis=0, keepdims=True)

    def take(r):
        p = tbl[ORDER, base + r]
        ready = rest[0][r]
        tout[p] = ready
        t = ready.astype(f32)
        return -jnp.sum(t * t * gap(r, lax.div(p, per_orb)), axis=0, keepdims=True)

    def each(step):
        parts = [step(r) for r in range(cap)]
        if not client:
            eout[pl.ds(base, cap), :] = jnp.concatenate(parts, axis=0)

    if mode == "served":
        pl.when(middle)(lambda: each(make))
        pl.when(jnp.logical_not(middle))(lambda: each(take))
    elif client:
        pl.when(middle)(lambda: each(make))
    else:
        each(make)


def amplitudes(mode, call, per_orb, tables, left, groups, cap, held=(), after=(), ready=()):
    tbl, rows, vcol = tables
    occ, nvd, half = vcol.shape
    client = mode == "client"
    sources = [x for group in groups for x in group]
    blocks = (rows, vcol, *left, *sources, *ready)
    operands = (tbl, *blocks, *after)
    aliases = {len(operands) + k: k for k in range(len(held))}
    if client:
        out_shape = jax.ShapeDtypeStruct((cap, nvd, half), bf16)
        out_specs = VMEM
    else:
        out_shape = (
            jax.ShapeDtypeStruct((occ * per_orb, nvd, half), bf16),
            jax.ShapeDtypeStruct((occ * per_orb, half), f32),
        )
        out_specs = (VMEM, VMEM)
    return pl.pallas_call(
        lambda *refs: amplitudes_kernel(mode, call, per_orb, [len(g) for g in groups], *refs),
        out_shape=out_shape,
        in_specs=[SMEM] + [VMEM] * len(blocks) + [HBM] * len(after) + [VMEM] * len(held),
        out_specs=out_specs,
        input_output_aliases=aliases,
        compiler_params=LIGHT,
        cost_estimate=TINY,
        name="amplitudes",
    )(*operands, *held)


def density_kernel(start, t, mine, away):
    count, half = mine.shape[:2]
    per_orb = t.shape[0] // count
    first = pl.multiple_of(start[0], half)
    for o in range(count):
        own = range(o * per_orb, (o + 1) * per_orb)
        right = jnp.concatenate([t[k] for k in own], axis=1)
        for out, row in ((away, pl.multiple_of(half - first, half)), (mine, first)):
            left = jnp.concatenate([t[k, pl.ds(row, half), :] for k in own], axis=1)
            out[o] = lax.dot_general(
                left, right, (((1,), (1,)), ((), ())), preferred_element_type=f32
            )


def densities(t_all, start, per_orb, half):
    npair, nvd, _ = t_all.shape
    shape = jax.ShapeDtypeStruct((npair // per_orb, half, nvd), f32)
    return pl.pallas_call(
        density_kernel,
        out_shape=(shape, shape),
        in_specs=[SMEM, VMEM],
        out_specs=(VMEM, VMEM),
        compiler_params=LIGHT,
        cost_estimate=TINY,
        name="densities",
    )(start.reshape(1), t_all)


def line_plan(blocks, vir_energy, occ_energy, domain_size, partner_owner, partner_slot):
    occ, qa, nvd = blocks.shape
    pair_dev = partner_slot.shape[0]
    per_orb = pair_dev // occ
    peers = 8
    cap = pair_dev // peers
    half = nvd // 2
    me, core = lax.axis_index("orb"), lax.axis_index("aux")
    col0 = core * half

    def pp(x, perm):
        return lax.ppermute(x, "orb", perm)

    def swap_core(x):
        return lax.ppermute(x, "aux", [(0, 1), (1, 0)])

    def flip(bits):
        return [(o, o ^ bits) for o in range(peers)]

    cross = [(2, 4), (3, 5), (4, 2), (5, 3)]
    outward = [(2, 0), (3, 1), (4, 6), (5, 7)]
    diagonal = [(2, 1), (3, 0), (4, 7), (5, 6)]
    y_middle = [(2, 3), (3, 2), (4, 5), (5, 4)]

    small, hit = lists(vir_energy, occ_energy, domain_size, partner_owner, partner_slot, cap)
    smalls = [small] + [pp(small, flip(bits)) for bits in range(1, peers)]

    other = swap_core(blocks)
    own = [lax.dynamic_slice_in_dim(x, col0, half, 2) for x in (blocks, other)]
    sent, smalls = lax.optimization_barrier((own[0], smalls))
    mid = [pp(x, cross) for x in (sent, own[1])]
    near = [pp(x, flip(2)) for x in (sent, own[1])]
    tbl, rows, client_tbl, client_rows, beside_list, relay_list = tables_of(
        jnp.stack([me, col0]), smalls, cap, per_orb, half
    )
    lists_of = [beside_list, relay_list]

    def spread(vir):
        return jnp.broadcast_to(vir[:, :, None], (occ, nvd, half))

    tables = (tbl, rows, spread(vir_energy))
    client = (client_tbl, client_rows, spread(smalls[2][:occ, :nvd]))

    def own_pairs(k, mode, groups, held=(), after=(), ready=()):
        return amplitudes(mode, k, per_orb, tables, left, groups, cap, held, after, ready)

    (packed,) = pack(lists_of, [(0, 0, own, False)], cap)
    beside = pp(packed, flip(1))
    left = turn([blocks, other])
    held = own_pairs(0, "slots", [own], after=(packed,))
    first, held = lax.optimization_barrier((near[0], held))
    far = [pp(first, cross)]
    across = [swap_core(first)]
    (packed,) = pack(lists_of, [(0, 1, [first], False)], cap, after=(held[1], mid[0]))
    beside_near = [pp(packed, flip(1))]
    held = own_pairs(4, "asked", [[beside]], held, (packed, beside_near[0]))
    second, held = lax.optimization_barrier((near[1], held))
    far.append(pp(second, cross))
    across.append(swap_core(second))
    near = [first, second]
    packed = pack(lists_of, [(1, 2, mid, True), (0, 2, mid, True)], cap, after=(held[1],))
    third_diagonal, third = pp(packed[0], diagonal), pp(packed[1], y_middle)
    (packed,) = pack(lists_of, [(0, 1, [second], False)], cap, after=(packed[0],))
    beside_near.append(pp(packed, flip(1)))
    client_left = turn(near + across)
    gone = amplitudes("client", 2, per_orb, client, client_left, [mid], cap, after=(packed,))
    ready_2 = pp(gone, outward)
    held = own_pairs(1, "slots", [near], held, (gone, third_diagonal))
    jobs = [(1, 3, far[:1], True), (0, 3, far[:1], True)]
    packed = pack(lists_of, jobs, cap, after=(held[1],))
    fourth_diagonal, fourth = [pp(packed[0], diagonal)], [pp(packed[1], y_middle)]
    held = own_pairs(2, "served", [mid], held, (packed[0],), (ready_2,))
    held = own_pairs(5, "asked", [beside_near], held)
    (packed,) = pack(lists_of, [(1, 3, far[1:], True)], cap, after=(held[1],))
    fourth_diagonal.append(pp(packed, diagonal))
    gone = amplitudes("client", 3, per_orb, client, client_left, [far], cap, after=(packed,))
    ready_3 = pp(gone, outward)
    (packed,) = pack(
        lists_of, [(0, 3, far[1:], True)], cap, after=(gone,)
    )
    fourth.append(pp(packed, y_middle))
    held = own_pairs(
        6, "asked", [[third], [third_diagonal]], held, (packed, fourth[0], fourth_diagonal[0])
    )
    held = own_pairs(3, "served", [far], held, (fourth_diagonal[1],), (ready_3,))
    t_all, e_all = own_pairs(7, "asked", [fourth, fourth_diagonal], held)

    mine, away = densities(t_all, col0, per_orb, half)
    density = mine + swap_core(away)

    energy = jnp.sum(hit * jnp.sum(e_all, axis=1)[None, :], axis=1)
    energy = (energy + swap_core(energy)) / nvd
    return (energy, density)


def solution(mesh):
    in_specs = (
        P(("mol", "orb"), "aux", None),
        P(("mol", "orb"), None),
        P(("mol", "orb")),
        P(("mol", "orb")),
        P(("mol", "orb"), None),
        P(("mol", "orb")),
    )
    out_specs = (P(("mol", "orb")), P(("mol", "orb"), "aux", None))
    return jax.shard_map(
        line_plan if fits_line(mesh) else by_requests, mesh=mesh, in_specs=in_specs, out_specs=out_specs, check_vma=False
    )
```

```python
import functools

import jax
import jax.numpy as jnp
from jax import lax
from jax.experimental import pallas as pl
from jax.experimental.pallas import tpu as pltpu
from jax.sharding import PartitionSpec as P

f32, bf16, i32 = jnp.float32, jnp.bfloat16, jnp.int32
HBM = pl.BlockSpec(memory_space=pltpu.HBM)
SMEM = pl.BlockSpec(memory_space=pltpu.SMEM)
VMEM = pl.BlockSpec(memory_space=pltpu.VMEM)
LIMIT = 12 * 1024 * 1024


def slot_ranks(owner):
    count = owner.shape[0]
    order = jnp.arange(count, dtype=jnp.int32)
    same = (owner[:, None] == owner[None, :]) & (order[None, :] < order[:, None])
    return jnp.sum(same.astype(jnp.int32), axis=1)


def by_requests(blocks, vir_energy, occ_energy, domain_size, partner_owner, partner_slot):
    occ_dev, half_aux, nvd = blocks.shape
    pair_dev = partner_slot.shape[0]
    per_orb = pair_dev // occ_dev
    peers = lax.axis_size("orb")
    cap = max(2, (pair_dev + peers - 1) // peers)
    owner = partner_owner[:, 0]
    ranks = slot_ranks(owner)
    target = owner * cap + ranks
    wanted = (target[:, None] == jnp.arange(peers * cap, dtype=jnp.int32)[None, :]).astype(
        jnp.int32
    )
    requests = jnp.sum(wanted * partner_slot[:, None], axis=0).reshape(peers, cap)
    incoming = lax.all_to_all(requests, "orb", split_axis=0, concat_axis=0, tiled=True)
    flat_in = incoming.reshape(-1)
    send_blocks = jnp.take(blocks, flat_in, axis=0).reshape(peers, cap, half_aux, nvd)
    send_vir = jnp.take(vir_energy, flat_in, axis=0).reshape(peers, cap, nvd)
    send_occ = jnp.take(occ_energy, flat_in).reshape(peers, cap)
    send_size = jnp.take(domain_size, flat_in).astype(jnp.float32).reshape(peers, cap)
    got_blocks = lax.all_to_all(send_blocks, "orb", split_axis=0, concat_axis=0, tiled=True)
    got_vir, got_occ, got_size = (
        lax.all_to_all(send_vir, "orb", split_axis=0, concat_axis=0, tiled=True),
        lax.all_to_all(send_occ, "orb", split_axis=0, concat_axis=0, tiled=True),
        lax.all_to_all(send_size, "orb", split_axis=0, concat_axis=0, tiled=True),
    )
    partner = jnp.take(got_blocks.reshape(peers * cap, half_aux, nvd), target, axis=0).reshape(
        occ_dev, per_orb, half_aux, nvd
    )
    partner_vir = jnp.take(got_vir.reshape(peers * cap, nvd), target, axis=0).reshape(
        occ_dev, per_orb, nvd
    )
    partner_occ = jnp.take(got_occ.reshape(-1), target).reshape(occ_dev, per_orb)
    partner_size = jnp.take(got_size.reshape(-1), target).reshape(occ_dev, per_orb)
    half = nvd // lax.axis_size("aux")
    integrals = lax.psum_scatter(
        jnp.einsum("oqa,opqb->aopb", blocks, partner, preferred_element_type=jnp.float32),
        "aux",
        scatter_dimension=0,
        tiled=True,
    )
    row_start = lax.axis_index("aux") * half
    rows = row_start + jnp.arange(half, dtype=jnp.int32)
    cols = jnp.arange(nvd, dtype=jnp.int32).astype(jnp.float32)
    mask = (rows[:, None, None, None] < domain_size[None, :, None, None]) & (
        cols[None, None, None, :] < partner_size[None, :, :, None]
    )
    integrals = jnp.where(mask, integrals, jnp.zeros_like(integrals))
    vir_rows = lax.dynamic_slice_in_dim(vir_energy, row_start, half, 1)
    gap = (
        vir_rows.T[:, :, None, None]
        + partner_vir[None, :, :, :]
        - occ_energy[None, :, None, None]
        - partner_occ[None, :, :, None]
    )
    amp_rows = (-integrals / gap).astype(jnp.bfloat16)
    partial_energy = jnp.sum(integrals * amp_rows.astype(jnp.float32), axis=(0, 3))
    energy = lax.psum(partial_energy, "aux").reshape(pair_dev) / nvd
    density = jnp.einsum(
        "aopb,copb->oac",
        amp_rows,
        lax.all_gather(amp_rows, "aux", axis=0, tiled=True),
        preferred_element_type=jnp.float32,
    )
    return (energy, density)


def fits_line(mesh):
    return mesh.shape["orb"] == 8 and mesh.shape["aux"] == 2


TINY = pl.CostEstimate(flops=1, bytes_accessed=1, transcendentals=0)
PARAMS = pltpu.CompilerParams(vmem_limit_bytes=LIMIT)
LIGHT = pltpu.CompilerParams(vmem_limit_bytes=LIMIT // 4)


def lists_kernel(cap, vir, occ, size, owner, slot, small, hit):
    n, (count, nvd) = hit.shape[0], vir.shape

    def column(row, m):
        eye = lax.broadcasted_iota(i32, (m, m), 0) == lax.broadcasted_iota(i32, (m, m), 1)
        return jnp.sum(jnp.where(eye, row, 0.0), axis=1, keepdims=True)

    down = lax.broadcasted_iota(i32, (n, n), 0).astype(f32)
    along = lax.broadcasted_iota(i32, (n, n), 1).astype(f32)
    owner_row = owner[...].astype(f32)
    owner_col = column(owner_row, n)
    before = (owner_col == owner_row) & (along < down)
    target = owner_col * cap + jnp.sum(jnp.where(before, 1.0, 0.0), axis=1, keepdims=True)
    found = target == along
    hit[...] = jnp.where(found, 1.0, 0.0)
    small[...] = jnp.zeros_like(small)
    small[:count, :nvd] = vir[...]
    lane = lax.broadcasted_iota(i32, (count, 128), 1)
    occ_col, size_col = column(occ[...], count), column(size[...].astype(f32), count)
    small[:count, nvd:] = jnp.where(lane == 0, occ_col, jnp.where(lane == 1, size_col, 0.0))
    small[count : count + 1, :n] = jnp.sum(jnp.where(found, down, 0.0), axis=0, keepdims=True)
    slot_col = column(slot[...].astype(f32), n)
    small[count : count + 1, 128 : 128 + n] = jnp.sum(
        jnp.where(found, slot_col, 0.0), axis=0, keepdims=True
    )


def lists(vir, occ, size, owner, slot, cap):
    count, nvd = vir.shape
    n = slot.shape[0]
    return pl.pallas_call(
        lambda *refs: lists_kernel(cap, *refs),
        out_shape=(
            jax.ShapeDtypeStruct((count + 8, nvd + 128), f32),
            jax.ShapeDtypeStruct((n, n), f32),
        ),
        in_specs=[VMEM] * 5,
        out_specs=(VMEM, VMEM),
        compiler_params=PARAMS,
        cost_estimate=TINY,
        name="lists",
    )(vir, occ.reshape(1, -1), size.reshape(1, -1), owner.reshape(1, -1), slot.reshape(1, -1))


ORDER, SLOT, SIZE_I, SIZE_J, HEAD = range(5)
MIDDLE, COLUMN = 8, 9


def pick(one, values):
    return lax.dot_general(
        one, values, (((0,), (0,)), ((), ())),
        precision=lax.Precision.HIGHEST, preferred_element_type=f32,
    )


def tables_kernel(cap, per_orb, meta, *refs):
    smalls, outs = refs[:8], refs[8:]
    count, nvd = smalls[0].shape[0] - 8, smalls[0].shape[1] - 128
    n = 8 * cap
    me, col0 = meta[0], meta[1]
    z, y = me // 2, me % 2
    lower = z < 2
    middle = jnp.where((z == 1) | (z == 2), 1, 0)
    places = [z, z ^ 1, jnp.where(lower, 2, 1), jnp.where(lower, 3, 0)]
    head = [(2 * p + y) * cap for p in places] + [(2 * p + 1 - y) * cap for p in places]
    lane = lax.broadcasted_iota(i32, (1, 128), 1)
    head_row = jnp.zeros((1, 128), i32)
    for k, value in enumerate(head + [middle, col0]):
        head_row = jnp.where(lane == k, value, head_row)
    orbitals = jnp.concatenate([x[:count, :] for x in smalls], axis=0)
    columns = jnp.where(col0 == 0, orbitals[:, : nvd // 2], orbitals[:, nvd // 2 : nvd])
    extra = orbitals[:, nvd:]

    def build(x, tbl, rows=None):
        order = smalls[x][count : count + 1, :n].astype(i32)
        slots = smalls[x][count : count + 1, 128 : 128 + n].astype(i32)
        tbl[...] = jnp.zeros_like(tbl)
        tbl[HEAD : HEAD + 1, :] = head_row
        tbl[SLOT : SLOT + 1, :n] = slots
        if rows is None:
            return
        tbl[ORDER : ORDER + 1, :n] = order
        pair = lax.broadcasted_iota(i32, (1, n), 1)
        owner = sum(jnp.where(pair >= k * cap, 1, 0) for k in range(1, 8))
        index = (owner ^ me) * count + slots
        theirs = jnp.where(lax.broadcasted_iota(i32, (8 * count, n), 0) == index, 1.0, 0.0)
        first = sum(jnp.where(order >= k * per_orb, 1, 0) for k in range(1, count))
        mine = jnp.where(lax.broadcasted_iota(i32, (count, n), 0) == first, 1.0, 0.0)
        own = smalls[x][:count, nvd:]
        rows[...] = pick(theirs, columns) - (pick(theirs, extra)[:, :1] + pick(mine, own)[:, :1])
        tbl[SIZE_I : SIZE_I + 1, :n] = pick(own, mine)[1:2, :].astype(i32)
        tbl[SIZE_J : SIZE_J + 1, :n] = pick(extra, theirs)[1:2, :].astype(i32) - col0

    build(0, outs[0], outs[1])
    build(2, outs[2], outs[3])
    build(1, outs[4])
    build(3, outs[5])


def tables_of(meta, smalls, cap, per_orb, half):
    table = jax.ShapeDtypeStruct((8, 128), i32)
    rows = jax.ShapeDtypeStruct((8 * cap, half), f32)
    return pl.pallas_call(
        lambda *refs: tables_kernel(cap, per_orb, *refs),
        out_shape=(table, rows, table, rows, table, table),
        in_specs=[SMEM] + [VMEM] * 8,
        out_specs=[VMEM] * 6,
        compiler_params=LIGHT,
        cost_estimate=TINY,
        name="tables",
    )(meta, *smalls)


def pack_kernel(jobs, tables, *refs):
    tbls, rest = refs[:tables], refs[tables:]
    outs = refs[-len(jobs) :]
    middle = tbls[0][HEAD, MIDDLE] == 1

    def gather(out, sources, tbl, call):
        base = tbl[HEAD, call]
        for q in range(out.shape[0]):
            for r in range(out.shape[1]):
                out[q, r] = sources[q][tbl[SLOT, base + r]]

    for out, (table, call, halves, only_middle) in zip(outs, jobs):
        sources, rest = rest[:halves], rest[halves:]
        if only_middle:
            pl.when(middle)(functools.partial(gather, out, sources, tbls[table], call))
        else:
            gather(out, sources, tbls[table], call)


def pack(tbls, jobs, cap, after=()):
    operands = [x for _, _, sources, _ in jobs for x in sources]
    kinds = [(table, call, len(sources), middle) for table, call, sources, middle in jobs]
    block = operands[0].shape[1:]
    return pl.pallas_call(
        lambda *refs: pack_kernel(kinds, len(tbls), *refs),
        out_shape=[jax.ShapeDtypeStruct((k[2], cap) + block, bf16) for k in kinds],
        in_specs=[SMEM] * len(tbls) + [VMEM] * len(operands) + [HBM] * len(after),
        out_specs=[VMEM] * len(jobs),
        compiler_params=LIGHT,
        cost_estimate=TINY,
        name="pack",
    )(*tbls, *operands, *after)


def turn_kernel(*refs):
    half = len(refs) // 2
    for x, out in zip(refs[:half], refs[half:]):
        for r in range(x.shape[0]):
            out[r] = x[r].T


def turn(arrays):
    count, rows, cols = arrays[0].shape
    step = 4 if count % 4 == 0 else 1
    n = len(arrays)
    return pl.pallas_call(
        turn_kernel,
        out_shape=[jax.ShapeDtypeStruct((count, cols, rows), bf16)] * n,
        grid=(count // step,),
        in_specs=[pl.BlockSpec((step, rows, cols), lambda i: (i, 0, 0))] * n,
        out_specs=[pl.BlockSpec((step, cols, rows), lambda i: (i, 0, 0))] * n,
        compiler_params=PARAMS,
        cost_estimate=TINY,
        name="turn",
    )(*arrays)


def amplitudes_kernel(mode, call, per_orb, groups, tbl, rows, vcol, *refs):
    client = mode == "client"
    if client:
        tout = refs[-1]
        left, rest = refs[:4], refs[4:]
    else:
        tout, eout = refs[-2:]
        left, rest = refs[:2], refs[2:]
    places = []
    for arrays in groups:
        if arrays == 1:
            places.append([rest[0].at[0], rest[0].at[1]])
        elif len(rest[0].shape) == 4:
            places.append([rest[0].at[0], rest[1].at[0]])
        else:
            places.append(rest[:2])
        rest = rest[arrays:]
    cap = rows.shape[0] // 8
    nvd, half = vcol.shape[1:]
    base = pl.multiple_of(tbl[HEAD, call], cap)
    middle = tbl[HEAD, MIDDLE] == 1
    row8 = rows[pl.ds(base, cap), :]

    def gap(r, i):
        return vcol[i] + row8[r : r + 1, :]

    def make(r):
        p = tbl[ORDER, base + r]
        i = lax.div(p, per_orb)
        slot = r if mode == "asked" else tbl[SLOT, base + r]
        b0, b1 = [x[slot] for x in places[0]]
        if len(places) == 2:
            b0, b1 = [jnp.where(middle, b, x[slot]) for b, x in zip((b0, b1), places[1])]

        def product(x0, x1):
            return jnp.dot(x0[i], b0, preferred_element_type=f32) + jnp.dot(
                x1[i], b1, preferred_element_type=f32
            )

        if client:
            here, there = product(left[0], left[1]), product(left[3], left[2])
            first = tbl[HEAD, COLUMN] == 0
            k = jnp.concatenate(
                [jnp.where(first, here, there), jnp.where(first, there, here)], axis=0
            )
        else:
            k = product(left[0], left[1])
        live_a = lax.broadcasted_iota(i32, (nvd, half), 0)
        live_b = lax.broadcasted_iota(i32, (nvd, half), 1)
        live = (live_a < tbl[SIZE_I, base + r]) & (live_b < tbl[SIZE_J, base + r])
        k = jnp.where(live, k, 0.0)
        t = (-k / gap(r, i)).astype(bf16)
        if client:
            tout[r] = t
            return None
        tout[p] = t
        return jnp.sum(k * t.astype(f32), axis=0, keepdims=True)

    def take(r):
        p = tbl[ORDER, base + r]
        ready = rest[0][r]
        tout[p] = ready
        t = ready.astype(f32)
        return -jnp.sum(t * t * gap(r, lax.div(p, per_orb)), axis=0, keepdims=True)

    def each(step):
        parts = [step(r) for r in range(cap)]
        if not client:
            eout[pl.ds(base, cap), :] = jnp.concatenate(parts, axis=0)

    if mode == "served":
        pl.when(middle)(lambda: each(make))
        pl.when(jnp.logical_not(middle))(lambda: each(take))
    elif client:
        pl.when(middle)(lambda: each(make))
    else:
        each(make)


def amplitudes(mode, call, per_orb, tables, left, groups, cap, held=(), after=(), ready=()):
    tbl, rows, vcol = tables
    occ, nvd, half = vcol.shape
    client = mode == "client"
    sources = [x for group in groups for x in group]
    blocks = (rows, vcol, *left, *sources, *ready)
    operands = (tbl, *blocks, *after)
    aliases = {len(operands) + k: k for k in range(len(held))}
    if client:
        out_shape = jax.ShapeDtypeStruct((cap, nvd, half), bf16)
        out_specs = VMEM
    else:
        out_shape = (
            jax.ShapeDtypeStruct((occ * per_orb, nvd, half), bf16),
            jax.ShapeDtypeStruct((occ * per_orb, half), f32),
        )
        out_specs = (VMEM, VMEM)
    return pl.pallas_call(
        lambda *refs: amplitudes_kernel(mode, call, per_orb, [len(g) for g in groups], *refs),
        out_shape=out_shape,
        in_specs=[SMEM] + [VMEM] * len(blocks) + [HBM] * len(after) + [VMEM] * len(held),
        out_specs=out_specs,
        input_output_aliases=aliases,
        compiler_params=LIGHT,
        cost_estimate=TINY,
        name="amplitudes",
    )(*operands, *held)


def density_kernel(start, t, d):
    count, half = d.shape[:2]
    per_orb = t.shape[0] // count
    first = pl.multiple_of(start[0], half)
    for o in range(count):
        own = range(o * per_orb, (o + 1) * per_orb)
        right = jnp.concatenate([t[k] for k in own], axis=1)
        left = jnp.concatenate([t[k, pl.ds(first, half), :] for k in own], axis=1)
        d[o] = lax.dot_general(left, right, (((1,), (1,)), ((), ())), preferred_element_type=f32)


def densities(t_all, start, per_orb, half):
    npair, nvd, _ = t_all.shape
    shape = jax.ShapeDtypeStruct((npair // per_orb, half, nvd), f32)
    return pl.pallas_call(
        density_kernel,
        out_shape=shape,
        in_specs=[SMEM, VMEM],
        out_specs=VMEM,
        compiler_params=LIGHT,
        cost_estimate=TINY,
        name="densities",
    )(start.reshape(1), t_all)


def line_plan(blocks, vir_energy, occ_energy, domain_size, partner_owner, partner_slot):
    occ, qa, nvd = blocks.shape
    pair_dev = partner_slot.shape[0]
    per_orb = pair_dev // occ
    peers = 8
    cap = pair_dev // peers
    half = nvd // 2
    me, core = lax.axis_index("orb"), lax.axis_index("aux")
    col0 = core * half

    def pp(x, perm):
        return lax.ppermute(x, "orb", perm)

    def swap_core(x):
        return lax.ppermute(x, "aux", [(0, 1), (1, 0)])

    def flip(bits):
        return [(o, o ^ bits) for o in range(peers)]

    cross = [(2, 4), (3, 5), (4, 2), (5, 3)]
    outward = [(2, 0), (3, 1), (4, 6), (5, 7)]
    diagonal = [(2, 1), (3, 0), (4, 7), (5, 6)]
    y_middle = [(2, 3), (3, 2), (4, 5), (5, 4)]

    small, hit = lists(vir_energy, occ_energy, domain_size, partner_owner, partner_slot, cap)
    smalls = [small] + [pp(small, flip(bits)) for bits in range(1, peers)]

    other = swap_core(blocks)
    own = [lax.dynamic_slice_in_dim(x, col0, half, 2) for x in (blocks, other)]
    sent, smalls = lax.optimization_barrier((own[0], smalls))
    mid = [pp(x, cross) for x in (sent, own[1])]
    near = [pp(x, flip(2)) for x in (sent, own[1])]
    tbl, rows, client_tbl, client_rows, beside_list, relay_list = tables_of(
        jnp.stack([me, col0]), smalls, cap, per_orb, half
    )
    lists_of = [beside_list, relay_list]

    def spread(vir):
        return jnp.broadcast_to(vir[:, :, None], (occ, nvd, half))

    tables = (tbl, rows, spread(vir_energy))
    client = (client_tbl, client_rows, spread(smalls[2][:occ, :nvd]))

    def own_pairs(k, mode, groups, held=(), after=(), ready=()):
        return amplitudes(mode, k, per_orb, tables, left, groups, cap, held, after, ready)

    (packed,) = pack(lists_of, [(0, 0, own, False)], cap)
    beside = pp(packed, flip(1))
    left = turn([blocks, other])
    held = own_pairs(0, "slots", [own], after=(packed, mid[0]))
    first, held = lax.optimization_barrier((near[0], held))
    far = [pp(first, cross)]
    across = [swap_core(first)]
    (packed,) = pack(lists_of, [(0, 1, [first], False)], cap, after=(held[1], mid[0]))
    beside_near = [pp(packed, flip(1))]
    held = own_pairs(4, "asked", [[beside]], held, (packed, beside_near[0]))
    second, held = lax.optimization_barrier((near[1], held))
    far.append(pp(second, cross))
    across.append(swap_core(second))
    near = [first, second]
    packed = pack(lists_of, [(1, 2, mid, True), (0, 2, mid, True)], cap, after=(held[1],))
    third_diagonal, third = pp(packed[0], diagonal), pp(packed[1], y_middle)
    (packed,) = pack(lists_of, [(0, 1, [second], False)], cap, after=(packed[0],))
    beside_near.append(pp(packed, flip(1)))
    client_left = turn(near + across)
    gone = amplitudes("client", 2, per_orb, client, client_left, [mid], cap, after=(packed,))
    ready_2 = pp(gone, outward)
    held = own_pairs(1, "slots", [near], held, (gone, third_diagonal))
    jobs = [(1, 3, far[:1], True), (0, 3, far[:1], True)]
    packed = pack(lists_of, jobs, cap, after=(held[1],))
    fourth_diagonal, fourth = [pp(packed[0], diagonal)], [pp(packed[1], y_middle)]
    held = own_pairs(2, "served", [mid], held, (packed[0],), (ready_2,))
    held = own_pairs(5, "asked", [beside_near], held)
    (packed,) = pack(lists_of, [(1, 3, far[1:], True)], cap, after=(held[1],))
    fourth_diagonal.append(pp(packed, diagonal))
    gone = amplitudes("client", 3, per_orb, client, client_left, [far], cap, after=(packed,))
    ready_3 = pp(gone, outward)
    (packed,) = pack(
        lists_of, [(0, 3, far[1:], True)], cap, after=(gone,)
    )
    fourth.append(pp(packed, y_middle))
    held = own_pairs(
        6, "asked", [[third], [third_diagonal]], held, (packed, fourth[0], fourth_diagonal[0])
    )
    held = own_pairs(3, "served", [far], held, (fourth_diagonal[1],), (ready_3,))
    t_all, e_all = own_pairs(7, "asked", [fourth, fourth_diagonal], held)

    away = swap_core(densities(t_all, half - col0, per_orb, half))
    density = densities(t_all, col0, per_orb, half) + away

    energy = jnp.sum(hit * jnp.sum(e_all, axis=1)[None, :], axis=1)
    energy = (energy + swap_core(energy)) / nvd
    return (energy, density)


def solution(mesh):
    in_specs = (
        P(("mol", "orb"), "aux", None),
        P(("mol", "orb"), None),
        P(("mol", "orb")),
        P(("mol", "orb")),
        P(("mol", "orb"), None),
        P(("mol", "orb")),
    )
    out_specs = (P(("mol", "orb")), P(("mol", "orb"), "aux", None))
    return jax.shard_map(
        line_plan if fits_line(mesh) else by_requests, mesh=mesh, in_specs=in_specs, out_specs=out_specs, check_vma=False
    )
```

```python
import functools

import jax
import jax.numpy as jnp
from jax import lax
from jax.experimental import pallas as pl
from jax.experimental.pallas import tpu as pltpu
from jax.sharding import PartitionSpec as P

f32, bf16, i32 = jnp.float32, jnp.bfloat16, jnp.int32
HBM = pl.BlockSpec(memory_space=pltpu.HBM)
SMEM = pl.BlockSpec(memory_space=pltpu.SMEM)
VMEM = pl.BlockSpec(memory_space=pltpu.VMEM)
LIMIT = 12 * 1024 * 1024


def slot_ranks(owner):
    count = owner.shape[0]
    order = jnp.arange(count, dtype=jnp.int32)
    same = (owner[:, None] == owner[None, :]) & (order[None, :] < order[:, None])
    return jnp.sum(same.astype(jnp.int32), axis=1)


def by_requests(blocks, vir_energy, occ_energy, domain_size, partner_owner, partner_slot):
    occ_dev, half_aux, nvd = blocks.shape
    pair_dev = partner_slot.shape[0]
    per_orb = pair_dev // occ_dev
    peers = lax.axis_size("orb")
    cap = max(2, (pair_dev + peers - 1) // peers)
    owner = partner_owner[:, 0]
    ranks = slot_ranks(owner)
    target = owner * cap + ranks
    wanted = (target[:, None] == jnp.arange(peers * cap, dtype=jnp.int32)[None, :]).astype(
        jnp.int32
    )
    requests = jnp.sum(wanted * partner_slot[:, None], axis=0).reshape(peers, cap)
    incoming = lax.all_to_all(requests, "orb", split_axis=0, concat_axis=0, tiled=True)
    flat_in = incoming.reshape(-1)
    send_blocks = jnp.take(blocks, flat_in, axis=0).reshape(peers, cap, half_aux, nvd)
    send_vir = jnp.take(vir_energy, flat_in, axis=0).reshape(peers, cap, nvd)
    send_occ = jnp.take(occ_energy, flat_in).reshape(peers, cap)
    send_size = jnp.take(domain_size, flat_in).astype(jnp.float32).reshape(peers, cap)
    got_blocks = lax.all_to_all(send_blocks, "orb", split_axis=0, concat_axis=0, tiled=True)
    got_vir, got_occ, got_size = (
        lax.all_to_all(send_vir, "orb", split_axis=0, concat_axis=0, tiled=True),
        lax.all_to_all(send_occ, "orb", split_axis=0, concat_axis=0, tiled=True),
        lax.all_to_all(send_size, "orb", split_axis=0, concat_axis=0, tiled=True),
    )
    partner = jnp.take(got_blocks.reshape(peers * cap, half_aux, nvd), target, axis=0).reshape(
        occ_dev, per_orb, half_aux, nvd
    )
    partner_vir = jnp.take(got_vir.reshape(peers * cap, nvd), target, axis=0).reshape(
        occ_dev, per_orb, nvd
    )
    partner_occ = jnp.take(got_occ.reshape(-1), target).reshape(occ_dev, per_orb)
    partner_size = jnp.take(got_size.reshape(-1), target).reshape(occ_dev, per_orb)
    half = nvd // lax.axis_size("aux")
    integrals = lax.psum_scatter(
        jnp.einsum("oqa,opqb->aopb", blocks, partner, preferred_element_type=jnp.float32),
        "aux",
        scatter_dimension=0,
        tiled=True,
    )
    row_start = lax.axis_index("aux") * half
    rows = row_start + jnp.arange(half, dtype=jnp.int32)
    cols = jnp.arange(nvd, dtype=jnp.int32).astype(jnp.float32)
    mask = (rows[:, None, None, None] < domain_size[None, :, None, None]) & (
        cols[None, None, None, :] < partner_size[None, :, :, None]
    )
    integrals = jnp.where(mask, integrals, jnp.zeros_like(integrals))
    vir_rows = lax.dynamic_slice_in_dim(vir_energy, row_start, half, 1)
    gap = (
        vir_rows.T[:, :, None, None]
        + partner_vir[None, :, :, :]
        - occ_energy[None, :, None, None]
        - partner_occ[None, :, :, None]
    )
    amp_rows = (-integrals / gap).astype(jnp.bfloat16)
    partial_energy = jnp.sum(integrals * amp_rows.astype(jnp.float32), axis=(0, 3))
    energy = lax.psum(partial_energy, "aux").reshape(pair_dev) / nvd
    density = jnp.einsum(
        "aopb,copb->oac",
        amp_rows,
        lax.all_gather(amp_rows, "aux", axis=0, tiled=True),
        preferred_element_type=jnp.float32,
    )
    return (energy, density)


def fits_line(mesh):
    return mesh.shape["orb"] == 8 and mesh.shape["aux"] == 2


TINY = pl.CostEstimate(flops=1, bytes_accessed=1, transcendentals=0)
PARAMS = pltpu.CompilerParams(vmem_limit_bytes=LIMIT)
LIGHT = pltpu.CompilerParams(vmem_limit_bytes=LIMIT // 4)


def lists_kernel(cap, vir, occ, size, owner, slot, small, hit):
    n, (count, nvd) = hit.shape[0], vir.shape

    def column(row, m):
        eye = lax.broadcasted_iota(i32, (m, m), 0) == lax.broadcasted_iota(i32, (m, m), 1)
        return jnp.sum(jnp.where(eye, row, 0.0), axis=1, keepdims=True)

    down = lax.broadcasted_iota(i32, (n, n), 0).astype(f32)
    along = lax.broadcasted_iota(i32, (n, n), 1).astype(f32)
    owner_row = owner[...].astype(f32)
    owner_col = column(owner_row, n)
    before = (owner_col == owner_row) & (along < down)
    target = owner_col * cap + jnp.sum(jnp.where(before, 1.0, 0.0), axis=1, keepdims=True)
    found = target == along
    hit[...] = jnp.where(found, 1.0, 0.0)
    small[...] = jnp.zeros_like(small)
    small[:count, :nvd] = vir[...]
    lane = lax.broadcasted_iota(i32, (count, 128), 1)
    occ_col, size_col = column(occ[...], count), column(size[...].astype(f32), count)
    small[:count, nvd:] = jnp.where(lane == 0, occ_col, jnp.where(lane == 1, size_col, 0.0))
    small[count : count + 1, :n] = jnp.sum(jnp.where(found, down, 0.0), axis=0, keepdims=True)
    slot_col = column(slot[...].astype(f32), n)
    small[count : count + 1, 128 : 128 + n] = jnp.sum(
        jnp.where(found, slot_col, 0.0), axis=0, keepdims=True
    )


def lists(vir, occ, size, owner, slot, cap):
    count, nvd = vir.shape
    n = slot.shape[0]
    return pl.pallas_call(
        lambda *refs: lists_kernel(cap, *refs),
        out_shape=(
            jax.ShapeDtypeStruct((count + 8, nvd + 128), f32),
            jax.ShapeDtypeStruct((n, n), f32),
        ),
        in_specs=[VMEM] * 5,
        out_specs=(VMEM, VMEM),
        compiler_params=PARAMS,
        cost_estimate=TINY,
        name="lists",
    )(vir, occ.reshape(1, -1), size.reshape(1, -1), owner.reshape(1, -1), slot.reshape(1, -1))


ORDER, SLOT, SIZE_I, SIZE_J, HEAD = range(5)
MIDDLE, COLUMN = 8, 9


def pick(one, values):
    return lax.dot_general(
        one, values, (((0,), (0,)), ((), ())),
        precision=lax.Precision.HIGHEST, preferred_element_type=f32,
    )


def tables_kernel(cap, per_orb, meta, *refs):
    smalls, outs = refs[:8], refs[8:]
    count, nvd = smalls[0].shape[0] - 8, smalls[0].shape[1] - 128
    n = 8 * cap
    me, col0 = meta[0], meta[1]
    z, y = me // 2, me % 2
    lower = z < 2
    middle = jnp.where((z == 1) | (z == 2), 1, 0)
    places = [z, z ^ 1, jnp.where(lower, 2, 1), jnp.where(lower, 3, 0)]
    head = [(2 * p + y) * cap for p in places] + [(2 * p + 1 - y) * cap for p in places]
    lane = lax.broadcasted_iota(i32, (1, 128), 1)
    head_row = jnp.zeros((1, 128), i32)
    for k, value in enumerate(head + [middle, col0]):
        head_row = jnp.where(lane == k, value, head_row)
    orbitals = jnp.concatenate([x[:count, :] for x in smalls], axis=0)
    columns = jnp.where(col0 == 0, orbitals[:, : nvd // 2], orbitals[:, nvd // 2 : nvd])
    extra = orbitals[:, nvd:]

    def build(x, tbl, rows=None):
        order = smalls[x][count : count + 1, :n].astype(i32)
        slots = smalls[x][count : count + 1, 128 : 128 + n].astype(i32)
        tbl[...] = jnp.zeros_like(tbl)
        tbl[HEAD : HEAD + 1, :] = head_row
        tbl[SLOT : SLOT + 1, :n] = slots
        if rows is None:
            return
        tbl[ORDER : ORDER + 1, :n] = order
        pair = lax.broadcasted_iota(i32, (1, n), 1)
        owner = sum(jnp.where(pair >= k * cap, 1, 0) for k in range(1, 8))
        index = (owner ^ me) * count + slots
        theirs = jnp.where(lax.broadcasted_iota(i32, (8 * count, n), 0) == index, 1.0, 0.0)
        first = sum(jnp.where(order >= k * per_orb, 1, 0) for k in range(1, count))
        mine = jnp.where(lax.broadcasted_iota(i32, (count, n), 0) == first, 1.0, 0.0)
        own = smalls[x][:count, nvd:]
        rows[...] = pick(theirs, columns) - (pick(theirs, extra)[:, :1] + pick(mine, own)[:, :1])
        tbl[SIZE_I : SIZE_I + 1, :n] = pick(own, mine)[1:2, :].astype(i32)
        tbl[SIZE_J : SIZE_J + 1, :n] = pick(extra, theirs)[1:2, :].astype(i32) - col0

    build(0, outs[0], outs[1])
    build(2, outs[2], outs[3])
    build(1, outs[4])
    build(3, outs[5])


def tables_of(meta, smalls, cap, per_orb, half):
    table = jax.ShapeDtypeStruct((8, 128), i32)
    rows = jax.ShapeDtypeStruct((8 * cap, half), f32)
    return pl.pallas_call(
        lambda *refs: tables_kernel(cap, per_orb, *refs),
        out_shape=(table, rows, table, rows, table, table),
        in_specs=[SMEM] + [VMEM] * 8,
        out_specs=[VMEM] * 6,
        compiler_params=LIGHT,
        cost_estimate=TINY,
        name="tables",
    )(meta, *smalls)


def pack_kernel(jobs, tables, *refs):
    tbls, rest = refs[:tables], refs[tables:]
    outs = refs[-len(jobs) :]
    middle = tbls[0][HEAD, MIDDLE] == 1

    def gather(out, sources, tbl, call):
        base = tbl[HEAD, call]
        for q in range(out.shape[0]):
            for r in range(out.shape[1]):
                out[q, r] = sources[q][tbl[SLOT, base + r]]

    for out, (table, call, halves, only_middle) in zip(outs, jobs):
        sources, rest = rest[:halves], rest[halves:]
        if only_middle:
            pl.when(middle)(functools.partial(gather, out, sources, tbls[table], call))
        else:
            gather(out, sources, tbls[table], call)


def pack(tbls, jobs, cap, after=()):
    operands = [x for _, _, sources, _ in jobs for x in sources]
    kinds = [(table, call, len(sources), middle) for table, call, sources, middle in jobs]
    block = operands[0].shape[1:]
    return pl.pallas_call(
        lambda *refs: pack_kernel(kinds, len(tbls), *refs),
        out_shape=[jax.ShapeDtypeStruct((k[2], cap) + block, bf16) for k in kinds],
        in_specs=[SMEM] * len(tbls) + [VMEM] * len(operands) + [HBM] * len(after),
        out_specs=[VMEM] * len(jobs),
        compiler_params=LIGHT,
        cost_estimate=TINY,
        name="pack",
    )(*tbls, *operands, *after)


def turn_kernel(*refs):
    half = len(refs) // 2
    for x, out in zip(refs[:half], refs[half:]):
        for r in range(x.shape[0]):
            out[r] = x[r].T


def turn(arrays):
    count, rows, cols = arrays[0].shape
    step = 4 if count % 4 == 0 else 1
    n = len(arrays)
    return pl.pallas_call(
        turn_kernel,
        out_shape=[jax.ShapeDtypeStruct((count, cols, rows), bf16)] * n,
        grid=(count // step,),
        in_specs=[pl.BlockSpec((step, rows, cols), lambda i: (i, 0, 0))] * n,
        out_specs=[pl.BlockSpec((step, cols, rows), lambda i: (i, 0, 0))] * n,
        compiler_params=PARAMS,
        cost_estimate=TINY,
        name="turn",
    )(*arrays)


def amplitudes_kernel(mode, call, per_orb, groups, tbl, rows, vcol, *refs):
    client = mode == "client"
    if client:
        tout = refs[-1]
        left, rest = refs[:4], refs[4:]
    else:
        tout, eout = refs[-2:]
        left, rest = refs[:2], refs[2:]
    places = []
    for arrays in groups:
        if arrays == 1:
            places.append([rest[0].at[0], rest[0].at[1]])
        elif len(rest[0].shape) == 4:
            places.append([rest[0].at[0], rest[1].at[0]])
        else:
            places.append(rest[:2])
        rest = rest[arrays:]
    cap = rows.shape[0] // 8
    nvd, half = vcol.shape[1:]
    base = pl.multiple_of(tbl[HEAD, call], cap)
    middle = tbl[HEAD, MIDDLE] == 1
    row8 = rows[pl.ds(base, cap), :]

    def gap(r, i):
        return vcol[i] + row8[r : r + 1, :]

    def make(r):
        p = tbl[ORDER, base + r]
        i = lax.div(p, per_orb)
        slot = r if mode == "asked" else tbl[SLOT, base + r]
        b0, b1 = [x[slot] for x in places[0]]
        if len(places) == 2:
            b0, b1 = [jnp.where(middle, b, x[slot]) for b, x in zip((b0, b1), places[1])]

        def product(x0, x1):
            return jnp.dot(x0[i], b0, preferred_element_type=f32) + jnp.dot(
                x1[i], b1, preferred_element_type=f32
            )

        if client:
            here, there = product(left[0], left[1]), product(left[3], left[2])
            first = tbl[HEAD, COLUMN] == 0
            k = jnp.concatenate(
                [jnp.where(first, here, there), jnp.where(first, there, here)], axis=0
            )
        else:
            k = product(left[0], left[1])
        live_a = lax.broadcasted_iota(i32, (nvd, half), 0)
        live_b = lax.broadcasted_iota(i32, (nvd, half), 1)
        live = (live_a < tbl[SIZE_I, base + r]) & (live_b < tbl[SIZE_J, base + r])
        k = jnp.where(live, k, 0.0)
        t = (-k / gap(r, i)).astype(bf16)
        if client:
            tout[r] = t
            return None
        tout[p] = t
        return jnp.sum(k * t.astype(f32), axis=0, keepdims=True)

    def take(r):
        p = tbl[ORDER, base + r]
        ready = rest[0][r]
        tout[p] = ready
        t = ready.astype(f32)
        return -jnp.sum(t * t * gap(r, lax.div(p, per_orb)), axis=0, keepdims=True)

    def each(step):
        parts = [step(r) for r in range(cap)]
        if not client:
            eout[pl.ds(base, cap), :] = jnp.concatenate(parts, axis=0)

    if mode == "served":
        pl.when(middle)(lambda: each(make))
        pl.when(jnp.logical_not(middle))(lambda: each(take))
    elif client:
        pl.when(middle)(lambda: each(make))
    else:
        each(make)


def amplitudes(mode, call, per_orb, tables, left, groups, cap, held=(), after=(), ready=()):
    tbl, rows, vcol = tables
    occ, nvd, half = vcol.shape
    client = mode == "client"
    sources = [x for group in groups for x in group]
    blocks = (rows, vcol, *left, *sources, *ready)
    operands = (tbl, *blocks, *after)
    aliases = {len(operands) + k: k for k in range(len(held))}
    if client:
        out_shape = jax.ShapeDtypeStruct((cap, nvd, half), bf16)
        out_specs = VMEM
    else:
        out_shape = (
            jax.ShapeDtypeStruct((occ * per_orb, nvd, half), bf16),
            jax.ShapeDtypeStruct((occ * per_orb, half), f32),
        )
        out_specs = (VMEM, VMEM)
    return pl.pallas_call(
        lambda *refs: amplitudes_kernel(mode, call, per_orb, [len(g) for g in groups], *refs),
        out_shape=out_shape,
        in_specs=[SMEM] + [VMEM] * len(blocks) + [HBM] * len(after) + [VMEM] * len(held),
        out_specs=out_specs,
        input_output_aliases=aliases,
        compiler_params=LIGHT,
        cost_estimate=TINY,
        name="amplitudes",
    )(*operands, *held)


def density_kernel(start, t, mine, away):
    count, half = mine.shape[:2]
    per_orb = t.shape[0] // count
    first = pl.multiple_of(start[0], half)
    for o in range(count):
        own = range(o * per_orb, (o + 1) * per_orb)
        right = jnp.concatenate([t[k] for k in own], axis=1)
        for out, row in ((away, pl.multiple_of(half - first, half)), (mine, first)):
            left = jnp.concatenate([t[k, pl.ds(row, half), :] for k in own], axis=1)
            out[o] = lax.dot_general(
                left, right, (((1,), (1,)), ((), ())), preferred_element_type=f32
            )


def densities(t_all, start, per_orb, half):
    npair, nvd, _ = t_all.shape
    shape = jax.ShapeDtypeStruct((npair // per_orb, half, nvd), f32)
    return pl.pallas_call(
        density_kernel,
        out_shape=(shape, shape),
        in_specs=[SMEM, VMEM],
        out_specs=(VMEM, VMEM),
        compiler_params=LIGHT,
        cost_estimate=TINY,
        name="densities",
    )(start.reshape(1), t_all)


def line_plan(blocks, vir_energy, occ_energy, domain_size, partner_owner, partner_slot):
    occ, qa, nvd = blocks.shape
    pair_dev = partner_slot.shape[0]
    per_orb = pair_dev // occ
    peers = 8
    cap = pair_dev // peers
    half = nvd // 2
    me, core = lax.axis_index("orb"), lax.axis_index("aux")
    col0 = core * half

    def pp(x, perm):
        return lax.ppermute(x, "orb", perm)

    def swap_core(x):
        return lax.ppermute(x, "aux", [(0, 1), (1, 0)])

    def flip(bits):
        return [(o, o ^ bits) for o in range(peers)]

    cross = [(2, 4), (3, 5), (4, 2), (5, 3)]
    outward = [(2, 0), (3, 1), (4, 6), (5, 7)]
    diagonal = [(2, 1), (3, 0), (4, 7), (5, 6)]
    y_middle = [(2, 3), (3, 2), (4, 5), (5, 4)]

    small, hit = lists(vir_energy, occ_energy, domain_size, partner_owner, partner_slot, cap)
    smalls = [small] + [pp(small, flip(bits)) for bits in range(1, peers)]

    other = swap_core(blocks)
    own = [lax.dynamic_slice_in_dim(x, col0, half, 2) for x in (blocks, other)]
    sent, smalls = lax.optimization_barrier((own[0], smalls))
    mid = [pp(x, cross) for x in (sent, own[1])]
    near = [pp(x, flip(2)) for x in (sent, own[1])]
    tbl, rows, client_tbl, client_rows, beside_list, relay_list = tables_of(
        jnp.stack([me, col0]), smalls, cap, per_orb, half
    )
    lists_of = [beside_list, relay_list]

    def spread(vir):
        return jnp.broadcast_to(vir[:, :, None], (occ, nvd, half))

    tables = (tbl, rows, spread(vir_energy))
    client = (client_tbl, client_rows, spread(smalls[2][:occ, :nvd]))

    def own_pairs(k, mode, groups, held=(), after=(), ready=()):
        return amplitudes(mode, k, per_orb, tables, left, groups, cap, held, after, ready)

    (packed,) = pack(lists_of, [(0, 0, own, False)], cap)
    beside = pp(packed, flip(1))
    left = turn([blocks, other])
    held = own_pairs(0, "slots", [own], after=(packed, mid[0]))
    first, held = lax.optimization_barrier((near[0], held))
    far = [pp(first, cross)]
    across = [swap_core(first)]
    (packed,) = pack(lists_of, [(0, 1, [first], False)], cap, after=(held[1], mid[0]))
    beside_near = [pp(packed, flip(1))]
    held = own_pairs(4, "asked", [[beside]], held, (packed, beside_near[0]))
    second, held = lax.optimization_barrier((near[1], held))
    far.append(pp(second, cross))
    across.append(swap_core(second))
    near = [first, second]
    packed = pack(lists_of, [(1, 2, mid, True), (0, 2, mid, True)], cap, after=(held[1],))
    third_diagonal, third = pp(packed[0], diagonal), pp(packed[1], y_middle)
    (packed,) = pack(lists_of, [(0, 1, [second], False)], cap, after=(packed[0],))
    beside_near.append(pp(packed, flip(1)))
    client_left = turn(near + across)
    gone = amplitudes("client", 2, per_orb, client, client_left, [mid], cap, after=(packed,))
    ready_2 = pp(gone, outward)
    held = own_pairs(1, "slots", [near], held, (gone, third_diagonal))
    jobs = [(1, 3, far[:1], True), (0, 3, far[:1], True)]
    packed = pack(lists_of, jobs, cap, after=(held[1],))
    fourth_diagonal, fourth = [pp(packed[0], diagonal)], [pp(packed[1], y_middle)]
    held = own_pairs(2, "served", [mid], held, (packed[0],), (ready_2,))
    held = own_pairs(5, "asked", [beside_near], held)
    (packed,) = pack(lists_of, [(1, 3, far[1:], True)], cap, after=(held[1],))
    fourth_diagonal.append(pp(packed, diagonal))
    gone = amplitudes("client", 3, per_orb, client, client_left, [far], cap, after=(packed,))
    ready_3 = pp(gone, outward)
    (packed,) = pack(
        lists_of, [(0, 3, far[1:], True)], cap, after=(gone,)
    )
    fourth.append(pp(packed, y_middle))
    held = own_pairs(
        6, "asked", [[third], [third_diagonal]], held, (packed, fourth[0], fourth_diagonal[0])
    )
    held = own_pairs(3, "served", [far], held, (fourth_diagonal[1],), (ready_3,))
    t_all, e_all = own_pairs(7, "asked", [fourth, fourth_diagonal], held)

    mine, away = densities(t_all, col0, per_orb, half)
    density = mine + swap_core(away)

    energy = jnp.sum(hit * jnp.sum(e_all, axis=1)[None, :], axis=1)
    energy = (energy + swap_core(energy)) / nvd
    return (energy, density)


def solution(mesh):
    in_specs = (
        P(("mol", "orb"), "aux", None),
        P(("mol", "orb"), None),
        P(("mol", "orb")),
        P(("mol", "orb")),
        P(("mol", "orb"), None),
        P(("mol", "orb")),
    )
    out_specs = (P(("mol", "orb")), P(("mol", "orb"), "aux", None))
    return jax.shard_map(
        line_plan if fits_line(mesh) else by_requests, mesh=mesh, in_specs=in_specs, out_specs=out_specs, check_vma=False
    )
```

```python
import functools

import jax
import jax.numpy as jnp
from jax import lax
from jax.experimental import pallas as pl
from jax.experimental.pallas import tpu as pltpu
from jax.sharding import PartitionSpec as P

f32, bf16, i32 = jnp.float32, jnp.bfloat16, jnp.int32
HBM = pl.BlockSpec(memory_space=pltpu.HBM)
SMEM = pl.BlockSpec(memory_space=pltpu.SMEM)
VMEM = pl.BlockSpec(memory_space=pltpu.VMEM)
LIMIT = 12 * 1024 * 1024


def slot_ranks(owner):
    count = owner.shape[0]
    order = jnp.arange(count, dtype=jnp.int32)
    same = (owner[:, None] == owner[None, :]) & (order[None, :] < order[:, None])
    return jnp.sum(same.astype(jnp.int32), axis=1)


def by_requests(blocks, vir_energy, occ_energy, domain_size, partner_owner, partner_slot):
    occ_dev, half_aux, nvd = blocks.shape
    pair_dev = partner_slot.shape[0]
    per_orb = pair_dev // occ_dev
    peers = lax.axis_size("orb")
    cap = max(2, (pair_dev + peers - 1) // peers)
    owner = partner_owner[:, 0]
    ranks = slot_ranks(owner)
    target = owner * cap + ranks
    wanted = (target[:, None] == jnp.arange(peers * cap, dtype=jnp.int32)[None, :]).astype(
        jnp.int32
    )
    requests = jnp.sum(wanted * partner_slot[:, None], axis=0).reshape(peers, cap)
    incoming = lax.all_to_all(requests, "orb", split_axis=0, concat_axis=0, tiled=True)
    flat_in = incoming.reshape(-1)
    send_blocks = jnp.take(blocks, flat_in, axis=0).reshape(peers, cap, half_aux, nvd)
    send_vir = jnp.take(vir_energy, flat_in, axis=0).reshape(peers, cap, nvd)
    send_occ = jnp.take(occ_energy, flat_in).reshape(peers, cap)
    send_size = jnp.take(domain_size, flat_in).astype(jnp.float32).reshape(peers, cap)
    got_blocks = lax.all_to_all(send_blocks, "orb", split_axis=0, concat_axis=0, tiled=True)
    got_vir, got_occ, got_size = (
        lax.all_to_all(send_vir, "orb", split_axis=0, concat_axis=0, tiled=True),
        lax.all_to_all(send_occ, "orb", split_axis=0, concat_axis=0, tiled=True),
        lax.all_to_all(send_size, "orb", split_axis=0, concat_axis=0, tiled=True),
    )
    partner = jnp.take(got_blocks.reshape(peers * cap, half_aux, nvd), target, axis=0).reshape(
        occ_dev, per_orb, half_aux, nvd
    )
    partner_vir = jnp.take(got_vir.reshape(peers * cap, nvd), target, axis=0).reshape(
        occ_dev, per_orb, nvd
    )
    partner_occ = jnp.take(got_occ.reshape(-1), target).reshape(occ_dev, per_orb)
    partner_size = jnp.take(got_size.reshape(-1), target).reshape(occ_dev, per_orb)
    half = nvd // lax.axis_size("aux")
    integrals = lax.psum_scatter(
        jnp.einsum("oqa,opqb->aopb", blocks, partner, preferred_element_type=jnp.float32),
        "aux",
        scatter_dimension=0,
        tiled=True,
    )
    row_start = lax.axis_index("aux") * half
    rows = row_start + jnp.arange(half, dtype=jnp.int32)
    cols = jnp.arange(nvd, dtype=jnp.int32).astype(jnp.float32)
    mask = (rows[:, None, None, None] < domain_size[None, :, None, None]) & (
        cols[None, None, None, :] < partner_size[None, :, :, None]
    )
    integrals = jnp.where(mask, integrals, jnp.zeros_like(integrals))
    vir_rows = lax.dynamic_slice_in_dim(vir_energy, row_start, half, 1)
    gap = (
        vir_rows.T[:, :, None, None]
        + partner_vir[None, :, :, :]
        - occ_energy[None, :, None, None]
        - partner_occ[None, :, :, None]
    )
    amp_rows = (-integrals / gap).astype(jnp.bfloat16)
    partial_energy = jnp.sum(integrals * amp_rows.astype(jnp.float32), axis=(0, 3))
    energy = lax.psum(partial_energy, "aux").reshape(pair_dev) / nvd
    density = jnp.einsum(
        "aopb,copb->oac",
        amp_rows,
        lax.all_gather(amp_rows, "aux", axis=0, tiled=True),
        preferred_element_type=jnp.float32,
    )
    return (energy, density)


def fits_line(mesh):
    return mesh.shape["orb"] == 8 and mesh.shape["aux"] == 2


TINY = pl.CostEstimate(flops=1, bytes_accessed=1, transcendentals=0)
PARAMS = pltpu.CompilerParams(vmem_limit_bytes=LIMIT)
LIGHT = pltpu.CompilerParams(vmem_limit_bytes=LIMIT // 4)


def lists_kernel(cap, vir, occ, size, owner, slot, small, hit):
    n, (count, nvd) = hit.shape[0], vir.shape

    def column(row, m):
        eye = lax.broadcasted_iota(i32, (m, m), 0) == lax.broadcasted_iota(i32, (m, m), 1)
        return jnp.sum(jnp.where(eye, row, 0.0), axis=1, keepdims=True)

    down = lax.broadcasted_iota(i32, (n, n), 0).astype(f32)
    along = lax.broadcasted_iota(i32, (n, n), 1).astype(f32)
    owner_row = owner[...].astype(f32)
    owner_col = column(owner_row, n)
    before = (owner_col == owner_row) & (along < down)
    target = owner_col * cap + jnp.sum(jnp.where(before, 1.0, 0.0), axis=1, keepdims=True)
    found = target == along
    hit[...] = jnp.where(found, 1.0, 0.0)
    small[...] = jnp.zeros_like(small)
    small[:count, :nvd] = vir[...]
    lane = lax.broadcasted_iota(i32, (count, 128), 1)
    occ_col, size_col = column(occ[...], count), column(size[...].astype(f32), count)
    small[:count, nvd:] = jnp.where(lane == 0, occ_col, jnp.where(lane == 1, size_col, 0.0))
    small[count : count + 1, :n] = jnp.sum(jnp.where(found, down, 0.0), axis=0, keepdims=True)
    slot_col = column(slot[...].astype(f32), n)
    small[count : count + 1, 128 : 128 + n] = jnp.sum(
        jnp.where(found, slot_col, 0.0), axis=0, keepdims=True
    )


def lists(vir, occ, size, owner, slot, cap):
    count, nvd = vir.shape
    n = slot.shape[0]
    return pl.pallas_call(
        lambda *refs: lists_kernel(cap, *refs),
        out_shape=(
            jax.ShapeDtypeStruct((count + 8, nvd + 128), f32),
            jax.ShapeDtypeStruct((n, n), f32),
        ),
        in_specs=[VMEM] * 5,
        out_specs=(VMEM, VMEM),
        compiler_params=PARAMS,
        cost_estimate=TINY,
        name="lists",
    )(vir, occ.reshape(1, -1), size.reshape(1, -1), owner.reshape(1, -1), slot.reshape(1, -1))


ORDER, SLOT, SIZE_I, SIZE_J, HEAD = range(5)
MIDDLE, COLUMN = 8, 9


def pick(one, values):
    return lax.dot_general(
        one, values, (((0,), (0,)), ((), ())),
        precision=lax.Precision.HIGHEST, preferred_element_type=f32,
    )


def tables_kernel(cap, per_orb, meta, *refs):
    smalls, outs = refs[:8], refs[8:]
    count, nvd = smalls[0].shape[0] - 8, smalls[0].shape[1] - 128
    n = 8 * cap
    me, col0 = meta[0], meta[1]
    z, y = me // 2, me % 2
    lower = z < 2
    middle = jnp.where((z == 1) | (z == 2), 1, 0)
    places = [z, z ^ 1, jnp.where(lower, 2, 1), jnp.where(lower, 3, 0)]
    head = [(2 * p + y) * cap for p in places] + [(2 * p + 1 - y) * cap for p in places]
    lane = lax.broadcasted_iota(i32, (1, 128), 1)
    head_row = jnp.zeros((1, 128), i32)
    for k, value in enumerate(head + [middle, col0]):
        head_row = jnp.where(lane == k, value, head_row)
    orbitals = jnp.concatenate([x[:count, :] for x in smalls], axis=0)
    columns = jnp.where(col0 == 0, orbitals[:, : nvd // 2], orbitals[:, nvd // 2 : nvd])
    extra = orbitals[:, nvd:]

    def build(x, tbl, rows=None):
        order = smalls[x][count : count + 1, :n].astype(i32)
        slots = smalls[x][count : count + 1, 128 : 128 + n].astype(i32)
        tbl[...] = jnp.zeros_like(tbl)
        tbl[HEAD : HEAD + 1, :] = head_row
        tbl[SLOT : SLOT + 1, :n] = slots
        if rows is None:
            return
        tbl[ORDER : ORDER + 1, :n] = order
        pair = lax.broadcasted_iota(i32, (1, n), 1)
        owner = sum(jnp.where(pair >= k * cap, 1, 0) for k in range(1, 8))
        index = (owner ^ me) * count + slots
        theirs = jnp.where(lax.broadcasted_iota(i32, (8 * count, n), 0) == index, 1.0, 0.0)
        first = sum(jnp.where(order >= k * per_orb, 1, 0) for k in range(1, count))
        mine = jnp.where(lax.broadcasted_iota(i32, (count, n), 0) == first, 1.0, 0.0)
        own = smalls[x][:count, nvd:]
        rows[...] = pick(theirs, columns) - (pick(theirs, extra)[:, :1] + pick(mine, own)[:, :1])
        tbl[SIZE_I : SIZE_I + 1, :n] = pick(own, mine)[1:2, :].astype(i32)
        tbl[SIZE_J : SIZE_J + 1, :n] = pick(extra, theirs)[1:2, :].astype(i32) - col0

    build(0, outs[0], outs[1])
    build(2, outs[2], outs[3])
    build(1, outs[4])
    build(3, outs[5])


def tables_of(meta, smalls, cap, per_orb, half):
    table = jax.ShapeDtypeStruct((8, 128), i32)
    rows = jax.ShapeDtypeStruct((8 * cap, half), f32)
    return pl.pallas_call(
        lambda *refs: tables_kernel(cap, per_orb, *refs),
        out_shape=(table, rows, table, rows, table, table),
        in_specs=[SMEM] + [VMEM] * 8,
        out_specs=[VMEM] * 6,
        compiler_params=LIGHT,
        cost_estimate=TINY,
        name="tables",
    )(meta, *smalls)


def pack_kernel(jobs, tables, *refs):
    tbls, rest = refs[:tables], refs[tables:]
    outs = refs[-len(jobs) :]
    middle = tbls[0][HEAD, MIDDLE] == 1

    def gather(out, sources, tbl, call):
        base = tbl[HEAD, call]
        for q in range(out.shape[0]):
            for r in range(out.shape[1]):
                out[q, r] = sources[q][tbl[SLOT, base + r]]

    for out, (table, call, halves, only_middle) in zip(outs, jobs):
        sources, rest = rest[:halves], rest[halves:]
        if only_middle:
            pl.when(middle)(functools.partial(gather, out, sources, tbls[table], call))
        else:
            gather(out, sources, tbls[table], call)


def pack(tbls, jobs, cap, after=()):
    operands = [x for _, _, sources, _ in jobs for x in sources]
    kinds = [(table, call, len(sources), middle) for table, call, sources, middle in jobs]
    block = operands[0].shape[1:]
    return pl.pallas_call(
        lambda *refs: pack_kernel(kinds, len(tbls), *refs),
        out_shape=[jax.ShapeDtypeStruct((k[2], cap) + block, bf16) for k in kinds],
        in_specs=[SMEM] * len(tbls) + [VMEM] * len(operands) + [HBM] * len(after),
        out_specs=[VMEM] * len(jobs),
        compiler_params=LIGHT,
        cost_estimate=TINY,
        name="pack",
    )(*tbls, *operands, *after)


def turn_kernel(*refs):
    half = len(refs) // 2
    for x, out in zip(refs[:half], refs[half:]):
        for r in range(x.shape[0]):
            out[r] = x[r].T


def turn(arrays):
    count, rows, cols = arrays[0].shape
    step = 4 if count % 4 == 0 else 1
    n = len(arrays)
    return pl.pallas_call(
        turn_kernel,
        out_shape=[jax.ShapeDtypeStruct((count, cols, rows), bf16)] * n,
        grid=(count // step,),
        in_specs=[pl.BlockSpec((step, rows, cols), lambda i: (i, 0, 0))] * n,
        out_specs=[pl.BlockSpec((step, cols, rows), lambda i: (i, 0, 0))] * n,
        compiler_params=PARAMS,
        cost_estimate=TINY,
        name="turn",
    )(*arrays)


def amplitudes_kernel(mode, call, per_orb, groups, tbl, rows, vcol, *refs):
    client = mode == "client"
    if client:
        tout = refs[-1]
        left, rest = refs[:4], refs[4:]
    else:
        tout, eout = refs[-2:]
        left, rest = refs[:2], refs[2:]
    places = []
    for arrays in groups:
        if arrays == 1:
            places.append([rest[0].at[0], rest[0].at[1]])
        elif len(rest[0].shape) == 4:
            places.append([rest[0].at[0], rest[1].at[0]])
        else:
            places.append(rest[:2])
        rest = rest[arrays:]
    cap = rows.shape[0] // 8
    nvd, half = vcol.shape[1:]
    base = pl.multiple_of(tbl[HEAD, call], cap)
    middle = tbl[HEAD, MIDDLE] == 1
    row8 = rows[pl.ds(base, cap), :]

    def gap(r, i):
        return vcol[i] + row8[r : r + 1, :]

    def make(r):
        p = tbl[ORDER, base + r]
        i = lax.div(p, per_orb)
        slot = r if mode == "asked" else tbl[SLOT, base + r]
        b0, b1 = [x[slot] for x in places[0]]
        if len(places) == 2:
            b0, b1 = [jnp.where(middle, b, x[slot]) for b, x in zip((b0, b1), places[1])]

        def product(x0, x1):
            return jnp.dot(x0[i], b0, preferred_element_type=f32) + jnp.dot(
                x1[i], b1, preferred_element_type=f32
            )

        if client:
            here, there = product(left[0], left[1]), product(left[3], left[2])
            first = tbl[HEAD, COLUMN] == 0
            k = jnp.concatenate(
                [jnp.where(first, here, there), jnp.where(first, there, here)], axis=0
            )
        else:
            k = product(left[0], left[1])
        live_a = lax.broadcasted_iota(i32, (nvd, half), 0)
        live_b = lax.broadcasted_iota(i32, (nvd, half), 1)
        live = (live_a < tbl[SIZE_I, base + r]) & (live_b < tbl[SIZE_J, base + r])
        k = jnp.where(live, k, 0.0)
        t = (-k / gap(r, i)).astype(bf16)
        if client:
            tout[r] = t
            return None
        tout[p] = t
        return jnp.sum(k * t.astype(f32), axis=0, keepdims=True)

    def take(r):
        p = tbl[ORDER, base + r]
        ready = rest[0][r]
        tout[p] = ready
        t = ready.astype(f32)
        return -jnp.sum(t * t * gap(r, lax.div(p, per_orb)), axis=0, keepdims=True)

    def each(step):
        parts = [step(r) for r in range(cap)]
        if not client:
            eout[pl.ds(base, cap), :] = jnp.concatenate(parts, axis=0)

    if mode == "served":
        pl.when(middle)(lambda: each(make))
        pl.when(jnp.logical_not(middle))(lambda: each(take))
    elif client:
        pl.when(middle)(lambda: each(make))
    else:
        each(make)


def amplitudes(mode, call, per_orb, tables, left, groups, cap, held=(), after=(), ready=()):
    tbl, rows, vcol = tables
    occ, nvd, half = vcol.shape
    client = mode == "client"
    sources = [x for group in groups for x in group]
    blocks = (rows, vcol, *left, *sources, *ready)
    operands = (tbl, *blocks, *after)
    aliases = {len(operands) + k: k for k in range(len(held))}
    if client:
        out_shape = jax.ShapeDtypeStruct((cap, nvd, half), bf16)
        out_specs = VMEM
    else:
        out_shape = (
            jax.ShapeDtypeStruct((occ * per_orb, nvd, half), bf16),
            jax.ShapeDtypeStruct((occ * per_orb, half), f32),
        )
        out_specs = (VMEM, VMEM)
    return pl.pallas_call(
        lambda *refs: amplitudes_kernel(mode, call, per_orb, [len(g) for g in groups], *refs),
        out_shape=out_shape,
        in_specs=[SMEM] + [VMEM] * len(blocks) + [HBM] * len(after) + [VMEM] * len(held),
        out_specs=out_specs,
        input_output_aliases=aliases,
        compiler_params=LIGHT,
        cost_estimate=TINY,
        name="amplitudes",
    )(*operands, *held)


def density_kernel(start, t, mine, away):
    count, half = mine.shape[:2]
    per_orb = t.shape[0] // count
    first = pl.multiple_of(start[0], half)
    for o in range(count):
        own = range(o * per_orb, (o + 1) * per_orb)
        right = jnp.concatenate([t[k] for k in own], axis=1)
        for out, row in ((away, pl.multiple_of(half - first, half)), (mine, first)):
            left = jnp.concatenate([t[k, pl.ds(row, half), :] for k in own], axis=1)
            out[o] = lax.dot_general(
                left, right, (((1,), (1,)), ((), ())), preferred_element_type=f32
            ).astype(out.dtype)


def densities(t_all, start, per_orb, half):
    npair, nvd, _ = t_all.shape
    shape = jax.ShapeDtypeStruct((npair // per_orb, half, nvd), f32)
    return pl.pallas_call(
        density_kernel,
        out_shape=(shape, jax.ShapeDtypeStruct(shape.shape, bf16)),
        in_specs=[SMEM, VMEM],
        out_specs=(VMEM, VMEM),
        compiler_params=LIGHT,
        cost_estimate=TINY,
        name="densities",
    )(start.reshape(1), t_all)


def line_plan(blocks, vir_energy, occ_energy, domain_size, partner_owner, partner_slot):
    occ, qa, nvd = blocks.shape
    pair_dev = partner_slot.shape[0]
    per_orb = pair_dev // occ
    peers = 8
    cap = pair_dev // peers
    half = nvd // 2
    me, core = lax.axis_index("orb"), lax.axis_index("aux")
    col0 = core * half

    def pp(x, perm):
        return lax.ppermute(x, "orb", perm)

    def swap_core(x):
        return lax.ppermute(x, "aux", [(0, 1), (1, 0)])

    def flip(bits):
        return [(o, o ^ bits) for o in range(peers)]

    cross = [(2, 4), (3, 5), (4, 2), (5, 3)]
    outward = [(2, 0), (3, 1), (4, 6), (5, 7)]
    diagonal = [(2, 1), (3, 0), (4, 7), (5, 6)]
    y_middle = [(2, 3), (3, 2), (4, 5), (5, 4)]

    small, hit = lists(vir_energy, occ_energy, domain_size, partner_owner, partner_slot, cap)
    smalls = [small] + [pp(small, flip(bits)) for bits in range(1, peers)]

    other = swap_core(blocks)
    own = [lax.dynamic_slice_in_dim(x, col0, half, 2) for x in (blocks, other)]
    sent, smalls = lax.optimization_barrier((own[0], smalls))
    mid = [pp(x, cross) for x in (sent, own[1])]
    near = [pp(x, flip(2)) for x in (sent, own[1])]
    tbl, rows, client_tbl, client_rows, beside_list, relay_list = tables_of(
        jnp.stack([me, col0]), smalls, cap, per_orb, half
    )
    lists_of = [beside_list, relay_list]

    def spread(vir):
        return jnp.broadcast_to(vir[:, :, None], (occ, nvd, half))

    tables = (tbl, rows, spread(vir_energy))
    client = (client_tbl, client_rows, spread(smalls[2][:occ, :nvd]))

    def own_pairs(k, mode, groups, held=(), after=(), ready=()):
        return amplitudes(mode, k, per_orb, tables, left, groups, cap, held, after, ready)

    (packed,) = pack(lists_of, [(0, 0, own, False)], cap)
    beside = pp(packed, flip(1))
    left = turn([blocks, other])
    held = own_pairs(0, "slots", [own], after=(packed,))
    first, held = lax.optimization_barrier((near[0], held))
    far = [pp(first, cross)]
    across = [swap_core(first)]
    (packed,) = pack(lists_of, [(0, 1, [first], False)], cap, after=(held[1], mid[0]))
    beside_near = [pp(packed, flip(1))]
    held = own_pairs(4, "asked", [[beside]], held, (packed, beside_near[0]))
    second, held = lax.optimization_barrier((near[1], held))
    far.append(pp(second, cross))
    across.append(swap_core(second))
    near = [first, second]
    packed = pack(lists_of, [(1, 2, mid, True), (0, 2, mid, True)], cap, after=(held[1],))
    third_diagonal, third = pp(packed[0], diagonal), pp(packed[1], y_middle)
    (packed,) = pack(lists_of, [(0, 1, [second], False)], cap, after=(packed[0],))
    beside_near.append(pp(packed, flip(1)))
    client_left = turn(near + across)
    gone = amplitudes("client", 2, per_orb, client, client_left, [mid], cap, after=(packed,))
    ready_2 = pp(gone, outward)
    held = own_pairs(1, "slots", [near], held, (gone, third_diagonal))
    jobs = [(1, 3, far[:1], True), (0, 3, far[:1], True)]
    packed = pack(lists_of, jobs, cap, after=(held[1],))
    fourth_diagonal, fourth = [pp(packed[0], diagonal)], [pp(packed[1], y_middle)]
    held = own_pairs(2, "served", [mid], held, (packed[0],), (ready_2,))
    held = own_pairs(5, "asked", [beside_near], held)
    (packed,) = pack(lists_of, [(1, 3, far[1:], True)], cap, after=(held[1],))
    fourth_diagonal.append(pp(packed, diagonal))
    gone = amplitudes("client", 3, per_orb, client, client_left, [far], cap, after=(packed,))
    ready_3 = pp(gone, outward)
    (packed,) = pack(
        lists_of, [(0, 3, far[1:], True)], cap, after=(gone,)
    )
    fourth.append(pp(packed, y_middle))
    held = own_pairs(
        6, "asked", [[third], [third_diagonal]], held, (packed, fourth[0], fourth_diagonal[0])
    )
    held = own_pairs(3, "served", [far], held, (fourth_diagonal[1],), (ready_3,))
    t_all, e_all = own_pairs(7, "asked", [fourth, fourth_diagonal], held)

    mine, away = densities(t_all, col0, per_orb, half)
    density = mine + swap_core(away).astype(f32)

    energy = jnp.sum(hit * jnp.sum(e_all, axis=1)[None, :], axis=1)
    energy = (energy + swap_core(energy)) / nvd
    return (energy, density)


def solution(mesh):
    in_specs = (
        P(("mol", "orb"), "aux", None),
        P(("mol", "orb"), None),
        P(("mol", "orb")),
        P(("mol", "orb")),
        P(("mol", "orb"), None),
        P(("mol", "orb")),
    )
    out_specs = (P(("mol", "orb")), P(("mol", "orb"), "aux", None))
    return jax.shard_map(
        line_plan if fits_line(mesh) else by_requests, mesh=mesh, in_specs=in_specs, out_specs=out_specs, check_vma=False
    )
```

```python
import functools

import jax
import jax.numpy as jnp
from jax import lax
from jax.experimental import pallas as pl
from jax.experimental.pallas import tpu as pltpu
from jax.sharding import PartitionSpec as P

f32, bf16, i32 = jnp.float32, jnp.bfloat16, jnp.int32
HBM = pl.BlockSpec(memory_space=pltpu.HBM)
SMEM = pl.BlockSpec(memory_space=pltpu.SMEM)
VMEM = pl.BlockSpec(memory_space=pltpu.VMEM)
LIMIT = 12 * 1024 * 1024


def slot_ranks(owner):
    count = owner.shape[0]
    order = jnp.arange(count, dtype=jnp.int32)
    same = (owner[:, None] == owner[None, :]) & (order[None, :] < order[:, None])
    return jnp.sum(same.astype(jnp.int32), axis=1)


def by_requests(blocks, vir_energy, occ_energy, domain_size, partner_owner, partner_slot):
    occ_dev, half_aux, nvd = blocks.shape
    pair_dev = partner_slot.shape[0]
    per_orb = pair_dev // occ_dev
    peers = lax.axis_size("orb")
    cap = max(2, (pair_dev + peers - 1) // peers)
    owner = partner_owner[:, 0]
    ranks = slot_ranks(owner)
    target = owner * cap + ranks
    wanted = (target[:, None] == jnp.arange(peers * cap, dtype=jnp.int32)[None, :]).astype(
        jnp.int32
    )
    requests = jnp.sum(wanted * partner_slot[:, None], axis=0).reshape(peers, cap)
    incoming = lax.all_to_all(requests, "orb", split_axis=0, concat_axis=0, tiled=True)
    flat_in = incoming.reshape(-1)
    send_blocks = jnp.take(blocks, flat_in, axis=0).reshape(peers, cap, half_aux, nvd)
    send_vir = jnp.take(vir_energy, flat_in, axis=0).reshape(peers, cap, nvd)
    send_occ = jnp.take(occ_energy, flat_in).reshape(peers, cap)
    send_size = jnp.take(domain_size, flat_in).astype(jnp.float32).reshape(peers, cap)
    got_blocks = lax.all_to_all(send_blocks, "orb", split_axis=0, concat_axis=0, tiled=True)
    got_vir, got_occ, got_size = (
        lax.all_to_all(send_vir, "orb", split_axis=0, concat_axis=0, tiled=True),
        lax.all_to_all(send_occ, "orb", split_axis=0, concat_axis=0, tiled=True),
        lax.all_to_all(send_size, "orb", split_axis=0, concat_axis=0, tiled=True),
    )
    partner = jnp.take(got_blocks.reshape(peers * cap, half_aux, nvd), target, axis=0).reshape(
        occ_dev, per_orb, half_aux, nvd
    )
    partner_vir = jnp.take(got_vir.reshape(peers * cap, nvd), target, axis=0).reshape(
        occ_dev, per_orb, nvd
    )
    partner_occ = jnp.take(got_occ.reshape(-1), target).reshape(occ_dev, per_orb)
    partner_size = jnp.take(got_size.reshape(-1), target).reshape(occ_dev, per_orb)
    half = nvd // lax.axis_size("aux")
    integrals = lax.psum_scatter(
        jnp.einsum("oqa,opqb->aopb", blocks, partner, preferred_element_type=jnp.float32),
        "aux",
        scatter_dimension=0,
        tiled=True,
    )
    row_start = lax.axis_index("aux") * half
    rows = row_start + jnp.arange(half, dtype=jnp.int32)
    cols = jnp.arange(nvd, dtype=jnp.int32).astype(jnp.float32)
    mask = (rows[:, None, None, None] < domain_size[None, :, None, None]) & (
        cols[None, None, None, :] < partner_size[None, :, :, None]
    )
    integrals = jnp.where(mask, integrals, jnp.zeros_like(integrals))
    vir_rows = lax.dynamic_slice_in_dim(vir_energy, row_start, half, 1)
    gap = (
        vir_rows.T[:, :, None, None]
        + partner_vir[None, :, :, :]
        - occ_energy[None, :, None, None]
        - partner_occ[None, :, :, None]
    )
    amp_rows = (-integrals / gap).astype(jnp.bfloat16)
    partial_energy = jnp.sum(integrals * amp_rows.astype(jnp.float32), axis=(0, 3))
    energy = lax.psum(partial_energy, "aux").reshape(pair_dev) / nvd
    density = jnp.einsum(
        "aopb,copb->oac",
        amp_rows,
        lax.all_gather(amp_rows, "aux", axis=0, tiled=True),
        preferred_element_type=jnp.float32,
    )
    return (energy, density)


def fits_line(mesh):
    return mesh.shape["orb"] == 8 and mesh.shape["aux"] == 2


TINY = pl.CostEstimate(flops=1, bytes_accessed=1, transcendentals=0)
PARAMS = pltpu.CompilerParams(vmem_limit_bytes=LIMIT)
LIGHT = pltpu.CompilerParams(vmem_limit_bytes=LIMIT // 4)


def lists_kernel(cap, vir, occ, size, owner, slot, small, hit):
    n, (count, nvd) = hit.shape[0], vir.shape

    def column(row, m):
        eye = lax.broadcasted_iota(i32, (m, m), 0) == lax.broadcasted_iota(i32, (m, m), 1)
        return jnp.sum(jnp.where(eye, row, 0.0), axis=1, keepdims=True)

    down = lax.broadcasted_iota(i32, (n, n), 0).astype(f32)
    along = lax.broadcasted_iota(i32, (n, n), 1).astype(f32)
    owner_row = owner[...].astype(f32)
    owner_col = column(owner_row, n)
    before = (owner_col == owner_row) & (along < down)
    target = owner_col * cap + jnp.sum(jnp.where(before, 1.0, 0.0), axis=1, keepdims=True)
    found = target == along
    hit[...] = jnp.where(found, 1.0, 0.0)
    small[...] = jnp.zeros_like(small)
    small[:count, :nvd] = vir[...]
    lane = lax.broadcasted_iota(i32, (count, 128), 1)
    occ_col, size_col = column(occ[...], count), column(size[...].astype(f32), count)
    small[:count, nvd:] = jnp.where(lane == 0, occ_col, jnp.where(lane == 1, size_col, 0.0))
    small[count : count + 1, :n] = jnp.sum(jnp.where(found, down, 0.0), axis=0, keepdims=True)
    slot_col = column(slot[...].astype(f32), n)
    small[count : count + 1, 128 : 128 + n] = jnp.sum(
        jnp.where(found, slot_col, 0.0), axis=0, keepdims=True
    )


def lists(vir, occ, size, owner, slot, cap):
    count, nvd = vir.shape
    n = slot.shape[0]
    return pl.pallas_call(
        lambda *refs: lists_kernel(cap, *refs),
        out_shape=(
            jax.ShapeDtypeStruct((count + 8, nvd + 128), f32),
            jax.ShapeDtypeStruct((n, n), f32),
        ),
        in_specs=[VMEM] * 5,
        out_specs=(VMEM, VMEM),
        compiler_params=PARAMS,
        cost_estimate=TINY,
        name="lists",
    )(vir, occ.reshape(1, -1), size.reshape(1, -1), owner.reshape(1, -1), slot.reshape(1, -1))


ORDER, SLOT, SIZE_I, SIZE_J, HEAD = range(5)
MIDDLE, COLUMN = 8, 9


def pick(one, values):
    return lax.dot_general(
        one, values, (((0,), (0,)), ((), ())),
        precision=lax.Precision.HIGHEST, preferred_element_type=f32,
    )


def tables_kernel(cap, per_orb, meta, *refs):
    smalls, outs = refs[:8], refs[8:]
    count, nvd = smalls[0].shape[0] - 8, smalls[0].shape[1] - 128
    n = 8 * cap
    me, col0 = meta[0], meta[1]
    z, y = me // 2, me % 2
    lower = z < 2
    middle = jnp.where((z == 1) | (z == 2), 1, 0)
    places = [z, z ^ 1, jnp.where(lower, 2, 1), jnp.where(lower, 3, 0)]
    head = [(2 * p + y) * cap for p in places] + [(2 * p + 1 - y) * cap for p in places]
    lane = lax.broadcasted_iota(i32, (1, 128), 1)
    head_row = jnp.zeros((1, 128), i32)
    for k, value in enumerate(head + [middle, col0]):
        head_row = jnp.where(lane == k, value, head_row)
    orbitals = jnp.concatenate([x[:count, :] for x in smalls], axis=0)
    columns = jnp.where(col0 == 0, orbitals[:, : nvd // 2], orbitals[:, nvd // 2 : nvd])
    extra = orbitals[:, nvd:]

    def build(x, tbl, rows=None):
        order = smalls[x][count : count + 1, :n].astype(i32)
        slots = smalls[x][count : count + 1, 128 : 128 + n].astype(i32)
        tbl[...] = jnp.zeros_like(tbl)
        tbl[HEAD : HEAD + 1, :] = head_row
        tbl[SLOT : SLOT + 1, :n] = slots
        if rows is None:
            return
        tbl[ORDER : ORDER + 1, :n] = order
        pair = lax.broadcasted_iota(i32, (1, n), 1)
        owner = sum(jnp.where(pair >= k * cap, 1, 0) for k in range(1, 8))
        index = (owner ^ me) * count + slots
        theirs = jnp.where(lax.broadcasted_iota(i32, (8 * count, n), 0) == index, 1.0, 0.0)
        first = sum(jnp.where(order >= k * per_orb, 1, 0) for k in range(1, count))
        mine = jnp.where(lax.broadcasted_iota(i32, (count, n), 0) == first, 1.0, 0.0)
        own = smalls[x][:count, nvd:]
        rows[...] = pick(theirs, columns) - (pick(theirs, extra)[:, :1] + pick(mine, own)[:, :1])
        tbl[SIZE_I : SIZE_I + 1, :n] = pick(own, mine)[1:2, :].astype(i32)
        tbl[SIZE_J : SIZE_J + 1, :n] = pick(extra, theirs)[1:2, :].astype(i32) - col0

    build(0, outs[0], outs[1])
    build(2, outs[2], outs[3])
    build(1, outs[4])
    build(3, outs[5])


def tables_of(meta, smalls, cap, per_orb, half):
    table = jax.ShapeDtypeStruct((8, 128), i32)
    rows = jax.ShapeDtypeStruct((8 * cap, half), f32)
    return pl.pallas_call(
        lambda *refs: tables_kernel(cap, per_orb, *refs),
        out_shape=(table, rows, table, rows, table, table),
        in_specs=[SMEM] + [VMEM] * 8,
        out_specs=[VMEM] * 6,
        compiler_params=LIGHT,
        cost_estimate=TINY,
        name="tables",
    )(meta, *smalls)


def pack_kernel(jobs, tables, *refs):
    tbls, rest = refs[:tables], refs[tables:]
    outs = refs[-len(jobs) :]
    middle = tbls[0][HEAD, MIDDLE] == 1

    def gather(out, sources, tbl, call):
        base = tbl[HEAD, call]
        for q in range(out.shape[0]):
            for r in range(out.shape[1]):
                out[q, r] = sources[q][tbl[SLOT, base + r]]

    for out, (table, call, halves, only_middle) in zip(outs, jobs):
        sources, rest = rest[:halves], rest[halves:]
        if only_middle:
            pl.when(middle)(functools.partial(gather, out, sources, tbls[table], call))
        else:
            gather(out, sources, tbls[table], call)


def pack(tbls, jobs, cap, after=()):
    operands = [x for _, _, sources, _ in jobs for x in sources]
    kinds = [(table, call, len(sources), middle) for table, call, sources, middle in jobs]
    block = operands[0].shape[1:]
    return pl.pallas_call(
        lambda *refs: pack_kernel(kinds, len(tbls), *refs),
        out_shape=[jax.ShapeDtypeStruct((k[2], cap) + block, bf16) for k in kinds],
        in_specs=[SMEM] * len(tbls) + [VMEM] * len(operands) + [HBM] * len(after),
        out_specs=[VMEM] * len(jobs),
        compiler_params=LIGHT,
        cost_estimate=TINY,
        name="pack",
    )(*tbls, *operands, *after)


def turn_kernel(*refs):
    half = len(refs) // 2
    for x, out in zip(refs[:half], refs[half:]):
        for r in range(x.shape[0]):
            out[r] = x[r].T


def turn(arrays):
    count, rows, cols = arrays[0].shape
    step = 4 if count % 4 == 0 else 1
    n = len(arrays)
    return pl.pallas_call(
        turn_kernel,
        out_shape=[jax.ShapeDtypeStruct((count, cols, rows), bf16)] * n,
        grid=(count // step,),
        in_specs=[pl.BlockSpec((step, rows, cols), lambda i: (i, 0, 0))] * n,
        out_specs=[pl.BlockSpec((step, cols, rows), lambda i: (i, 0, 0))] * n,
        compiler_params=PARAMS,
        cost_estimate=TINY,
        name="turn",
    )(*arrays)


def amplitudes_kernel(mode, call, per_orb, groups, tbl, rows, vcol, *refs):
    client = mode == "client"
    if client:
        tout = refs[-1]
        left, rest = refs[:4], refs[4:]
    else:
        tout, eout = refs[-2:]
        left, rest = refs[:2], refs[2:]
    places = []
    for arrays in groups:
        if arrays == 1:
            places.append([rest[0].at[0], rest[0].at[1]])
        elif len(rest[0].shape) == 4:
            places.append([rest[0].at[0], rest[1].at[0]])
        else:
            places.append(rest[:2])
        rest = rest[arrays:]
    cap = rows.shape[0] // 8
    nvd, half = vcol.shape[1:]
    base = pl.multiple_of(tbl[HEAD, call], cap)
    middle = tbl[HEAD, MIDDLE] == 1
    row8 = rows[pl.ds(base, cap), :]

    def gap(r, i):
        return vcol[i] + row8[r : r + 1, :]

    def make(r):
        p = tbl[ORDER, base + r]
        i = lax.div(p, per_orb)
        slot = r if mode == "asked" else tbl[SLOT, base + r]
        b0, b1 = [x[slot] for x in places[0]]
        if len(places) == 2:
            b0, b1 = [jnp.where(middle, b, x[slot]) for b, x in zip((b0, b1), places[1])]

        def product(x0, x1):
            return jnp.dot(x0[i], b0, preferred_element_type=f32) + jnp.dot(
                x1[i], b1, preferred_element_type=f32
            )

        if client:
            here, there = product(left[0], left[1]), product(left[3], left[2])
            first = tbl[HEAD, COLUMN] == 0
            k = jnp.concatenate(
                [jnp.where(first, here, there), jnp.where(first, there, here)], axis=0
            )
        else:
            k = product(left[0], left[1])
        live_a = lax.broadcasted_iota(i32, (nvd, half), 0)
        live_b = lax.broadcasted_iota(i32, (nvd, half), 1)
        live = (live_a < tbl[SIZE_I, base + r]) & (live_b < tbl[SIZE_J, base + r])
        k = jnp.where(live, k, 0.0)
        t = (-k / gap(r, i)).astype(bf16)
        if client:
            tout[r] = t
            return None
        tout[p] = t
        return jnp.sum(k * t.astype(f32), axis=0, keepdims=True)

    def take(r):
        p = tbl[ORDER, base + r]
        ready = rest[0][r]
        tout[p] = ready
        t = ready.astype(f32)
        return -jnp.sum(t * t * gap(r, lax.div(p, per_orb)), axis=0, keepdims=True)

    def each(step):
        parts = [step(r) for r in range(cap)]
        if not client:
            eout[pl.ds(base, cap), :] = jnp.concatenate(parts, axis=0)

    if mode == "served":
        pl.when(middle)(lambda: each(make))
        pl.when(jnp.logical_not(middle))(lambda: each(take))
    elif client:
        pl.when(middle)(lambda: each(make))
    else:
        each(make)


def amplitudes(mode, call, per_orb, tables, left, groups, cap, held=(), after=(), ready=()):
    tbl, rows, vcol = tables
    occ, nvd, half = vcol.shape
    client = mode == "client"
    sources = [x for group in groups for x in group]
    blocks = (rows, vcol, *left, *sources, *ready)
    operands = (tbl, *blocks, *after)
    aliases = {len(operands) + k: k for k in range(len(held))}
    if client:
        out_shape = jax.ShapeDtypeStruct((cap, nvd, half), bf16)
        out_specs = VMEM
    else:
        out_shape = (
            jax.ShapeDtypeStruct((occ * per_orb, nvd, half), bf16),
            jax.ShapeDtypeStruct((occ * per_orb, half), f32),
        )
        out_specs = (VMEM, VMEM)
    return pl.pallas_call(
        lambda *refs: amplitudes_kernel(mode, call, per_orb, [len(g) for g in groups], *refs),
        out_shape=out_shape,
        in_specs=[SMEM] + [VMEM] * len(blocks) + [HBM] * len(after) + [VMEM] * len(held),
        out_specs=out_specs,
        input_output_aliases=aliases,
        compiler_params=LIGHT,
        cost_estimate=TINY,
        name="amplitudes",
    )(*operands, *held)


def density_kernel(start, t, mine, away):
    count, half = mine.shape[:2]
    per_orb = t.shape[0] // count
    first = pl.multiple_of(start[0], half)
    for o in range(count):
        own = range(o * per_orb, (o + 1) * per_orb)
        right = jnp.concatenate([t[k] for k in own], axis=1)
        for out, row in ((away, pl.multiple_of(half - first, half)), (mine, first)):
            left = jnp.concatenate([t[k, pl.ds(row, half), :] for k in own], axis=1)
            out[o] = lax.dot_general(
                left, right, (((1,), (1,)), ((), ())), preferred_element_type=f32
            ).astype(out.dtype)


def densities(t_all, start, per_orb, half):
    npair, nvd, _ = t_all.shape
    shape = jax.ShapeDtypeStruct((npair // per_orb, half, nvd), f32)
    return pl.pallas_call(
        density_kernel,
        out_shape=(shape, jax.ShapeDtypeStruct(shape.shape, bf16)),
        in_specs=[SMEM, VMEM],
        out_specs=(VMEM, VMEM),
        compiler_params=LIGHT,
        cost_estimate=TINY,
        name="densities",
    )(start.reshape(1), t_all)


def line_plan(blocks, vir_energy, occ_energy, domain_size, partner_owner, partner_slot):
    occ, qa, nvd = blocks.shape
    pair_dev = partner_slot.shape[0]
    per_orb = pair_dev // occ
    peers = 8
    cap = pair_dev // peers
    half = nvd // 2
    me, core = lax.axis_index("orb"), lax.axis_index("aux")
    col0 = core * half

    def pp(x, perm):
        return lax.ppermute(x, "orb", perm)

    def swap_core(x):
        return lax.ppermute(x, "aux", [(0, 1), (1, 0)])

    def flip(bits):
        return [(o, o ^ bits) for o in range(peers)]

    cross = [(2, 4), (3, 5), (4, 2), (5, 3)]
    outward = [(2, 0), (3, 1), (4, 6), (5, 7)]
    diagonal = [(2, 1), (3, 0), (4, 7), (5, 6)]
    y_middle = [(2, 3), (3, 2), (4, 5), (5, 4)]

    small, hit = lists(vir_energy, occ_energy, domain_size, partner_owner, partner_slot, cap)
    smalls = [small] + [pp(small, flip(bits)) for bits in range(1, peers)]

    other = swap_core(blocks)
    own = [lax.dynamic_slice_in_dim(x, col0, half, 2) for x in (blocks, other)]
    sent, smalls = lax.optimization_barrier((own[0], smalls))
    mid = [pp(x, cross) for x in (sent, own[1])]
    near = [pp(x, flip(2)) for x in (sent, own[1])]
    tbl, rows, client_tbl, client_rows, beside_list, relay_list = tables_of(
        jnp.stack([me, col0]), smalls, cap, per_orb, half
    )
    lists_of = [beside_list, relay_list]

    def spread(vir):
        return jnp.broadcast_to(vir[:, :, None], (occ, nvd, half))

    tables = (tbl, rows, spread(vir_energy))
    client = (client_tbl, client_rows, spread(smalls[2][:occ, :nvd]))

    def own_pairs(k, mode, groups, held=(), after=(), ready=()):
        return amplitudes(mode, k, per_orb, tables, left, groups, cap, held, after, ready)

    (packed,) = pack(lists_of, [(0, 0, own, False)], cap)
    beside = pp(packed, flip(1))
    left = turn([blocks, other])
    held = own_pairs(0, "slots", [own], after=(packed,))
    first, held = lax.optimization_barrier((near[0], held))
    far = [pp(first, cross)]
    across = [swap_core(first)]
    (packed,) = pack(lists_of, [(0, 1, [first], False)], cap, after=(held[1], mid[0]))
    beside_near = [pp(packed, flip(1))]
    held = own_pairs(4, "asked", [[beside]], held, (packed, beside_near[0]))
    second, held = lax.optimization_barrier((near[1], held))
    far.append(pp(second, cross))
    across.append(swap_core(second))
    near = [first, second]
    packed = pack(lists_of, [(1, 2, mid, True), (0, 2, mid, True)], cap, after=(held[1],))
    third_diagonal, third = pp(packed[0], diagonal), pp(packed[1], y_middle)
    (packed,) = pack(lists_of, [(0, 1, [second], False)], cap, after=(packed[0],))
    beside_near.append(pp(packed, flip(1)))
    client_left = turn(near + across)
    gone = amplitudes("client", 2, per_orb, client, client_left, [mid], cap, after=(packed,))
    ready_2 = pp(gone, outward)
    held = own_pairs(1, "slots", [near], held, (gone, third_diagonal))
    jobs = [(1, 3, far[:1], True), (0, 3, far[:1], True)]
    packed = pack(lists_of, jobs, cap, after=(held[1],))
    fourth_diagonal, fourth = [pp(packed[0], diagonal)], [pp(packed[1], y_middle)]
    held = own_pairs(2, "served", [mid], held, (packed[0],), (ready_2,))
    held = own_pairs(5, "asked", [beside_near], held)
    (packed,) = pack(lists_of, [(1, 3, far[1:], True)], cap, after=(held[1],))
    fourth_diagonal.append(pp(packed, diagonal))
    gone = amplitudes("client", 3, per_orb, client, client_left, [far], cap, after=(packed,))
    ready_3 = pp(gone, outward)
    (packed,) = pack(
        lists_of, [(0, 3, far[1:], True)], cap, after=(gone,)
    )
    fourth.append(pp(packed, y_middle))
    held = own_pairs(
        6, "asked", [[third], [third_diagonal]], held, (packed, fourth[0], fourth_diagonal[0])
    )
    held = own_pairs(3, "served", [far], held, (fourth_diagonal[1],), (ready_3,))
    t_all, e_all = own_pairs(7, "asked", [fourth, fourth_diagonal], held)

    energy = jnp.sum(hit * jnp.sum(e_all, axis=1)[None, :], axis=1)
    t_all, energy = lax.optimization_barrier((t_all, energy))
    crossed = swap_core(energy)
    mine, away = densities(t_all, col0, per_orb, half)
    density = mine + swap_core(away).astype(f32)
    return ((energy + crossed) / nvd, density)


def solution(mesh):
    in_specs = (
        P(("mol", "orb"), "aux", None),
        P(("mol", "orb"), None),
        P(("mol", "orb")),
        P(("mol", "orb")),
        P(("mol", "orb"), None),
        P(("mol", "orb")),
    )
    out_specs = (P(("mol", "orb")), P(("mol", "orb"), "aux", None))
    return jax.shard_map(
        line_plan if fits_line(mesh) else by_requests, mesh=mesh, in_specs=in_specs, out_specs=out_specs, check_vma=False
    )
```

```python
import functools

import jax
import jax.numpy as jnp
from jax import lax
from jax.experimental import pallas as pl
from jax.experimental.pallas import tpu as pltpu
from jax.sharding import PartitionSpec as P

f32, bf16, i32 = jnp.float32, jnp.bfloat16, jnp.int32
HBM = pl.BlockSpec(memory_space=pltpu.HBM)
SMEM = pl.BlockSpec(memory_space=pltpu.SMEM)
VMEM = pl.BlockSpec(memory_space=pltpu.VMEM)
LIMIT = 12 * 1024 * 1024


def slot_ranks(owner):
    count = owner.shape[0]
    order = jnp.arange(count, dtype=jnp.int32)
    same = (owner[:, None] == owner[None, :]) & (order[None, :] < order[:, None])
    return jnp.sum(same.astype(jnp.int32), axis=1)


def by_requests(blocks, vir_energy, occ_energy, domain_size, partner_owner, partner_slot):
    occ_dev, half_aux, nvd = blocks.shape
    pair_dev = partner_slot.shape[0]
    per_orb = pair_dev // occ_dev
    peers = lax.axis_size("orb")
    cap = max(2, (pair_dev + peers - 1) // peers)
    owner = partner_owner[:, 0]
    ranks = slot_ranks(owner)
    target = owner * cap + ranks
    wanted = (target[:, None] == jnp.arange(peers * cap, dtype=jnp.int32)[None, :]).astype(
        jnp.int32
    )
    requests = jnp.sum(wanted * partner_slot[:, None], axis=0).reshape(peers, cap)
    incoming = lax.all_to_all(requests, "orb", split_axis=0, concat_axis=0, tiled=True)
    flat_in = incoming.reshape(-1)
    send_blocks = jnp.take(blocks, flat_in, axis=0).reshape(peers, cap, half_aux, nvd)
    send_vir = jnp.take(vir_energy, flat_in, axis=0).reshape(peers, cap, nvd)
    send_occ = jnp.take(occ_energy, flat_in).reshape(peers, cap)
    send_size = jnp.take(domain_size, flat_in).astype(jnp.float32).reshape(peers, cap)
    got_blocks = lax.all_to_all(send_blocks, "orb", split_axis=0, concat_axis=0, tiled=True)
    got_vir, got_occ, got_size = (
        lax.all_to_all(send_vir, "orb", split_axis=0, concat_axis=0, tiled=True),
        lax.all_to_all(send_occ, "orb", split_axis=0, concat_axis=0, tiled=True),
        lax.all_to_all(send_size, "orb", split_axis=0, concat_axis=0, tiled=True),
    )
    partner = jnp.take(got_blocks.reshape(peers * cap, half_aux, nvd), target, axis=0).reshape(
        occ_dev, per_orb, half_aux, nvd
    )
    partner_vir = jnp.take(got_vir.reshape(peers * cap, nvd), target, axis=0).reshape(
        occ_dev, per_orb, nvd
    )
    partner_occ = jnp.take(got_occ.reshape(-1), target).reshape(occ_dev, per_orb)
    partner_size = jnp.take(got_size.reshape(-1), target).reshape(occ_dev, per_orb)
    half = nvd // lax.axis_size("aux")
    integrals = lax.psum_scatter(
        jnp.einsum("oqa,opqb->aopb", blocks, partner, preferred_element_type=jnp.float32),
        "aux",
        scatter_dimension=0,
        tiled=True,
    )
    row_start = lax.axis_index("aux") * half
    rows = row_start + jnp.arange(half, dtype=jnp.int32)
    cols = jnp.arange(nvd, dtype=jnp.int32).astype(jnp.float32)
    mask = (rows[:, None, None, None] < domain_size[None, :, None, None]) & (
        cols[None, None, None, :] < partner_size[None, :, :, None]
    )
    integrals = jnp.where(mask, integrals, jnp.zeros_like(integrals))
    vir_rows = lax.dynamic_slice_in_dim(vir_energy, row_start, half, 1)
    gap = (
        vir_rows.T[:, :, None, None]
        + partner_vir[None, :, :, :]
        - occ_energy[None, :, None, None]
        - partner_occ[None, :, :, None]
    )
    amp_rows = (-integrals / gap).astype(jnp.bfloat16)
    partial_energy = jnp.sum(integrals * amp_rows.astype(jnp.float32), axis=(0, 3))
    energy = lax.psum(partial_energy, "aux").reshape(pair_dev) / nvd
    density = jnp.einsum(
        "aopb,copb->oac",
        amp_rows,
        lax.all_gather(amp_rows, "aux", axis=0, tiled=True),
        preferred_element_type=jnp.float32,
    )
    return (energy, density)


def fits_line(mesh):
    return mesh.shape["orb"] == 8 and mesh.shape["aux"] == 2


TINY = pl.CostEstimate(flops=1, bytes_accessed=1, transcendentals=0)
PARAMS = pltpu.CompilerParams(vmem_limit_bytes=LIMIT)
LIGHT = pltpu.CompilerParams(vmem_limit_bytes=LIMIT // 4)


def lists_kernel(cap, vir, vectors, small, hit):
    n, (count, nvd) = hit.shape[0], vir.shape
    occ, size = vectors[0:1, :count], vectors[1:2, :count]
    owner, slot = vectors[2:3, :n], vectors[3:4, :n]

    def column(row, m):
        eye = lax.broadcasted_iota(i32, (m, m), 0) == lax.broadcasted_iota(i32, (m, m), 1)
        return jnp.sum(jnp.where(eye, row, 0.0), axis=1, keepdims=True)

    down = lax.broadcasted_iota(i32, (n, n), 0).astype(f32)
    along = lax.broadcasted_iota(i32, (n, n), 1).astype(f32)
    owner_row = owner
    owner_col = column(owner_row, n)
    before = (owner_col == owner_row) & (along < down)
    target = owner_col * cap + jnp.sum(jnp.where(before, 1.0, 0.0), axis=1, keepdims=True)
    found = target == along
    hit[...] = jnp.where(found, 1.0, 0.0)
    small[...] = jnp.zeros_like(small)
    small[:count, :nvd] = vir[...]
    lane = lax.broadcasted_iota(i32, (count, 128), 1)
    occ_col, size_col = column(occ, count), column(size, count)
    small[:count, nvd:] = jnp.where(lane == 0, occ_col, jnp.where(lane == 1, size_col, 0.0))
    small[count : count + 1, :n] = jnp.sum(jnp.where(found, down, 0.0), axis=0, keepdims=True)
    slot_col = column(slot, n)
    small[count : count + 1, 128 : 128 + n] = jnp.sum(
        jnp.where(found, slot_col, 0.0), axis=0, keepdims=True
    )


def lists(vir, occ, size, owner, slot, cap):
    count, nvd = vir.shape
    n = slot.shape[0]
    vectors = jnp.stack(
        [
            jnp.pad(x.reshape(-1).astype(f32), (0, 128 - x.size))
            for x in (occ, size, owner, slot)
        ]
    )
    return pl.pallas_call(
        lambda *refs: lists_kernel(cap, *refs),
        out_shape=(
            jax.ShapeDtypeStruct((count + 8, nvd + 128), f32),
            jax.ShapeDtypeStruct((n, n), f32),
        ),
        in_specs=[VMEM] * 2,
        out_specs=(VMEM, VMEM),
        compiler_params=PARAMS,
        cost_estimate=TINY,
        name="lists",
    )(vir, vectors)


ORDER, SLOT, SIZE_I, SIZE_J, HEAD = range(5)
MIDDLE, COLUMN = 8, 9


def pick(one, values):
    return lax.dot_general(
        one, values, (((0,), (0,)), ((), ())),
        precision=lax.Precision.HIGHEST, preferred_element_type=f32,
    )


def tables_kernel(cap, per_orb, meta, *refs):
    smalls, outs = refs[:8], refs[8:]
    count, nvd = smalls[0].shape[0] - 8, smalls[0].shape[1] - 128
    n = 8 * cap
    me, col0 = meta[0], meta[1]
    z, y = me // 2, me % 2
    lower = z < 2
    middle = jnp.where((z == 1) | (z == 2), 1, 0)
    places = [z, z ^ 1, jnp.where(lower, 2, 1), jnp.where(lower, 3, 0)]
    head = [(2 * p + y) * cap for p in places] + [(2 * p + 1 - y) * cap for p in places]
    lane = lax.broadcasted_iota(i32, (1, 128), 1)
    head_row = jnp.zeros((1, 128), i32)
    for k, value in enumerate(head + [middle, col0]):
        head_row = jnp.where(lane == k, value, head_row)
    orbitals = jnp.concatenate([x[:count, :] for x in smalls], axis=0)
    columns = jnp.where(col0 == 0, orbitals[:, : nvd // 2], orbitals[:, nvd // 2 : nvd])
    extra = orbitals[:, nvd:]

    def build(x, tbl, rows=None):
        order = smalls[x][count : count + 1, :n].astype(i32)
        slots = smalls[x][count : count + 1, 128 : 128 + n].astype(i32)
        tbl[...] = jnp.zeros_like(tbl)
        tbl[HEAD : HEAD + 1, :] = head_row
        tbl[SLOT : SLOT + 1, :n] = slots
        if rows is None:
            return
        tbl[ORDER : ORDER + 1, :n] = order
        pair = lax.broadcasted_iota(i32, (1, n), 1)
        owner = sum(jnp.where(pair >= k * cap, 1, 0) for k in range(1, 8))
        index = (owner ^ me) * count + slots
        theirs = jnp.where(lax.broadcasted_iota(i32, (8 * count, n), 0) == index, 1.0, 0.0)
        first = sum(jnp.where(order >= k * per_orb, 1, 0) for k in range(1, count))
        mine = jnp.where(lax.broadcasted_iota(i32, (count, n), 0) == first, 1.0, 0.0)
        own = smalls[x][:count, nvd:]
        rows[...] = pick(theirs, columns) - (pick(theirs, extra)[:, :1] + pick(mine, own)[:, :1])
        tbl[SIZE_I : SIZE_I + 1, :n] = pick(own, mine)[1:2, :].astype(i32)
        tbl[SIZE_J : SIZE_J + 1, :n] = pick(extra, theirs)[1:2, :].astype(i32) - col0

    build(0, outs[0], outs[1])
    build(2, outs[2], outs[3])
    build(1, outs[4])
    build(3, outs[5])


def tables_of(meta, smalls, cap, per_orb, half):
    table = jax.ShapeDtypeStruct((8, 128), i32)
    rows = jax.ShapeDtypeStruct((8 * cap, half), f32)
    return pl.pallas_call(
        lambda *refs: tables_kernel(cap, per_orb, *refs),
        out_shape=(table, rows, table, rows, table, table),
        in_specs=[SMEM] + [VMEM] * 8,
        out_specs=[VMEM] * 6,
        compiler_params=LIGHT,
        cost_estimate=TINY,
        name="tables",
    )(meta, *smalls)


def pack_kernel(jobs, tables, *refs):
    tbls, rest = refs[:tables], refs[tables:]
    outs = refs[-len(jobs) :]
    middle = tbls[0][HEAD, MIDDLE] == 1

    def gather(out, sources, tbl, call):
        base = tbl[HEAD, call]
        for q in range(out.shape[0]):
            for r in range(out.shape[1]):
                out[q, r] = sources[q][tbl[SLOT, base + r]]

    for out, (table, call, halves, only_middle) in zip(outs, jobs):
        sources, rest = rest[:halves], rest[halves:]
        if only_middle:
            pl.when(middle)(functools.partial(gather, out, sources, tbls[table], call))
        else:
            gather(out, sources, tbls[table], call)


def pack(tbls, jobs, cap, after=()):
    operands = [x for _, _, sources, _ in jobs for x in sources]
    kinds = [(table, call, len(sources), middle) for table, call, sources, middle in jobs]
    block = operands[0].shape[1:]
    return pl.pallas_call(
        lambda *refs: pack_kernel(kinds, len(tbls), *refs),
        out_shape=[jax.ShapeDtypeStruct((k[2], cap) + block, bf16) for k in kinds],
        in_specs=[SMEM] * len(tbls) + [VMEM] * len(operands) + [HBM] * len(after),
        out_specs=[VMEM] * len(jobs),
        compiler_params=LIGHT,
        cost_estimate=TINY,
        name="pack",
    )(*tbls, *operands, *after)


def turn_kernel(*refs):
    half = len(refs) // 2
    for x, out in zip(refs[:half], refs[half:]):
        for r in range(x.shape[0]):
            out[r] = x[r].T


def turn(arrays):
    count, rows, cols = arrays[0].shape
    step = 4 if count % 4 == 0 else 1
    n = len(arrays)
    return pl.pallas_call(
        turn_kernel,
        out_shape=[jax.ShapeDtypeStruct((count, cols, rows), bf16)] * n,
        grid=(count // step,),
        in_specs=[pl.BlockSpec((step, rows, cols), lambda i: (i, 0, 0))] * n,
        out_specs=[pl.BlockSpec((step, cols, rows), lambda i: (i, 0, 0))] * n,
        compiler_params=PARAMS,
        cost_estimate=TINY,
        name="turn",
    )(*arrays)


def amplitudes_kernel(mode, call, per_orb, groups, tbl, rows, vcol, *refs):
    client = mode == "client"
    if client:
        tout = refs[-1]
        left, rest = refs[:4], refs[4:]
    else:
        tout, eout = refs[-2:]
        left, rest = refs[:2], refs[2:]
    places = []
    for arrays in groups:
        if arrays == 1:
            places.append([rest[0].at[0], rest[0].at[1]])
        elif len(rest[0].shape) == 4:
            places.append([rest[0].at[0], rest[1].at[0]])
        else:
            places.append(rest[:2])
        rest = rest[arrays:]
    cap = rows.shape[0] // 8
    nvd, half = vcol.shape[1:]
    base = pl.multiple_of(tbl[HEAD, call], cap)
    middle = tbl[HEAD, MIDDLE] == 1
    row8 = rows[pl.ds(base, cap), :]

    def gap(r, i):
        return vcol[i] + row8[r : r + 1, :]

    def make(r):
        p = tbl[ORDER, base + r]
        i = lax.div(p, per_orb)
        slot = r if mode == "asked" else tbl[SLOT, base + r]
        b0, b1 = [x[slot] for x in places[0]]
        if len(places) == 2:
            b0, b1 = [jnp.where(middle, b, x[slot]) for b, x in zip((b0, b1), places[1])]

        def product(x0, x1):
            return jnp.dot(x0[i], b0, preferred_element_type=f32) + jnp.dot(
                x1[i], b1, preferred_element_type=f32
            )

        if client:
            here, there = product(left[0], left[1]), product(left[3], left[2])
            first = tbl[HEAD, COLUMN] == 0
            k = jnp.concatenate(
                [jnp.where(first, here, there), jnp.where(first, there, here)], axis=0
            )
        else:
            k = product(left[0], left[1])
        live_a = lax.broadcasted_iota(i32, (nvd, half), 0)
        live_b = lax.broadcasted_iota(i32, (nvd, half), 1)
        live = (live_a < tbl[SIZE_I, base + r]) & (live_b < tbl[SIZE_J, base + r])
        k = jnp.where(live, k, 0.0)
        t = (-k / gap(r, i)).astype(bf16)
        if client:
            tout[r] = t
            return None
        tout[p] = t
        return jnp.sum(k * t.astype(f32), axis=0, keepdims=True)

    def take(r):
        p = tbl[ORDER, base + r]
        ready = rest[0][r]
        tout[p] = ready
        t = ready.astype(f32)
        return -jnp.sum(t * t * gap(r, lax.div(p, per_orb)), axis=0, keepdims=True)

    def each(step):
        parts = [step(r) for r in range(cap)]
        if not client:
            eout[pl.ds(base, cap), :] = jnp.concatenate(parts, axis=0)

    if mode == "served":
        pl.when(middle)(lambda: each(make))
        pl.when(jnp.logical_not(middle))(lambda: each(take))
    elif client:
        pl.when(middle)(lambda: each(make))
    else:
        each(make)


def amplitudes(mode, call, per_orb, tables, left, groups, cap, held=(), after=(), ready=()):
    tbl, rows, vcol = tables
    occ, nvd, half = vcol.shape
    client = mode == "client"
    sources = [x for group in groups for x in group]
    blocks = (rows, vcol, *left, *sources, *ready)
    operands = (tbl, *blocks, *after)
    aliases = {len(operands) + k: k for k in range(len(held))}
    if client:
        out_shape = jax.ShapeDtypeStruct((cap, nvd, half), bf16)
        out_specs = VMEM
    else:
        out_shape = (
            jax.ShapeDtypeStruct((occ * per_orb, nvd, half), bf16),
            jax.ShapeDtypeStruct((occ * per_orb, half), f32),
        )
        out_specs = (VMEM, VMEM)
    return pl.pallas_call(
        lambda *refs: amplitudes_kernel(mode, call, per_orb, [len(g) for g in groups], *refs),
        out_shape=out_shape,
        in_specs=[SMEM] + [VMEM] * len(blocks) + [HBM] * len(after) + [VMEM] * len(held),
        out_specs=out_specs,
        input_output_aliases=aliases,
        compiler_params=LIGHT,
        cost_estimate=TINY,
        name="amplitudes",
    )(*operands, *held)


def density_kernel(start, t, mine, away):
    count, half = mine.shape[:2]
    per_orb = t.shape[0] // count
    first = pl.multiple_of(start[0], half)
    for o in range(count):
        own = range(o * per_orb, (o + 1) * per_orb)
        right = jnp.concatenate([t[k] for k in own], axis=1)
        for out, row in ((away, pl.multiple_of(half - first, half)), (mine, first)):
            left = jnp.concatenate([t[k, pl.ds(row, half), :] for k in own], axis=1)
            out[o] = lax.dot_general(
                left, right, (((1,), (1,)), ((), ())), preferred_element_type=f32
            ).astype(out.dtype)


def densities(t_all, start, per_orb, half):
    npair, nvd, _ = t_all.shape
    shape = jax.ShapeDtypeStruct((npair // per_orb, half, nvd), f32)
    return pl.pallas_call(
        density_kernel,
        out_shape=(shape, jax.ShapeDtypeStruct(shape.shape, bf16)),
        in_specs=[SMEM, VMEM],
        out_specs=(VMEM, VMEM),
        compiler_params=LIGHT,
        cost_estimate=TINY,
        name="densities",
    )(start.reshape(1), t_all)


def line_plan(blocks, vir_energy, occ_energy, domain_size, partner_owner, partner_slot):
    occ, qa, nvd = blocks.shape
    pair_dev = partner_slot.shape[0]
    per_orb = pair_dev // occ
    peers = 8
    cap = pair_dev // peers
    half = nvd // 2
    me, core = lax.axis_index("orb"), lax.axis_index("aux")
    col0 = core * half

    def pp(x, perm):
        return lax.ppermute(x, "orb", perm)

    def swap_core(x):
        return lax.ppermute(x, "aux", [(0, 1), (1, 0)])

    def flip(bits):
        return [(o, o ^ bits) for o in range(peers)]

    cross = [(2, 4), (3, 5), (4, 2), (5, 3)]
    outward = [(2, 0), (3, 1), (4, 6), (5, 7)]
    diagonal = [(2, 1), (3, 0), (4, 7), (5, 6)]
    y_middle = [(2, 3), (3, 2), (4, 5), (5, 4)]

    small, hit = lists(vir_energy, occ_energy, domain_size, partner_owner, partner_slot, cap)
    smalls = [small] + [pp(small, flip(bits)) for bits in range(1, peers)]

    other = swap_core(blocks)
    own = [lax.dynamic_slice_in_dim(x, col0, half, 2) for x in (blocks, other)]
    sent, smalls = lax.optimization_barrier((own[0], smalls))
    mid = [pp(x, cross) for x in (sent, own[1])]
    near = [pp(x, flip(2)) for x in (sent, own[1])]
    tbl, rows, client_tbl, client_rows, beside_list, relay_list = tables_of(
        jnp.stack([me, col0]), smalls, cap, per_orb, half
    )
    lists_of = [beside_list, relay_list]

    def spread(vir):
        return jnp.broadcast_to(vir[:, :, None], (occ, nvd, half))

    tables = (tbl, rows, spread(vir_energy))
    client = (client_tbl, client_rows, spread(smalls[2][:occ, :nvd]))

    def own_pairs(k, mode, groups, held=(), after=(), ready=()):
        return amplitudes(mode, k, per_orb, tables, left, groups, cap, held, after, ready)

    (packed,) = pack(lists_of, [(0, 0, own, False)], cap)
    beside = pp(packed, flip(1))
    left = turn([blocks, other])
    held = own_pairs(0, "slots", [own], after=(packed,))
    first, held = lax.optimization_barrier((near[0], held))
    far = [pp(first, cross)]
    across = [swap_core(first)]
    (packed,) = pack(lists_of, [(0, 1, [first], False)], cap, after=(held[1], mid[0]))
    beside_near = [pp(packed, flip(1))]
    held = own_pairs(4, "asked", [[beside]], held, (packed, beside_near[0]))
    second, held = lax.optimization_barrier((near[1], held))
    far.append(pp(second, cross))
    across.append(swap_core(second))
    near = [first, second]
    packed = pack(lists_of, [(1, 2, mid, True), (0, 2, mid, True)], cap, after=(held[1],))
    third_diagonal, third = pp(packed[0], diagonal), pp(packed[1], y_middle)
    (packed,) = pack(lists_of, [(0, 1, [second], False)], cap, after=(packed[0],))
    beside_near.append(pp(packed, flip(1)))
    client_left = turn(near + across)
    gone = amplitudes("client", 2, per_orb, client, client_left, [mid], cap, after=(packed,))
    ready_2 = pp(gone, outward)
    held = own_pairs(1, "slots", [near], held, (gone, third_diagonal))
    jobs = [(1, 3, far[:1], True), (0, 3, far[:1], True)]
    packed = pack(lists_of, jobs, cap, after=(held[1],))
    fourth_diagonal, fourth = [pp(packed[0], diagonal)], [pp(packed[1], y_middle)]
    held = own_pairs(2, "served", [mid], held, (packed[0],), (ready_2,))
    held = own_pairs(5, "asked", [beside_near], held)
    (packed,) = pack(lists_of, [(1, 3, far[1:], True)], cap, after=(held[1],))
    fourth_diagonal.append(pp(packed, diagonal))
    gone = amplitudes("client", 3, per_orb, client, client_left, [far], cap, after=(packed,))
    ready_3 = pp(gone, outward)
    (packed,) = pack(
        lists_of, [(0, 3, far[1:], True)], cap, after=(gone,)
    )
    fourth.append(pp(packed, y_middle))
    held = own_pairs(
        6, "asked", [[third], [third_diagonal]], held, (packed, fourth[0], fourth_diagonal[0])
    )
    held = own_pairs(3, "served", [far], held, (fourth_diagonal[1],), (ready_3,))
    t_all, e_all = own_pairs(7, "asked", [fourth, fourth_diagonal], held)

    mine, away = densities(t_all, col0, per_orb, half)
    density = mine + swap_core(away).astype(f32)

    energy = jnp.sum(hit * jnp.sum(e_all, axis=1)[None, :], axis=1)
    energy = (energy + swap_core(energy)) / nvd
    return (energy, density)


def solution(mesh):
    in_specs = (
        P(("mol", "orb"), "aux", None),
        P(("mol", "orb"), None),
        P(("mol", "orb")),
        P(("mol", "orb")),
        P(("mol", "orb"), None),
        P(("mol", "orb")),
    )
    out_specs = (P(("mol", "orb")), P(("mol", "orb"), "aux", None))
    return jax.shard_map(
        line_plan if fits_line(mesh) else by_requests, mesh=mesh, in_specs=in_specs, out_specs=out_specs, check_vma=False
    )
```
